32 devices in a mesh: img: 4 (over y, x), row: 8 (over z, core).
Axes of the slice: x: 2, y: 2, z: 4, core: 2. Of those that a mesh axis runs over, the one named last changes fastest.
Arguments:
- kspace: float32 [2, 4, 16, 2, 320, 320], P(None, 'img', None, None, 'row'), may hold values from -6 to 6
- coil_maps: float32 [2, 4, 16, 2, 320, 320], P(None, 'img', None, None, 'row'), may hold values from -1.5 to 1.5
- target: float32 [2, 4, 2, 320, 320], P(None, 'img', None, 'row'), may hold values from -6 to 6
- row_mask: int32 [2, 4, 320], P(None, 'img'), may hold values from 0 to 1, as said below
- foreground: int32 [2, 4, 320, 320], P(None, 'img', 'row'), may hold values from 0 to 1
- anatomy: int32 [2, 4], P(None, 'img'), may hold values from 0 to 1
- first_weight: float32 [9, 64, 2], replicated, may hold values from -1.5 to 1.5
- middle_weight: float32 [3, 9, 64, 64], replicated, may hold values from -0.25 to 0.25
- last_weight: float32 [9, 2, 64], replicated, may hold values from -0.25 to 0.25
- norm_gains: float32 [4, 64], replicated, may hold values from 0.5 to 1.5
- norm_shifts: float32 [4, 64], replicated, may hold values from -1.5 to 1.5
- extra_params: float32 [3], replicated, may hold values from -1.5 to 1.5
- first_mean: float32 [9, 64, 2], replicated, may hold values from -0.0048828125 to 0.0048828125
- first_square: float32 [9, 64, 2], replicated, may hold values from 1.0986328e-08 to 4.3945313e-08
- middle_mean: float32 [3, 9, 64, 64], replicated, may hold values from -0.0048828125 to 0.0048828125
- middle_square: float32 [3, 9, 64, 64], replicated, may hold values from 1.0986328e-08 to 4.3945313e-08
- last_mean: float32 [9, 2, 64], replicated, may hold values from -0.0048828125 to 0.0048828125
- last_square: float32 [9, 2, 64], replicated, may hold values from 1.0986328e-08 to 4.3945313e-08
- gains_mean: float32 [4, 64], replicated, may hold values from -0.0048828125 to 0.0048828125
- gains_square: float32 [4, 64], replicated, may hold values from 1.0986328e-08 to 4.3945313e-08
- shifts_mean: float32 [4, 64], replicated, may hold values from -0.0048828125 to 0.0048828125
- shifts_square: float32 [4, 64], replicated, may hold values from 1.0986328e-08 to 4.3945313e-08
- extra_mean: float32 [3], replicated, may hold values from -0.046875 to 0.046875
- extra_square: float32 [3], replicated, may hold values from 1.0986328e-06 to 4.394531e-06
Outputs:
- first_updated: float32 [9, 64, 2], replicated
- first_average: float32 [9, 64, 2], replicated
- first_energy: float32 [9, 64, 2], replicated
- first_copy: bfloat16 [9, 64, 2], replicated
- middle_updated: float32 [3, 9, 64, 64], replicated
- middle_average: float32 [3, 9, 64, 64], replicated
- middle_energy: float32 [3, 9, 64, 64], replicated
- middle_copy: bfloat16 [3, 9, 64, 64], replicated
- last_updated: float32 [9, 2, 64], replicated
- last_average: float32 [9, 2, 64], replicated
- last_energy: float32 [9, 2, 64], replicated
- last_copy: bfloat16 [9, 2, 64], replicated
- gains_updated: float32 [4, 64], replicated
- gains_average: float32 [4, 64], replicated
- gains_energy: float32 [4, 64], replicated
- shifts_updated: float32 [4, 64], replicated
- shifts_average: float32 [4, 64], replicated
- shifts_energy: float32 [4, 64], replicated
- extra_updated: float32 [3], replicated
- extra_average: float32 [3], replicated
- extra_energy: float32 [3], replicated
- loss_total: float32 [], replicated
- pixel_count: int32 [], replicated
The draws below stay inside these ranges and needn't reach their ends.
Inputs may be any that keep to these rules, and one draw needn't show every extreme that they name: `row_mask`: 1 on every row with |row - 160| < 20.
All inputs are finite; a program needn't handle non-finite values.
Results may differ from the reference program's by a relative error of at most 0.004.
The reference program's roundings to bfloat16 on the way count: a program that leaves them out, or rounds other values in their place, can miss the bound.
Values may be sent and summed in bfloat16 or wider, within the bound.
A program may use at most 320 MiB of HBM per device.

```python
import math
import jax
import jax.numpy as jnp
from jax import lax

RES = 320
COILS = 16
BRAIN_COILS = 12
CH = 64
MICRO = 2
UNROLLS = 1
CG_STEPS = 2
STEP = 10
IMAGES_MB = 4


def draw_row_mask(key, part):
    key = jax.random.fold_in(key, 11)
    index = jnp.arange(RES, dtype=jnp.int32)
    centre = jnp.abs(index - RES // 2) < RES // 16
    picked = jax.random.randint(key, (MICRO, IMAGES_MB, RES), 0, 4) == 0
    return jnp.where(centre[None, None, :] | picked, 1, 0).astype(jnp.int32)


def draw_foreground(key, part):
    key = jax.random.fold_in(key, 23)
    height = jnp.arange(RES, dtype=jnp.int32)[None, None, :, None]
    images = jnp.arange(IMAGES_MB, dtype=jnp.int32)[None, :, None, None]
    level = 120 * (RES + 2 * height) * (IMAGES_MB + 2 * images) // (RES * IMAGES_MB)
    level = jnp.minimum(level, 950)
    drawn = jax.random.randint(key, (MICRO, IMAGES_MB, RES, RES), 0, 1000)
    return jnp.where(drawn < level, 1, 0).astype(jnp.int32)


def set_ends(entries, rng, least, top_value):
    extent = entries.shape
    index_at = [jax.random.randint(jax.random.fold_in(rng, axis), (), 0, extent[axis]) for axis in range(len(extent))]
    entries = entries.at[tuple(index_at)].set(least)
    longest = extent.index(max(extent))
    index_at[longest] = (index_at[longest] + 1) % extent[longest]
    return entries.at[tuple(index_at)].set(top_value)


def level_of(own_key, shape, pieces, least, high):
    level, own = 1.0, jax.random.fold_in(own_key, 6)
    for position, parts in pieces:
        draws = jnp.exp(jax.random.uniform(jax.random.fold_in(own, position), (parts,), jnp.float32, least / len(pieces), high / len(pieces)))
        level = level * jnp.repeat(draws, shape[position] // parts).reshape([-1 if axis == position else 1 for axis in range(len(shape))])
    return level


def gaussian(own_key, shape, scale, bound, shards=(), kind=jnp.bfloat16):
    entries = jax.random.normal(own_key, shape, jnp.float32) * scale
    if len(shards) > 0:
        entries = level_of(own_key, shape, shards, -0.22, 0.18) * entries
    return jnp.clip(entries, min=-bound, max=bound).astype(kind)


def setup_inputs(seed: int = 0) -> dict:
    seeds = jax.random.split(jax.random.key(seed), 25)
    return {
        "kspace": gaussian(seeds[0], (MICRO, IMAGES_MB, COILS, 2, RES, RES), 1.0, 6.0, ((1, 4), (4, 8)), jnp.float32),
        "coil_maps": gaussian(seeds[1], (MICRO, IMAGES_MB, COILS, 2, RES, RES), 0.25, 1.5, ((1, 4), (4, 8)), jnp.float32),
        "target": gaussian(seeds[2], (MICRO, IMAGES_MB, 2, RES, RES), 1.0, 6.0, ((1, 4), (3, 8)), jnp.float32),
        "row_mask": draw_row_mask(jax.random.fold_in(seeds[24], 71), 0),
        "foreground": draw_foreground(jax.random.fold_in(seeds[24], 71), 0),
        "anatomy": set_ends(jax.random.randint(seeds[5], (MICRO, IMAGES_MB), 0, 2), jax.random.fold_in(seeds[5], 1), 0, 1).astype(jnp.int32),
        "first_weight": gaussian(seeds[6], (9, CH, 2), 18 ** -0.5, 1.5, (), jnp.float32),
        "middle_weight": gaussian(seeds[7], (3, 9, CH, CH), (9 * CH) ** -0.5, 0.25, (), jnp.float32),
        "last_weight": gaussian(seeds[8], (9, 2, CH), (9 * CH) ** -0.5, 0.25, (), jnp.float32),
        "norm_gains": jnp.clip(1.0 + 0.1 * jax.random.normal(seeds[9], (4, CH), jnp.float32), 0.5, 1.5),
        "norm_shifts": gaussian(seeds[10], (4, CH), 0.3, 1.5, (), jnp.float32),
        "extra_params": gaussian(seeds[11], (3,), 0.5, 1.5, (), jnp.float32),
        "first_mean": gaussian(seeds[12], (9, CH, 2), (0.33 * (MICRO * IMAGES_MB * RES * RES) ** -0.5), 0.0048828125, (), jnp.float32),
        "first_square": jnp.clip(jnp.exp(jax.random.uniform(seeds[13], (9, CH, 2), jnp.float32, math.log(1.0986328291551217e-08), math.log(4.394531316620487e-08))), 1.0986328291551217e-08, 4.394531316620487e-08),
        "middle_mean": gaussian(seeds[14], (3, 9, CH, CH), (0.33 * (MICRO * IMAGES_MB * RES * RES) ** -0.5), 0.0048828125, (), jnp.float32),
        "middle_square": jnp.clip(jnp.exp(jax.random.uniform(seeds[15], (3, 9, CH, CH), jnp.float32, math.log(1.0986328291551217e-08), math.log(4.394531316620487e-08))), 1.0986328291551217e-08, 4.394531316620487e-08),
        "last_mean": gaussian(seeds[16], (9, 2, CH), (0.33 * (MICRO * IMAGES_MB * RES * RES) ** -0.5), 0.0048828125, (), jnp.float32),
        "last_square": jnp.clip(jnp.exp(jax.random.uniform(seeds[17], (9, 2, CH), jnp.float32, math.log(1.0986328291551217e-08), math.log(4.394531316620487e-08))), 1.0986328291551217e-08, 4.394531316620487e-08),
        "gains_mean": gaussian(seeds[18], (4, CH), (0.33 * (MICRO * IMAGES_MB * RES * RES) ** -0.5), 0.0048828125, (), jnp.float32),
        "gains_square": jnp.clip(jnp.exp(jax.random.uniform(seeds[19], (4, CH), jnp.float32, math.log(1.0986328291551217e-08), math.log(4.394531316620487e-08))), 1.0986328291551217e-08, 4.394531316620487e-08),
        "shifts_mean": gaussian(seeds[20], (4, CH), (0.33 * (MICRO * IMAGES_MB * RES * RES) ** -0.5), 0.0048828125, (), jnp.float32),
        "shifts_square": jnp.clip(jnp.exp(jax.random.uniform(seeds[21], (4, CH), jnp.float32, math.log(1.0986328291551217e-08), math.log(4.394531316620487e-08))), 1.0986328291551217e-08, 4.394531316620487e-08),
        "extra_mean": gaussian(seeds[22], (3,), (3.0 * (MICRO * IMAGES_MB * RES * RES) ** -0.5), 0.046875, (), jnp.float32),
        "extra_square": jnp.clip(jnp.exp(jax.random.uniform(seeds[23], (3,), jnp.float32, math.log(1.0986327652062755e-06), math.log(4.394531060825102e-06))), 1.0986327652062755e-06, 4.394531060825102e-06),
    }


@jax.custom_vjp
def low(v):
    return lax.optimization_barrier(v.astype(jnp.bfloat16)).astype(jnp.float32)

@jax.custom_vjp
def low_back(v):
    return v

def low_keep(v):
    return (low(v), None)

def low_pass(kept, grad):
    return (grad,)

def back_keep(v):
    return (v, None)

def back_low(kept, grad):
    return (low(grad),)
low.defvjp(low_keep, low_pass)
low_back.defvjp(back_keep, back_low)
PRECISE = lax.Precision.HIGHEST
EPS_NORM = 1e-05
BETA_ONE = 0.9
BETA_TWO = 0.999
ADAM_EPS = 1e-08
DECAY_RATE = 0.01
LEARN_RATES = (0.3, 0.05, 0.05, 0.4, 0.4, 0.4)

def dft_table(length, direction):
    index = jnp.arange(length, dtype=jnp.int32)
    phase = (index[:, None] * index[None, :] % length).astype(jnp.float32) * (2.0 * jnp.pi / length)
    factor = 1.0 / jnp.sqrt(jnp.float32(length))
    cosine = jnp.cos(phase) * factor
    sine = jnp.sin(phase) * factor * direction
    return jnp.stack([jnp.stack([cosine, -sine], 1), jnp.stack([sine, cosine], 1)], 0)

def along_width(field, table):
    return jnp.einsum('bcprw,pwqk->bcqrk', field, table, precision=PRECISE)

def along_height(field, table):
    return jnp.einsum('bcprw,prqk->bcqkw', field, table, precision=PRECISE)

def expand(image, maps):
    real_part, imag_part = (image[:, None, 0], image[:, None, 1])
    maps_re, maps_im = (maps[:, :, 0], maps[:, :, 1])
    return jnp.stack([maps_re * real_part - maps_im * imag_part, maps_re * imag_part + maps_im * real_part], 2)

def combine(field, maps):
    field_re, field_im = (field[:, :, 0], field[:, :, 1])
    maps_re, maps_im = (maps[:, :, 0], maps[:, :, 1])
    return jnp.stack([lax.optimization_barrier(jnp.sum(maps_re * field_re + maps_im * field_im, 1)), lax.optimization_barrier(jnp.sum(maps_re * field_im - maps_im * field_re, 1))], 1)

def normal_apply(image, maps, mask_rows, forward, inverse):
    spectrum = along_height(along_width(expand(image, maps), forward), forward) * mask_rows
    return combine(along_width(along_height(spectrum, inverse), inverse), maps)

def convolve(activation, weight):
    kernel = weight.reshape(3, 3, weight.shape[1], weight.shape[2]).transpose(2, 3, 0, 1)
    return lax.conv_general_dilated(activation, kernel, (1, 1), ((1, 1), (1, 1)), dimension_numbers=('NCHW', 'OIHW', 'NCHW'), precision=PRECISE)

def cnn_apply(image, weights, gains, shifts, offset):
    activation = low(image)
    for layer_index in range(4):
        linear = low_back(convolve(activation, weights[layer_index]))
        average = lax.optimization_barrier(jnp.mean(linear, axis=(0, 2, 3), keepdims=True))
        centred = linear - average
        spread = lax.optimization_barrier(jnp.mean(centred * centred, axis=(0, 2, 3), keepdims=True))
        normed = centred * lax.rsqrt(spread + EPS_NORM)
        shaped = gains[layer_index][None, :, None, None] * normed + shifts[layer_index][None, :, None, None]
        activation = low(jax.nn.silu(shaped))
    result = low_back(convolve(activation, weights[4]))
    return image + result + offset[None, :, None, None]

def inner(left, right):
    return lax.optimization_barrier(jnp.sum(left * right, axis=(1, 2, 3)))

def per_image(values):
    return values[:, None, None, None]

def solve(rhs, penalty, operator):
    state = jnp.zeros_like(rhs)
    residue = rhs
    search = rhs
    norm_now = inner(residue, residue)
    for iterate in range(CG_STEPS):
        mapped = operator(search) + penalty * search
        stepsize = norm_now / inner(search, mapped)
        state = state + per_image(stepsize) * search
        residue = residue - per_image(stepsize) * mapped
        norm_next = inner(residue, residue)
        search = residue + per_image(norm_next / norm_now) * search
        norm_now = norm_next
    return state

def adamw(weight, gradient, moment_one, moment_two, rate):
    first_new = BETA_ONE * moment_one + (1.0 - BETA_ONE) * gradient
    second_new = BETA_TWO * moment_two + (1.0 - BETA_TWO) * gradient * gradient
    corrected = first_new / (1.0 - BETA_ONE ** STEP)
    divisor = jnp.sqrt(second_new / (1.0 - BETA_TWO ** STEP)) + ADAM_EPS
    updated = weight - rate * (corrected / divisor + DECAY_RATE * weight)
    return (updated, first_new, second_new)

def reference(kspace, coil_maps, target, row_mask, foreground, anatomy, first_weight, middle_weight, last_weight, norm_gains, norm_shifts, extra_params, first_mean, first_square, middle_mean, middle_square, last_mean, last_square, gains_mean, gains_square, shifts_mean, shifts_square, extra_mean, extra_square):
    forward = dft_table(RES, 1.0)
    inverse = dft_table(RES, -1.0)
    pixel_total = jnp.sum(foreground)
    inv_count = 1.0 / pixel_total.astype(jnp.float32)
    params = (first_weight, middle_weight, last_weight, norm_gains, norm_shifts, extra_params)
    gradients = jax.tree.map(jnp.zeros_like, params)
    loss_total = jnp.float32(0.0)
    cnn_checked = jax.checkpoint(cnn_apply)
    normal_checked = jax.checkpoint(normal_apply)
    for microbatch in range(MICRO):
        limit = jnp.where(anatomy[microbatch] == 0, BRAIN_COILS, COILS)
        coil_on = (jnp.arange(COILS)[None, :] < limit[:, None]).astype(jnp.float32)
        maps = coil_maps[microbatch] * coil_on[:, :, None, None, None]
        mask_rows = row_mask[microbatch].astype(jnp.float32)[:, None, None, :, None]
        zero_filled = combine(along_width(along_height(kspace[microbatch] * mask_rows, inverse), inverse), maps)
        fg_mask = foreground[microbatch].astype(jnp.float32)[:, None]
        truth = target[microbatch]

        def operator(image):
            return normal_checked(image, maps, mask_rows, forward, inverse)

        def micro_loss(weights_in):
            first_w, middle_w, last_w, gains, shifts, extra = weights_in
            middle_low = low(middle_w)
            conv_weights = [low(first_w), middle_low[0], middle_low[1], middle_low[2], low(last_w)]
            penalty = jnp.exp(extra[2])
            state = zero_filled
            for unroll in range(UNROLLS):
                denoised = cnn_checked(state, conv_weights, gains, shifts, extra[:2])
                state = solve(zero_filled + penalty * denoised, penalty, operator)
            difference = state - truth
            return jnp.sum(fg_mask * difference * difference)
        loss_value, pullback = jax.vjp(micro_loss, params)
        micro_grads, = pullback(inv_count)
        gradients = jax.tree.map(lambda total, part: total + part, gradients, micro_grads)
        loss_total = loss_total + loss_value
    moments = ((first_mean, first_square), (middle_mean, middle_square), (last_mean, last_square), (gains_mean, gains_square), (shifts_mean, shifts_square), (extra_mean, extra_square))
    results = []
    for group in range(6):
        updated, first_new, second_new = adamw(params[group], gradients[group], moments[group][0], moments[group][1], LEARN_RATES[group])
        results.extend([updated, first_new, second_new])
        if group < 3:
            results.append(updated.astype(jnp.bfloat16))
    return tuple(results) + (loss_total, pixel_total.astype(jnp.int32))
```

```python
import functools

import jax
import jax.numpy as jnp
import numpy as np
from jax import lax
from jax.experimental import pallas as pl
from jax.experimental.pallas import tpu as pltpu
from jax.sharding import PartitionSpec as P

COILS = 16
BRAIN_COILS = 12
UNROLLS = 1
CG_STEPS = 2
STEP = 10


PRECISE = lax.Precision.HIGHEST
EPS_NORM = 1e-05
BETA_ONE = 0.9
BETA_TWO = 0.999
ADAM_EPS = 1e-08
DECAY_RATE = 0.01
LEARN_RATES = (0.3, 0.05, 0.05, 0.4, 0.4, 0.4)


def with_halo(cells, sides, width):
    for axis, dim in sides:
        count = lax.axis_size(axis)
        ends = count - 1
        head = lax.slice_in_dim(cells, 0, width, axis=dim)
        tail = lax.slice_in_dim(cells, cells.shape[dim] - width, cells.shape[dim], axis=dim)
        cells = jnp.concatenate(
            [
                lax.ppermute(tail, axis, [(i, (i + 1) % count) for i in range(ends)]),
                cells,
                lax.ppermute(head, axis, [((i + 1) % count, i) for i in range(ends)]),
            ],
            axis=dim,
        )
    return cells


def dft_table(length, direction):
    index = jnp.arange(length, dtype=jnp.int32)
    phase = (index[:, None] * index[None, :] % length).astype(jnp.float32) * (2.0 * jnp.pi / length)
    factor = 1.0 / jnp.sqrt(jnp.float32(length))
    cosine = jnp.cos(phase) * factor
    sine = jnp.sin(phase) * factor * direction
    return jnp.stack([jnp.stack([cosine, -sine], 1), jnp.stack([sine, cosine], 1)], 0)


def along_width(field, table):
    return jnp.einsum("bcprw,pwqk->bcqrk", field, table, precision=PRECISE)


def along_height(field, table):
    return jnp.einsum("bcprw,prqk->bcqkw", field, table, precision=PRECISE)


def expand(image, maps):
    real_part, imag_part = (image[:, None, 0], image[:, None, 1])
    maps_re, maps_im = (maps[:, :, 0], maps[:, :, 1])
    return jnp.stack(
        [maps_re * real_part - maps_im * imag_part, maps_re * imag_part + maps_im * real_part], 2
    )


def combine(field, maps):
    field_re, field_im = (field[:, :, 0], field[:, :, 1])
    maps_re, maps_im = (maps[:, :, 0], maps[:, :, 1])
    return jnp.stack(
        [
            jnp.sum(maps_re * field_re + maps_im * field_im, 1),
            jnp.sum(maps_re * field_im - maps_im * field_re, 1),
        ],
        1,
    )


def to_columns(field):
    return lax.all_to_all(
        field.astype(jnp.bfloat16), "row", split_axis=4, concat_axis=3, tiled=True
    ).astype(field.dtype)


def to_rows(field):
    return lax.all_to_all(
        field.astype(jnp.bfloat16), "row", split_axis=3, concat_axis=4, tiled=True
    ).astype(field.dtype)


def make_normal(maps, mask_rows, forward, inverse, measured):
    zero_filled = combine(to_rows(along_height(measured * mask_rows, inverse)), maps)

    def normal(image):
        spectrum = to_columns(along_width(expand(image, maps), forward))
        spectrum = along_height(spectrum, forward) * mask_rows
        spectrum = to_rows(along_height(spectrum, inverse))
        return combine(along_width(spectrum, inverse), maps)

    return (normal, zero_filled)


def inner(left, right):
    return jnp.sum(left * right, axis=(1, 2, 3))


def per_image(values):
    return values[:, None, None, None]


def row_sums(values):
    return lax.psum(values, "row")


def solve(rhs, penalty, normal):
    state = jnp.zeros_like(rhs)
    residue = rhs
    search = rhs
    norm_now = row_sums(inner(residue, residue))
    kept = []
    for iterate in range(CG_STEPS):
        mapped = normal(search) + penalty * search
        curvature = row_sums(inner(search, mapped))
        stepsize = norm_now / curvature
        state = state + per_image(stepsize) * search
        residue = residue - per_image(stepsize) * mapped
        norm_next = row_sums(inner(residue, residue))
        kept.append((search, mapped, residue, norm_now, norm_next, curvature))
        search = residue + per_image(norm_next / norm_now) * search
        norm_now = norm_next
    return (state, kept)


def solve_backward(state_grad, kept, rhs, denoised, penalty, normal):
    search_grad = jnp.zeros_like(rhs)
    residue_grad = jnp.zeros_like(rhs)
    norm_grad = jnp.zeros(rhs.shape[0], jnp.float32)
    penalty_part = jnp.float32(0.0)
    for iterate in reversed(range(CG_STEPS)):
        search, mapped, residue, norm_now, norm_next, curvature = kept[iterate]
        factor_grad, along_search, joint_mapped, residue_mapped = lax.psum(
            (
                inner(search_grad, search),
                inner(state_grad, search),
                inner(residue_grad + search_grad, mapped),
                inner(residue, mapped),
            ),
            "row",
        )
        stepsize = norm_now / curvature
        factor = norm_next / norm_now
        norm_total = norm_grad + factor_grad / norm_now
        residue_full = residue_grad + search_grad + per_image(2.0 * norm_total) * residue
        stepsize_grad = along_search - (joint_mapped + 2.0 * norm_total * residue_mapped)
        curvature_grad = -stepsize_grad * norm_now / (curvature * curvature)
        mapped_grad = -per_image(stepsize) * residue_full + per_image(curvature_grad) * search
        penalty_part = penalty_part + jnp.sum(mapped_grad * search)
        search_grad = (
            per_image(factor) * search_grad
            + per_image(stepsize) * state_grad
            + per_image(curvature_grad) * mapped
            + normal(mapped_grad)
            + penalty * mapped_grad
        )
        residue_grad = residue_full
        norm_grad = -factor_grad * norm_next / (norm_now * norm_now) + stepsize_grad / curvature
    rhs_grad = residue_grad + search_grad + per_image(2.0 * norm_grad) * rhs
    penalty_part = penalty_part + jnp.sum(rhs_grad * denoised)
    return (penalty * rhs_grad, penalty_part)


def conv_forward(activation, weight):
    height, breadth = (activation.shape[2], activation.shape[3])
    padded = with_halo(activation, (("row", 2),), 1)
    padded = jnp.pad(padded, ((0, 0), (0, 0), (0, 0), (1, 1)))
    summed = jnp.zeros((activation.shape[0], weight.shape[1], height, breadth), jnp.float32)
    for tap_index in range(9):
        window = padded[
            :, :, tap_index // 3 : tap_index // 3 + height, tap_index % 3 : tap_index % 3 + breadth
        ]
        summed = summed + jnp.einsum(
            "oi,birw->borw", weight[tap_index], window, preferred_element_type=jnp.float32
        )
    return (summed, padded)


def conv_backward(upstream, padded, weight, need_input):
    height, breadth = (upstream.shape[2], upstream.shape[3])
    weight_grad = jnp.stack(
        [
            jnp.einsum(
                "borw,birw->oi",
                upstream,
                padded[
                    :,
                    :,
                    tap_index // 3 : tap_index // 3 + height,
                    tap_index % 3 : tap_index % 3 + breadth,
                ],
                preferred_element_type=jnp.float32,
            )
            for tap_index in range(9)
        ]
    )
    if not need_input:
        return (weight_grad, None)
    widened = with_halo(upstream, (("row", 2),), 1)
    widened = jnp.pad(widened, ((0, 0), (0, 0), (0, 0), (1, 1)))
    summed = jnp.zeros((upstream.shape[0], weight.shape[2], height, breadth), jnp.float32)
    for tap_index in range(9):
        start_r = 2 - tap_index // 3
        start_c = 2 - tap_index % 3
        window = widened[:, :, start_r : start_r + height, start_c : start_c + breadth]
        summed = summed + jnp.einsum(
            "oi,borw->birw", weight[tap_index], window, preferred_element_type=jnp.float32
        )
    return (weight_grad, summed)


def norm_sums(values):
    return lax.psum(values, ("img", "row"))


def channel(values):
    return values[None, :, None, None]


def cnn_forward(image, weights, gains, shifts, offset, pixels):
    activation = image.astype(jnp.bfloat16)
    kept = []
    for layer_index in range(4):
        linear, padded = conv_forward(activation, weights[layer_index])
        average = norm_sums(jnp.sum(linear, axis=(0, 2, 3))) / pixels
        centred = linear - channel(average)
        spread = norm_sums(jnp.sum(centred * centred, axis=(0, 2, 3))) / pixels
        inv_std = lax.rsqrt(spread + EPS_NORM)
        normed = centred * channel(inv_std)
        shaped = channel(gains[layer_index]) * normed + channel(shifts[layer_index])
        activation = jax.nn.silu(shaped).astype(jnp.bfloat16)
        kept.append((padded, normed, shaped, inv_std))
    result, padded = conv_forward(activation, weights[4])
    kept.append(padded)
    return (image + result + channel(offset), kept)


def cnn_backward(denoised_grad, kept, weights, gains, pixels, need_input):
    offset_grad = jnp.sum(denoised_grad, axis=(0, 2, 3))
    weight_grads = [None] * 5
    gain_grads = [None] * 4
    shift_grads = [None] * 4
    weight_grads[4], upstream = conv_backward(
        denoised_grad.astype(jnp.bfloat16), kept[4], weights[4], True
    )
    for layer_index in (3, 2, 1, 0):
        padded, normed, shaped, inv_std = kept[layer_index]
        sigmoid_val = jax.nn.sigmoid(shaped)
        shaped_grad = upstream * sigmoid_val * (1.0 + shaped * (1.0 - sigmoid_val))
        shift_local = jnp.sum(shaped_grad, axis=(0, 2, 3))
        gain_local = jnp.sum(shaped_grad * normed, axis=(0, 2, 3))
        shift_total, gain_total = lax.psum((shift_local, gain_local), ("img", "row"))
        gain_vec = gains[layer_index]
        linear_grad = channel(inv_std) * (
            shaped_grad * channel(gain_vec)
            - channel(gain_vec * shift_total / pixels)
            - normed * channel(gain_vec * gain_total / pixels)
        )
        shift_grads[layer_index] = shift_local
        gain_grads[layer_index] = gain_local
        weight_grads[layer_index], upstream = conv_backward(
            linear_grad.astype(jnp.bfloat16),
            padded,
            weights[layer_index],
            layer_index > 0 or need_input,
        )
    image_grad = None
    return (image_grad, weight_grads, jnp.stack(gain_grads), jnp.stack(shift_grads), offset_grad)


def adamw(weight, gradient, moment_one, moment_two, rate):
    first_new = BETA_ONE * moment_one + (1.0 - BETA_ONE) * gradient
    second_new = BETA_TWO * moment_two + (1.0 - BETA_TWO) * gradient * gradient
    corrected = first_new / (1.0 - BETA_ONE**STEP)
    divisor = jnp.sqrt(second_new / (1.0 - BETA_TWO**STEP)) + ADAM_EPS
    updated = weight - rate * (corrected / divisor + DECAY_RATE * weight)
    return (updated, first_new, second_new)


def general_local(arrays):
    (
        kspace, coil_maps, target, row_mask, foreground, anatomy, first_weight, middle_weight, last_weight, norm_gains, norm_shifts, extra_params,
    ) = arrays
    length = kspace.shape[-1]
    forward = dft_table(length, 1.0)
    inverse = dft_table(length, -1.0)
    pixel_total = lax.psum(jnp.sum(foreground).astype(jnp.float32), ("img", "row"))
    inv_count = 1.0 / pixel_total
    middle_low = middle_weight.astype(jnp.bfloat16)
    conv_weights = [
        first_weight.astype(jnp.bfloat16),
        middle_low[0],
        middle_low[1],
        middle_low[2],
        last_weight.astype(jnp.bfloat16),
    ]
    penalty = jnp.exp(extra_params[2])
    offset = extra_params[:2]
    images_here = kspace.shape[1]
    pixels = images_here * kspace.shape[4] * length * lax.axis_size("img") * lax.axis_size("row")
    first_grad = jnp.zeros_like(first_weight)
    middle_grad = jnp.zeros_like(middle_weight)
    last_grad = jnp.zeros_like(last_weight)
    gains_grad = jnp.zeros_like(norm_gains)
    shifts_grad = jnp.zeros_like(norm_shifts)
    offset_grad = jnp.zeros((2,), jnp.float32)
    penalty_grad = jnp.float32(0.0)
    loss_part = jnp.float32(0.0)
    for microbatch in range(kspace.shape[0]):
        limit = jnp.where(anatomy[microbatch] == 0, BRAIN_COILS, COILS)
        coil_on = (jnp.arange(kspace.shape[2])[None, :] < limit[:, None]).astype(jnp.float32)
        maps = coil_maps[microbatch] * coil_on[:, :, None, None, None]
        mask_rows = row_mask[microbatch].astype(jnp.float32)[:, None, None, :, None]
        measured = to_columns(along_width(kspace[microbatch], inverse))
        normal, zero_filled = make_normal(maps, mask_rows, forward, inverse, measured)
        state = zero_filled
        unroll = 0
        denoised, cnn_kept = cnn_forward(
            state, conv_weights, norm_gains, norm_shifts, offset, pixels
        )
        rhs = zero_filled + penalty * denoised
        state, cg_kept = solve(rhs, penalty, normal)
        saved = [(cnn_kept, cg_kept, rhs, denoised)]
        fg_mask = foreground[microbatch].astype(jnp.float32)[:, None]
        difference = state - target[microbatch]
        loss_part = loss_part + jnp.sum(fg_mask * difference * difference)
        state_grad = inv_count * 2.0 * fg_mask * difference
        for unroll in reversed(range(UNROLLS)):
            cnn_kept, cg_kept, rhs, denoised = saved[unroll]
            denoised_grad, penalty_part = solve_backward(
                state_grad, cg_kept, rhs, denoised, penalty, normal
            )
            penalty_grad = penalty_grad + penalty_part
            state_grad, weight_grads, gain_part, shift_part, offset_part = cnn_backward(
                denoised_grad, cnn_kept, conv_weights, norm_gains, pixels, unroll > 0
            )
            first_grad = first_grad + weight_grads[0]
            middle_grad = middle_grad + jnp.stack(weight_grads[1:4])
            last_grad = last_grad + weight_grads[4]
            gains_grad = gains_grad + gain_part
            shifts_grad = shifts_grad + shift_part
            offset_grad = offset_grad + offset_part
    extra_grad = jnp.concatenate([offset_grad, (penalty * penalty_grad)[None]])
    totals = lax.psum(
        (first_grad, middle_grad, last_grad, gains_grad, shifts_grad, extra_grad, loss_part),
        ("img", "row"),
    )
    return totals, pixel_total


BF16 = jnp.bfloat16
F32 = jnp.float32
MESH = pl.DeviceIdType.MESH
TILE = 128
BLOCK = 8
VMEM_BYTES = 58 * 1024 * 1024


def padded(length):
    return -(-length // TILE) * TILE


def fits(kspace, first_weight, mesh_rows):
    micro, images, coils, _, rows, length = kspace.shape
    channels = first_weight.shape[1]
    return (
        images == 1
        and micro * channels == TILE
        and channels % 16 == 0
        and rows * mesh_rows == length
        and rows % BLOCK == 0
        and (2 * rows) % 16 == 0
        and (coils * rows) % TILE == 0
        and padded(length) > length
    )


def phases(length):
    index = np.arange(length)
    angle = 2.0 * np.pi * (np.outer(index, index) % length) / length
    return np.cos(angle) / np.sqrt(length), np.sin(angle) / np.sqrt(length)


def high_low(table):
    high = table.astype(BF16)
    low = (table - high.astype(F32)).astype(BF16)
    return high, low


def np_high_low(table):
    table = np.asarray(table, np.float32)
    high = table.astype(BF16)
    low = (table - high.astype(np.float32)).astype(BF16)
    return jnp.asarray(high), jnp.asarray(low)


def dot(left, right):
    return jnp.dot(left, right, preferred_element_type=F32)


def dot_nt(left, right):
    return lax.dot_general(left, right, (((1,), (1,)), ((), ())), preferred_element_type=F32)


def greet(peers):
    barrier = pltpu.get_barrier_semaphore()
    for peer in peers:
        pl.semaphore_signal(barrier, inc=1, device_id=peer, device_id_type=MESH)
    pl.semaphore_wait(barrier, len(peers))


def row_peers(rows):
    image, row = lax.axis_index("img"), lax.axis_index("row")
    return [(image, lax.rem(row + step, rows)) for step in range(1, rows)]


def image_peers(images):
    image, row = lax.axis_index("img"), lax.axis_index("row")
    return [(lax.rem(image + step, images), row) for step in range(1, images)]


def remote(source, target, send, receive, peer):
    copy = pltpu.make_async_remote_copy(
        src_ref=source,
        dst_ref=target,
        send_sem=send,
        recv_sem=receive,
        device_id=peer,
        device_id_type=MESH,
    )
    copy.start()
    return copy


def params(vmem=VMEM_BYTES, **kwargs):
    return pltpu.CompilerParams(vmem_limit_bytes=vmem, **kwargs)


def in_vmem():
    return pl.BlockSpec(memory_space=pltpu.VMEM)


def anywhere():
    return pl.BlockSpec(memory_space=pl.ANY)


def exchange_kernel(
    sizes, kspace, maps, turn_high, turn_low, pick, mask, cosine, sine, spread, normal_high, normal_low, staged, send, receive, own
):
    micro, coils, rows, length, parts = sizes
    wide = padded(length)
    image, me = lax.axis_index("img"), lax.axis_index("row")
    peers = row_peers(parts)
    greet(peers)
    copies = []
    slabs = 2 * rows
    for batch in range(micro):
        for kind in range(2):
            total = None
            for part in range(2):
                source = (kspace, maps)[kind]
                field = source[batch, :, part].reshape(coils * rows, length)
                if kind == 0:
                    high, low = high_low(field)
                    term = (
                        dot_nt(turn_high[part], high)
                        + dot_nt(turn_low[part], high)
                        + dot_nt(turn_high[part], low)
                    )
                else:
                    term = dot_nt(pick[part], field.astype(BF16))
                total = term if total is None else total + term
            slot = 2 * batch + kind
            staged[slot] = total.astype(BF16).reshape(parts, slabs, coils * rows)
            local = pltpu.make_async_copy(staged.at[slot, me], spread.at[slot, me], own.at[slot])
            local.start()
            copies.append(local)
            order = sorted(range(1, parts), key=lambda step: -min(step, parts - step))
            for step in order:
                peer = peers[step - 1]
                copies.append(
                    remote(
                        staged.at[slot, peer[1]],
                        spread.at[slot, me],
                        send.at[slot, step - 1],
                        receive.at[slot, step - 1],
                        peer,
                    )
                )
    for batch in range(micro):
        chosen = mask[batch]
        cos_on, sin_on = cosine[...] * chosen, sine[...] * chosen

        def product(left, right):
            return jnp.dot(left, right, precision=PRECISE, preferred_element_type=F32)

        real = product(cos_on, cosine[...]) + product(sin_on, sine[...])
        imag = product(sin_on, cosine[...]) - product(cos_on, sine[...])
        for block, value in (((0, 0), real), ((0, 1), -imag), ((1, 0), imag), ((1, 1), real)):
            high, low = high_low(value)
            at = (batch, pl.ds(block[0] * wide, wide), pl.ds(block[1] * wide, wide))
            normal_high[at] = high
            normal_low[at] = low
    for copy in copies:
        copy.wait()


def exchange(kspace, maps, mask, parts):
    micro, coils, _, rows, length = kspace.shape
    wide = padded(length)
    cosine, sine = phases(length)
    inverse = np.stack([np.stack([cosine, sine], 0), np.stack([-sine, cosine], 0)], 0)
    turn = inverse.reshape(2, 2, length, parts, rows).transpose(0, 3, 1, 4, 2).reshape(2, 2 * length, length)
    pick = np.zeros((2, parts, 2, rows, length), np.float32)
    for part in range(2):
        for block in range(parts):
            pick[part, block, part, :, block * rows : (block + 1) * rows] = np.eye(rows)
    pick = jnp.asarray(pick.reshape(2, 2 * length, length).astype(BF16))
    turn_high, turn_low = np_high_low(turn)
    edge = ((0, wide - length), (0, wide - length))
    cosine = jnp.asarray(np.pad(cosine, edge), F32)
    sine = jnp.asarray(np.pad(sine, edge), F32)
    sizes = (micro, coils, rows, length, parts)
    slots = 2 * micro
    return pl.pallas_call(
        functools.partial(exchange_kernel, sizes),
        out_shape=[
            jax.ShapeDtypeStruct((slots, parts, 2 * rows, coils * rows), BF16),
            jax.ShapeDtypeStruct((micro, 2 * wide, 2 * wide), BF16),
            jax.ShapeDtypeStruct((micro, 2 * wide, 2 * wide), BF16),
        ],
        in_specs=[in_vmem()] * 8,
        out_specs=[anywhere(), in_vmem(), in_vmem()],
        scratch_shapes=[
            pltpu.VMEM((slots, parts, 2 * rows, coils * rows), BF16),
            pltpu.SemaphoreType.DMA((slots, parts - 1)),
            pltpu.SemaphoreType.DMA((slots, parts - 1)),
            pltpu.SemaphoreType.DMA((slots,)),
        ],
        compiler_params=params(collective_id=1, has_side_effects=True),
        name="exchange",
    )(kspace, maps, turn_high, turn_low, pick, mask, cosine, sine)


def gather_lanes(blocks, coil, rows, wide):
    pieces = [block[:, coil * rows : (coil + 1) * rows] for block in blocks]
    height = pieces[0].shape[0]
    short = wide - rows * len(pieces)
    return jnp.concatenate(pieces + [jnp.zeros((height, short), pieces[0].dtype)], axis=1)


def zero_fill_kernel(sizes, limit, fields, mask, fourier_high, fourier_low, filled, maps_out, edges):
    coils, rows, length, parts = sizes
    wide = padded(length)
    chosen = mask[...].astype(BF16)
    real = jnp.zeros((rows, wide), F32)
    imag = jnp.zeros((rows, wide), F32)
    group = 4
    for first in range(0, coils, group):
        stack = []
        for coil in range(first, first + group):
            on = jnp.where(coil < limit[pl.program_id(0)], 1.0, 0.0).astype(BF16)
            maps_out[coil] = gather_lanes([fields[1, s] for s in range(parts)], coil, rows, wide) * on
            stack.append(gather_lanes([fields[0, s] for s in range(parts)], coil, rows, wide) * chosen)
        stack = jnp.concatenate(stack, axis=0)
        turned = dot(stack, fourier_high[...]) + dot(stack, fourier_low[...])
        for place in range(group):
            top = 2 * rows * place
            upper, lower = turned[top : top + rows], turned[top + rows : top + 2 * rows]
            field_re = upper[:, :wide] - lower[:, wide:]
            field_im = upper[:, wide:] + lower[:, :wide]
            sense = maps_out[first + place].astype(F32)
            sense_re, sense_im = sense[:rows], sense[rows:]
            real = real + sense_re * field_re + sense_im * field_im
            imag = imag + sense_re * field_im - sense_im * field_re
    filled[0] = real
    filled[1] = imag
    put_edges(edges, real, imag)


def put_edges(edges, real, imag):
    rows, wide = real.shape
    zeros = jnp.zeros((6, wide), F32)
    edges[0] = jnp.concatenate([real[:1], imag[:1], zeros], axis=0)
    edges[1] = jnp.concatenate([real[rows - 1 :], imag[rows - 1 :], zeros], axis=0)


def zero_fill(fields, mask, limit, rows, length):
    slots, parts, slabs, lanes = fields.shape
    micro, coils, wide = slots // 2, lanes // rows, padded(length)
    cosine, sine = phases(length)
    table = np.zeros((wide, 2, wide))
    table[:length, 0, :length] = cosine
    table[:length, 1, :length] = sine
    high, low = np_high_low(table.reshape(wide, 2 * wide))
    sizes = (coils, rows, length, parts)
    return pl.pallas_call(
        functools.partial(zero_fill_kernel, sizes),
        grid_spec=pltpu.PrefetchScalarGridSpec(
            num_scalar_prefetch=1,
            grid=(micro,),
            in_specs=[
                pl.BlockSpec((None, 2, parts, slabs, lanes), lambda b, _: (b, 0, 0, 0, 0)),
                pl.BlockSpec((None, 1, wide), lambda b, _: (b, 0, 0)),
                pl.BlockSpec((wide, 2 * wide), lambda b, _: (0, 0)),
                pl.BlockSpec((wide, 2 * wide), lambda b, _: (0, 0)),
            ],
            out_specs=[
                pl.BlockSpec((None, 2, rows, wide), lambda b, _: (b, 0, 0, 0)),
                pl.BlockSpec((None, coils, slabs, wide), lambda b, _: (b, 0, 0, 0)),
                pl.BlockSpec((2, None, 8, wide), lambda b, _: (0, b, 0, 0)),
            ],
        ),
        out_shape=[
            jax.ShapeDtypeStruct((micro, 2, rows, wide), F32),
            jax.ShapeDtypeStruct((micro, coils, slabs, wide), BF16),
            jax.ShapeDtypeStruct((2, micro, 8, wide), F32),
        ],
        compiler_params=params(),
        name="zero_fill",
    )(limit, fields.reshape(micro, 2, parts, slabs, lanes), mask, high, low)


def start_halo(parts, sources, target, send, receive):
    image, me = lax.axis_index("img"), lax.axis_index("row")
    left, right = lax.rem(me + parts - 1, parts), lax.rem(me + 1, parts)
    return [
        remote(sources[0], target.at[1], send.at[0], receive.at[0], (image, left)),
        remote(sources[1], target.at[0], send.at[1], receive.at[1], (image, right)),
    ]


def halo_kernel(parts, edges, halo, send, receive):
    image, me = lax.axis_index("img"), lax.axis_index("row")
    greet([(image, lax.rem(me + parts - 1, parts)), (image, lax.rem(me + 1, parts))])
    for copy in start_halo(parts, (edges.at[0], edges.at[1]), halo, send, receive):
        copy.wait()


def halo_exchange(edges, parts, identity):
    return pl.pallas_call(
        functools.partial(halo_kernel, parts),
        out_shape=jax.ShapeDtypeStruct(edges.shape, edges.dtype),
        in_specs=[in_vmem()],
        out_specs=in_vmem(),
        scratch_shapes=[pltpu.SemaphoreType.DMA((2,)), pltpu.SemaphoreType.DMA((2,))],
        compiler_params=params(collective_id=identity, has_side_effects=True),
        name="halo",
    )(edges)


def sum_rows_kernel(parts, values, totals, held, send, receive):
    peers = row_peers(parts)
    greet(peers)
    copies = [
        remote(values, held.at[index], send.at[index], receive.at[index], peer)
        for index, peer in enumerate(peers)
    ]
    total = values[...]
    for index, copy in enumerate(copies):
        copy.wait_recv()
        total = total + held[index]
    totals[...] = total
    for copy in copies:
        copy.wait_send()


def sum_rows(values, parts, identity):
    return pl.pallas_call(
        functools.partial(sum_rows_kernel, parts),
        out_shape=jax.ShapeDtypeStruct(values.shape, F32),
        in_specs=[in_vmem()],
        out_specs=in_vmem(),
        scratch_shapes=[
            pltpu.VMEM((parts - 1,) + values.shape, F32),
            pltpu.SemaphoreType.DMA((parts - 1,)),
            pltpu.SemaphoreType.DMA((parts - 1,)),
        ],
        compiler_params=params(collective_id=identity, has_side_effects=True),
        name="sum_rows",
    )(values)


def lane_row(columns):
    return jnp.sum(columns.T, axis=0, keepdims=True)


def spread_row(row):
    return jnp.broadcast_to(row, (TILE, TILE)).T


def merge(sums, squares, count):
    total = functools.reduce(jnp.add, sums)
    mean = total / (count * len(sums))
    square = None
    for part, own in zip(sums, squares):
        shift = part / count - mean
        term = own + count * shift * shift
        square = term if square is None else square + term
    return total, square


def layer_sums_kernel(
    backward, parts, images, count, layer, stats, affine, extra, halo, coefs, rows_out, message, held, second, held_second, send, receive, send_halo, receive_halo
):
    image, me = lax.axis_index("img"), lax.axis_index("row")
    rows, cols = row_peers(parts), image_peers(images)
    greet(rows + cols)
    width = layer.shape[1]
    halos = start_halo(parts, (layer.at[:, 0], layer.at[:, width - 1]), halo, send_halo, receive_halo)
    channels = stats.shape[0] * stats.shape[2]
    first = lane_row(stats[:, 0].reshape(channels, TILE))
    other = lane_row(stats[:, 1].reshape(channels, TILE))
    message[...] = jnp.concatenate([first, other, extra[...], jnp.zeros((5, TILE), F32)], axis=0)

    def exchange_step(source, peers, target, base):
        copies = [
            remote(source, target.at[index], send.at[base + index], receive.at[base + index], peer)
            for index, peer in enumerate(peers)
        ]
        blocks = [source[...]]
        for index, copy in enumerate(copies):
            copy.wait_recv()
            blocks.append(target[index])
        return copies, blocks

    def join(blocks, number):
        added = functools.reduce(jnp.add, blocks)
        if backward:
            return added[0:1], added[1:2], added[2:3]
        total, square = merge([b[0:1] for b in blocks], [b[1:2] for b in blocks], number)
        return total, square, added[2:3]

    sent, blocks = exchange_step(message, rows, held, 0)
    first, other, plain = join(blocks, count)
    second[...] = jnp.concatenate([first, other, plain, jnp.zeros((5, TILE), F32)], axis=0)
    sent_second, blocks = exchange_step(second, cols, held_second, parts - 1)
    first, other, plain = join(blocks, count * parts)
    pixels = count * parts * images
    if backward:
        gain, inverse, offset = affine[0:1], affine[2:3], affine[3:4]
        scale = inverse * gain
        coefs[0] = spread_row(scale)
        coefs[1] = spread_row(-scale * inverse * other / pixels)
        coefs[2] = spread_row(-scale * (first + offset * other) / pixels)
        rows_out[...] = jnp.concatenate([first, other, jnp.zeros((6, TILE), F32)], axis=0)
    else:
        gain, shift = affine[0:1], affine[1:2]
        mean = first / pixels
        inverse = lax.rsqrt(other / pixels + EPS_NORM)
        offset = -mean * inverse
        coefs[0] = spread_row(0.5 * gain * inverse)
        coefs[1] = spread_row(0.5 * (shift + gain * offset))
        coefs[2] = spread_row(inverse)
        coefs[3] = spread_row(offset)
        rows_out[...] = jnp.concatenate([gain, shift, inverse, offset, plain, jnp.zeros((3, TILE), F32)], axis=0)
    for copy in sent + sent_second:
        copy.wait_send()
    for copy in halos:
        copy.wait()


def layer_sums(layer, stats, affine, extra, parts, images, count, backward, identity):
    micro, width, channels, wide = layer.shape
    number = 3 if backward else 4
    return pl.pallas_call(
        functools.partial(layer_sums_kernel, backward, parts, images, count),
        out_shape=[
            jax.ShapeDtypeStruct((2, micro, channels, wide), F32),
            jax.ShapeDtypeStruct((number, TILE, TILE), F32),
            jax.ShapeDtypeStruct((8, TILE), F32),
        ],
        in_specs=[anywhere(), in_vmem(), in_vmem(), in_vmem()],
        out_specs=[anywhere(), in_vmem(), in_vmem()],
        scratch_shapes=[
            pltpu.VMEM((8, TILE), F32),
            pltpu.VMEM((parts - 1, 8, TILE), F32),
            pltpu.VMEM((8, TILE), F32),
            pltpu.VMEM((images - 1, 8, TILE), F32),
            pltpu.SemaphoreType.DMA((parts + images - 2,)),
            pltpu.SemaphoreType.DMA((parts + images - 2,)),
            pltpu.SemaphoreType.DMA((2,)),
            pltpu.SemaphoreType.DMA((2,)),
        ],
        compiler_params=params(collective_id=identity, has_side_effects=True),
        name="layer_sums_back" if backward else "layer_sums",
    )(layer, stats, affine, extra)


def repeat_lanes(block, wide):
    return jnp.concatenate([block] * (wide // TILE), axis=1)


def lane_mask(length, wide):
    whole = length // TILE * TILE

    def clear(values):
        tail = values[:, whole:]
        keep = lax.broadcasted_iota(jnp.int32, tail.shape, 1) < length - whole
        return jnp.concatenate([values[:, :whole], jnp.where(keep, tail, 0.0)], axis=1)

    return clear


def fold(values):
    parts = [values[:, at : at + TILE] for at in range(0, values.shape[1], TILE)]
    return functools.reduce(jnp.add, parts)


def put_shifted(stack, values, at):
    channels, wide = values.shape
    stack[0:channels, pl.ds(at, wide)] = pltpu.roll(values, 1, 1)
    stack[channels : 2 * channels, pl.ds(at, wide)] = values
    stack[2 * channels : 3 * channels, pl.ds(at, wide)] = pltpu.roll(values, wide - 1, 1)


def lane_at(column, wide):
    return pl.multiple_of(column * wide, TILE) if not isinstance(column, int) else column * wide


def columns_at(stack, column, number, wide):
    return stack[:, pl.ds(lane_at(column, wide), number * wide)]


def ring_sum(table, stack, carry, first, out_rows, wide, emit):
    pieces = []
    for pair in range(BLOCK // 2):
        product = dot(table[...], columns_at(stack, first + 2 * pair, 2, wide))
        pieces += [product[:, :wide], product[:, wide:]]
    older, newer = carry[0:out_rows], carry[out_rows : 2 * out_rows]
    for place, piece in enumerate(pieces):
        emit(place, older + piece[2 * out_rows : 3 * out_rows])
        older = newer + piece[out_rows : 2 * out_rows]
        newer = piece[0:out_rows]
    carry[0:out_rows] = older
    carry[out_rows : 2 * out_rows] = newer


def ring_start(table, stack, carry, out_rows, wide):
    product = dot(table[...], stack[:, 0 : 2 * wide])
    carry[0:out_rows] = product[0:out_rows, :wide] + product[out_rows : 2 * out_rows, wide:]
    carry[out_rows : 2 * out_rows] = product[0:out_rows, wide:]


def edge_flags(parts):
    me = lax.axis_index("row")
    return me > 0, me < parts - 1


def block_loop(width, body):
    blocks = width // BLOCK

    def step(index, carry):
        body(index, False)
        return carry

    lax.fori_loop(0, blocks - 1, step, 0)
    body(blocks - 1, True)


def finish_stats(out, stats, total, clear, width, length):
    channels, wide = total.shape
    mean = jnp.sum(total[...], axis=1, keepdims=True) / (width * length)

    def step(index, square):
        for place in range(BLOCK):
            shift = clear(out[index * BLOCK + place] - mean)
            square = square + shift * shift
        return square

    square = lax.fori_loop(0, width // BLOCK, step, jnp.zeros((channels, wide), F32))
    stats[0] = fold(total[...])
    stats[1] = fold(square)


def first_kernel(length, stack, table, out, stats, carry, total):
    width, channels, wide = out.shape
    clear = lane_mask(length, wide)
    ring_start(table, stack, carry, channels, wide)
    total[...] = jnp.zeros_like(total)

    def body(block, last):
        def emit(place, value):
            out[block * BLOCK + place] = value
            total[...] += clear(value)

        ring_sum(table, stack, carry, block * BLOCK + 2, channels, wide, emit)

    block_loop(width, body)
    finish_stats(out, stats, total, clear, width, length)


def first_layer(stack, table, width, length):
    micro, depth, lanes = stack.shape
    wide = padded(length)
    channels = table.shape[0] // 3
    return pl.pallas_call(
        functools.partial(first_kernel, length),
        grid=(micro,),
        in_specs=[
            pl.BlockSpec((None, depth, lanes), lambda b: (b, 0, 0)),
            pl.BlockSpec(table.shape, lambda b: (0, 0)),
        ],
        out_specs=[
            pl.BlockSpec((None, width, channels, wide), lambda b: (b, 0, 0, 0)),
            pl.BlockSpec((None, 2, channels, TILE), lambda b: (b, 0, 0, 0)),
        ],
        out_shape=[
            jax.ShapeDtypeStruct((micro, width, channels, wide), F32),
            jax.ShapeDtypeStruct((micro, 2, channels, TILE), F32),
        ],
        scratch_shapes=[pltpu.VMEM((2 * channels, wide), F32), pltpu.VMEM((channels, wide), F32)],
        compiler_params=params(),
        name="first_layer",
    )(stack, table)


def silu_half(values, scale, offset):
    half = values * scale + offset
    curve = jnp.tanh(half)
    return half, curve


def middle_kernel(length, parts, last_layer, source, halo, coefs, table, *rest):
    if last_layer:
        out, stack, carry = rest
    else:
        out, stats, stack, carry, total = rest
    width, channels, wide = source.shape
    rows = table.shape[0] // 3
    clear = lane_mask(length, wide)
    scale, offset = repeat_lanes(coefs[0], wide), repeat_lanes(coefs[1], wide)
    inner_left, inner_right = edge_flags(parts)

    def put(values, column, keep=None):
        half, curve = silu_half(values, scale, offset)
        active = clear(half * curve + half)
        if keep is not None:
            active = jnp.where(keep, active, 0.0)
        put_shifted(stack, active.astype(BF16), lane_at(column, wide))

    put(halo[0], 0, inner_left)
    put(source[0], 1)
    ring_start(table, stack, carry, rows, wide)
    if not last_layer:
        total[...] = jnp.zeros_like(total)

    def body(block, last):
        for place in range(BLOCK):
            column = block * BLOCK + 2 + place
            if last and place == BLOCK - 1:
                put(halo[1], column, inner_right)
            else:
                put(source[column - 1], column)

        def emit(place, value):
            out[block * BLOCK + place] = value
            if not last_layer:
                total[...] += clear(value)

        ring_sum(table, stack, carry, block * BLOCK + 2, rows, wide, emit)

    block_loop(width, body)
    if not last_layer:
        finish_stats(out, stats, total, clear, width, length)


def layer_spec(width, channels, wide):
    return pl.BlockSpec((None, width, channels, wide), lambda b: (b, 0, 0, 0))


def halo_spec(channels, wide):
    return pl.BlockSpec((2, None, channels, wide), lambda b: (0, b, 0, 0))


def coef_spec(number, channels):
    return pl.BlockSpec((number, channels, TILE), lambda b: (0, b, 0))


def middle_layer(source, halo, coefs, table, length, parts, last_layer):
    micro, width, channels, wide = source.shape
    rows = table.shape[0] // 3
    out_specs = [layer_spec(width, rows, wide)]
    out_shape = [jax.ShapeDtypeStruct((micro, width, rows, wide), F32)]
    scratch = [pltpu.VMEM((3 * channels, (width + 2) * wide), BF16), pltpu.VMEM((2 * rows, wide), F32)]
    if not last_layer:
        out_specs.append(pl.BlockSpec((None, 2, rows, TILE), lambda b: (b, 0, 0, 0)))
        out_shape.append(jax.ShapeDtypeStruct((micro, 2, rows, TILE), F32))
        scratch.append(pltpu.VMEM((rows, wide), F32))
    return pl.pallas_call(
        functools.partial(middle_kernel, length, parts, last_layer),
        grid=(micro,),
        in_specs=[
            layer_spec(width, channels, wide),
            halo_spec(channels, wide),
            coef_spec(4, channels),
            pl.BlockSpec(table.shape, lambda b: (0, 0)),
        ],
        out_specs=out_specs,
        out_shape=out_shape,
        scratch_shapes=scratch,
        compiler_params=params(),
        name="last_layer" if last_layer else "middle_layer",
    )(source, halo, coefs, table)


def backward_kernel(length, parts, given, *refs):
    if given:
        stack_in, below, below_halo, below_coefs, table, out, stats, weight_out, inputs, slope, carry, total, along = refs
        stack = stack_in
    else:
        (
            grads, grads_halo, layer, layer_halo, coefs, below, below_halo, below_coefs, table,
            out, stats, weight_out, stack, inputs, slope, carry, total, along,
        ) = refs
    width, channels, wide = below.shape
    clear = lane_mask(length, wide)
    inner_left, inner_right = edge_flags(parts)
    scale, offset = repeat_lanes(below_coefs[0], wide), repeat_lanes(below_coefs[1], wide)
    if not given:
        on_grad, on_layer, base = (repeat_lanes(coefs[index], wide) for index in range(3))

    def put_grad(values, linear, column, keep=None):
        upstream = clear(on_grad * values + on_layer * linear + base)
        if keep is not None:
            upstream = jnp.where(keep, upstream, 0.0)
        put_shifted(stack, upstream.astype(BF16), lane_at(column, wide))

    def put_input(values, column, keep=None):
        half, curve = silu_half(values, scale, offset)
        active = clear(half * curve + half)
        if keep is not None:
            active = jnp.where(keep, active, 0.0)
        inputs[:, pl.ds(lane_at(column, wide), wide)] = active.astype(BF16)
        return half, curve

    def put_inner(column):
        half, curve = put_input(below[column - 1], column)
        slope[column - 1] = 0.5 * (1.0 + curve) * (1.0 + half * (1.0 - curve))
        if not given:
            put_grad(grads[column - 1], layer[column - 1], column)

    put_input(below_halo[0], 0, inner_left)
    if not given:
        put_grad(grads_halo[0], layer_halo[0], 0, inner_left)
    put_inner(1)
    ring_start(table, stack, carry, channels, wide)
    total[...] = jnp.zeros_like(total)
    along[...] = jnp.zeros_like(along)

    @pl.when(pl.program_id(0) == 0)
    def _():
        weight_out[...] = jnp.zeros_like(weight_out)

    def body(block, last):
        for place in range(BLOCK):
            column = block * BLOCK + 2 + place
            if last and place == BLOCK - 1:
                put_input(below_halo[1], column, inner_right)
                if not given:
                    put_grad(grads_halo[1], layer_halo[1], column, inner_right)
            else:
                put_inner(column)
        inverse, centre = repeat_lanes(below_coefs[2], wide), repeat_lanes(below_coefs[3], wide)

        def emit(place, value):
            column = block * BLOCK + place
            shaped = clear(value * slope[column])
            out[column] = shaped
            total[...] += shaped
            along[...] += shaped * (below[column] * inverse + centre)

        ring_sum(table, stack, carry, block * BLOCK + 2, channels, wide, emit)
        first = block * BLOCK
        around = jnp.concatenate([columns_at(inputs, first + tap, BLOCK, wide) for tap in range(3)], axis=0)
        weight_out[...] += dot_nt(columns_at(stack, first + 1, BLOCK, wide), around)

    block_loop(width, body)
    stats[0] = fold(total[...])
    stats[1] = fold(along[...])


def backward_layer(grad_parts, below, below_halo, below_coefs, table, length, parts):
    micro, width, channels, wide = below.shape
    given = len(grad_parts) == 1
    depth = table.shape[1]
    scratch = [
        pltpu.VMEM((channels, (width + 2) * wide), BF16),
        pltpu.VMEM((width, channels, wide), F32),
        pltpu.VMEM((2 * channels, wide), F32),
        pltpu.VMEM((channels, wide), F32),
        pltpu.VMEM((channels, wide), F32),
    ]
    if given:
        grad_specs = [pl.BlockSpec((None,) + grad_parts[0].shape[1:], lambda b: (b, 0, 0))]
    else:
        upper = grad_parts[0].shape[2]
        grad_specs = [
            layer_spec(width, upper, wide),
            halo_spec(upper, wide),
            layer_spec(width, upper, wide),
            halo_spec(upper, wide),
            coef_spec(3, upper),
        ]
        scratch = [pltpu.VMEM((3 * upper, (width + 2) * wide), BF16)] + scratch
    return pl.pallas_call(
        functools.partial(backward_kernel, length, parts, given),
        grid=(micro,),
        in_specs=grad_specs
        + [
            layer_spec(width, channels, wide),
            halo_spec(channels, wide),
            coef_spec(4, channels),
            pl.BlockSpec(table.shape, lambda b: (0, 0)),
        ],
        out_specs=[
            layer_spec(width, channels, wide),
            pl.BlockSpec((None, 2, channels, TILE), lambda b: (b, 0, 0, 0)),
            pl.BlockSpec((depth, 3 * channels), lambda b: (0, 0)),
        ],
        out_shape=[
            jax.ShapeDtypeStruct((micro, width, channels, wide), F32),
            jax.ShapeDtypeStruct((micro, 2, channels, TILE), F32),
            jax.ShapeDtypeStruct((depth, 3 * channels), F32),
        ],
        scratch_shapes=scratch,
        compiler_params=params(),
        name="backward_last" if given else "backward_layer",
    )(*grad_parts, below, below_halo, below_coefs, table)


def backward_first_kernel(length, grads, layer, coefs, image, weight_out, stack):
    width, channels, wide = grads.shape
    clear = lane_mask(length, wide)
    on_grad, on_layer, base = (repeat_lanes(coefs[index], wide) for index in range(3))

    @pl.when(pl.program_id(0) == 0)
    def _():
        weight_out[...] = jnp.zeros_like(weight_out)

    def body(block, last):
        for place in range(BLOCK):
            column = block * BLOCK + place
            upstream = clear(on_grad * grads[column] + on_layer * layer[column] + base)
            put_shifted(stack, upstream.astype(BF16), place * wide)
        around = jnp.concatenate([columns_at(image, block * BLOCK + tap, BLOCK, wide) for tap in range(3)], axis=0)
        weight_out[...] += dot_nt(stack[...], around)

    block_loop(width, body)


def backward_first(grads, layer, coefs, image, length):
    micro, width, channels, wide = grads.shape
    depth = image.shape[1]
    return pl.pallas_call(
        functools.partial(backward_first_kernel, length),
        grid=(micro,),
        in_specs=[
            layer_spec(width, channels, wide),
            layer_spec(width, channels, wide),
            coef_spec(3, channels),
            pl.BlockSpec((None,) + image.shape[1:], lambda b: (b, 0, 0)),
        ],
        out_specs=pl.BlockSpec((3 * channels, 3 * depth), lambda b: (0, 0)),
        out_shape=jax.ShapeDtypeStruct((3 * channels, 3 * depth), F32),
        scratch_shapes=[pltpu.VMEM((3 * channels, BLOCK * wide), BF16)],
        compiler_params=params(),
        name="backward_first",
    )(grads, layer, coefs, image)


def apply_normal(image, maps, normal_high, normal_low):
    coils, slabs, wide = maps.shape
    rows = slabs // 2
    real, imag = image
    stack = []
    for coil in range(coils):
        sense = maps[coil].astype(F32)
        sense_re, sense_im = sense[:rows], sense[rows:]
        stack.append(
            jnp.concatenate(
                [sense_re * real - sense_im * imag, sense_re * imag + sense_im * real], axis=1
            )
        )
    stack = jnp.concatenate(stack, axis=0).astype(BF16)
    out_re = jnp.zeros((rows, wide), F32)
    out_im = jnp.zeros((rows, wide), F32)
    turned = dot(stack, normal_high[...]) + dot(stack, normal_low[...])
    for coil in range(coils):
        sense = maps[coil].astype(F32)
        sense_re, sense_im = sense[:rows], sense[rows:]
        field = turned[coil * rows : (coil + 1) * rows]
        field_re, field_im = field[:, :wide], field[:, wide:]
        out_re = out_re + sense_re * field_re + sense_im * field_im
        out_im = out_im + sense_re * field_im - sense_im * field_re
    return out_re, out_im


def pair(ref):
    return ref[0], ref[1]


def put_pair(ref, values):
    ref[0] = values[0]
    ref[1] = values[1]


def blend(*terms):
    return tuple(functools.reduce(jnp.add, [factor * image[part] for factor, image in terms]) for part in range(2))


def inner_of(left, right):
    product = left[0] * right[0] + left[1] * right[1]
    return jnp.sum(jnp.sum(product, axis=1, keepdims=True), axis=0, keepdims=True)


def put_sums(ref, values):
    filler = [jnp.zeros((1, TILE), F32)] * (8 - len(values))
    ref[...] = jnp.concatenate([jnp.broadcast_to(value, (1, TILE)) for value in values] + filler, axis=0)


def scalar_at(ref, index):
    return ref[index : index + 1, 0:1]


def solve_one_kernel(length, consts, filled, result, maps, normal_high, normal_low, denoised, right, mapped, sums):
    _, rows, wide = filled.shape
    inside = lax.broadcasted_iota(jnp.int32, (rows, wide), 1) < length
    penalty = consts[2]
    images = []
    for part in range(2):
        value = jnp.where(inside, filled[part] + result[part] + consts[part], 0.0)
        denoised[part] = value
        images.append(filled[part] + penalty * value)
    put_pair(right, images)
    mapped_now = blend((1.0, apply_normal(images, maps, normal_high, normal_low)), (penalty, images))
    put_pair(mapped, mapped_now)
    put_sums(sums, [inner_of(images, images), inner_of(images, mapped_now)])


def solve_two_kernel(consts, right, mapped, totals, maps, normal_high, normal_low, residue, through, sums):
    penalty = consts[2]
    stepsize = scalar_at(totals, 0) / scalar_at(totals, 1)
    start, image = pair(right), pair(mapped)
    left_over = blend((1.0, start), (-stepsize, image))
    put_pair(residue, left_over)
    mapped_now = blend((1.0, apply_normal(left_over, maps, normal_high, normal_low)), (penalty, left_over))
    put_pair(through, mapped_now)
    put_sums(
        sums,
        [
            inner_of(left_over, left_over),
            inner_of(left_over, mapped_now),
            inner_of(left_over, image),
            inner_of(start, mapped_now),
        ],
    )


def step_scalars(totals_one, totals_two):
    norm_0, curve_0 = scalar_at(totals_one, 0), scalar_at(totals_one, 1)
    norm_1 = scalar_at(totals_two, 0)
    factor = norm_1 / norm_0
    curve_1 = (
        scalar_at(totals_two, 1)
        + factor * (scalar_at(totals_two, 2) + scalar_at(totals_two, 3))
        + factor * factor * curve_0
    )
    return norm_0, curve_0, norm_1, curve_1, factor


def solve_three_kernel(consts, right, mapped, residue, through, totals_one, totals_two, target, chosen, search, searched, slope, sums):
    norm_0, curve_0, norm_1, curve_1, factor = step_scalars(totals_one, totals_two)
    start, image = pair(right), pair(mapped)
    direction = blend((1.0, pair(residue)), (factor, start))
    image_1 = blend((1.0, pair(through)), (factor, image))
    put_pair(search, direction)
    put_pair(searched, image_1)
    state = blend((norm_0 / curve_0, start), (norm_1 / curve_1, direction))
    weight = chosen[...]
    difference = [state[part] - target[part] for part in range(2)]
    grad = [consts[3] * 2.0 * weight * difference[part] for part in range(2)]
    put_pair(slope, grad)
    masked = [weight * difference[part] for part in range(2)]
    put_sums(
        sums,
        [
            inner_of(grad, direction),
            inner_of(grad, start),
            inner_of(grad, image),
            inner_of(image_1, start),
            inner_of(image_1, image),
            inner_of(direction, direction),
            inner_of(masked, difference),
        ],
    )


def solve_four_kernel(
    consts, right, mapped, residue, denoised, search, searched, slope, totals_one, totals_two, totals_three, own_sums, maps, normal_high, normal_low, grad_out, edges, sums
):
    penalty = consts[2]
    norm_0, curve_0, norm_1, curve_1, factor = step_scalars(totals_one, totals_two)
    step_0, step_1 = norm_0 / curve_0, norm_1 / curve_1
    start, image, left_over = pair(right), pair(mapped), pair(residue)
    image_1, grad = pair(searched), pair(slope)
    grad_search, grad_start, grad_image = (scalar_at(totals_three, index) for index in range(3))
    cross_start, cross_image = scalar_at(totals_three, 3), scalar_at(totals_three, 4)
    residue_image = scalar_at(totals_two, 2)
    curve_grad_1 = -grad_search * norm_1 / (curve_1 * curve_1)
    norm_grad_1 = grad_search / curve_1
    search_grad = blend((step_1, grad), (2.0 * curve_grad_1, image_1))
    factor_grad = step_1 * grad_start + 2.0 * curve_grad_1 * cross_start
    joint = step_1 * grad_image + 2.0 * curve_grad_1 * cross_image
    norm_total = norm_grad_1 + factor_grad / norm_0
    residue_full = blend((1.0, search_grad), (2.0 * norm_total, left_over))
    step_grad = grad_start - (joint + 2.0 * norm_total * residue_image)
    curve_grad_0 = -step_grad * norm_0 / (curve_0 * curve_0)
    mapped_grad = blend((-step_0, residue_full), (curve_grad_0, start))
    through = apply_normal(mapped_grad, maps, normal_high, normal_low)
    norm_grad_0 = -factor_grad * norm_1 / (norm_0 * norm_0) + step_grad / curve_0
    right_grad = blend(
        (1.0, residue_full),
        (factor, search_grad),
        (step_0, grad),
        (curve_grad_0, image),
        (1.0, through),
        (penalty, mapped_grad),
        (2.0 * norm_grad_0, start),
    )
    penalty_part = (
        curve_grad_1 * scalar_at(own_sums, 5) + inner_of(mapped_grad, start) + inner_of(right_grad, pair(denoised))
    )
    grad_pair = [penalty * right_grad[part] for part in range(2)]
    put_pair(grad_out, grad_pair)
    put_edges(edges, *grad_pair)
    offsets = [jnp.sum(jnp.sum(grad_pair[part], axis=1, keepdims=True), axis=0, keepdims=True) for part in range(2)]
    put_sums(sums, [offsets[0], offsets[1], penalty_part, scalar_at(own_sums, 6)])


def solve_call(kernel, name, consts, operands, outputs):
    def spec(shape, lead):
        block = tuple(None if axis == lead else size for axis, size in enumerate(shape))
        return pl.BlockSpec(block, lambda b: tuple(b if axis == lead else 0 for axis in range(len(shape))))

    micro = operands[0].shape[0]
    return pl.pallas_call(
        kernel,
        grid=(micro,),
        in_specs=[pl.BlockSpec(memory_space=pltpu.SMEM)] + [spec(operand.shape, 0) for operand in operands],
        out_specs=[spec(shape, lead) for shape, lead in outputs],
        out_shape=[jax.ShapeDtypeStruct(shape, F32) for shape, _ in outputs],
        compiler_params=params(),
        name=name,
    )(consts, *operands)


def shifted_image(image, halo, parts):
    micro, channels, width, wide = image.shape
    me = lax.axis_index("row")
    left = jnp.where(me > 0, halo[0, :, :channels], 0.0)[:, :, None]
    right = jnp.where(me < parts - 1, halo[1, :, :channels], 0.0)[:, :, None]
    wider = jnp.concatenate([left, image, right], axis=2).astype(BF16)
    stack = jnp.concatenate([jnp.roll(wider, 1, 3), wider, jnp.roll(wider, -1, 3)], axis=1)
    stack = stack.reshape(micro, 3 * channels, (width + 2) * wide)
    return jnp.pad(stack, ((0, 0), (0, 16 - 3 * channels), (0, 0)))


def forward_table(weight):
    _, outputs, inputs = weight.shape
    return weight.reshape(3, 3, outputs, inputs).transpose(1, 2, 0, 3).reshape(3 * outputs, 3 * inputs)


def backward_table(weight):
    _, outputs, inputs = weight.shape
    flipped = weight.reshape(3, 3, outputs, inputs)[::-1, ::-1]
    return flipped.transpose(1, 3, 0, 2).reshape(3 * inputs, 3 * outputs)


def weight_grad_of(sums, outputs, inputs):
    return sums.reshape(3, outputs, 3, inputs)[::-1].transpose(0, 2, 1, 3).reshape(9, outputs, inputs)


def to_bands(image):
    micro, planes, rows, length = image.shape
    swapped = lax.all_to_all(image, "row", split_axis=3, concat_axis=2, tiled=True)
    return swapped.transpose(0, 1, 3, 2)


def fast_local(arrays):
    (
        kspace, coil_maps, target, row_mask, foreground, anatomy, first_weight, middle_weight, last_weight, norm_gains, norm_shifts, extra_params,
    ) = arrays
    micro, _, coils, _, rows, length = kspace.shape
    channels = first_weight.shape[1]
    parts, images = lax.axis_size("row"), lax.axis_size("img")
    wide = padded(length)
    count = rows * length
    edge = wide - length
    mask = row_mask.astype(F32)
    mask_wide = jnp.pad(mask, ((0, 0), (0, 0), (0, edge)))
    limit = jnp.where(anatomy[:, 0] == 0, BRAIN_COILS, COILS).astype(jnp.int32)
    fields, normal_high, normal_low = exchange(kspace[:, 0], coil_maps[:, 0], mask_wide, parts)
    filled, maps, edges = zero_fill(fields, mask_wide, limit, rows, length)
    planes = jnp.concatenate([target[:, 0], foreground.astype(F32)], axis=1)
    planes = jnp.pad(to_bands(planes), ((0, 0), (0, 0), (0, 0), (0, edge)))

    low = [first_weight.astype(BF16)] + [middle_weight[index].astype(BF16) for index in range(3)] + [last_weight.astype(BF16)]
    gains = jnp.tile(norm_gains, (1, micro))
    shifts = jnp.tile(norm_shifts, (1, micro))
    pixel_part = jnp.broadcast_to(jnp.sum(foreground).astype(F32), (1, TILE))

    halo = halo_exchange(edges, parts, 2)
    image_stack = shifted_image(filled, halo, parts)
    table = jnp.pad(forward_table(low[0]), ((0, 0), (0, 16 - 3 * low[0].shape[2])))
    layer, stats = first_layer(image_stack, table, rows, length)
    kept = []
    for index in range(4):
        affine = jnp.pad(jnp.stack([gains[index], shifts[index]]), ((0, 6), (0, 0)))
        halo, coefs, rows_out = layer_sums(layer, stats, affine, pixel_part, parts, images, count, False, 3)
        kept.append((layer, halo, coefs, rows_out))
        if index < 3:
            layer, stats = middle_layer(layer, halo, coefs, forward_table(low[index + 1]), length, parts, False)
    last = jnp.pad(low[4], ((0, 0), (0, 8 - low[4].shape[1]), (0, 0)))
    (result,) = middle_layer(layer, halo, coefs, forward_table(last), length, parts, True)
    result = result[:, :, :2].transpose(0, 2, 1, 3)
    pixel_total = kept[0][3][4, 0]

    penalty = jnp.exp(extra_params[2])
    consts = jnp.stack([extra_params[0], extra_params[1], penalty, 1.0 / pixel_total])
    shape, sums_shape = filled.shape, (micro, 8, TILE)
    image_out, sums_out = (shape, 0), (sums_shape, 0)
    denoised, right, mapped, sums = solve_call(
        functools.partial(solve_one_kernel, length), "solve_one", consts,
        [filled, result, maps, normal_high, normal_low], [image_out, image_out, image_out, sums_out],
    )
    totals_one = sum_rows(sums, parts, 4)
    residue, through, sums = solve_call(
        solve_two_kernel, "solve_two", consts,
        [right, mapped, totals_one, maps, normal_high, normal_low], [image_out, image_out, sums_out],
    )
    totals_two = sum_rows(sums, parts, 4)
    search, searched, slope, own_sums = solve_call(
        solve_three_kernel, "solve_three", consts,
        [right, mapped, residue, through, totals_one, totals_two, planes[:, :2], planes[:, 2]],
        [image_out, image_out, image_out, sums_out],
    )
    totals_three = sum_rows(own_sums, parts, 4)
    grad, edges, scalars = solve_call(
        solve_four_kernel, "solve_four", consts,
        [right, mapped, residue, denoised, search, searched, slope, totals_one, totals_two, totals_three, own_sums, maps, normal_high, normal_low],
        [image_out, ((2, micro, 8, wide), 1), sums_out],
    )

    halo = halo_exchange(edges, parts, 2)
    grad_stack = shifted_image(grad, halo, parts)
    weight_sums = [None] * 5
    gain_rows, shift_rows = [None] * 4, [None] * 4
    table = jnp.pad(backward_table(low[4]), ((0, 0), (0, 16 - 3 * low[4].shape[1])))
    layer, halo, coefs, rows_out = kept[3]
    grads, stats, weight_sums[4] = backward_layer([grad_stack], layer, halo, coefs, table, length, parts)
    for index in (3, 2, 1, 0):
        layer, halo, coefs, rows_out = kept[index]
        grads_halo, coefs_back, totals = layer_sums(grads, stats, rows_out, pixel_part, parts, images, count, True, 5)
        shift_rows[index] = jnp.sum(totals[0].reshape(micro, channels), 0)
        gain_rows[index] = jnp.sum(totals[1].reshape(micro, channels), 0)
        if index > 0:
            below, below_halo, below_coefs, _ = kept[index - 1]
            grads, stats, weight_sums[index] = backward_layer(
                [grads, grads_halo, layer, halo, coefs_back], below, below_halo, below_coefs, backward_table(low[index]), length, parts
            )
        else:
            centre = jnp.pad(image_stack[:, 2:4], ((0, 0), (0, 14), (0, 0)))
            weight_sums[0] = backward_first(grads, layer, coefs_back, centre, length)
    first_grad = weight_grad_of(weight_sums[0], channels, 16)[:, :, :2]
    middle_grad = jnp.stack([weight_grad_of(weight_sums[index], channels, channels) for index in (1, 2, 3)])
    last_grad = weight_grad_of(weight_sums[4][:6], 2, channels)
    scalars = jnp.sum(scalars[:, :, 0], axis=0)
    extra_grad = jnp.stack([scalars[0], scalars[1], penalty * scalars[2]])
    first_grad, middle_grad, last_grad, extra_grad, loss = lax.psum(
        (first_grad, middle_grad, last_grad, extra_grad, scalars[3]), ("img", "row")
    )
    return (first_grad, middle_grad, last_grad, jnp.stack(gain_rows), jnp.stack(shift_rows), extra_grad, loss), pixel_total


def local(
    kspace,
    coil_maps,
    target,
    row_mask,
    foreground,
    anatomy,
    first_weight,
    middle_weight,
    last_weight,
    norm_gains,
    norm_shifts,
    extra_params,
    first_mean,
    first_square,
    middle_mean,
    middle_square,
    last_mean,
    last_square,
    gains_mean,
    gains_square,
    shifts_mean,
    shifts_square,
    extra_mean,
    extra_square,
):
    arrays = (
        kspace, coil_maps, target, row_mask, foreground, anatomy, first_weight, middle_weight, last_weight, norm_gains, norm_shifts, extra_params,
    )
    gradients = fast_local if fits(kspace, first_weight, lax.axis_size("row")) else general_local
    totals, pixel_total = gradients(arrays)
    params = (first_weight, middle_weight, last_weight, norm_gains, norm_shifts, extra_params)
    moments = (
        (first_mean, first_square),
        (middle_mean, middle_square),
        (last_mean, last_square),
        (gains_mean, gains_square),
        (shifts_mean, shifts_square),
        (extra_mean, extra_square),
    )
    results = []
    for group in range(6):
        updated, first_new, second_new = adamw(
            params[group], totals[group], moments[group][0], moments[group][1], LEARN_RATES[group]
        )
        results.extend([updated, first_new, second_new])
        if group < 3:
            results.append(updated.astype(jnp.bfloat16))
    return tuple(results) + (totals[6], pixel_total.astype(jnp.int32))


def solution(mesh):
    in_specs = (
        P(None, "img", None, None, "row", None),
        P(None, "img", None, None, "row", None),
        P(None, "img", None, "row", None),
        P(None, "img", None),
        P(None, "img", "row", None),
        P(None, "img"),
        P(),
        P(),
        P(),
        P(),
        P(),
        P(),
        P(),
        P(),
        P(),
        P(),
        P(),
        P(),
        P(),
        P(),
        P(),
        P(),
        P(),
        P(),
    )
    out_specs = (
        P(),
        P(),
        P(),
        P(),
        P(),
        P(),
        P(),
        P(),
        P(),
        P(),
        P(),
        P(),
        P(),
        P(),
        P(),
        P(),
        P(),
        P(),
        P(),
        P(),
        P(),
        P(),
        P(),
    )
    return jax.shard_map(local, mesh=mesh, in_specs=in_specs, out_specs=out_specs, check_vma=False)
```

```python
import functools

import jax
import jax.numpy as jnp
import numpy as np
from jax import lax
from jax.experimental import pallas as pl
from jax.experimental.pallas import tpu as pltpu
from jax.sharding import PartitionSpec as P

COILS = 16
BRAIN_COILS = 12
UNROLLS = 1
CG_STEPS = 2
STEP = 10


PRECISE = lax.Precision.HIGHEST
EPS_NORM = 1e-05
BETA_ONE = 0.9
BETA_TWO = 0.999
ADAM_EPS = 1e-08
DECAY_RATE = 0.01
LEARN_RATES = (0.3, 0.05, 0.05, 0.4, 0.4, 0.4)


def with_halo(cells, sides, width):
    for axis, dim in sides:
        count = lax.axis_size(axis)
        ends = count - 1
        head = lax.slice_in_dim(cells, 0, width, axis=dim)
        tail = lax.slice_in_dim(cells, cells.shape[dim] - width, cells.shape[dim], axis=dim)
        cells = jnp.concatenate(
            [
                lax.ppermute(tail, axis, [(i, (i + 1) % count) for i in range(ends)]),
                cells,
                lax.ppermute(head, axis, [((i + 1) % count, i) for i in range(ends)]),
            ],
            axis=dim,
        )
    return cells


def dft_table(length, direction):
    index = jnp.arange(length, dtype=jnp.int32)
    phase = (index[:, None] * index[None, :] % length).astype(jnp.float32) * (2.0 * jnp.pi / length)
    factor = 1.0 / jnp.sqrt(jnp.float32(length))
    cosine = jnp.cos(phase) * factor
    sine = jnp.sin(phase) * factor * direction
    return jnp.stack([jnp.stack([cosine, -sine], 1), jnp.stack([sine, cosine], 1)], 0)


def along_width(field, table):
    return jnp.einsum("bcprw,pwqk->bcqrk", field, table, precision=PRECISE)


def along_height(field, table):
    return jnp.einsum("bcprw,prqk->bcqkw", field, table, precision=PRECISE)


def expand(image, maps):
    real_part, imag_part = (image[:, None, 0], image[:, None, 1])
    maps_re, maps_im = (maps[:, :, 0], maps[:, :, 1])
    return jnp.stack(
        [maps_re * real_part - maps_im * imag_part, maps_re * imag_part + maps_im * real_part], 2
    )


def combine(field, maps):
    field_re, field_im = (field[:, :, 0], field[:, :, 1])
    maps_re, maps_im = (maps[:, :, 0], maps[:, :, 1])
    return jnp.stack(
        [
            jnp.sum(maps_re * field_re + maps_im * field_im, 1),
            jnp.sum(maps_re * field_im - maps_im * field_re, 1),
        ],
        1,
    )


def to_columns(field):
    return lax.all_to_all(
        field.astype(jnp.bfloat16), "row", split_axis=4, concat_axis=3, tiled=True
    ).astype(field.dtype)


def to_rows(field):
    return lax.all_to_all(
        field.astype(jnp.bfloat16), "row", split_axis=3, concat_axis=4, tiled=True
    ).astype(field.dtype)


def make_normal(maps, mask_rows, forward, inverse, measured):
    zero_filled = combine(to_rows(along_height(measured * mask_rows, inverse)), maps)

    def normal(image):
        spectrum = to_columns(along_width(expand(image, maps), forward))
        spectrum = along_height(spectrum, forward) * mask_rows
        spectrum = to_rows(along_height(spectrum, inverse))
        return combine(along_width(spectrum, inverse), maps)

    return (normal, zero_filled)


def inner(left, right):
    return jnp.sum(left * right, axis=(1, 2, 3))


def per_image(values):
    return values[:, None, None, None]


def row_sums(values):
    return lax.psum(values, "row")


def solve(rhs, penalty, normal):
    state = jnp.zeros_like(rhs)
    residue = rhs
    search = rhs
    norm_now = row_sums(inner(residue, residue))
    kept = []
    for iterate in range(CG_STEPS):
        mapped = normal(search) + penalty * search
        curvature = row_sums(inner(search, mapped))
        stepsize = norm_now / curvature
        state = state + per_image(stepsize) * search
        residue = residue - per_image(stepsize) * mapped
        norm_next = row_sums(inner(residue, residue))
        kept.append((search, mapped, residue, norm_now, norm_next, curvature))
        search = residue + per_image(norm_next / norm_now) * search
        norm_now = norm_next
    return (state, kept)


def solve_backward(state_grad, kept, rhs, denoised, penalty, normal):
    search_grad = jnp.zeros_like(rhs)
    residue_grad = jnp.zeros_like(rhs)
    norm_grad = jnp.zeros(rhs.shape[0], jnp.float32)
    penalty_part = jnp.float32(0.0)
    for iterate in reversed(range(CG_STEPS)):
        search, mapped, residue, norm_now, norm_next, curvature = kept[iterate]
        factor_grad, along_search, joint_mapped, residue_mapped = lax.psum(
            (
                inner(search_grad, search),
                inner(state_grad, search),
                inner(residue_grad + search_grad, mapped),
                inner(residue, mapped),
            ),
            "row",
        )
        stepsize = norm_now / curvature
        factor = norm_next / norm_now
        norm_total = norm_grad + factor_grad / norm_now
        residue_full = residue_grad + search_grad + per_image(2.0 * norm_total) * residue
        stepsize_grad = along_search - (joint_mapped + 2.0 * norm_total * residue_mapped)
        curvature_grad = -stepsize_grad * norm_now / (curvature * curvature)
        mapped_grad = -per_image(stepsize) * residue_full + per_image(curvature_grad) * search
        penalty_part = penalty_part + jnp.sum(mapped_grad * search)
        search_grad = (
            per_image(factor) * search_grad
            + per_image(stepsize) * state_grad
            + per_image(curvature_grad) * mapped
            + normal(mapped_grad)
            + penalty * mapped_grad
        )
        residue_grad = residue_full
        norm_grad = -factor_grad * norm_next / (norm_now * norm_now) + stepsize_grad / curvature
    rhs_grad = residue_grad + search_grad + per_image(2.0 * norm_grad) * rhs
    penalty_part = penalty_part + jnp.sum(rhs_grad * denoised)
    return (penalty * rhs_grad, penalty_part)


def conv_forward(activation, weight):
    height, breadth = (activation.shape[2], activation.shape[3])
    padded = with_halo(activation, (("row", 2),), 1)
    padded = jnp.pad(padded, ((0, 0), (0, 0), (0, 0), (1, 1)))
    summed = jnp.zeros((activation.shape[0], weight.shape[1], height, breadth), jnp.float32)
    for tap_index in range(9):
        window = padded[
            :, :, tap_index // 3 : tap_index // 3 + height, tap_index % 3 : tap_index % 3 + breadth
        ]
        summed = summed + jnp.einsum(
            "oi,birw->borw", weight[tap_index], window, preferred_element_type=jnp.float32
        )
    return (summed, padded)


def conv_backward(upstream, padded, weight, need_input):
    height, breadth = (upstream.shape[2], upstream.shape[3])
    weight_grad = jnp.stack(
        [
            jnp.einsum(
                "borw,birw->oi",
                upstream,
                padded[
                    :,
                    :,
                    tap_index // 3 : tap_index // 3 + height,
                    tap_index % 3 : tap_index % 3 + breadth,
                ],
                preferred_element_type=jnp.float32,
            )
            for tap_index in range(9)
        ]
    )
    if not need_input:
        return (weight_grad, None)
    widened = with_halo(upstream, (("row", 2),), 1)
    widened = jnp.pad(widened, ((0, 0), (0, 0), (0, 0), (1, 1)))
    summed = jnp.zeros((upstream.shape[0], weight.shape[2], height, breadth), jnp.float32)
    for tap_index in range(9):
        start_r = 2 - tap_index // 3
        start_c = 2 - tap_index % 3
        window = widened[:, :, start_r : start_r + height, start_c : start_c + breadth]
        summed = summed + jnp.einsum(
            "oi,borw->birw", weight[tap_index], window, preferred_element_type=jnp.float32
        )
    return (weight_grad, summed)


def norm_sums(values):
    return lax.psum(values, ("img", "row"))


def channel(values):
    return values[None, :, None, None]


def cnn_forward(image, weights, gains, shifts, offset, pixels):
    activation = image.astype(jnp.bfloat16)
    kept = []
    for layer_index in range(4):
        linear, padded = conv_forward(activation, weights[layer_index])
        average = norm_sums(jnp.sum(linear, axis=(0, 2, 3))) / pixels
        centred = linear - channel(average)
        spread = norm_sums(jnp.sum(centred * centred, axis=(0, 2, 3))) / pixels
        inv_std = lax.rsqrt(spread + EPS_NORM)
        normed = centred * channel(inv_std)
        shaped = channel(gains[layer_index]) * normed + channel(shifts[layer_index])
        activation = jax.nn.silu(shaped).astype(jnp.bfloat16)
        kept.append((padded, normed, shaped, inv_std))
    result, padded = conv_forward(activation, weights[4])
    kept.append(padded)
    return (image + result + channel(offset), kept)


def cnn_backward(denoised_grad, kept, weights, gains, pixels, need_input):
    offset_grad = jnp.sum(denoised_grad, axis=(0, 2, 3))
    weight_grads = [None] * 5
    gain_grads = [None] * 4
    shift_grads = [None] * 4
    weight_grads[4], upstream = conv_backward(
        denoised_grad.astype(jnp.bfloat16), kept[4], weights[4], True
    )
    for layer_index in (3, 2, 1, 0):
        padded, normed, shaped, inv_std = kept[layer_index]
        sigmoid_val = jax.nn.sigmoid(shaped)
        shaped_grad = upstream * sigmoid_val * (1.0 + shaped * (1.0 - sigmoid_val))
        shift_local = jnp.sum(shaped_grad, axis=(0, 2, 3))
        gain_local = jnp.sum(shaped_grad * normed, axis=(0, 2, 3))
        shift_total, gain_total = lax.psum((shift_local, gain_local), ("img", "row"))
        gain_vec = gains[layer_index]
        linear_grad = channel(inv_std) * (
            shaped_grad * channel(gain_vec)
            - channel(gain_vec * shift_total / pixels)
            - normed * channel(gain_vec * gain_total / pixels)
        )
        shift_grads[layer_index] = shift_local
        gain_grads[layer_index] = gain_local
        weight_grads[layer_index], upstream = conv_backward(
            linear_grad.astype(jnp.bfloat16),
            padded,
            weights[layer_index],
            layer_index > 0 or need_input,
        )
    image_grad = None
    return (image_grad, weight_grads, jnp.stack(gain_grads), jnp.stack(shift_grads), offset_grad)


def adamw(weight, gradient, moment_one, moment_two, rate):
    first_new = BETA_ONE * moment_one + (1.0 - BETA_ONE) * gradient
    second_new = BETA_TWO * moment_two + (1.0 - BETA_TWO) * gradient * gradient
    corrected = first_new / (1.0 - BETA_ONE**STEP)
    divisor = jnp.sqrt(second_new / (1.0 - BETA_TWO**STEP)) + ADAM_EPS
    updated = weight - rate * (corrected / divisor + DECAY_RATE * weight)
    return (updated, first_new, second_new)


def general_local(arrays):
    (
        kspace, coil_maps, target, row_mask, foreground, anatomy, first_weight, middle_weight, last_weight, norm_gains, norm_shifts, extra_params,
    ) = arrays
    length = kspace.shape[-1]
    forward = dft_table(length, 1.0)
    inverse = dft_table(length, -1.0)
    pixel_total = lax.psum(jnp.sum(foreground).astype(jnp.float32), ("img", "row"))
    inv_count = 1.0 / pixel_total
    middle_low = middle_weight.astype(jnp.bfloat16)
    conv_weights = [
        first_weight.astype(jnp.bfloat16),
        middle_low[0],
        middle_low[1],
        middle_low[2],
        last_weight.astype(jnp.bfloat16),
    ]
    penalty = jnp.exp(extra_params[2])
    offset = extra_params[:2]
    images_here = kspace.shape[1]
    pixels = images_here * kspace.shape[4] * length * lax.axis_size("img") * lax.axis_size("row")
    first_grad = jnp.zeros_like(first_weight)
    middle_grad = jnp.zeros_like(middle_weight)
    last_grad = jnp.zeros_like(last_weight)
    gains_grad = jnp.zeros_like(norm_gains)
    shifts_grad = jnp.zeros_like(norm_shifts)
    offset_grad = jnp.zeros((2,), jnp.float32)
    penalty_grad = jnp.float32(0.0)
    loss_part = jnp.float32(0.0)
    for microbatch in range(kspace.shape[0]):
        limit = jnp.where(anatomy[microbatch] == 0, BRAIN_COILS, COILS)
        coil_on = (jnp.arange(kspace.shape[2])[None, :] < limit[:, None]).astype(jnp.float32)
        maps = coil_maps[microbatch] * coil_on[:, :, None, None, None]
        mask_rows = row_mask[microbatch].astype(jnp.float32)[:, None, None, :, None]
        measured = to_columns(along_width(kspace[microbatch], inverse))
        normal, zero_filled = make_normal(maps, mask_rows, forward, inverse, measured)
        state = zero_filled
        unroll = 0
        denoised, cnn_kept = cnn_forward(
            state, conv_weights, norm_gains, norm_shifts, offset, pixels
        )
        rhs = zero_filled + penalty * denoised
        state, cg_kept = solve(rhs, penalty, normal)
        saved = [(cnn_kept, cg_kept, rhs, denoised)]
        fg_mask = foreground[microbatch].astype(jnp.float32)[:, None]
        difference = state - target[microbatch]
        loss_part = loss_part + jnp.sum(fg_mask * difference * difference)
        state_grad = inv_count * 2.0 * fg_mask * difference
        for unroll in reversed(range(UNROLLS)):
            cnn_kept, cg_kept, rhs, denoised = saved[unroll]
            denoised_grad, penalty_part = solve_backward(
                state_grad, cg_kept, rhs, denoised, penalty, normal
            )
            penalty_grad = penalty_grad + penalty_part
            state_grad, weight_grads, gain_part, shift_part, offset_part = cnn_backward(
                denoised_grad, cnn_kept, conv_weights, norm_gains, pixels, unroll > 0
            )
            first_grad = first_grad + weight_grads[0]
            middle_grad = middle_grad + jnp.stack(weight_grads[1:4])
            last_grad = last_grad + weight_grads[4]
            gains_grad = gains_grad + gain_part
            shifts_grad = shifts_grad + shift_part
            offset_grad = offset_grad + offset_part
    extra_grad = jnp.concatenate([offset_grad, (penalty * penalty_grad)[None]])
    totals = lax.psum(
        (first_grad, middle_grad, last_grad, gains_grad, shifts_grad, extra_grad, loss_part),
        ("img", "row"),
    )
    return totals, pixel_total


BF16 = jnp.bfloat16
F32 = jnp.float32
MESH = pl.DeviceIdType.MESH
TILE = 128
BLOCK = 8
VMEM_BYTES = 58 * 1024 * 1024


def padded(length):
    return -(-length // TILE) * TILE


def fits(kspace, first_weight, mesh_rows):
    micro, images, coils, _, rows, length = kspace.shape
    channels = first_weight.shape[1]
    return (
        images == 1
        and micro == 2
        and 2 * channels == TILE
        and channels % 16 == 0
        and rows * mesh_rows == length
        and rows % BLOCK == 0
        and (2 * rows) % 16 == 0
        and (coils * rows) % TILE == 0
        and padded(length) > length
    )


def phases(length):
    index = np.arange(length)
    angle = 2.0 * np.pi * (np.outer(index, index) % length) / length
    return np.cos(angle) / np.sqrt(length), np.sin(angle) / np.sqrt(length)


def high_low(table):
    high = table.astype(BF16)
    low = (table - high.astype(F32)).astype(BF16)
    return high, low


def np_high_low(table):
    table = np.asarray(table, np.float32)
    high = table.astype(BF16)
    low = (table - high.astype(np.float32)).astype(BF16)
    return jnp.asarray(high), jnp.asarray(low)


def dot(left, right):
    return jnp.dot(left, right, preferred_element_type=F32)


def dot_nt(left, right):
    return lax.dot_general(left, right, (((1,), (1,)), ((), ())), preferred_element_type=F32)


def greet(peers):
    barrier = pltpu.get_barrier_semaphore()
    for peer in peers:
        pl.semaphore_signal(barrier, inc=1, device_id=peer, device_id_type=MESH)
    pl.semaphore_wait(barrier, len(peers))


def row_peers(rows):
    image, row = lax.axis_index("img"), lax.axis_index("row")
    return [(image, lax.rem(row + step, rows)) for step in range(1, rows)]


def image_peers(images):
    image, row = lax.axis_index("img"), lax.axis_index("row")
    return [(lax.rem(image + step, images), row) for step in range(1, images)]


def remote(source, target, send, receive, peer):
    return pltpu.make_async_remote_copy(
        src_ref=source,
        dst_ref=target,
        send_sem=send,
        recv_sem=receive,
        device_id=peer,
        device_id_type=MESH,
    )


def params(vmem=VMEM_BYTES, **kwargs):
    return pltpu.CompilerParams(vmem_limit_bytes=vmem, **kwargs)


def in_vmem():
    return pl.BlockSpec(memory_space=pltpu.VMEM)


def anywhere():
    return pl.BlockSpec(memory_space=pl.ANY)


def three_parts(values):
    high = values.astype(BF16)
    rest = values - high.astype(F32)
    middle = rest.astype(BF16)
    return high, middle, (rest - middle.astype(F32)).astype(BF16)


def join_lanes(pieces, wide):
    short = wide - sum(piece.shape[1] for piece in pieces)
    if short:
        pieces = pieces + [jnp.zeros((pieces[0].shape[0], short), pieces[0].dtype)]
    return jnp.concatenate(pieces, axis=1)


def join_rows(pieces, height):
    short = height - sum(piece.shape[0] for piece in pieces)
    if short:
        pieces = pieces + [jnp.zeros((short, pieces[0].shape[1]), pieces[0].dtype)]
    return jnp.concatenate(pieces, axis=0)


def exchange_kernel(
    sizes, kspace, maps, target, foreground, row_mask, first, middle, last, turn_high, turn_low, pick, cosine, sine,
    spread, planes, normal_high, normal_low, first_table, middle_tables, last_table, middle_back, last_back, counted,
    staged, flat, landed, send, receive, own, send_flat, receive_flat,
):
    micro, coils, rows, length, parts = sizes
    wide = padded(length)
    me = lax.axis_index("row")
    peers = row_peers(parts)
    greet(peers)
    copies = []
    slabs = 2 * rows
    order = sorted(range(1, parts), key=lambda step: -min(step, parts - step))
    for batch in range(micro):
        for kind in range(2):
            total = None
            for part in range(2):
                source = (kspace, maps)[kind]
                field = source[batch, :, part].reshape(coils * rows, length)
                if kind == 0:
                    high, low = high_low(field)
                    term = (
                        dot_nt(turn_high[part], high)
                        + dot_nt(turn_low[part], high)
                        + dot_nt(turn_high[part], low)
                    )
                else:
                    term = dot_nt(pick[part], field.astype(BF16))
                total = term if total is None else total + term
            slot = 2 * batch + kind
            staged[slot] = total.astype(BF16).reshape(parts, slabs, coils * rows)
            local = pltpu.make_async_copy(staged.at[slot, me], spread.at[slot, me], own.at[slot])
            local.start()
            copies.append(local)
            for step in order:
                peer = peers[step - 1]
                copy = remote(
                    staged.at[slot, peer[1]],
                    spread.at[slot, me],
                    send.at[slot, step - 1],
                    receive.at[slot, step - 1],
                    peer,
                )
                copy.start()
                copies.append(copy)
    shown = [foreground[batch].astype(F32) for batch in range(micro)]
    count = functools.reduce(jnp.add, [jnp.sum(jnp.sum(s, axis=1, keepdims=True), axis=0, keepdims=True) for s in shown])
    counted[...] = jnp.broadcast_to(count, (1, TILE))
    stack = []
    for batch in range(micro):
        stack += [target[batch, 0], target[batch, 1], shown[batch]]
    stack = jnp.concatenate(stack, axis=0)
    plain = pick[0].reshape(parts, slabs, length)[:, :rows].reshape(length, length)
    turned = functools.reduce(jnp.add, [dot_nt(plain, piece) for piece in three_parts(stack)])
    lanes = flat.shape[2]
    flat[...] = join_lanes([turned], lanes).reshape(parts, rows, lanes)
    landed[me] = flat[me]
    flats = []
    for step in order:
        peer = peers[step - 1]
        copy = remote(flat.at[peer[1]], landed.at[me], send_flat.at[step - 1], receive_flat.at[step - 1], peer)
        copy.start()
        flats.append(copy)
    for batch in range(micro):
        chosen = join_lanes([row_mask[batch].astype(F32)], wide)
        cos_on, sin_on = cosine[...] * chosen, sine[...] * chosen

        def product(left, right):
            return jnp.dot(left, right, precision=PRECISE, preferred_element_type=F32)

        real = product(cos_on, cosine[...]) + product(sin_on, sine[...])
        imag = product(sin_on, cosine[...]) - product(cos_on, sine[...])
        for block, value in (((0, 0), real), ((0, 1), -imag), ((1, 0), imag), ((1, 1), real)):
            high, low = high_low(value)
            at = (batch, pl.ds(block[0] * wide, wide), pl.ds(block[1] * wide, wide))
            normal_high[at] = high
            normal_low[at] = low
    put_tables(first, middle, last, first_table, middle_tables, last_table, middle_back, last_back)
    for copy in flats:
        copy.wait()
    for batch in range(micro):
        for plane in range(3):
            at = (3 * batch + plane) * rows
            planes[batch, plane] = join_lanes([landed[block, :, at : at + rows] for block in range(parts)], wide)
    for copy in copies:
        copy.wait()


def put_tables(first, middle, last, first_table, middle_tables, last_table, middle_back, last_back):
    taps = range(3)
    first_table[...] = jnp.concatenate(
        [join_lanes([first[3 * kr + kw] for kr in taps], 16) for kw in taps], axis=0
    ).astype(BF16)
    last_table[...] = jnp.concatenate(
        [join_rows([jnp.concatenate([last[3 * kr + kw] for kr in taps], axis=1)], 8) for kw in taps], axis=0
    ).astype(BF16)
    turned = [join_rows([last[tap]], 8).T[:, :2] for tap in range(9)]
    last_back[...] = jnp.concatenate(
        [join_lanes([turned[3 * (2 - m) + 2 - n] for m in taps], 16) for n in taps], axis=0
    ).astype(BF16)
    for layer in range(3):
        weights = [middle[layer, tap] for tap in range(9)]
        turned = [weight.T for weight in weights]
        middle_tables[layer] = jnp.concatenate(
            [jnp.concatenate([weights[3 * kr + kw] for kr in taps], axis=1) for kw in taps], axis=0
        ).astype(BF16)
        middle_back[layer] = jnp.concatenate(
            [jnp.concatenate([turned[3 * (2 - m) + 2 - n] for m in taps], axis=1) for n in taps], axis=0
        ).astype(BF16)


def exchange(kspace, maps, target, foreground, row_mask, first, middle, last, parts):
    micro, coils, _, rows, length = kspace.shape
    wide = padded(length)
    channels = first.shape[1]
    cosine, sine = phases(length)
    inverse = np.stack([np.stack([cosine, sine], 0), np.stack([-sine, cosine], 0)], 0)
    turn = inverse.reshape(2, 2, length, parts, rows).transpose(0, 3, 1, 4, 2).reshape(2, 2 * length, length)
    pick = np.zeros((2, parts, 2, rows, length), np.float32)
    for part in range(2):
        for block in range(parts):
            pick[part, block, part, :, block * rows : (block + 1) * rows] = np.eye(rows)
    pick = jnp.asarray(pick.reshape(2, 2 * length, length).astype(BF16))
    turn_high, turn_low = np_high_low(turn)
    edge = ((0, wide - length), (0, wide - length))
    cosine = jnp.asarray(np.pad(cosine, edge), F32)
    sine = jnp.asarray(np.pad(sine, edge), F32)
    sizes = (micro, coils, rows, length, parts)
    slots = 2 * micro
    lanes = padded(3 * micro * rows)
    shapes = [
        ((slots, parts, 2 * rows, coils * rows), BF16),
        ((micro, 3, rows, wide), F32),
        ((micro, 2 * wide, 2 * wide), BF16),
        ((micro, 2 * wide, 2 * wide), BF16),
        ((3 * channels, 16), BF16),
        ((3, 3 * channels, 3 * channels), BF16),
        ((24, 3 * channels), BF16),
        ((3, 3 * channels, 3 * channels), BF16),
        ((3 * channels, 16), BF16),
        ((1, TILE), F32),
    ]
    return pl.pallas_call(
        functools.partial(exchange_kernel, sizes),
        out_shape=[jax.ShapeDtypeStruct(*shape) for shape in shapes],
        in_specs=[in_vmem()] * 13,
        out_specs=[anywhere()] + [in_vmem()] * 9,
        scratch_shapes=[
            pltpu.VMEM((slots, parts, 2 * rows, coils * rows), BF16),
            pltpu.VMEM((parts, rows, lanes), F32),
            pltpu.VMEM((parts, rows, lanes), F32),
            pltpu.SemaphoreType.DMA((slots, parts - 1)),
            pltpu.SemaphoreType.DMA((slots, parts - 1)),
            pltpu.SemaphoreType.DMA((slots,)),
            pltpu.SemaphoreType.DMA((parts - 1,)),
            pltpu.SemaphoreType.DMA((parts - 1,)),
        ],
        compiler_params=params(collective_id=1, has_side_effects=True),
        name="exchange",
    )(kspace, maps, target, foreground, row_mask, first, middle, last, turn_high, turn_low, pick, cosine, sine)


def gather_lanes(blocks, coil, rows, wide):
    pieces = [block[:, coil * rows : (coil + 1) * rows] for block in blocks]
    height = pieces[0].shape[0]
    short = wide - rows * len(pieces)
    return jnp.concatenate(pieces + [jnp.zeros((height, short), pieces[0].dtype)], axis=1)


def zero_fill_kernel(sizes, anatomy, fields, mask, fourier_high, fourier_low, filled, maps_out, edges):
    coils, rows, length, parts = sizes
    wide = padded(length)
    chosen = join_lanes([mask[...].astype(F32)], wide).astype(BF16)
    knee = anatomy[pl.program_id(0)]
    real = jnp.zeros((rows, wide), F32)
    imag = jnp.zeros((rows, wide), F32)
    group = 4
    for first in range(0, coils, group):
        stack = []
        for coil in range(first, first + group):
            on = jnp.where((coil < BRAIN_COILS) | (knee > 0), 1.0, 0.0).astype(BF16)
            maps_out[coil] = gather_lanes([fields[1, s] for s in range(parts)], coil, rows, wide) * on
            stack.append(gather_lanes([fields[0, s] for s in range(parts)], coil, rows, wide) * chosen)
        stack = jnp.concatenate(stack, axis=0)
        turned = dot(stack, fourier_high[...]) + dot(stack, fourier_low[...])
        for place in range(group):
            top = 2 * rows * place
            upper, lower = turned[top : top + rows], turned[top + rows : top + 2 * rows]
            field_re = upper[:, :wide] - lower[:, wide:]
            field_im = upper[:, wide:] + lower[:, :wide]
            sense = maps_out[first + place].astype(F32)
            sense_re, sense_im = sense[:rows], sense[rows:]
            real = real + sense_re * field_re + sense_im * field_im
            imag = imag + sense_re * field_im - sense_im * field_re
    filled[0] = real
    filled[1] = imag
    put_edges(edges, real, imag)


def put_edges(edges, real, imag):
    rows, wide = real.shape
    zeros = jnp.zeros((6, wide), F32)
    edges[0] = jnp.concatenate([real[:1], imag[:1], zeros], axis=0)
    edges[1] = jnp.concatenate([real[rows - 1 :], imag[rows - 1 :], zeros], axis=0)


def zero_fill(fields, mask, anatomy, rows, length):
    slots, parts, slabs, lanes = fields.shape
    micro, coils, wide = slots // 2, lanes // rows, padded(length)
    cosine, sine = phases(length)
    table = np.zeros((wide, 2, wide))
    table[:length, 0, :length] = cosine
    table[:length, 1, :length] = sine
    high, low = np_high_low(table.reshape(wide, 2 * wide))
    sizes = (coils, rows, length, parts)
    return pl.pallas_call(
        functools.partial(zero_fill_kernel, sizes),
        grid_spec=pltpu.PrefetchScalarGridSpec(
            num_scalar_prefetch=1,
            grid=(micro,),
            in_specs=[
                pl.BlockSpec((None, 2, parts, slabs, lanes), lambda b, _: (b, 0, 0, 0, 0)),
                pl.BlockSpec((None, 1, length), lambda b, _: (b, 0, 0)),
                pl.BlockSpec((wide, 2 * wide), lambda b, _: (0, 0)),
                pl.BlockSpec((wide, 2 * wide), lambda b, _: (0, 0)),
            ],
            out_specs=[
                pl.BlockSpec((None, 2, rows, wide), lambda b, _: (b, 0, 0, 0)),
                pl.BlockSpec((None, coils, slabs, wide), lambda b, _: (b, 0, 0, 0)),
                pl.BlockSpec((2, None, 8, wide), lambda b, _: (0, b, 0, 0)),
            ],
        ),
        out_shape=[
            jax.ShapeDtypeStruct((micro, 2, rows, wide), F32),
            jax.ShapeDtypeStruct((micro, coils, slabs, wide), BF16),
            jax.ShapeDtypeStruct((2, micro, 8, wide), F32),
        ],
        compiler_params=params(),
        name="zero_fill",
    )(anatomy, fields.reshape(micro, 2, parts, slabs, lanes), mask, high, low)


def lane_row(columns):
    return jnp.sum(columns.T, axis=0, keepdims=True)


def spread_row(row):
    return jnp.broadcast_to(row, (TILE, row.shape[1])).T


def padded_rows(rows):
    return join_rows([join_lanes([row], TILE) for row in rows], 8)


def merge(sums, squares, count):
    total = functools.reduce(jnp.add, sums)
    mean = total / (count * len(sums))
    square = None
    for part, own in zip(sums, squares):
        shift = part / count - mean
        term = own + count * shift * shift
        square = term if square is None else square + term
    return total, square


def repeat_lanes(block, wide):
    return jnp.concatenate([block] * (wide // TILE), axis=1)


def lane_mask(length, wide):
    whole = length // TILE * TILE

    def clear(values):
        tail = values[:, whole:]
        keep = lax.broadcasted_iota(jnp.int32, tail.shape, 1) < length - whole
        return jnp.concatenate([values[:, :whole], jnp.where(keep, tail, 0.0)], axis=1)

    return clear


def fold(values):
    parts = [values[:, at : at + TILE] for at in range(0, values.shape[1], TILE)]
    return functools.reduce(jnp.add, parts)


def put_shifted(stack, values, at):
    channels, wide = values.shape
    stack[0:channels, pl.ds(at, wide)] = pltpu.roll(values, 1, 1)
    stack[channels : 2 * channels, pl.ds(at, wide)] = values
    stack[2 * channels : 3 * channels, pl.ds(at, wide)] = pltpu.roll(values, wide - 1, 1)


def lane_at(column, wide):
    return pl.multiple_of(column * wide, TILE) if not isinstance(column, int) else column * wide


def columns_at(stack, column, number, wide):
    return stack[:, pl.ds(lane_at(column, wide), number * wide)]


class Sums:
    def __init__(self, parts, images, refs):
        self.message, self.held, self.second, self.held_second, self.send, self.receive = refs
        self.rows, self.cols = row_peers(parts), image_peers(images)

    def copies(self, slot, stage):
        source, target = ((self.message, self.held), (self.second, self.held_second))[stage]
        peers = (self.rows, self.cols)[stage]
        base = stage * len(self.rows)
        return [
            remote(
                source.at[slot],
                target.at[slot + (index,)],
                self.send.at[slot + (base + index,)],
                self.receive.at[slot + (base + index,)],
                peer,
            )
            for index, peer in enumerate(peers)
        ]

    def start(self, slot, stage, values):
        (self.message, self.second)[stage][slot] = values
        for copy in self.copies(slot, stage):
            copy.start()

    def collect(self, slot, stage):
        blocks = [(self.message, self.second)[stage][slot]]
        for index, copy in enumerate(self.copies(slot, stage)):
            copy.wait_recv()
            blocks.append((self.held, self.held_second)[stage][slot + (index,)])
        return blocks

    def settle(self, slot, stages=(0, 1)):
        for stage in stages:
            for copy in self.copies(slot, stage):
                copy.wait_send()

    @staticmethod
    def scratch(slots, parts, images):
        return [
            pltpu.VMEM(slots + (8, TILE), F32),
            pltpu.VMEM(slots + (parts - 1, 8, TILE), F32),
            pltpu.VMEM(slots + (8, TILE), F32),
            pltpu.VMEM(slots + (max(images - 1, 1), 8, TILE), F32),
            pltpu.SemaphoreType.DMA(slots + (parts + images - 2,)),
            pltpu.SemaphoreType.DMA(slots + (parts + images - 2,)),
        ]


class Halo:
    def __init__(self, parts, send, receive):
        self.image, self.me = lax.axis_index("img"), lax.axis_index("row")
        self.parts, self.send, self.receive = parts, send, receive
        self.has_left, self.has_right = self.me > 0, self.me < parts - 1

    def copies(self, band, slot):
        width = band.shape[0] - 2
        left = (self.image, jnp.maximum(self.me - 1, 0))
        right = (self.image, jnp.minimum(self.me + 1, self.parts - 1))
        send, receive = self.send, self.receive
        to_left = remote(band.at[1], band.at[width + 1], send.at[slot + (0,)], receive.at[slot + (0,)], left)
        to_right = remote(band.at[width], band.at[0], send.at[slot + (1,)], receive.at[slot + (1,)], right)
        return to_left, to_right

    def start(self, band, slot):
        to_left, to_right = self.copies(band, slot)
        pl.when(self.has_left)(to_left.start)
        pl.when(self.has_right)(to_right.start)

    def arrive(self, band, slot):
        to_left, to_right = self.copies(band, slot)
        pl.when(self.has_right)(to_left.wait_recv)
        pl.when(self.has_left)(to_right.wait_recv)

    def settle(self, band, slot):
        to_left, to_right = self.copies(band, slot)
        pl.when(self.has_left)(to_left.wait_send)
        pl.when(self.has_right)(to_right.wait_send)


def ring_sum(table, stack, carry, first, out_rows, wide, emit):
    older, newer = carry[0:out_rows], carry[out_rows : 2 * out_rows]
    for couple in range(BLOCK // 2):
        product = dot(table, columns_at(stack, first + 2 * couple, 2, wide))
        for place in range(2):
            piece = product[:, place * wide : (place + 1) * wide]
            emit(2 * couple + place, older + piece[2 * out_rows : 3 * out_rows])
            older = newer + piece[out_rows : 2 * out_rows]
            newer = piece[0:out_rows]
    carry[0:out_rows] = older
    carry[out_rows : 2 * out_rows] = newer


def ring_start(table, stack, carry, out_rows, wide):
    product = dot(table, columns_at(stack, 0, 2, wide))
    carry[0:out_rows] = product[0:out_rows, :wide] + product[out_rows : 2 * out_rows, wide:]
    carry[out_rows : 2 * out_rows] = product[0:out_rows, wide:]


def block_loop(width, body, hook=None, at=2):
    def step(block, carry):
        if hook is not None:
            pl.when(block == at)(hook)
        body(block)
        return carry

    lax.fori_loop(0, width // BLOCK, step, 0)


def silu_half(values, scale, offset):
    half = values * scale + offset
    return half, jnp.tanh(half)


def put_image(image, halo, place, stack, keep_left, keep_right):
    _, width, wide = image.shape

    def put(column, real, imag):
        rows = [pltpu.roll(real, 1, 1), pltpu.roll(imag, 1, 1), real, imag, pltpu.roll(real, wide - 1, 1), pltpu.roll(imag, wide - 1, 1)]
        stack[:, pl.ds(lane_at(column, wide), wide)] = join_rows(rows, 16).astype(BF16)

    left, right = halo[0, place], halo[1, place]
    put(0, jnp.where(keep_left, left[0:1], 0.0), jnp.where(keep_left, left[1:2], 0.0))
    put(width + 1, jnp.where(keep_right, right[0:1], 0.0), jnp.where(keep_right, right[1:2], 0.0))

    def step(block, carry):
        real, imag = image[0, pl.ds(pl.multiple_of(8 * block, 8), 8)], image[1, pl.ds(pl.multiple_of(8 * block, 8), 8)]
        for place in range(8):
            put(8 * block + place + 1, real[place : place + 1], imag[place : place + 1])
        return carry

    lax.fori_loop(0, width // 8, step, 0)


def image_halo(parts, edges, halo, send, receive):
    image, me = lax.axis_index("img"), lax.axis_index("row")
    left, right = lax.rem(me + parts - 1, parts), lax.rem(me + 1, parts)
    return [
        remote(edges.at[0], halo.at[1], send.at[0], receive.at[0], (image, left)),
        remote(edges.at[1], halo.at[0], send.at[1], receive.at[1], (image, right)),
    ]


def forward_kernel(
    sizes, filled, edges, first_table, middle_tables, last_table, gains, shifts, counted,
    layers, coefs, rows_out, images_out, result,
    lin, stack, carry, pivot, total, square, halo_image, *refs,
):
    micro, parts, images, length = sizes
    _, _, width, wide = filled.shape
    channels = lin.shape[3]
    count = width * length
    whole = length // TILE * TILE
    sums = Sums(parts, images, refs[:6])
    halo_send, halo_receive, image_send, image_receive, saved = refs[6:]
    halo = Halo(parts, halo_send, halo_receive)
    clear = lane_mask(length, wide)
    clear_edges(lin)
    greet(sums.rows + sums.cols)
    moved = image_halo(parts, edges, halo_image, image_send, image_receive)
    for copy in moved:
        copy.start()
    for copy in moved:
        copy.wait()

    def save(layer, batch):
        return pltpu.make_async_copy(lin.at[batch, lax.rem(layer, 2)], layers.at[layer, batch], saved.at[layer, batch])

    def band(layer, batch):
        return lin.at[batch, lax.rem(layer, 2)]

    def begin(layer, batch, not_first):
        if not_first:
            save(layer - 1, batch).wait()
            halo.settle(band(layer - 1, batch), (layer - 1, batch))
        halo.start(band(layer, batch), (layer, batch))
        moments = jnp.concatenate([total[...], square[...]], axis=0).T
        moments = jnp.sum(moments, axis=0, keepdims=True)
        delta = moments[:, :channels] / count
        spread = moments[:, channels:] - count * delta * delta
        centre = pivot[...].T[0:1]
        sums.start((layer, batch), 0, padded_rows([count * (centre + delta), spread, counted[:, :channels]]))

    def join(blocks, number):
        blocks = [block[:, :channels] for block in blocks]
        added, spread = merge([block[0:1] for block in blocks], [block[1:2] for block in blocks], number)
        return added, spread, functools.reduce(jnp.add, [block[2:3] for block in blocks])

    def middle(layer, batch):
        joined = join(sums.collect((layer, batch), 0), count)
        sums.start((layer, batch), 1, padded_rows(joined))

    def end(layer, batch):
        added, spread, plain = join(sums.collect((layer, batch), 1), count * parts)
        pixels = count * parts * images
        gain, shift = gains[pl.ds(layer, 1), :], shifts[pl.ds(layer, 1), :]
        inverse = lax.rsqrt(spread / pixels + EPS_NORM)
        offset = -(added / pixels) * inverse
        coefs[layer, batch, 0] = spread_row(0.5 * gain * inverse)
        coefs[layer, batch, 1] = spread_row(0.5 * (shift + gain * offset))
        coefs[layer, batch, 2] = spread_row(inverse)
        coefs[layer, batch, 3] = spread_row(offset)
        rows_out[layer, batch] = join_rows([gain, shift, inverse, offset, plain], 8)
        halo.arrive(band(layer, batch), (layer, batch))
        save(layer, batch).start()

    def keeper(out):
        total[...] = jnp.zeros_like(total)
        square[...] = jnp.zeros_like(square)

        def emitter(block):
            held = []

            def emit(place, value):
                out[1 + block * BLOCK + place] = value
                if place == 0:

                    @pl.when(block == 0)
                    def _():
                        mean = jnp.sum(clear(value), axis=1, keepdims=True) / length
                        pivot[...] = jnp.broadcast_to(mean, pivot.shape)

                    held[:] = [jnp.zeros((channels, TILE), F32), jnp.zeros((channels, TILE), F32)]
                centre = pivot[...]
                for at in range(0, wide, TILE):
                    shift = value[:, at : at + TILE] - centre
                    if at >= whole:
                        lane = lax.broadcasted_iota(jnp.int32, shift.shape, 1)
                        shift = jnp.where(lane < length - at, shift, 0.0)
                    held[0] = held[0] + shift
                    held[1] = held[1] + shift * shift
                if place == BLOCK - 1:
                    total[...] += held[0]
                    square[...] += held[1]

            return emit

        return emitter

    def first_layer(batch, hook):
        source = images_out.at[batch]
        put_image(filled.at[batch], halo_image, batch, source, halo.has_left, halo.has_right)
        table = first_table[...]
        ring_start(table, source, carry, channels, wide)
        emitter = keeper(lin.at[batch, 0])
        block_loop(
            width, lambda block: ring_sum(table, source, carry, block * BLOCK + 2, channels, wide, emitter(block)), hook
        )

    def inner_layer(layer, batch, table, out_rows, hook, emitter):
        source = band(layer, batch)
        scale, offset = repeat_lanes(coefs[layer, batch, 0], wide), repeat_lanes(coefs[layer, batch, 1], wide)

        def put(column, keep=None):
            half, curve = silu_half(source[column], scale, offset)
            active = clear(half * curve + half)
            if keep is not None:
                active = jnp.where(keep, active, 0.0)
            put_shifted(stack, active.astype(BF16), lane_at(column, wide))

        put(0, halo.has_left)
        put(1)
        ring_start(table, stack, carry, out_rows, wide)

        def body(block):
            for place in range(BLOCK):
                keep = None
                if place == BLOCK - 1:
                    keep = jnp.logical_or(block < width // BLOCK - 1, halo.has_right)
                put(block * BLOCK + 2 + place, keep)
            ring_sum(table, stack, carry, block * BLOCK + 2, out_rows, wide, emitter(block))

        block_loop(width, body, hook)

    first_layer(0, None)
    begin(0, 0, False)
    first_layer(1, lambda: middle(0, 0))
    begin(0, 1, False)
    end(0, 0)

    def layer_step(layer, carried):
        table = middle_tables[layer - 1]
        inner_layer(layer - 1, 0, table, channels, lambda: middle(layer - 1, 1), keeper(band(layer, 0)))
        begin(layer, 0, True)
        end(layer - 1, 1)
        inner_layer(layer - 1, 1, table, channels, lambda: middle(layer, 0), keeper(band(layer, 1)))
        begin(layer, 1, True)
        end(layer, 0)
        return carried

    lax.fori_loop(1, 4, layer_step, 0)

    def result_emitter(batch):
        def emitter(block):
            def emit(place, value):
                column = block * BLOCK + place
                result[batch, 0, pl.ds(column, 1)] = value[0:1]
                result[batch, 1, pl.ds(column, 1)] = value[1:2]

            return emit

        return emitter

    table = last_table[...]
    inner_layer(3, 0, table, 8, lambda: middle(3, 1), result_emitter(0))
    end(3, 1)
    inner_layer(3, 1, table, 8, None, result_emitter(1))
    for batch in range(2):
        save(3, batch).wait()
        halo.settle(band(3, batch), (3, batch))

    def settle(layer, carried):
        for batch in range(2):
            sums.settle((layer, batch))
        return carried

    lax.fori_loop(0, 4, settle, 0)


def forward(filled, edges, tables, gains, shifts, counted, parts, images, length):
    micro, _, width, wide = filled.shape
    channels = gains.shape[1]
    first_table, middle_tables, last_table = tables
    shapes = [
        ((4, micro, width + 2, channels, wide), F32),
        ((4, micro, 4, channels, TILE), F32),
        ((4, micro, 8, channels), F32),
        ((micro, 16, (width + 2) * wide), BF16),
        ((micro, 2, width, wide), F32),
    ]
    slots = (4, micro)
    return pl.pallas_call(
        functools.partial(forward_kernel, (micro, parts, images, length)),
        out_shape=[jax.ShapeDtypeStruct(*shape) for shape in shapes],
        in_specs=[in_vmem()] * 8,
        out_specs=[anywhere()] + [in_vmem()] * 4,
        scratch_shapes=[
            pltpu.VMEM((micro, 2, width + 2, channels, wide), F32),
            pltpu.VMEM((3 * channels, (width + 2) * wide), BF16),
            pltpu.VMEM((2 * channels, wide), F32),
            pltpu.VMEM((channels, TILE), F32),
            pltpu.VMEM((channels, TILE), F32),
            pltpu.VMEM((channels, TILE), F32),
            pltpu.VMEM(edges.shape, F32),
        ]
        + Sums.scratch(slots, parts, images)
        + [
            pltpu.SemaphoreType.DMA(slots + (2,)),
            pltpu.SemaphoreType.DMA(slots + (2,)),
            pltpu.SemaphoreType.DMA((2,)),
            pltpu.SemaphoreType.DMA((2,)),
            pltpu.SemaphoreType.DMA(slots),
        ],
        compiler_params=params(collective_id=2, has_side_effects=True),
        name="forward",
    )(filled, edges, first_table, middle_tables, last_table, gains, shifts, counted)


def clear_edges(bands):
    empty = jnp.zeros(bands.shape[3:], F32)
    for batch in range(bands.shape[0]):
        for slot in range(2):
            bands[batch, slot, 0] = empty
            bands[batch, slot, bands.shape[2] - 1] = empty


def backward_kernel(
    sizes, grad, edges, layers, coefs, rows_in, images_in, middle_back, last_back,
    first_sums, middle_sums, last_sums, rows_out,
    upper, lin, stack, thin, inputs, slope, carry, total, along, mix, halo_image, *refs,
):
    micro, parts, images, length = sizes
    _, _, width, wide = grad.shape
    channels = lin.shape[3]
    pixels = width * length * parts * images
    sums = Sums(parts, images, refs[:6])
    halo_send, halo_receive, image_send, image_receive, loaded = refs[6:]
    halo = Halo(parts, halo_send, halo_receive)
    clear = lane_mask(length, wide)
    last_block = width // BLOCK - 1

    def load(layer, batch):
        return pltpu.make_async_copy(layers.at[layer, batch], lin.at[batch, lax.rem(layer, 2)], loaded.at[layer, batch])

    for layer in (3, 2):
        for batch in range(micro):
            load(layer, batch).start()
    clear_edges(upper)
    first_sums[...] = jnp.zeros_like(first_sums)
    middle_sums[...] = jnp.zeros_like(middle_sums)
    last_sums[...] = jnp.zeros_like(last_sums)
    greet(sums.rows + sums.cols)
    moved = image_halo(parts, edges, halo_image, image_send, image_receive)
    for copy in moved:
        copy.start()
    for copy in moved:
        copy.wait()

    def band(layer, batch):
        return upper.at[batch, lax.rem(layer, 2)]

    def begin(layer, batch):
        halo.start(band(layer, batch), (layer, batch))
        added = jnp.concatenate([total[...], along[...]], axis=0).T
        added = jnp.sum(added, axis=0, keepdims=True)
        sums.start((layer, batch), 0, padded_rows([added]))

    def middle(layer, batch):
        sums.start((layer, batch), 1, functools.reduce(jnp.add, sums.collect((layer, batch), 0)))

    def end(layer, batch):
        added = functools.reduce(jnp.add, sums.collect((layer, batch), 1))
        shift_sum, gain_sum = added[0:1, :channels], added[0:1, channels:]
        rows = rows_in[layer, batch]
        gain, inverse, offset = rows[0:1], rows[2:3], rows[3:4]
        scale = inverse * gain
        mix[batch, 0] = spread_row(scale)
        mix[batch, 1] = spread_row(-scale * inverse * gain_sum / pixels)
        mix[batch, 2] = spread_row(-scale * (shift_sum + offset * gain_sum) / pixels)
        rows_out[layer, batch] = join_rows([shift_sum, gain_sum], 8)
        halo.arrive(band(layer, batch), (layer, batch))
        halo.settle(band(layer, batch), (layer, batch))

    def grad_putter(layer, batch):
        grads, linear = band(layer, batch), lin.at[batch, lax.rem(layer, 2)]
        on_grad, on_layer, base = (repeat_lanes(mix[batch, index], wide) for index in range(3))

        def put(column, keep=None, at=None):
            upstream = clear(on_grad * grads[column] + on_layer * linear[column] + base)
            if keep is not None:
                upstream = jnp.where(keep, upstream, 0.0)
            put_shifted(stack, upstream.astype(BF16), lane_at(column if at is None else at, wide))

        return put

    def layer_back(layer, batch, source, table, weight_out, put_grad, hook):
        below = lin.at[batch, lax.rem(layer, 2)]
        out = band(layer, batch)
        scale, offset = repeat_lanes(coefs[layer, batch, 0], wide), repeat_lanes(coefs[layer, batch, 1], wide)

        def put_input(column, keep=None):
            half, curve = silu_half(below[column], scale, offset)
            active = clear(half * curve + half)
            if keep is not None:
                active = jnp.where(keep, active, 0.0)
            inputs[:, pl.ds(lane_at(column, wide), wide)] = active.astype(BF16)
            return 0.5 * (1.0 + curve) * (1.0 + half * (1.0 - curve))

        put_input(0, halo.has_left)
        slope[1] = put_input(1)
        if put_grad is not None:
            put_grad(0, halo.has_left)
            put_grad(1)
        ring_start(table, source, carry, channels, wide)
        total[...] = jnp.zeros_like(total)
        along[...] = jnp.zeros_like(along)

        def body(block):
            for place in range(BLOCK):
                column = block * BLOCK + 2 + place
                keep = jnp.logical_or(block < last_block, halo.has_right) if place == BLOCK - 1 else None
                slope[column] = put_input(column, keep)
                if put_grad is not None:
                    put_grad(column, keep)
            inverse, centre = repeat_lanes(coefs[layer, batch, 2], wide), repeat_lanes(coefs[layer, batch, 3], wide)
            held = [jnp.zeros((channels, TILE), F32), jnp.zeros((channels, TILE), F32)]

            def emit(place, value):
                column = block * BLOCK + place + 1
                shaped = clear(value * slope[column])
                out[column] = shaped
                held[0] = held[0] + fold(shaped)
                held[1] = held[1] + fold(shaped * (below[column] * inverse + centre))
                if place == BLOCK - 1:
                    total[...] += held[0]
                    along[...] += held[1]

            ring_sum(table, source, carry, block * BLOCK + 2, channels, wide, emit)
            first = block * BLOCK
            around = jnp.concatenate([columns_at(inputs, first + tap, BLOCK, wide) for tap in range(3)], axis=0)
            weight_out[...] += dot_nt(columns_at(source, first + 1, BLOCK, wide), around)

        block_loop(width, body, hook)

    def first_back(batch, hook):
        put_grad = grad_putter(0, batch)
        source = images_in.at[batch]

        def body(block):
            for place in range(BLOCK):
                put_grad(block * BLOCK + place + 1)
            first = block * BLOCK
            around = jnp.concatenate([columns_at(source, first + tap, BLOCK, wide) for tap in range(3)], axis=0)
            first_sums[...] += dot_nt(columns_at(stack, first + 1, BLOCK, wide), around)

        block_loop(width, body, hook)

    def outer(batch, hook):
        put_image(grad.at[batch], halo_image, batch, thin, halo.has_left, halo.has_right)
        load(3, batch).wait()
        layer_back(3, batch, thin, last_back[...], last_sums, None, hook)

    outer(0, None)
    begin(3, 0)
    outer(1, lambda: middle(3, 0))
    begin(3, 1)
    end(3, 0)

    def layer_step(step, carried):
        layer = 3 - step
        table = middle_back[layer - 1]
        weight_out = middle_sums.at[layer - 1]
        for batch in range(2):
            load(layer - 1, batch).wait()
            if batch == 0:
                hook = lambda: middle(layer, 1)
            else:
                hook = lambda: middle(layer - 1, 0)
            layer_back(layer - 1, batch, stack, table, weight_out, grad_putter(layer, batch), hook)

            @pl.when(layer > 1)
            def _():
                load(layer - 2, batch).start()

            begin(layer - 1, batch)
            if batch == 0:
                end(layer, 1)
            else:
                end(layer - 1, 0)
        return carried

    lax.fori_loop(0, 3, layer_step, 0)
    first_back(0, lambda: middle(0, 1))
    end(0, 1)
    first_back(1, None)

    def settle(layer, carried):
        for batch in range(2):
            sums.settle((layer, batch))
        return carried

    lax.fori_loop(0, 4, settle, 0)


def backward(grad, edges, kept, tables, parts, images, length):
    layers, coefs, rows_in, images_in = kept
    micro, _, width, wide = grad.shape
    channels = layers.shape[3]
    lanes = (width + 2) * wide
    shapes = [(3 * channels, 48), (3, 3 * channels, 3 * channels), (16, 3 * channels), (4, micro, 8, channels)]
    slots = (4, micro)
    return pl.pallas_call(
        functools.partial(backward_kernel, (micro, parts, images, length)),
        out_shape=[jax.ShapeDtypeStruct(shape, F32) for shape in shapes],
        in_specs=[in_vmem(), in_vmem(), anywhere()] + [in_vmem()] * 5,
        out_specs=[in_vmem()] * 4,
        scratch_shapes=[
            pltpu.VMEM((micro, 2, width + 2, channels, wide), F32),
            pltpu.VMEM((micro, 2, width + 2, channels, wide), F32),
            pltpu.VMEM((3 * channels, lanes), BF16),
            pltpu.VMEM((16, lanes), BF16),
            pltpu.VMEM((channels, lanes), BF16),
            pltpu.VMEM((width + 2, channels, wide), F32),
            pltpu.VMEM((2 * channels, wide), F32),
            pltpu.VMEM((channels, TILE), F32),
            pltpu.VMEM((channels, TILE), F32),
            pltpu.VMEM((micro, 3, channels, TILE), F32),
            pltpu.VMEM(edges.shape, F32),
        ]
        + Sums.scratch(slots, parts, images)
        + [
            pltpu.SemaphoreType.DMA(slots + (2,)),
            pltpu.SemaphoreType.DMA(slots + (2,)),
            pltpu.SemaphoreType.DMA((2,)),
            pltpu.SemaphoreType.DMA((2,)),
            pltpu.SemaphoreType.DMA(slots),
        ],
        compiler_params=params(collective_id=3, has_side_effects=True),
        name="backward",
    )(grad, edges, layers, coefs, rows_in, images_in, *tables)


def reduce_kernel(parts, images, first_sums, middle_sums, last_sums, scalars, first_grad, middle_grad, last_grad, totals, whole, final, quarter, landed, eighth, landed_rows, send, receive):
    image, me = lax.axis_index("img"), lax.axis_index("row")
    rows, cols = row_peers(parts), image_peers(images)
    channels = middle_sums.shape[1] // 3
    taps = [(kr, kw) for kr in range(3) for kw in range(3)]
    pieces = [
        middle_sums[layer, (2 - kr) * channels : (3 - kr) * channels, kw * channels : (kw + 1) * channels]
        for layer in range(3)
        for kr, kw in taps
    ]
    firsts = [first_sums[(2 - kr) * channels : (3 - kr) * channels, 16 * kw + 2 : 16 * kw + 4] for kr, kw in taps]
    pieces.append(join_lanes(firsts, channels))
    for index in range(0, len(pieces), 2):
        at = index // 2 * channels
        whole[at : at + channels] = jnp.concatenate(pieces[index : index + 2], axis=1)
    at = len(pieces) // 2 * channels
    lasts = [last_sums[2 * (2 - kr) : 2 * (3 - kr), kw * channels : (kw + 1) * channels] for kr, kw in taps]
    added = functools.reduce(jnp.add, [scalars[batch] for batch in range(scalars.shape[0])])
    whole[at : at + 24] = jnp.concatenate([join_rows(lasts, 24), join_rows([added[:, :channels]], 24)], axis=1)
    whole[at + 24 :] = jnp.zeros((whole.shape[0] - at - 24, TILE), F32)
    greet(rows + cols)
    big, small = quarter.shape[0], eighth.shape[0]
    images_here, parts_here = len(cols), len(rows)

    def place(index, size):
        return pl.ds(pl.multiple_of(index * size, 8), size)

    sent = []
    for index, peer in enumerate(cols):
        copy = remote(whole.at[place(peer[0], big)], landed.at[index], send.at[index], receive.at[index], peer)
        copy.start()
        sent.append(copy)
    for copy in sent:
        copy.wait_recv()
    total = whole[place(image, big)]
    for index in range(images_here):
        total = total + landed[index]
    quarter[...] = total
    base = images_here
    arrived = []
    for index, peer in enumerate(rows):
        copy = remote(
            quarter.at[place(peer[1], small)], landed_rows.at[index], send.at[base + index], receive.at[base + index], peer
        )
        copy.start()
        arrived.append(copy)
    for copy in arrived:
        copy.wait_recv()
    total = quarter[place(me, small)]
    for index in range(parts_here):
        total = total + landed_rows[index]
    eighth[...] = total
    for copy in sent + arrived:
        copy.wait_send()
    base += parts_here
    returned = []
    mine = pl.ds(pl.multiple_of(image * big + me * small, 8), small)
    for index, peer in enumerate(rows):
        copy = remote(eighth, final.at[mine], send.at[base + index], receive.at[base + index], peer)
        copy.start()
        returned.append(copy)
    final[mine] = total
    for copy in returned:
        copy.wait()
    base += parts_here
    returned = []
    for index, peer in enumerate(cols):
        copy = remote(final.at[place(image, big)], final.at[place(image, big)], send.at[base + index], receive.at[base + index], peer)
        copy.start()
        returned.append(copy)
    for copy in returned:
        copy.wait()
    for index in range(27):
        from_row = index // 2 * channels
        from_lane = index % 2 * channels
        middle_grad[index // 9, index % 9] = final[from_row : from_row + channels, from_lane : from_lane + channels]
    first_grad[...] = final[13 * channels : 14 * channels, channels:]
    last_grad[...] = final[at : at + 24, :channels]
    totals[...] = final[at : at + 8, channels:]


def reduce_all(first_sums, middle_sums, last_sums, scalars, parts, images):
    channels = middle_sums.shape[1] // 3
    unit = 8 * parts * images
    height = -(-(14 * channels + 24) // unit) * unit
    copies = 2 * (parts + images - 2)
    shapes = [(channels, channels), (3, 9, channels, channels), (24, channels), (8, channels)]
    return pl.pallas_call(
        functools.partial(reduce_kernel, parts, images),
        out_shape=[jax.ShapeDtypeStruct(shape, F32) for shape in shapes],
        in_specs=[in_vmem()] * 4,
        out_specs=[in_vmem()] * 4,
        scratch_shapes=[
            pltpu.VMEM((height, TILE), F32),
            pltpu.VMEM((height, TILE), F32),
            pltpu.VMEM((height // images, TILE), F32),
            pltpu.VMEM((images - 1, height // images, TILE), F32),
            pltpu.VMEM((height // images // parts, TILE), F32),
            pltpu.VMEM((parts - 1, height // images // parts, TILE), F32),
            pltpu.SemaphoreType.DMA((copies,)),
            pltpu.SemaphoreType.DMA((copies,)),
        ],
        compiler_params=params(collective_id=4, has_side_effects=True),
        name="reduce_all",
    )(first_sums, middle_sums, last_sums, scalars)


def apply_normal(image, maps, normal_high, normal_low):
    coils, slabs, wide = maps.shape
    rows = slabs // 2
    real, imag = image
    stack = []
    for coil in range(coils):
        sense = maps[coil].astype(F32)
        sense_re, sense_im = sense[:rows], sense[rows:]
        stack.append(
            jnp.concatenate(
                [sense_re * real - sense_im * imag, sense_re * imag + sense_im * real], axis=1
            )
        )
    stack = jnp.concatenate(stack, axis=0).astype(BF16)
    out_re = jnp.zeros((rows, wide), F32)
    out_im = jnp.zeros((rows, wide), F32)
    turned = dot(stack, normal_high[...]) + dot(stack, normal_low[...])
    for coil in range(coils):
        sense = maps[coil].astype(F32)
        sense_re, sense_im = sense[:rows], sense[rows:]
        field = turned[coil * rows : (coil + 1) * rows]
        field_re, field_im = field[:, :wide], field[:, wide:]
        out_re = out_re + sense_re * field_re + sense_im * field_im
        out_im = out_im + sense_re * field_im - sense_im * field_re
    return out_re, out_im


def pair(ref):
    return ref[0], ref[1]


def put_pair(ref, values):
    ref[0] = values[0]
    ref[1] = values[1]


def blend(*terms):
    return tuple(functools.reduce(jnp.add, [factor * image[part] for factor, image in terms]) for part in range(2))


def inner_of(left, right):
    product = left[0] * right[0] + left[1] * right[1]
    return jnp.sum(jnp.sum(product, axis=1, keepdims=True), axis=0, keepdims=True)


class RowSums:
    def __init__(self, parts, refs):
        self.message, self.held, self.send, self.receive = refs
        self.peers = row_peers(parts)

    def copies(self, slot):
        return [
            remote(
                self.message.at[slot],
                self.held.at[slot + (index,)],
                self.send.at[slot + (index,)],
                self.receive.at[slot + (index,)],
                peer,
            )
            for index, peer in enumerate(self.peers)
        ]

    def start(self, slot, values):
        filler = [jnp.zeros((1, TILE), F32)] * (8 - len(values))
        self.message[slot] = jnp.concatenate([jnp.broadcast_to(value, (1, TILE)) for value in values] + filler, axis=0)
        for copy in self.copies(slot):
            copy.start()

    def finish(self, slot):
        total = self.message[slot]
        for index, copy in enumerate(self.copies(slot)):
            copy.wait_recv()
            total = total + self.held[slot + (index,)]
        return [total[index : index + 1, 0:1] for index in range(8)]

    def settle(self, slot):
        for copy in self.copies(slot):
            copy.wait_send()


def solve_kernel(
    sizes, filled, result, maps, normal_high, normal_low, planes, rows_in, extra, grad_out, edges, scalars,
    work, *refs,
):
    micro, parts, length = sizes
    _, _, rows, wide = filled.shape
    sums = RowSums(parts, refs)
    greet(sums.peers)
    inside = lax.broadcasted_iota(jnp.int32, (rows, wide), 1) < length
    penalty = jnp.exp(jnp.full((1, 1), extra[2], F32))
    inv_count = 1.0 / rows_in[0, 0, 4:5, 0:1]
    names = ("denoised", "right", "mapped", "residue", "through", "search", "searched", "slope")

    def at(name, batch):
        return work.at[batch, names.index(name)]

    def get(name, batch):
        return pair(at(name, batch))

    def through_normal(image, batch):
        out = apply_normal(image, maps.at[batch], normal_high.at[batch], normal_low.at[batch])
        return blend((1.0, out), (penalty, image))

    for batch in range(micro):
        images = []
        for part in range(2):
            value = filled[batch, part] + result[batch, part] + jnp.full((1, 1), extra[part], F32)
            value = jnp.where(inside, value, 0.0)
            at("denoised", batch)[part] = value
            images.append(filled[batch, part] + penalty * value)
        put_pair(at("right", batch), images)
        mapped = through_normal(images, batch)
        put_pair(at("mapped", batch), mapped)
        sums.start((0, batch), [inner_of(images, images), inner_of(images, mapped)])
    ones, twos = [], []
    for batch in range(micro):
        ones.append(sums.finish((0, batch)))
        start, image = get("right", batch), get("mapped", batch)
        left_over = blend((1.0, start), (-ones[batch][0] / ones[batch][1], image))
        put_pair(at("residue", batch), left_over)
        mapped = through_normal(left_over, batch)
        put_pair(at("through", batch), mapped)
        sums.start(
            (1, batch),
            [
                inner_of(left_over, left_over),
                inner_of(left_over, mapped),
                inner_of(left_over, image),
                inner_of(start, mapped),
            ],
        )
    kept = []
    for batch in range(micro):
        twos.append(sums.finish((1, batch)))
        norm_0, curve_0 = ones[batch][:2]
        norm_1 = twos[batch][0]
        factor = norm_1 / norm_0
        curve_1 = twos[batch][1] + factor * (twos[batch][2] + twos[batch][3]) + factor * factor * curve_0
        start, image = get("right", batch), get("mapped", batch)
        direction = blend((1.0, get("residue", batch)), (factor, start))
        image_1 = blend((1.0, get("through", batch)), (factor, image))
        put_pair(at("searched", batch), image_1)
        state = blend((norm_0 / curve_0, start), (norm_1 / curve_1, direction))
        weight = planes[batch, 2]
        difference = [state[part] - planes[batch, part] for part in range(2)]
        grad = [inv_count * 2.0 * weight * difference[part] for part in range(2)]
        put_pair(at("slope", batch), grad)
        masked = [weight * difference[part] for part in range(2)]
        sums.start(
            (2, batch),
            [
                inner_of(grad, direction),
                inner_of(grad, start),
                inner_of(grad, image),
                inner_of(image_1, start),
                inner_of(image_1, image),
            ],
        )
        kept.append((norm_0, curve_0, norm_1, curve_1, factor, inner_of(direction, direction), inner_of(masked, difference)))
    for batch in range(micro):
        grad_search, grad_start, grad_image, cross_start, cross_image = sums.finish((2, batch))[:5]
        norm_0, curve_0, norm_1, curve_1, factor, own_search, own_loss = kept[batch]
        step_0, step_1 = norm_0 / curve_0, norm_1 / curve_1
        start, image, left_over = get("right", batch), get("mapped", batch), get("residue", batch)
        image_1, grad = get("searched", batch), get("slope", batch)
        residue_image = twos[batch][2]
        curve_grad_1 = -grad_search * norm_1 / (curve_1 * curve_1)
        norm_grad_1 = grad_search / curve_1
        search_grad = blend((step_1, grad), (2.0 * curve_grad_1, image_1))
        factor_grad = step_1 * grad_start + 2.0 * curve_grad_1 * cross_start
        joint = step_1 * grad_image + 2.0 * curve_grad_1 * cross_image
        norm_total = norm_grad_1 + factor_grad / norm_0
        residue_full = blend((1.0, search_grad), (2.0 * norm_total, left_over))
        step_grad = grad_start - (joint + 2.0 * norm_total * residue_image)
        curve_grad_0 = -step_grad * norm_0 / (curve_0 * curve_0)
        mapped_grad = blend((-step_0, residue_full), (curve_grad_0, start))
        through = through_normal(mapped_grad, batch)
        norm_grad_0 = -factor_grad * norm_1 / (norm_0 * norm_0) + step_grad / curve_0
        right_grad = blend(
            (1.0, residue_full),
            (factor, search_grad),
            (step_0, grad),
            (curve_grad_0, image),
            (1.0, through),
            (2.0 * norm_grad_0, start),
        )
        penalty_part = (
            curve_grad_1 * own_search + inner_of(mapped_grad, start) + inner_of(right_grad, get("denoised", batch))
        )
        grad_pair = [penalty * right_grad[part] for part in range(2)]
        put_pair(grad_out.at[batch], grad_pair)
        put_edges(edges.at[:, batch], *grad_pair)
        offsets = [jnp.sum(jnp.sum(grad_pair[part], axis=1, keepdims=True), axis=0, keepdims=True) for part in range(2)]
        values = [offsets[0], offsets[1], penalty * penalty_part, own_loss]
        scalars[batch] = join_rows([jnp.broadcast_to(value, (1, TILE)) for value in values], 8)
    for stage in range(3):
        for batch in range(micro):
            sums.settle((stage, batch))


def solve_all(filled, result, maps, normal_high, normal_low, planes, rows_in, extra, parts, length):
    micro, _, rows, wide = filled.shape
    shapes = [(micro, 2, rows, wide), (2, micro, 8, wide), (micro, 8, TILE)]
    slots = (3, micro)
    return pl.pallas_call(
        functools.partial(solve_kernel, (micro, parts, length)),
        out_shape=[jax.ShapeDtypeStruct(shape, F32) for shape in shapes],
        in_specs=[in_vmem()] * 7 + [pl.BlockSpec(memory_space=pltpu.SMEM)],
        out_specs=[in_vmem()] * 3,
        scratch_shapes=[
            pltpu.VMEM((micro, 8, 2, rows, wide), F32),
            pltpu.VMEM(slots + (8, TILE), F32),
            pltpu.VMEM(slots + (parts - 1, 8, TILE), F32),
            pltpu.SemaphoreType.DMA(slots + (parts - 1,)),
            pltpu.SemaphoreType.DMA(slots + (parts - 1,)),
        ],
        compiler_params=params(collective_id=5, has_side_effects=True),
        name="solve_all",
    )(filled, result, maps, normal_high, normal_low, planes, rows_in, extra)


def fast_local(arrays):
    (
        kspace, coil_maps, target, row_mask, foreground, anatomy, first_weight, middle_weight, last_weight, norm_gains, norm_shifts, extra_params,
    ) = arrays
    micro, _, coils, _, rows, length = kspace.shape
    channels = first_weight.shape[1]
    parts, images = lax.axis_size("row"), lax.axis_size("img")
    spread, planes, normal_high, normal_low, first_table, middle_tables, last_table, middle_back, last_back, counted = exchange(
        kspace[:, 0], coil_maps[:, 0], target[:, 0], foreground[:, 0], row_mask, first_weight, middle_weight, last_weight, parts
    )
    filled, maps, edges = zero_fill(spread, row_mask, anatomy[:, 0], rows, length)
    layers, coefs, rows_out, images_out, result = forward(
        filled, edges, (first_table, middle_tables, last_table), norm_gains, norm_shifts, counted, parts, images, length
    )
    grad, edges, scalars = solve_all(
        filled, result, maps, normal_high, normal_low, planes, rows_out, extra_params, parts, length
    )
    first_sums, middle_sums, last_sums, rows_back = backward(
        grad, edges, (layers, coefs, rows_out, images_out), (middle_back, last_back), parts, images, length
    )
    first_grad, middle_grad, last_grad, totals = reduce_all(first_sums, middle_sums, last_sums, scalars, parts, images)
    first_grad = first_grad[:, :18].reshape(channels, 9, 2).transpose(1, 0, 2)
    last_grad = last_grad[:18].reshape(9, 2, channels)
    affine = jnp.sum(rows_back, axis=1)
    extra_grad = totals[:3, 0]
    return (first_grad, middle_grad, last_grad, affine[:, 1], affine[:, 0], extra_grad, totals[3, 0]), rows_out[0, 0, 4, 0]


def local(
    kspace,
    coil_maps,
    target,
    row_mask,
    foreground,
    anatomy,
    first_weight,
    middle_weight,
    last_weight,
    norm_gains,
    norm_shifts,
    extra_params,
    first_mean,
    first_square,
    middle_mean,
    middle_square,
    last_mean,
    last_square,
    gains_mean,
    gains_square,
    shifts_mean,
    shifts_square,
    extra_mean,
    extra_square,
):
    arrays = (
        kspace, coil_maps, target, row_mask, foreground, anatomy, first_weight, middle_weight, last_weight, norm_gains, norm_shifts, extra_params,
    )
    gradients = fast_local if fits(kspace, first_weight, lax.axis_size("row")) else general_local
    totals, pixel_total = gradients(arrays)
    params = (first_weight, middle_weight, last_weight, norm_gains, norm_shifts, extra_params)
    moments = (
        (first_mean, first_square),
        (middle_mean, middle_square),
        (last_mean, last_square),
        (gains_mean, gains_square),
        (shifts_mean, shifts_square),
        (extra_mean, extra_square),
    )
    results = []
    for group in range(6):
        updated, first_new, second_new = adamw(
            params[group], totals[group], moments[group][0], moments[group][1], LEARN_RATES[group]
        )
        results.extend([updated, first_new, second_new])
        if group < 3:
            results.append(updated.astype(jnp.bfloat16))
    return tuple(results) + (totals[6], pixel_total.astype(jnp.int32))


def solution(mesh):
    in_specs = (
        P(None, "img", None, None, "row", None),
        P(None, "img", None, None, "row", None),
        P(None, "img", None, "row", None),
        P(None, "img", None),
        P(None, "img", "row", None),
        P(None, "img"),
        P(),
        P(),
        P(),
        P(),
        P(),
        P(),
        P(),
        P(),
        P(),
        P(),
        P(),
        P(),
        P(),
        P(),
        P(),
        P(),
        P(),
        P(),
    )
    out_specs = (
        P(),
        P(),
        P(),
        P(),
        P(),
        P(),
        P(),
        P(),
        P(),
        P(),
        P(),
        P(),
        P(),
        P(),
        P(),
        P(),
        P(),
        P(),
        P(),
        P(),
        P(),
        P(),
        P(),
    )
    return jax.shard_map(local, mesh=mesh, in_specs=in_specs, out_specs=out_specs, check_vma=False)
```

```python
import functools

import jax
import jax.numpy as jnp
import numpy as np
from jax import lax
from jax.experimental import pallas as pl
from jax.experimental.pallas import tpu as pltpu
from jax.sharding import PartitionSpec as P

COILS = 16
BRAIN_COILS = 12
UNROLLS = 1
CG_STEPS = 2
STEP = 10


PRECISE = lax.Precision.HIGHEST
EPS_NORM = 1e-05
BETA_ONE = 0.9
BETA_TWO = 0.999
ADAM_EPS = 1e-08
DECAY_RATE = 0.01
LEARN_RATES = (0.3, 0.05, 0.05, 0.4, 0.4, 0.4)


def with_halo(cells, sides, width):
    for axis, dim in sides:
        count = lax.axis_size(axis)
        ends = count - 1
        head = lax.slice_in_dim(cells, 0, width, axis=dim)
        tail = lax.slice_in_dim(cells, cells.shape[dim] - width, cells.shape[dim], axis=dim)
        cells = jnp.concatenate(
            [
                lax.ppermute(tail, axis, [(i, (i + 1) % count) for i in range(ends)]),
                cells,
                lax.ppermute(head, axis, [((i + 1) % count, i) for i in range(ends)]),
            ],
            axis=dim,
        )
    return cells


def dft_table(length, direction):
    index = jnp.arange(length, dtype=jnp.int32)
    phase = (index[:, None] * index[None, :] % length).astype(jnp.float32) * (2.0 * jnp.pi / length)
    factor = 1.0 / jnp.sqrt(jnp.float32(length))
    cosine = jnp.cos(phase) * factor
    sine = jnp.sin(phase) * factor * direction
    return jnp.stack([jnp.stack([cosine, -sine], 1), jnp.stack([sine, cosine], 1)], 0)


def along_width(field, table):
    return jnp.einsum("bcprw,pwqk->bcqrk", field, table, precision=PRECISE)


def along_height(field, table):
    return jnp.einsum("bcprw,prqk->bcqkw", field, table, precision=PRECISE)


def expand(image, maps):
    real_part, imag_part = (image[:, None, 0], image[:, None, 1])
    maps_re, maps_im = (maps[:, :, 0], maps[:, :, 1])
    return jnp.stack(
        [maps_re * real_part - maps_im * imag_part, maps_re * imag_part + maps_im * real_part], 2
    )


def combine(field, maps):
    field_re, field_im = (field[:, :, 0], field[:, :, 1])
    maps_re, maps_im = (maps[:, :, 0], maps[:, :, 1])
    return jnp.stack(
        [
            jnp.sum(maps_re * field_re + maps_im * field_im, 1),
            jnp.sum(maps_re * field_im - maps_im * field_re, 1),
        ],
        1,
    )


def to_columns(field):
    return lax.all_to_all(
        field.astype(jnp.bfloat16), "row", split_axis=4, concat_axis=3, tiled=True
    ).astype(field.dtype)


def to_rows(field):
    return lax.all_to_all(
        field.astype(jnp.bfloat16), "row", split_axis=3, concat_axis=4, tiled=True
    ).astype(field.dtype)


def make_normal(maps, mask_rows, forward, inverse, measured):
    zero_filled = combine(to_rows(along_height(measured * mask_rows, inverse)), maps)

    def normal(image):
        spectrum = to_columns(along_width(expand(image, maps), forward))
        spectrum = along_height(spectrum, forward) * mask_rows
        spectrum = to_rows(along_height(spectrum, inverse))
        return combine(along_width(spectrum, inverse), maps)

    return (normal, zero_filled)


def inner(left, right):
    return jnp.sum(left * right, axis=(1, 2, 3))


def per_image(values):
    return values[:, None, None, None]


def row_sums(values):
    return lax.psum(values, "row")


def solve(rhs, penalty, normal):
    state = jnp.zeros_like(rhs)
    residue = rhs
    search = rhs
    norm_now = row_sums(inner(residue, residue))
    kept = []
    for iterate in range(CG_STEPS):
        mapped = normal(search) + penalty * search
        curvature = row_sums(inner(search, mapped))
        stepsize = norm_now / curvature
        state = state + per_image(stepsize) * search
        residue = residue - per_image(stepsize) * mapped
        norm_next = row_sums(inner(residue, residue))
        kept.append((search, mapped, residue, norm_now, norm_next, curvature))
        search = residue + per_image(norm_next / norm_now) * search
        norm_now = norm_next
    return (state, kept)


def solve_backward(state_grad, kept, rhs, denoised, penalty, normal):
    search_grad = jnp.zeros_like(rhs)
    residue_grad = jnp.zeros_like(rhs)
    norm_grad = jnp.zeros(rhs.shape[0], jnp.float32)
    penalty_part = jnp.float32(0.0)
    for iterate in reversed(range(CG_STEPS)):
        search, mapped, residue, norm_now, norm_next, curvature = kept[iterate]
        factor_grad, along_search, joint_mapped, residue_mapped = lax.psum(
            (
                inner(search_grad, search),
                inner(state_grad, search),
                inner(residue_grad + search_grad, mapped),
                inner(residue, mapped),
            ),
            "row",
        )
        stepsize = norm_now / curvature
        factor = norm_next / norm_now
        norm_total = norm_grad + factor_grad / norm_now
        residue_full = residue_grad + search_grad + per_image(2.0 * norm_total) * residue
        stepsize_grad = along_search - (joint_mapped + 2.0 * norm_total * residue_mapped)
        curvature_grad = -stepsize_grad * norm_now / (curvature * curvature)
        mapped_grad = -per_image(stepsize) * residue_full + per_image(curvature_grad) * search
        penalty_part = penalty_part + jnp.sum(mapped_grad * search)
        search_grad = (
            per_image(factor) * search_grad
            + per_image(stepsize) * state_grad
            + per_image(curvature_grad) * mapped
            + normal(mapped_grad)
            + penalty * mapped_grad
        )
        residue_grad = residue_full
        norm_grad = -factor_grad * norm_next / (norm_now * norm_now) + stepsize_grad / curvature
    rhs_grad = residue_grad + search_grad + per_image(2.0 * norm_grad) * rhs
    penalty_part = penalty_part + jnp.sum(rhs_grad * denoised)
    return (penalty * rhs_grad, penalty_part)


def conv_forward(activation, weight):
    height, breadth = (activation.shape[2], activation.shape[3])
    padded = with_halo(activation, (("row", 2),), 1)
    padded = jnp.pad(padded, ((0, 0), (0, 0), (0, 0), (1, 1)))
    summed = jnp.zeros((activation.shape[0], weight.shape[1], height, breadth), jnp.float32)
    for tap_index in range(9):
        window = padded[
            :, :, tap_index // 3 : tap_index // 3 + height, tap_index % 3 : tap_index % 3 + breadth
        ]
        summed = summed + jnp.einsum(
            "oi,birw->borw", weight[tap_index], window, preferred_element_type=jnp.float32
        )
    return (summed, padded)


def conv_backward(upstream, padded, weight, need_input):
    height, breadth = (upstream.shape[2], upstream.shape[3])
    weight_grad = jnp.stack(
        [
            jnp.einsum(
                "borw,birw->oi",
                upstream,
                padded[
                    :,
                    :,
                    tap_index // 3 : tap_index // 3 + height,
                    tap_index % 3 : tap_index % 3 + breadth,
                ],
                preferred_element_type=jnp.float32,
            )
            for tap_index in range(9)
        ]
    )
    if not need_input:
        return (weight_grad, None)
    widened = with_halo(upstream, (("row", 2),), 1)
    widened = jnp.pad(widened, ((0, 0), (0, 0), (0, 0), (1, 1)))
    summed = jnp.zeros((upstream.shape[0], weight.shape[2], height, breadth), jnp.float32)
    for tap_index in range(9):
        start_r = 2 - tap_index // 3
        start_c = 2 - tap_index % 3
        window = widened[:, :, start_r : start_r + height, start_c : start_c + breadth]
        summed = summed + jnp.einsum(
            "oi,borw->birw", weight[tap_index], window, preferred_element_type=jnp.float32
        )
    return (weight_grad, summed)


def norm_sums(values):
    return lax.psum(values, ("img", "row"))


def channel(values):
    return values[None, :, None, None]


def cnn_forward(image, weights, gains, shifts, offset, pixels):
    activation = image.astype(jnp.bfloat16)
    kept = []
    for layer_index in range(4):
        linear, padded = conv_forward(activation, weights[layer_index])
        average = norm_sums(jnp.sum(linear, axis=(0, 2, 3))) / pixels
        centred = linear - channel(average)
        spread = norm_sums(jnp.sum(centred * centred, axis=(0, 2, 3))) / pixels
        inv_std = lax.rsqrt(spread + EPS_NORM)
        normed = centred * channel(inv_std)
        shaped = channel(gains[layer_index]) * normed + channel(shifts[layer_index])
        activation = jax.nn.silu(shaped).astype(jnp.bfloat16)
        kept.append((padded, normed, shaped, inv_std))
    result, padded = conv_forward(activation, weights[4])
    kept.append(padded)
    return (image + result + channel(offset), kept)


def cnn_backward(denoised_grad, kept, weights, gains, pixels, need_input):
    offset_grad = jnp.sum(denoised_grad, axis=(0, 2, 3))
    weight_grads = [None] * 5
    gain_grads = [None] * 4
    shift_grads = [None] * 4
    weight_grads[4], upstream = conv_backward(
        denoised_grad.astype(jnp.bfloat16), kept[4], weights[4], True
    )
    for layer_index in (3, 2, 1, 0):
        padded, normed, shaped, inv_std = kept[layer_index]
        sigmoid_val = jax.nn.sigmoid(shaped)
        shaped_grad = upstream * sigmoid_val * (1.0 + shaped * (1.0 - sigmoid_val))
        shift_local = jnp.sum(shaped_grad, axis=(0, 2, 3))
        gain_local = jnp.sum(shaped_grad * normed, axis=(0, 2, 3))
        shift_total, gain_total = lax.psum((shift_local, gain_local), ("img", "row"))
        gain_vec = gains[layer_index]
        linear_grad = channel(inv_std) * (
            shaped_grad * channel(gain_vec)
            - channel(gain_vec * shift_total / pixels)
            - normed * channel(gain_vec * gain_total / pixels)
        )
        shift_grads[layer_index] = shift_local
        gain_grads[layer_index] = gain_local
        weight_grads[layer_index], upstream = conv_backward(
            linear_grad.astype(jnp.bfloat16),
            padded,
            weights[layer_index],
            layer_index > 0 or need_input,
        )
    image_grad = None
    return (image_grad, weight_grads, jnp.stack(gain_grads), jnp.stack(shift_grads), offset_grad)


def adamw(weight, gradient, moment_one, moment_two, rate):
    first_new = BETA_ONE * moment_one + (1.0 - BETA_ONE) * gradient
    second_new = BETA_TWO * moment_two + (1.0 - BETA_TWO) * gradient * gradient
    corrected = first_new / (1.0 - BETA_ONE**STEP)
    divisor = jnp.sqrt(second_new / (1.0 - BETA_TWO**STEP)) + ADAM_EPS
    updated = weight - rate * (corrected / divisor + DECAY_RATE * weight)
    return (updated, first_new, second_new)


def general_local(arrays):
    (
        kspace, coil_maps, target, row_mask, foreground, anatomy, first_weight, middle_weight, last_weight, norm_gains, norm_shifts, extra_params,
    ) = arrays
    length = kspace.shape[-1]
    forward = dft_table(length, 1.0)
    inverse = dft_table(length, -1.0)
    pixel_total = lax.psum(jnp.sum(foreground).astype(jnp.float32), ("img", "row"))
    inv_count = 1.0 / pixel_total
    middle_low = middle_weight.astype(jnp.bfloat16)
    conv_weights = [
        first_weight.astype(jnp.bfloat16),
        middle_low[0],
        middle_low[1],
        middle_low[2],
        last_weight.astype(jnp.bfloat16),
    ]
    penalty = jnp.exp(extra_params[2])
    offset = extra_params[:2]
    images_here = kspace.shape[1]
    pixels = images_here * kspace.shape[4] * length * lax.axis_size("img") * lax.axis_size("row")
    first_grad = jnp.zeros_like(first_weight)
    middle_grad = jnp.zeros_like(middle_weight)
    last_grad = jnp.zeros_like(last_weight)
    gains_grad = jnp.zeros_like(norm_gains)
    shifts_grad = jnp.zeros_like(norm_shifts)
    offset_grad = jnp.zeros((2,), jnp.float32)
    penalty_grad = jnp.float32(0.0)
    loss_part = jnp.float32(0.0)
    for microbatch in range(kspace.shape[0]):
        limit = jnp.where(anatomy[microbatch] == 0, BRAIN_COILS, COILS)
        coil_on = (jnp.arange(kspace.shape[2])[None, :] < limit[:, None]).astype(jnp.float32)
        maps = coil_maps[microbatch] * coil_on[:, :, None, None, None]
        mask_rows = row_mask[microbatch].astype(jnp.float32)[:, None, None, :, None]
        measured = to_columns(along_width(kspace[microbatch], inverse))
        normal, zero_filled = make_normal(maps, mask_rows, forward, inverse, measured)
        state = zero_filled
        unroll = 0
        denoised, cnn_kept = cnn_forward(
            state, conv_weights, norm_gains, norm_shifts, offset, pixels
        )
        rhs = zero_filled + penalty * denoised
        state, cg_kept = solve(rhs, penalty, normal)
        saved = [(cnn_kept, cg_kept, rhs, denoised)]
        fg_mask = foreground[microbatch].astype(jnp.float32)[:, None]
        difference = state - target[microbatch]
        loss_part = loss_part + jnp.sum(fg_mask * difference * difference)
        state_grad = inv_count * 2.0 * fg_mask * difference
        for unroll in reversed(range(UNROLLS)):
            cnn_kept, cg_kept, rhs, denoised = saved[unroll]
            denoised_grad, penalty_part = solve_backward(
                state_grad, cg_kept, rhs, denoised, penalty, normal
            )
            penalty_grad = penalty_grad + penalty_part
            state_grad, weight_grads, gain_part, shift_part, offset_part = cnn_backward(
                denoised_grad, cnn_kept, conv_weights, norm_gains, pixels, unroll > 0
            )
            first_grad = first_grad + weight_grads[0]
            middle_grad = middle_grad + jnp.stack(weight_grads[1:4])
            last_grad = last_grad + weight_grads[4]
            gains_grad = gains_grad + gain_part
            shifts_grad = shifts_grad + shift_part
            offset_grad = offset_grad + offset_part
    extra_grad = jnp.concatenate([offset_grad, (penalty * penalty_grad)[None]])
    totals = lax.psum(
        (first_grad, middle_grad, last_grad, gains_grad, shifts_grad, extra_grad, loss_part),
        ("img", "row"),
    )
    return totals, pixel_total


BF16 = jnp.bfloat16
F32 = jnp.float32
MESH = pl.DeviceIdType.MESH
TILE = 128
BLOCK = 8
BACK_REACH = 3
FIRST_REACH = 6
GROUP = 4
HOOK_PART = 4
REACH = 8
VMEM_BYTES = 58 * 1024 * 1024


def padded(length):
    return -(-length // TILE) * TILE


def fits(kspace, first_weight, mesh_rows):
    micro, images, coils, _, rows, length = kspace.shape
    channels = first_weight.shape[1]
    return (
        images == 1
        and micro == 2
        and 2 * channels == TILE
        and channels % 16 == 0
        and rows * mesh_rows == length
        and mesh_rows & (mesh_rows - 1) == 0
        and rows % BLOCK == 0
        and (2 * rows) % 16 == 0
        and (coils * rows) % TILE == 0
        and padded(length) > length
    )


def phases(length):
    index = np.arange(length)
    angle = 2.0 * np.pi * (np.outer(index, index) % length) / length
    return np.cos(angle) / np.sqrt(length), np.sin(angle) / np.sqrt(length)


def high_low(table):
    high = table.astype(BF16)
    low = (table - high.astype(F32)).astype(BF16)
    return high, low


def np_high_low(table):
    table = np.asarray(table, np.float32)
    high = table.astype(BF16)
    low = (table - high.astype(np.float32)).astype(BF16)
    return jnp.asarray(high), jnp.asarray(low)


def dot(left, right):
    return jnp.dot(left, right, preferred_element_type=F32)


def dot_nt(left, right):
    return lax.dot_general(left, right, (((1,), (1,)), ((), ())), preferred_element_type=F32)


def greet(peers):
    barrier = pltpu.get_barrier_semaphore()
    for peer in peers:
        pl.semaphore_signal(barrier, inc=1, device_id=peer, device_id_type=MESH)
    pl.semaphore_wait(barrier, len(peers))


def row_peers(rows):
    image, row = lax.axis_index("img"), lax.axis_index("row")
    return [(image, lax.rem(row + step, rows)) for step in range(1, rows)]


def image_peers(images):
    image, row = lax.axis_index("img"), lax.axis_index("row")
    return [(lax.rem(image + step, images), row) for step in range(1, images)]


def remote(source, target, send, receive, peer):
    return pltpu.make_async_remote_copy(
        src_ref=source,
        dst_ref=target,
        send_sem=send,
        recv_sem=receive,
        device_id=peer,
        device_id_type=MESH,
    )


def params(vmem=VMEM_BYTES, **kwargs):
    return pltpu.CompilerParams(vmem_limit_bytes=vmem, **kwargs)


def in_vmem():
    return pl.BlockSpec(memory_space=pltpu.VMEM)


def anywhere():
    return pl.BlockSpec(memory_space=pl.ANY)


def three_parts(values):
    high = values.astype(BF16)
    rest = values - high.astype(F32)
    middle = rest.astype(BF16)
    return high, middle, (rest - middle.astype(F32)).astype(BF16)


def join_lanes(pieces, wide):
    short = wide - sum(piece.shape[1] for piece in pieces)
    if short:
        pieces = pieces + [jnp.zeros((pieces[0].shape[0], short), pieces[0].dtype)]
    return jnp.concatenate(pieces, axis=1)


def join_rows(pieces, height):
    short = height - sum(piece.shape[0] for piece in pieces)
    if short:
        pieces = pieces + [jnp.zeros((short, pieces[0].shape[1]), pieces[0].dtype)]
    return jnp.concatenate(pieces, axis=0)


def partner(me, step):
    other, bit = 0, 1
    while bit <= step:
        own = lax.rem(lax.div(me, bit), 2)
        other = other + bit * (1 - own if step & bit else own)
        bit *= 2
    return other + lax.div(me, bit) * bit


def exchange_kernel(
    sizes, kspace, maps, target, foreground, row_mask, anatomy, first, middle, last, turn_high, turn_low, pick, cosine, sine,
    fourier_high, fourier_low,
    filled, maps_out, edges, planes, normal, first_table, middle_tables, last_table, middle_back, last_back, counted,
    fields, staged, spread, flat, landed, loaded, send, receive, own, send_flat, receive_flat,
):
    micro, coils, rows, length, parts = sizes
    wide = padded(length)
    image, me = lax.axis_index("img"), lax.axis_index("row")
    order = sorted(range(1, parts), key=lambda step: (-step.bit_length(), step))
    peers = [(image, partner(me, step)) for step in range(1, parts)]
    slots = [(batch, kind) for batch in range(micro) for kind in (1, 0)]
    loads = {}
    for index, (batch, kind) in enumerate(slots):
        for part in range(2):
            source = (kspace, maps)[kind].at[batch, :, part]
            copy = pltpu.make_async_copy(source, fields.at[index, part], loaded.at[index, part])
            copy.start()
            loads[index, part] = copy
    greet(peers)
    arrivals = [[] for _ in range(micro)]
    slabs = 2 * rows
    for index, (batch, kind) in enumerate(slots):
        total = None
        for part in range(2):
            loads[index, part].wait()
            field = fields[index, part].reshape(coils * rows, length)
            if kind == 0:
                high, low = high_low(field)
                term = (
                    dot_nt(turn_high[part], high)
                    + dot_nt(turn_low[part], high)
                    + dot_nt(turn_high[part], low)
                )
            else:
                term = dot_nt(pick[part], field.astype(BF16))
            total = term if total is None else total + term
        slot = 2 * batch + kind
        staged[slot] = total.astype(BF16).reshape(parts, slabs, coils * rows)
        for step in order:
            peer = peers[step - 1]
            copy = remote(
                staged.at[slot, peer[1]],
                spread.at[slot, me],
                send.at[slot, step - 1],
                receive.at[slot, step - 1],
                peer,
            )
            copy.start()
            arrivals[batch].append(copy)
        local = pltpu.make_async_copy(staged.at[slot, me], spread.at[slot, me], own.at[slot])
        local.start()
        arrivals[batch].append(local)
        if index == 0:
            flats = exchange_planes(
                sizes, target, foreground, pick, counted, flat, landed, send_flat, receive_flat, me, peers, order
            )
    for batch in range(micro):
        chosen = join_lanes([row_mask[batch].astype(F32)], wide)
        cos_on, sin_on = cosine[...] * chosen, sine[...] * chosen

        def product(left, right):
            return jnp.dot(left, right, precision=PRECISE, preferred_element_type=F32)

        real = product(cos_on, cosine[...]) + product(sin_on, sine[...])
        imag = product(sin_on, cosine[...]) - product(cos_on, sine[...])
        diagonal = [lax.broadcasted_iota(jnp.int32, real.shape, axis) for axis in range(2)]
        real = jnp.where(diagonal[0] == diagonal[1], 0.0, real)
        for block, value in (((0, 0), real), ((0, 1), -imag), ((1, 0), imag), ((1, 1), real)):
            normal[batch, pl.ds(block[0] * wide, wide), pl.ds(block[1] * wide, wide)] = value.astype(BF16)
    put_tables(first, middle, last, first_table, middle_tables, last_table, middle_back, last_back)
    for copy in flats:
        copy.wait()
    for batch in range(micro):
        for plane in range(3):
            at = (3 * batch + plane) * rows
            planes[batch, plane] = join_lanes([landed[block, :, at : at + rows] for block in range(parts)], wide)
    for batch in range(micro):
        for copy in arrivals[batch]:
            copy.wait()
        knee = jnp.where(anatomy[batch : batch + 1, 0:1] == 0, 0.0, 1.0)
        real, imag = zero_fill(
            (coils, rows, parts, wide),
            knee,
            spread.at[2 * batch],
            spread.at[2 * batch + 1],
            join_lanes([row_mask[batch].astype(F32)], wide),
            fourier_high,
            fourier_low,
            maps_out.at[batch],
        )
        put_pair(filled.at[batch], (real, imag))
        put_edges(edges.at[:, batch], real, imag)


def exchange_planes(
    sizes, target, foreground, pick, counted, flat, landed, send_flat, receive_flat, me, peers, order
):
    micro, _, rows, length, parts = sizes
    shown = [foreground[batch].astype(F32) for batch in range(micro)]
    count = functools.reduce(jnp.add, [jnp.sum(jnp.sum(s, axis=1, keepdims=True), axis=0, keepdims=True) for s in shown])
    counted[...] = jnp.broadcast_to(count, (1, TILE))
    stack = []
    for batch in range(micro):
        stack += [target[batch, 0], target[batch, 1], shown[batch]]
    stack = jnp.concatenate(stack, axis=0)
    plain = pick[0].reshape(parts, 2 * rows, length)[:, :rows].reshape(length, length)
    turned = functools.reduce(jnp.add, [dot_nt(plain, piece) for piece in three_parts(stack)])
    lanes = flat.shape[2]
    flat[...] = join_lanes([turned], lanes).reshape(parts, rows, lanes)
    landed[me] = flat[me]
    flats = []
    for step in order:
        peer = peers[step - 1]
        copy = remote(flat.at[peer[1]], landed.at[me], send_flat.at[step - 1], receive_flat.at[step - 1], peer)
        copy.start()
        flats.append(copy)
    return flats


def put_tables(first, middle, last, first_table, middle_tables, last_table, middle_back, last_back):
    taps = range(3)
    turned = [join_rows([first[tap]], 8).T[:, :2] for tap in range(9)]
    first_table[...] = jnp.concatenate(
        [join_lanes([turned[3 * kr + kw] for kr in taps], 16) for kw in taps], axis=0
    ).astype(BF16)
    last_table[...] = jnp.concatenate(
        [join_rows([jnp.concatenate([last[3 * kr + kw] for kr in taps], axis=1)], 8) for kw in taps], axis=0
    ).astype(BF16)
    turned = [join_rows([last[tap]], 8).T[:, :2] for tap in range(9)]
    last_back[...] = jnp.concatenate(
        [join_lanes([turned[3 * (2 - m) + 2 - n] for m in taps], 16) for n in taps], axis=0
    ).astype(BF16)
    for layer in range(3):
        weights = [middle[layer, tap] for tap in range(9)]
        turned = [weight.T for weight in weights]
        middle_tables[layer] = jnp.concatenate(
            [jnp.concatenate([weights[3 * kr + kw] for kr in taps], axis=1) for kw in taps], axis=0
        ).astype(BF16)
        middle_back[layer] = jnp.concatenate(
            [jnp.concatenate([turned[3 * (2 - m) + 2 - n] for m in taps], axis=1) for n in taps], axis=0
        ).astype(BF16)


def exchange(kspace, maps, target, foreground, row_mask, anatomy, first, middle, last, parts):
    micro, coils, _, rows, length = kspace.shape
    wide = padded(length)
    channels = first.shape[2]
    cosine, sine = phases(length)
    fourier = np.zeros((wide, 2, wide))
    fourier[:length, 0, :length] = cosine
    fourier[:length, 1, :length] = sine
    fourier_high, fourier_low = np_high_low(fourier.reshape(wide, 2 * wide))
    inverse = np.stack([np.stack([cosine, sine], 0), np.stack([-sine, cosine], 0)], 0)
    turn = inverse.reshape(2, 2, length, parts, rows).transpose(0, 3, 1, 4, 2).reshape(2, 2 * length, length)
    pick = np.zeros((2, parts, 2, rows, length), np.float32)
    for part in range(2):
        for block in range(parts):
            pick[part, block, part, :, block * rows : (block + 1) * rows] = np.eye(rows)
    pick = jnp.asarray(pick.reshape(2, 2 * length, length).astype(BF16))
    turn_high, turn_low = np_high_low(turn)
    edge = ((0, wide - length), (0, wide - length))
    cosine = jnp.asarray(np.pad(cosine, edge), F32)
    sine = jnp.asarray(np.pad(sine, edge), F32)
    sizes = (micro, coils, rows, length, parts)
    slots = 2 * micro
    lanes = padded(3 * micro * rows)
    shapes = [
        ((micro, 2, rows, wide), F32),
        ((micro, coils, 2 * rows, wide), BF16),
        ((2, micro, 2 * REACH, wide), F32),
        ((micro, 3, rows, wide), F32),
        ((micro, 2 * wide, 2 * wide), BF16),
        ((3 * channels, 16), BF16),
        ((3, 3 * channels, 3 * channels), BF16),
        ((24, 3 * channels), BF16),
        ((3, 3 * channels, 3 * channels), BF16),
        ((3 * channels, 16), BF16),
        ((1, TILE), F32),
    ]
    return pl.pallas_call(
        functools.partial(exchange_kernel, sizes),
        out_shape=[jax.ShapeDtypeStruct(*shape) for shape in shapes],
        in_specs=[anywhere()] * 2 + [in_vmem()] * 14,
        out_specs=[in_vmem()] * 11,
        scratch_shapes=[
            pltpu.VMEM((slots, 2, coils, rows, length), F32),
            pltpu.VMEM((slots, parts, 2 * rows, coils * rows), BF16),
            pltpu.VMEM((slots, parts, 2 * rows, coils * rows), BF16),
            pltpu.VMEM((parts, rows, lanes), F32),
            pltpu.VMEM((parts, rows, lanes), F32),
            pltpu.SemaphoreType.DMA((slots, 2)),
            pltpu.SemaphoreType.DMA((slots, parts - 1)),
            pltpu.SemaphoreType.DMA((slots, parts - 1)),
            pltpu.SemaphoreType.DMA((slots,)),
            pltpu.SemaphoreType.DMA((parts - 1,)),
            pltpu.SemaphoreType.DMA((parts - 1,)),
        ],
        compiler_params=params(collective_id=1, has_side_effects=True),
        name="exchange",
    )(
        kspace, maps, target, foreground, row_mask, anatomy, first, middle, last, turn_high, turn_low, pick, cosine, sine,
        fourier_high, fourier_low,
    )


def gather_lanes(blocks, coil, rows, wide):
    pieces = [block[:, coil * rows : (coil + 1) * rows] for block in blocks]
    height = pieces[0].shape[0]
    short = wide - rows * len(pieces)
    return jnp.concatenate(pieces + [jnp.zeros((height, short), pieces[0].dtype)], axis=1)


def zero_fill(sizes, knee, fields, senses, chosen, fourier_high, fourier_low, maps_out):
    coils, rows, parts, wide = sizes
    real = jnp.zeros((rows, wide), F32)
    imag = jnp.zeros((rows, wide), F32)
    chosen = chosen.astype(BF16)
    group = 4
    for first in range(0, coils, group):
        stack = []
        for coil in range(first, first + group):
            sense = gather_lanes([senses[s] for s in range(parts)], coil, rows, wide)
            maps_out[coil] = sense if coil < BRAIN_COILS else sense * knee.astype(BF16)
            stack.append(gather_lanes([fields[s] for s in range(parts)], coil, rows, wide) * chosen)
        stack = jnp.concatenate(stack, axis=0)
        turned = dot(stack, fourier_high[...]) + dot(stack, fourier_low[...])
        for place in range(group):
            top = 2 * rows * place
            upper, lower = turned[top : top + rows], turned[top + rows : top + 2 * rows]
            field_re = upper[:, :wide] - lower[:, wide:]
            field_im = upper[:, wide:] + lower[:, :wide]
            sense = maps_out[first + place].astype(F32)
            sense_re, sense_im = sense[:rows], sense[rows:]
            real = real + sense_re * field_re + sense_im * field_im
            imag = imag + sense_re * field_im - sense_im * field_re
    return real, imag


def put_edges(edges, real, imag):
    rows = real.shape[0]
    edges[0] = jnp.concatenate([real[:REACH], imag[:REACH]], axis=0)
    edges[1] = jnp.concatenate([real[rows - REACH :], imag[rows - REACH :]], axis=0)


def lane_row(columns):
    return jnp.sum(columns.T, axis=0, keepdims=True)


def spread_row(row):
    return jnp.broadcast_to(row, (TILE, row.shape[1])).T


def padded_rows(rows):
    return join_rows([join_lanes([row], TILE) for row in rows], 8)


def merge(sums, squares, count):
    total = functools.reduce(jnp.add, sums)
    mean = total / (count * len(sums))
    square = None
    for part, own in zip(sums, squares):
        shift = part / count - mean
        term = own + count * shift * shift
        square = term if square is None else square + term
    return total, square


def repeat_lanes(block, wide):
    return jnp.concatenate([block] * (wide // TILE), axis=1)


def lane_mask(length, wide):
    whole = length // TILE * TILE

    def clear(values):
        tail = values[:, whole:]
        keep = lax.broadcasted_iota(jnp.int32, tail.shape, 1) < length - whole
        return jnp.concatenate([values[:, :whole], jnp.where(keep, tail, 0.0)], axis=1)

    return clear


def fold(values):
    parts = [values[:, at : at + TILE] for at in range(0, values.shape[1], TILE)]
    return functools.reduce(jnp.add, parts)


def put_shifted(stack, values, at):
    channels, wide = values.shape
    stack[0:channels, at : at + wide] = pltpu.roll(values, 1, 1)
    stack[channels : 2 * channels, at : at + wide] = values
    stack[2 * channels : 3 * channels, at : at + wide] = pltpu.roll(values, wide - 1, 1)


def lane_at(column, wide):
    return pl.multiple_of(column * wide, TILE) if not isinstance(column, int) else column * wide


class Sums:
    def __init__(self, parts, images, refs):
        self.message, self.held, self.second, self.held_second, self.send, self.receive = refs
        self.rows, self.cols = row_peers(parts), image_peers(images)

    def copies(self, slot, stage):
        source, target = ((self.message, self.held), (self.second, self.held_second))[stage]
        peers = (self.rows, self.cols)[stage]
        base = stage * len(self.rows)
        return [
            remote(
                source.at[slot],
                target.at[slot + (index,)],
                self.send.at[slot + (base + index,)],
                self.receive.at[slot + (base + index,)],
                peer,
            )
            for index, peer in enumerate(peers)
        ]

    def start(self, slot, stage, values):
        (self.message, self.second)[stage][slot] = values
        for copy in self.copies(slot, stage):
            copy.start()

    def collect(self, slot, stage):
        blocks = [(self.message, self.second)[stage][slot]]
        for index, copy in enumerate(self.copies(slot, stage)):
            copy.wait_recv()
            blocks.append((self.held, self.held_second)[stage][slot + (index,)])
        return blocks

    def settle(self, slot, stages=(0, 1)):
        for stage in stages:
            for copy in self.copies(slot, stage):
                copy.wait_send()

    @staticmethod
    def scratch(slots, parts, images):
        return [
            pltpu.VMEM(slots + (8, TILE), F32),
            pltpu.VMEM(slots + (parts - 1, 8, TILE), F32),
            pltpu.VMEM(slots + (8, TILE), F32),
            pltpu.VMEM(slots + (max(images - 1, 1), 8, TILE), F32),
            pltpu.SemaphoreType.DMA(slots + (parts + images - 2,)),
            pltpu.SemaphoreType.DMA(slots + (parts + images - 2,)),
        ]


class Ends:
    def __init__(self, parts):
        me = lax.axis_index("row")
        self.left, self.right = me > 0, me < parts - 1

    def clear(self, values, column, width):
        if column < 0:
            return jnp.where(self.left, values, 0.0)
        if column >= width:
            return jnp.where(self.right, values, 0.0)
        return values


def ring_pass(table, take, fill, emit, out_rows, width, wide, hook):
    fill(0)
    fill(1)
    product = dot(table, take(0))
    older = product[0:out_rows, :wide] + product[out_rows : 2 * out_rows, wide:]
    newer = product[0:out_rows, wide:]
    last = width // 2
    for couple in range(1, last + 1):
        if hook is not None and couple == last * HOOK_PART // 8:
            hook()
        product = dot(table, take(couple))
        if couple < last:
            fill(couple + 1)
        for place in range(2):
            piece = product[:, place * wide : (place + 1) * wide]
            emit(2 * couple - 2 + place, older + piece[2 * out_rows : 3 * out_rows])
            older = newer + piece[out_rows : 2 * out_rows]
            newer = piece[0:out_rows]


def silu_half(values, scale, offset):
    half = values * scale + offset
    return half, jnp.tanh(half)


def put_image(image, halo, place, stack, ends, reach):
    _, width, wide = image.shape
    blocks = {-REACH: (halo[0, place, :REACH], halo[0, place, REACH:]), width: (halo[1, place, :REACH], halo[1, place, REACH:])}
    for first in range(0, width, 8):
        blocks[first] = (image[0, first : first + 8], image[1, first : first + 8])
    for first, (real, imag) in blocks.items():
        real, imag = ends.clear(real, first, width), ends.clear(imag, first, width)
        rolled = [pltpu.roll(real, 1, 1), pltpu.roll(imag, 1, 1), real, imag, pltpu.roll(real, wide - 1, 1), pltpu.roll(imag, wide - 1, 1)]
        for offset in range(8):
            at = first + offset + reach
            if 0 <= at < width + 2 * reach:
                rows = [block[offset : offset + 1] for block in rolled]
                stack[:, at * wide : (at + 1) * wide] = join_rows(rows, 16).astype(BF16)


def image_halo(parts, edges, halo, send, receive):
    image, me = lax.axis_index("img"), lax.axis_index("row")
    left, right = lax.rem(me + parts - 1, parts), lax.rem(me + 1, parts)
    return [
        remote(edges.at[0], halo.at[1], send.at[0], receive.at[0], (image, left)),
        remote(edges.at[1], halo.at[0], send.at[1], receive.at[1], (image, right)),
    ]


def forward_kernel(
    sizes, filled, edges, first_table, middle_tables, last_table, gains, shifts, counted,
    layers, coefs, rows_out, images_out, result,
    lin, even, odd, pivot, total, square, halo_image, *refs,
):
    micro, parts, images, length = sizes
    _, _, width, wide = filled.shape
    channels = lin.shape[3]
    count = width * length
    whole = length // TILE * TILE
    stacks = (even, odd)
    sums = Sums(parts, images, refs[:6])
    image_send, image_receive, saved = refs[6:]
    ends = Ends(parts)
    clear = lane_mask(length, wide)
    greet(sums.rows + sums.cols)
    moved = image_halo(parts, edges, halo_image, image_send, image_receive)
    for copy in moved:
        copy.start()
    for copy in moved:
        copy.wait()

    def band(layer, batch):
        return lin.at[batch, lax.rem(layer, 2)]

    def save(layer, batch):
        kept = band(layer, batch).at[pl.ds(FIRST_REACH - BACK_REACH, width + 2 * BACK_REACH)]
        return pltpu.make_async_copy(kept, layers.at[layer, batch], saved.at[layer, batch])

    def begin(layer, batch, not_first):
        if not_first:
            save(layer - 1, batch).wait()
        moments = jnp.concatenate([total[...], square[...]], axis=0).T
        moments = jnp.sum(moments, axis=0, keepdims=True)
        delta = moments[:, :channels] / count
        spread = moments[:, channels:] - count * delta * delta
        centre = pivot[...].T[0:1]
        sums.start((layer, batch), 0, padded_rows([count * (centre + delta), spread, counted[:, :channels]]))
        save(layer, batch).start()

    def join(blocks, number):
        blocks = [block[:, :channels] for block in blocks]
        added, spread = merge([block[0:1] for block in blocks], [block[1:2] for block in blocks], number)
        return added, spread, functools.reduce(jnp.add, [block[2:3] for block in blocks])

    def middle(layer, batch):
        joined = join(sums.collect((layer, batch), 0), count)
        sums.start((layer, batch), 1, padded_rows(joined))

    def end(layer, batch):
        added, spread, plain = join(sums.collect((layer, batch), 1), count * parts)
        pixels = count * parts * images
        gain, shift = gains[pl.ds(layer, 1), :], shifts[pl.ds(layer, 1), :]
        inverse = lax.rsqrt(spread / pixels + EPS_NORM)
        offset = -(added / pixels) * inverse
        coefs[layer, batch, 0] = spread_row(0.5 * gain * inverse)
        coefs[layer, batch, 1] = spread_row(0.5 * (shift + gain * offset))
        coefs[layer, batch, 2] = spread_row(inverse)
        coefs[layer, batch, 3] = spread_row(offset)
        rows_out[layer, batch] = join_rows([gain, shift, inverse, offset, plain], 8)

    def keeper(out, reach):
        held = []

        def emit(column, value):
            column = column - reach
            out[FIRST_REACH + column] = value
            if not 0 <= column < width:
                return
            if column == 0:
                mean = jnp.sum(clear(value), axis=1, keepdims=True) / length
                pivot[...] = jnp.broadcast_to(mean, pivot.shape)
            if column % BLOCK == 0:
                held[:] = [jnp.zeros((channels, TILE), F32), jnp.zeros((channels, TILE), F32)]
            centre = pivot[...]
            for at in range(0, wide, TILE):
                shift = value[:, at : at + TILE] - centre
                if at >= whole:
                    lane = lax.broadcasted_iota(jnp.int32, shift.shape, 1)
                    shift = jnp.where(lane < length - at, shift, 0.0)
                held[0] = held[0] + shift
                held[1] = held[1] + shift * shift
            if column == BLOCK - 1:
                total[...], square[...] = held
            elif column % BLOCK == BLOCK - 1:
                total[...] += held[0]
                square[...] += held[1]

        return emit

    def place_of(index):
        return lax.div(index, 2), lax.rem(index, 2)

    def first_layer(batch, hook):
        source = images_out.at[batch]
        put_image(filled.at[batch], halo_image, batch, source, ends, FIRST_REACH + 1)
        ring_pass(
            first_table[...],
            lambda couple: source[:, 2 * couple * wide : 2 * (couple + 1) * wide],
            lambda couple: None,
            keeper(band(0, batch), FIRST_REACH),
            channels,
            width + 2 * FIRST_REACH,
            wide,
            hook,
        )

    def inner_layer(layer, batch, table, out_rows, reach, emit, hook):
        source = band(layer, batch)
        scale, offset = repeat_lanes(coefs[layer, batch, 0], wide), repeat_lanes(coefs[layer, batch, 1], wide)

        def fill(couple):
            for place in range(2):
                column = 2 * couple + place - reach - 1
                half, curve = silu_half(source[FIRST_REACH + column], scale, offset)
                active = ends.clear(clear(half * curve + half), column, width)
                put_shifted(stacks[couple % 2], active.astype(BF16), place * wide)

        ring_pass(table, lambda couple: stacks[couple % 2][...], fill, emit, out_rows, width + 2 * reach, wide, hook)

    def first_step(batch, carried):
        first_layer(batch, lambda: pl.when(batch > 0)(lambda: middle(0, 0)))
        begin(0, batch, False)
        pl.when(batch > 0)(lambda: end(0, 0))
        return carried

    lax.fori_loop(0, 2, first_step, 0)

    def layer_step(index, carried):
        layer, batch = place_of(index)
        before = place_of(index - 1)
        reach = FIRST_REACH - 1
        emit = keeper(band(layer, batch), reach)
        inner_layer(layer - 1, batch, middle_tables[layer - 1], channels, reach, emit, lambda: middle(*before))
        begin(layer, batch, True)
        end(*before)
        return carried

    lax.fori_loop(2, 8, layer_step, 0)

    def last_step(batch, carried):
        def emit(column, value):
            result[batch, 0, column : column + 1] = value[0:1]
            result[batch, 1, column : column + 1] = value[1:2]

        inner_layer(3, batch, last_table[...], 8, 0, emit, lambda: pl.when(batch == 0)(lambda: middle(3, 1)))
        pl.when(batch == 0)(lambda: end(3, 1))
        return carried

    lax.fori_loop(0, 2, last_step, 0)
    for batch in range(2):
        save(3, batch).wait()
    for layer in range(4):
        for batch in range(2):
            sums.settle((layer, batch))


def forward(filled, edges, tables, gains, shifts, counted, parts, images, length):
    micro, _, width, wide = filled.shape
    channels = gains.shape[1]
    first_table, middle_tables, last_table = tables
    shapes = [
        ((4, micro, width + 2 * BACK_REACH, channels, wide), F32),
        ((4, micro, 4, channels, TILE), F32),
        ((4, micro, 8, channels), F32),
        ((micro, 16, (width + 2 * FIRST_REACH + 2) * wide), BF16),
        ((micro, 2, width, wide), F32),
    ]
    slots = (4, micro)
    return pl.pallas_call(
        functools.partial(forward_kernel, (micro, parts, images, length)),
        out_shape=[jax.ShapeDtypeStruct(*shape) for shape in shapes],
        in_specs=[in_vmem()] * 8,
        out_specs=[anywhere()] + [in_vmem()] * 4,
        scratch_shapes=[
            pltpu.VMEM((micro, 2, width + 2 * FIRST_REACH, channels, wide), F32),
            pltpu.VMEM((3 * channels, 2 * wide), BF16),
            pltpu.VMEM((3 * channels, 2 * wide), BF16),
            pltpu.VMEM((channels, TILE), F32),
            pltpu.VMEM((channels, TILE), F32),
            pltpu.VMEM((channels, TILE), F32),
            pltpu.VMEM(edges.shape, F32),
        ]
        + Sums.scratch(slots, parts, images)
        + [
            pltpu.SemaphoreType.DMA((2,)),
            pltpu.SemaphoreType.DMA((2,)),
            pltpu.SemaphoreType.DMA(slots),
        ],
        compiler_params=params(collective_id=2, has_side_effects=True),
        name="forward",
    )(filled, edges, first_table, middle_tables, last_table, gains, shifts, counted)


def backward_kernel(
    sizes, grad, edges, layers, coefs, rows_in, images_in, middle_back, last_back,
    first_sums, middle_sums, last_sums, rows_out,
    upper, lin, stack, thin, inputs, slope, total, along, mix, halo_image, *refs,
):
    micro, parts, images, length = sizes
    _, _, width, wide = grad.shape
    channels = lin.shape[3]
    pixels = width * length * parts * images
    sums = Sums(parts, images, refs[:6])
    image_send, image_receive, loaded = refs[6:]
    ends = Ends(parts)
    clear = lane_mask(length, wide)

    def load(layer, batch):
        return pltpu.make_async_copy(layers.at[layer, batch], lin.at[batch, lax.rem(layer, 2)], loaded.at[layer, batch])

    for layer in (3, 2):
        for batch in range(micro):
            load(layer, batch).start()
    first_sums[...] = jnp.zeros_like(first_sums)
    middle_sums[...] = jnp.zeros_like(middle_sums)
    last_sums[...] = jnp.zeros_like(last_sums)
    greet(sums.rows + sums.cols)
    moved = image_halo(parts, edges, halo_image, image_send, image_receive)
    for copy in moved:
        copy.start()
    for copy in moved:
        copy.wait()

    def band(layer, batch):
        return upper.at[batch, lax.rem(layer, 2)]

    def begin(layer, batch):
        added = jnp.concatenate([total[...], along[...]], axis=0).T
        added = jnp.sum(added, axis=0, keepdims=True)
        sums.start((layer, batch), 0, padded_rows([added]))

    def middle(layer, batch):
        sums.start((layer, batch), 1, functools.reduce(jnp.add, sums.collect((layer, batch), 0)))

    def end(layer, batch):
        added = functools.reduce(jnp.add, sums.collect((layer, batch), 1))
        shift_sum, gain_sum = added[0:1, :channels], added[0:1, channels:]
        rows = rows_in[layer, batch]
        gain, inverse, offset = rows[0:1], rows[2:3], rows[3:4]
        scale = inverse * gain
        mix[batch, 0] = spread_row(scale)
        mix[batch, 1] = spread_row(-scale * inverse * gain_sum / pixels)
        mix[batch, 2] = spread_row(-scale * (shift_sum + offset * gain_sum) / pixels)
        rows_out[layer, batch] = join_rows([shift_sum, gain_sum], 8)

    def place_of(index):
        return 3 - lax.div(index, 2), lax.rem(index, 2)

    def grad_putter(layer, batch):
        grads, linear = band(layer, batch), lin.at[batch, lax.rem(layer, 2)]
        on_grad, on_layer, base = (repeat_lanes(mix[batch, index], wide) for index in range(3))

        def put(column):
            at = column + BACK_REACH
            upstream = clear(on_grad * grads[at] + on_layer * linear[at] + base)
            put_shifted(stack, ends.clear(upstream, column, width).astype(BF16), at * wide)

        return put

    def add_weights(weight_out, source, reach, around, around_reach, first):
        at = first + around_reach - 1
        columns = [around[:, (at + tap) * wide : (at + tap + GROUP) * wide] for tap in range(3)]
        at = first + reach
        weight_out[...] += dot_nt(source[:, at * wide : (at + GROUP) * wide], jnp.concatenate(columns, axis=0))

    def layer_back(layer, batch, source, reach, table, weight_out, put_grad, hook):
        below = lin.at[batch, lax.rem(layer, 2)]
        out = band(layer, batch)
        scale, offset = repeat_lanes(coefs[layer, batch, 0], wide), repeat_lanes(coefs[layer, batch, 1], wide)
        inverse, centre = repeat_lanes(coefs[layer, batch, 2], wide), repeat_lanes(coefs[layer, batch, 3], wide)

        def fill(couple):
            for place in range(2):
                column = 2 * couple + place - reach - 1
                if put_grad is not None:
                    put_grad(column)
                if not -reach <= column < width + reach:
                    continue
                at = column + BACK_REACH
                half, curve = silu_half(below[at], scale, offset)
                slope[at] = 0.5 * (1.0 + curve) * (1.0 + half * (1.0 - curve))
                if -1 <= column <= width:
                    active = ends.clear(clear(half * curve + half), column, width)
                    inputs[:, (column + 1) * wide : (column + 2) * wide] = active.astype(BF16)

        held = []

        def emit(column, value):
            column = column - reach
            at = column + BACK_REACH
            shaped = clear(value * slope[at])
            out[at] = shaped
            if not 0 <= column < width:
                return
            if column % BLOCK == 0:
                held[:] = [jnp.zeros((channels, TILE), F32), jnp.zeros((channels, TILE), F32)]
            held[0] = held[0] + fold(shaped)
            held[1] = held[1] + fold(shaped * (below[at] * inverse + centre))
            if column == BLOCK - 1:
                total[...], along[...] = held
            elif column % BLOCK == BLOCK - 1:
                total[...] += held[0]
                along[...] += held[1]
            if column % GROUP == GROUP - 1:
                add_weights(weight_out, source, reach + 1, inputs, 1, column + 1 - GROUP)

        ring_pass(
            table,
            lambda couple: source[:, 2 * couple * wide : 2 * (couple + 1) * wide],
            fill,
            emit,
            channels,
            width + 2 * reach,
            wide,
            hook,
        )

    def outer_step(batch, carried):
        put_image(grad.at[batch], halo_image, batch, thin, ends, BACK_REACH + 1)
        load(3, batch).wait()
        hook = lambda: pl.when(batch > 0)(lambda: middle(3, 0))
        layer_back(3, batch, thin, BACK_REACH, last_back[...], last_sums, None, hook)
        begin(3, batch)
        pl.when(batch > 0)(lambda: end(3, 0))
        return carried

    lax.fori_loop(0, 2, outer_step, 0)

    def layer_step(index, carried):
        layer, batch = place_of(index)
        before = place_of(index - 1)
        load(layer, batch).wait()
        layer_back(
            layer,
            batch,
            stack,
            BACK_REACH - 1,
            middle_back[layer],
            middle_sums.at[layer],
            grad_putter(layer + 1, batch),
            lambda: middle(*before),
        )
        pl.when(layer > 0)(lambda: load(layer - 1, batch).start())
        begin(layer, batch)
        end(*before)
        return carried

    lax.fori_loop(2, 8, layer_step, 0)

    def first_step(batch, carried):
        put_grad = grad_putter(0, batch)
        for column in range(width):
            if column == width // 2:
                pl.when(batch == 0)(lambda: middle(0, 1))
            put_grad(column)
            if column % GROUP == GROUP - 1:
                add_weights(first_sums, stack, BACK_REACH, images_in.at[batch], FIRST_REACH + 1, column + 1 - GROUP)
        pl.when(batch == 0)(lambda: end(0, 1))
        return carried

    lax.fori_loop(0, 2, first_step, 0)
    for layer in range(4):
        for batch in range(2):
            sums.settle((layer, batch))


def backward(grad, edges, kept, tables, parts, images, length):
    layers, coefs, rows_in, images_in = kept
    micro, _, width, wide = grad.shape
    channels = layers.shape[3]
    band = (micro, 2, width + 2 * BACK_REACH, channels, wide)
    lanes = (width + 2 * BACK_REACH) * wide
    shapes = [(3 * channels, 48), (3, 3 * channels, 3 * channels), (16, 3 * channels), (4, micro, 8, channels)]
    slots = (4, micro)
    return pl.pallas_call(
        functools.partial(backward_kernel, (micro, parts, images, length)),
        out_shape=[jax.ShapeDtypeStruct(shape, F32) for shape in shapes],
        in_specs=[in_vmem(), in_vmem(), anywhere()] + [in_vmem()] * 5,
        out_specs=[in_vmem()] * 4,
        scratch_shapes=[
            pltpu.VMEM(band, F32),
            pltpu.VMEM(band, F32),
            pltpu.VMEM((3 * channels, lanes), BF16),
            pltpu.VMEM((16, lanes + 2 * wide), BF16),
            pltpu.VMEM((channels, (width + 2) * wide), BF16),
            pltpu.VMEM(band[2:], F32),
            pltpu.VMEM((channels, TILE), F32),
            pltpu.VMEM((channels, TILE), F32),
            pltpu.VMEM((micro, 3, channels, TILE), F32),
            pltpu.VMEM(edges.shape, F32),
        ]
        + Sums.scratch(slots, parts, images)
        + [
            pltpu.SemaphoreType.DMA((2,)),
            pltpu.SemaphoreType.DMA((2,)),
            pltpu.SemaphoreType.DMA(slots),
        ],
        compiler_params=params(collective_id=3, has_side_effects=True),
        name="backward",
    )(grad, edges, layers, coefs, rows_in, images_in, *tables)


def reduce_kernel(parts, images, first_sums, middle_sums, last_sums, scalars, first_grad, middle_grad, last_grad, totals, whole, final, quarter, landed, eighth, landed_rows, send, receive):
    image, me = lax.axis_index("img"), lax.axis_index("row")
    rows, cols = row_peers(parts), image_peers(images)
    channels = middle_sums.shape[1] // 3
    taps = [(kr, kw) for kr in range(3) for kw in range(3)]
    pieces = [
        middle_sums[layer, (2 - kr) * channels : (3 - kr) * channels, kw * channels : (kw + 1) * channels]
        for layer in range(3)
        for kr, kw in taps
    ]
    firsts = [first_sums[(2 - kr) * channels : (3 - kr) * channels, 16 * kw + 2 : 16 * kw + 4] for kr, kw in taps]
    pieces.append(join_lanes(firsts, channels))
    for index in range(0, len(pieces), 2):
        at = index // 2 * channels
        whole[at : at + channels] = jnp.concatenate(pieces[index : index + 2], axis=1)
    at = len(pieces) // 2 * channels
    lasts = [last_sums[2 * (2 - kr) : 2 * (3 - kr), kw * channels : (kw + 1) * channels] for kr, kw in taps]
    added = functools.reduce(jnp.add, [scalars[batch] for batch in range(scalars.shape[0])])
    whole[at : at + 24] = jnp.concatenate([join_rows(lasts, 24), join_rows([added[:, :channels]], 24)], axis=1)
    whole[at + 24 :] = jnp.zeros((whole.shape[0] - at - 24, TILE), F32)
    greet(rows + cols)
    big, small = quarter.shape[0], eighth.shape[0]
    images_here, parts_here = len(cols), len(rows)

    def place(index, size):
        return pl.ds(pl.multiple_of(index * size, 8), size)

    sent = []
    for index, peer in enumerate(cols):
        copy = remote(whole.at[place(peer[0], big)], landed.at[index], send.at[index], receive.at[index], peer)
        copy.start()
        sent.append(copy)
    for copy in sent:
        copy.wait_recv()
    total = whole[place(image, big)]
    for index in range(images_here):
        total = total + landed[index]
    quarter[...] = total
    base = images_here
    arrived = []
    for index, peer in enumerate(rows):
        copy = remote(
            quarter.at[place(peer[1], small)], landed_rows.at[index], send.at[base + index], receive.at[base + index], peer
        )
        copy.start()
        arrived.append(copy)
    for copy in arrived:
        copy.wait_recv()
    total = quarter[place(me, small)]
    for index in range(parts_here):
        total = total + landed_rows[index]
    eighth[...] = total
    for copy in sent + arrived:
        copy.wait_send()
    base += parts_here
    returned = []
    mine = pl.ds(pl.multiple_of(image * big + me * small, 8), small)
    for index, peer in enumerate(rows):
        copy = remote(eighth, final.at[mine], send.at[base + index], receive.at[base + index], peer)
        copy.start()
        returned.append(copy)
    final[mine] = total
    for copy in returned:
        copy.wait()
    base += parts_here
    returned = []
    for index, peer in enumerate(cols):
        copy = remote(final.at[place(image, big)], final.at[place(image, big)], send.at[base + index], receive.at[base + index], peer)
        copy.start()
        returned.append(copy)
    for copy in returned:
        copy.wait()
    for index in range(27):
        from_row = index // 2 * channels
        from_lane = index % 2 * channels
        middle_grad[index // 9, index % 9] = final[from_row : from_row + channels, from_lane : from_lane + channels]
    turned = final[13 * channels : 14 * channels, channels:].T
    for tap in range(9):
        first_grad[tap] = turned[2 * tap : 2 * tap + 2]
        last_grad[tap] = final[at + 2 * tap : at + 2 * tap + 2, :channels]
    totals[...] = final[at : at + 8, channels:]


def reduce_all(first_sums, middle_sums, last_sums, scalars, parts, images):
    channels = middle_sums.shape[1] // 3
    unit = 8 * parts * images
    height = -(-(14 * channels + 24) // unit) * unit
    copies = 2 * (parts + images - 2)
    shapes = [(9, 2, channels), (3, 9, channels, channels), (9, 2, channels), (8, channels)]
    return pl.pallas_call(
        functools.partial(reduce_kernel, parts, images),
        out_shape=[jax.ShapeDtypeStruct(shape, F32) for shape in shapes],
        in_specs=[in_vmem()] * 4,
        out_specs=[in_vmem()] * 4,
        scratch_shapes=[
            pltpu.VMEM((height, TILE), F32),
            pltpu.VMEM((height, TILE), F32),
            pltpu.VMEM((height // images, TILE), F32),
            pltpu.VMEM((images - 1, height // images, TILE), F32),
            pltpu.VMEM((height // images // parts, TILE), F32),
            pltpu.VMEM((parts - 1, height // images // parts, TILE), F32),
            pltpu.SemaphoreType.DMA((copies,)),
            pltpu.SemaphoreType.DMA((copies,)),
        ],
        compiler_params=params(collective_id=4, has_side_effects=True),
        name="reduce_all",
    )(first_sums, middle_sums, last_sums, scalars)


def apply_normal(image, maps, normal, diagonal):
    coils, slabs, wide = maps.shape
    rows = slabs // 2
    real, imag = image
    stack, power = [], jnp.zeros((rows, wide), F32)
    for coil in range(coils):
        sense = maps[coil].astype(F32)
        sense_re, sense_im = sense[:rows], sense[rows:]
        power = power + sense_re * sense_re + sense_im * sense_im
        field = [sense_re * real - sense_im * imag, sense_re * imag + sense_im * real]
        stack.append(jnp.concatenate(field, axis=1))
    stack = jnp.concatenate(stack, axis=0).astype(BF16)
    power = diagonal * power
    out_re, out_im = power * real, power * imag
    turned = dot(stack, normal[...])
    for coil in range(coils):
        sense = maps[coil].astype(F32)
        sense_re, sense_im = sense[:rows], sense[rows:]
        field = turned[coil * rows : (coil + 1) * rows]
        field_re, field_im = field[:, :wide], field[:, wide:]
        out_re = out_re + sense_re * field_re + sense_im * field_im
        out_im = out_im + sense_re * field_im - sense_im * field_re
    return out_re, out_im


def pair(ref):
    return ref[0], ref[1]


def put_pair(ref, values):
    ref[0] = values[0]
    ref[1] = values[1]


def blend(*terms):
    return tuple(functools.reduce(jnp.add, [factor * image[part] for factor, image in terms]) for part in range(2))


def inner_of(left, right):
    product = left[0] * right[0] + left[1] * right[1]
    return jnp.sum(jnp.sum(product, axis=1, keepdims=True), axis=0, keepdims=True)


class RowSums:
    def __init__(self, parts, refs):
        self.message, self.held, self.send, self.receive = refs
        self.peers = row_peers(parts)

    def copies(self, slot):
        return [
            remote(
                self.message.at[slot],
                self.held.at[slot + (index,)],
                self.send.at[slot + (index,)],
                self.receive.at[slot + (index,)],
                peer,
            )
            for index, peer in enumerate(self.peers)
        ]

    def start(self, slot, values):
        filler = [jnp.zeros((1, TILE), F32)] * (8 - len(values))
        self.message[slot] = jnp.concatenate([jnp.broadcast_to(value, (1, TILE)) for value in values] + filler, axis=0)
        for copy in self.copies(slot):
            copy.start()

    def finish(self, slot):
        total = self.message[slot]
        for index, copy in enumerate(self.copies(slot)):
            copy.wait_recv()
            total = total + self.held[slot + (index,)]
        return [total[index : index + 1, 0:1] for index in range(8)]

    def settle(self, slot):
        for copy in self.copies(slot):
            copy.wait_send()


def solve_kernel(
    sizes, filled, result, maps, normal, planes, rows_in, row_mask, extra, grad_out, edges, scalars,
    work, *refs,
):
    micro, parts, length = sizes
    _, _, rows, wide = filled.shape
    sums = RowSums(parts, refs)
    greet(sums.peers)
    inside = lax.broadcasted_iota(jnp.int32, (rows, wide), 1) < length
    penalty = jnp.exp(jnp.full((1, 1), extra[2], F32))
    inv_count = 1.0 / rows_in[0, 0, 4:5, 0:1]
    diagonals = [jnp.sum(row_mask[batch].astype(F32), axis=1, keepdims=True) / length for batch in range(micro)]
    names = ("denoised", "right", "mapped", "residue", "through", "search", "searched", "slope")

    def at(name, batch):
        return work.at[batch, names.index(name)]

    def get(name, batch):
        return pair(at(name, batch))

    def through_normal(image, batch):
        out = apply_normal(image, maps.at[batch], normal.at[batch], diagonals[batch])
        return blend((1.0, out), (penalty, image))

    for batch in range(micro):
        images = []
        for part in range(2):
            value = filled[batch, part] + result[batch, part] + jnp.full((1, 1), extra[part], F32)
            value = jnp.where(inside, value, 0.0)
            at("denoised", batch)[part] = value
            images.append(filled[batch, part] + penalty * value)
        put_pair(at("right", batch), images)
        mapped = through_normal(images, batch)
        put_pair(at("mapped", batch), mapped)
        sums.start((0, batch), [inner_of(images, images), inner_of(images, mapped)])
    ones, twos = [], []
    for batch in range(micro):
        ones.append(sums.finish((0, batch)))
        start, image = get("right", batch), get("mapped", batch)
        left_over = blend((1.0, start), (-ones[batch][0] / ones[batch][1], image))
        put_pair(at("residue", batch), left_over)
        mapped = through_normal(left_over, batch)
        put_pair(at("through", batch), mapped)
        sums.start(
            (1, batch),
            [
                inner_of(left_over, left_over),
                inner_of(left_over, mapped),
                inner_of(left_over, image),
                inner_of(start, mapped),
            ],
        )
    kept = []
    for batch in range(micro):
        twos.append(sums.finish((1, batch)))
        norm_0, curve_0 = ones[batch][:2]
        norm_1 = twos[batch][0]
        factor = norm_1 / norm_0
        curve_1 = twos[batch][1] + factor * (twos[batch][2] + twos[batch][3]) + factor * factor * curve_0
        start, image = get("right", batch), get("mapped", batch)
        direction = blend((1.0, get("residue", batch)), (factor, start))
        image_1 = blend((1.0, get("through", batch)), (factor, image))
        put_pair(at("searched", batch), image_1)
        state = blend((norm_0 / curve_0, start), (norm_1 / curve_1, direction))
        weight = planes[batch, 2]
        difference = [state[part] - planes[batch, part] for part in range(2)]
        grad = [inv_count * 2.0 * weight * difference[part] for part in range(2)]
        put_pair(at("slope", batch), grad)
        masked = [weight * difference[part] for part in range(2)]
        sums.start(
            (2, batch),
            [
                inner_of(grad, direction),
                inner_of(grad, start),
                inner_of(grad, image),
                inner_of(image_1, start),
                inner_of(image_1, image),
            ],
        )
        kept.append((norm_0, curve_0, norm_1, curve_1, factor, inner_of(direction, direction), inner_of(masked, difference)))
    for batch in range(micro):
        grad_search, grad_start, grad_image, cross_start, cross_image = sums.finish((2, batch))[:5]
        norm_0, curve_0, norm_1, curve_1, factor, own_search, own_loss = kept[batch]
        step_0, step_1 = norm_0 / curve_0, norm_1 / curve_1
        start, image, left_over = get("right", batch), get("mapped", batch), get("residue", batch)
        image_1, grad = get("searched", batch), get("slope", batch)
        residue_image = twos[batch][2]
        curve_grad_1 = -grad_search * norm_1 / (curve_1 * curve_1)
        norm_grad_1 = grad_search / curve_1
        search_grad = blend((step_1, grad), (2.0 * curve_grad_1, image_1))
        factor_grad = step_1 * grad_start + 2.0 * curve_grad_1 * cross_start
        joint = step_1 * grad_image + 2.0 * curve_grad_1 * cross_image
        norm_total = norm_grad_1 + factor_grad / norm_0
        residue_full = blend((1.0, search_grad), (2.0 * norm_total, left_over))
        step_grad = grad_start - (joint + 2.0 * norm_total * residue_image)
        curve_grad_0 = -step_grad * norm_0 / (curve_0 * curve_0)
        mapped_grad = blend((-step_0, residue_full), (curve_grad_0, start))
        through = through_normal(mapped_grad, batch)
        norm_grad_0 = -factor_grad * norm_1 / (norm_0 * norm_0) + step_grad / curve_0
        right_grad = blend(
            (1.0, residue_full),
            (factor, search_grad),
            (step_0, grad),
            (curve_grad_0, image),
            (1.0, through),
            (2.0 * norm_grad_0, start),
        )
        penalty_part = (
            curve_grad_1 * own_search + inner_of(mapped_grad, start) + inner_of(right_grad, get("denoised", batch))
        )
        grad_pair = [penalty * right_grad[part] for part in range(2)]
        put_pair(grad_out.at[batch], grad_pair)
        put_edges(edges.at[:, batch], *grad_pair)
        offsets = [jnp.sum(jnp.sum(grad_pair[part], axis=1, keepdims=True), axis=0, keepdims=True) for part in range(2)]
        values = [offsets[0], offsets[1], penalty * penalty_part, own_loss]
        scalars[batch] = join_rows([jnp.broadcast_to(value, (1, TILE)) for value in values], 8)
    for stage in range(3):
        for batch in range(micro):
            sums.settle((stage, batch))


def solve_all(filled, result, maps, normal, planes, rows_in, row_mask, extra, parts, length):
    micro, _, rows, wide = filled.shape
    shapes = [(micro, 2, rows, wide), (2, micro, 2 * REACH, wide), (micro, 8, TILE)]
    slots = (3, micro)
    return pl.pallas_call(
        functools.partial(solve_kernel, (micro, parts, length)),
        out_shape=[jax.ShapeDtypeStruct(shape, F32) for shape in shapes],
        in_specs=[in_vmem()] * 7 + [pl.BlockSpec(memory_space=pltpu.SMEM)],
        out_specs=[in_vmem()] * 3,
        scratch_shapes=[
            pltpu.VMEM((micro, 8, 2, rows, wide), F32),
            pltpu.VMEM(slots + (8, TILE), F32),
            pltpu.VMEM(slots + (parts - 1, 8, TILE), F32),
            pltpu.SemaphoreType.DMA(slots + (parts - 1,)),
            pltpu.SemaphoreType.DMA(slots + (parts - 1,)),
        ],
        compiler_params=params(collective_id=5, has_side_effects=True),
        name="solve_all",
    )(filled, result, maps, normal, planes, rows_in, row_mask, extra)


def update_kernel(weights, means, squares, grads, rows_back, totals, rows_in, outs):
    first_grad, middle_grad, last_grad = grads
    affine = []
    for row in (1, 0):
        rows = [functools.reduce(jnp.add, [rows_back[layer, batch, row : row + 1] for batch in range(rows_back.shape[1])]) for layer in range(4)]
        affine.append(jnp.concatenate(rows, axis=0))
    extra = join_lanes([totals[index : index + 1, 0:1] for index in range(3)], 3)

    def put(group, at, gradient, refs):
        results = adamw(weights[group][at], gradient, means[group][at], squares[group][at], LEARN_RATES[group])
        for ref, value in zip(refs, results + (results[0].astype(BF16),)):
            ref[at] = value

    everything = (slice(None), slice(None))
    for tap in range(9):
        put(0, tap, first_grad[tap], outs[0:4])
        put(2, tap, last_grad[tap], outs[8:12])
        for layer in range(3):
            put(1, (layer, tap), middle_grad[layer, tap], outs[4:8])
    put(3, everything, affine[0], outs[12:15])
    put(4, everything, affine[1], outs[15:18])
    put(5, everything, extra, outs[18:21])
    outs[21][...] = totals[3:4, 0:1]
    outs[22][...] = rows_in[0, 0, 4:5, 0:1].astype(jnp.int32)


def update(weights, means, squares, grads, rows_back, totals, rows_in):
    shapes = []
    for group, weight in enumerate(weights):
        shapes += [jax.ShapeDtypeStruct(weight.shape, F32)] * 3
        if group < 3:
            shapes.append(jax.ShapeDtypeStruct(weight.shape, BF16))
    shapes += [jax.ShapeDtypeStruct((1, 1), F32), jax.ShapeDtypeStruct((1, 1), jnp.int32)]

    def kernel(*refs):
        update_kernel(refs[0:6], refs[6:12], refs[12:18], refs[18:21], refs[21], refs[22], refs[23], refs[24:])

    return pl.pallas_call(
        kernel,
        out_shape=shapes,
        in_specs=[in_vmem()] * 24,
        out_specs=[in_vmem()] * len(shapes),
        compiler_params=params(),
        name="update",
    )(*weights, *means, *squares, *grads, rows_back, totals, rows_in)


def fast_step(arrays, moments):
    (
        kspace, coil_maps, target, row_mask, foreground, anatomy, first_weight, middle_weight, last_weight, norm_gains, norm_shifts, extra_params,
    ) = arrays
    length = kspace.shape[-1]
    parts, images = lax.axis_size("row"), lax.axis_size("img")
    filled, maps, edges, planes, normal, first_table, middle_tables, last_table, middle_back, last_back, counted = exchange(
        kspace[:, 0], coil_maps[:, 0], target[:, 0], foreground[:, 0], row_mask, anatomy,
        first_weight.transpose(0, 2, 1), middle_weight, last_weight, parts,
    )
    layers, coefs, rows_out, images_out, result = forward(
        filled, edges, (first_table, middle_tables, last_table), norm_gains, norm_shifts, counted, parts, images, length
    )
    grad, edges, scalars = solve_all(
        filled, result, maps, normal, planes, rows_out, row_mask, extra_params, parts, length
    )
    first_sums, middle_sums, last_sums, rows_back = backward(
        grad, edges, (layers, coefs, rows_out, images_out), (middle_back, last_back), parts, images, length
    )
    *grads, totals = reduce_all(first_sums, middle_sums, last_sums, scalars, parts, images)

    def turn(group):
        first, middle, last, gains, shifts, extra = group
        return [first.transpose(0, 2, 1), middle, last, gains, shifts, extra.reshape(1, 3)]

    weights = (first_weight, middle_weight, last_weight, norm_gains, norm_shifts, extra_params)
    means, squares = zip(*moments)
    outs = list(update(turn(weights), turn(means), turn(squares), grads, rows_back, totals, rows_out))
    outs[0:4] = [value.transpose(0, 2, 1) for value in outs[0:4]]
    outs[18:21] = [value.reshape(3) for value in outs[18:21]]
    return tuple(outs[:21]) + (outs[21].reshape(()), outs[22].reshape(()))


def local(
    kspace,
    coil_maps,
    target,
    row_mask,
    foreground,
    anatomy,
    first_weight,
    middle_weight,
    last_weight,
    norm_gains,
    norm_shifts,
    extra_params,
    first_mean,
    first_square,
    middle_mean,
    middle_square,
    last_mean,
    last_square,
    gains_mean,
    gains_square,
    shifts_mean,
    shifts_square,
    extra_mean,
    extra_square,
):
    arrays = (
        kspace, coil_maps, target, row_mask, foreground, anatomy, first_weight, middle_weight, last_weight, norm_gains, norm_shifts, extra_params,
    )
    moments = (
        (first_mean, first_square),
        (middle_mean, middle_square),
        (last_mean, last_square),
        (gains_mean, gains_square),
        (shifts_mean, shifts_square),
        (extra_mean, extra_square),
    )
    if fits(kspace, first_weight, lax.axis_size("row")):
        return fast_step(arrays, moments)
    totals, pixel_total = general_local(arrays)
    params = (first_weight, middle_weight, last_weight, norm_gains, norm_shifts, extra_params)
    results = []
    for group in range(6):
        updated, first_new, second_new = adamw(
            params[group], totals[group], moments[group][0], moments[group][1], LEARN_RATES[group]
        )
        results.extend([updated, first_new, second_new])
        if group < 3:
            results.append(updated.astype(jnp.bfloat16))
    return tuple(results) + (totals[6], pixel_total.astype(jnp.int32))


def solution(mesh):
    in_specs = (
        P(None, "img", None, None, "row", None),
        P(None, "img", None, None, "row", None),
        P(None, "img", None, "row", None),
        P(None, "img", None),
        P(None, "img", "row", None),
        P(None, "img"),
        P(),
        P(),
        P(),
        P(),
        P(),
        P(),
        P(),
        P(),
        P(),
        P(),
        P(),
        P(),
        P(),
        P(),
        P(),
        P(),
        P(),
        P(),
    )
    out_specs = (
        P(),
        P(),
        P(),
        P(),
        P(),
        P(),
        P(),
        P(),
        P(),
        P(),
        P(),
        P(),
        P(),
        P(),
        P(),
        P(),
        P(),
        P(),
        P(),
        P(),
        P(),
        P(),
        P(),
    )
    return jax.shard_map(local, mesh=mesh, in_specs=in_specs, out_specs=out_specs, check_vma=False)
```

```python
import functools

import jax
import jax.numpy as jnp
import numpy as np
from jax import lax
from jax.experimental import pallas as pl
from jax.experimental.pallas import tpu as pltpu
from jax.sharding import PartitionSpec as P

COILS = 16
BRAIN_COILS = 12
UNROLLS = 1
CG_STEPS = 2
STEP = 10


PRECISE = lax.Precision.HIGHEST
EPS_NORM = 1e-05
BETA_ONE = 0.9
BETA_TWO = 0.999
ADAM_EPS = 1e-08
DECAY_RATE = 0.01
LEARN_RATES = (0.3, 0.05, 0.05, 0.4, 0.4, 0.4)


def with_halo(cells, sides, width):
    for axis, dim in sides:
        count = lax.axis_size(axis)
        ends = count - 1
        head = lax.slice_in_dim(cells, 0, width, axis=dim)
        tail = lax.slice_in_dim(cells, cells.shape[dim] - width, cells.shape[dim], axis=dim)
        cells = jnp.concatenate(
            [
                lax.ppermute(tail, axis, [(i, (i + 1) % count) for i in range(ends)]),
                cells,
                lax.ppermute(head, axis, [((i + 1) % count, i) for i in range(ends)]),
            ],
            axis=dim,
        )
    return cells


def dft_table(length, direction):
    index = jnp.arange(length, dtype=jnp.int32)
    phase = (index[:, None] * index[None, :] % length).astype(jnp.float32) * (2.0 * jnp.pi / length)
    factor = 1.0 / jnp.sqrt(jnp.float32(length))
    cosine = jnp.cos(phase) * factor
    sine = jnp.sin(phase) * factor * direction
    return jnp.stack([jnp.stack([cosine, -sine], 1), jnp.stack([sine, cosine], 1)], 0)


def along_width(field, table):
    return jnp.einsum("bcprw,pwqk->bcqrk", field, table, precision=PRECISE)


def along_height(field, table):
    return jnp.einsum("bcprw,prqk->bcqkw", field, table, precision=PRECISE)


def expand(image, maps):
    real_part, imag_part = (image[:, None, 0], image[:, None, 1])
    maps_re, maps_im = (maps[:, :, 0], maps[:, :, 1])
    return jnp.stack(
        [maps_re * real_part - maps_im * imag_part, maps_re * imag_part + maps_im * real_part], 2
    )


def combine(field, maps):
    field_re, field_im = (field[:, :, 0], field[:, :, 1])
    maps_re, maps_im = (maps[:, :, 0], maps[:, :, 1])
    return jnp.stack(
        [
            jnp.sum(maps_re * field_re + maps_im * field_im, 1),
            jnp.sum(maps_re * field_im - maps_im * field_re, 1),
        ],
        1,
    )


def to_columns(field):
    return lax.all_to_all(
        field.astype(jnp.bfloat16), "row", split_axis=4, concat_axis=3, tiled=True
    ).astype(field.dtype)


def to_rows(field):
    return lax.all_to_all(
        field.astype(jnp.bfloat16), "row", split_axis=3, concat_axis=4, tiled=True
    ).astype(field.dtype)


def make_normal(maps, mask_rows, forward, inverse, measured):
    zero_filled = combine(to_rows(along_height(measured * mask_rows, inverse)), maps)

    def normal(image):
        spectrum = to_columns(along_width(expand(image, maps), forward))
        spectrum = along_height(spectrum, forward) * mask_rows
        spectrum = to_rows(along_height(spectrum, inverse))
        return combine(along_width(spectrum, inverse), maps)

    return (normal, zero_filled)


def inner(left, right):
    return jnp.sum(left * right, axis=(1, 2, 3))


def per_image(values):
    return values[:, None, None, None]


def row_sums(values):
    return lax.psum(values, "row")


def solve(rhs, penalty, normal):
    state = jnp.zeros_like(rhs)
    residue = rhs
    search = rhs
    norm_now = row_sums(inner(residue, residue))
    kept = []
    for iterate in range(CG_STEPS):
        mapped = normal(search) + penalty * search
        curvature = row_sums(inner(search, mapped))
        stepsize = norm_now / curvature
        state = state + per_image(stepsize) * search
        residue = residue - per_image(stepsize) * mapped
        norm_next = row_sums(inner(residue, residue))
        kept.append((search, mapped, residue, norm_now, norm_next, curvature))
        search = residue + per_image(norm_next / norm_now) * search
        norm_now = norm_next
    return (state, kept)


def solve_backward(state_grad, kept, rhs, denoised, penalty, normal):
    search_grad = jnp.zeros_like(rhs)
    residue_grad = jnp.zeros_like(rhs)
    norm_grad = jnp.zeros(rhs.shape[0], jnp.float32)
    penalty_part = jnp.float32(0.0)
    for iterate in reversed(range(CG_STEPS)):
        search, mapped, residue, norm_now, norm_next, curvature = kept[iterate]
        factor_grad, along_search, joint_mapped, residue_mapped = lax.psum(
            (
                inner(search_grad, search),
                inner(state_grad, search),
                inner(residue_grad + search_grad, mapped),
                inner(residue, mapped),
            ),
            "row",
        )
        stepsize = norm_now / curvature
        factor = norm_next / norm_now
        norm_total = norm_grad + factor_grad / norm_now
        residue_full = residue_grad + search_grad + per_image(2.0 * norm_total) * residue
        stepsize_grad = along_search - (joint_mapped + 2.0 * norm_total * residue_mapped)
        curvature_grad = -stepsize_grad * norm_now / (curvature * curvature)
        mapped_grad = -per_image(stepsize) * residue_full + per_image(curvature_grad) * search
        penalty_part = penalty_part + jnp.sum(mapped_grad * search)
        search_grad = (
            per_image(factor) * search_grad
            + per_image(stepsize) * state_grad
            + per_image(curvature_grad) * mapped
            + normal(mapped_grad)
            + penalty * mapped_grad
        )
        residue_grad = residue_full
        norm_grad = -factor_grad * norm_next / (norm_now * norm_now) + stepsize_grad / curvature
    rhs_grad = residue_grad + search_grad + per_image(2.0 * norm_grad) * rhs
    penalty_part = penalty_part + jnp.sum(rhs_grad * denoised)
    return (penalty * rhs_grad, penalty_part)


def conv_forward(activation, weight):
    height, breadth = (activation.shape[2], activation.shape[3])
    padded = with_halo(activation, (("row", 2),), 1)
    padded = jnp.pad(padded, ((0, 0), (0, 0), (0, 0), (1, 1)))
    summed = jnp.zeros((activation.shape[0], weight.shape[1], height, breadth), jnp.float32)
    for tap_index in range(9):
        window = padded[
            :, :, tap_index // 3 : tap_index // 3 + height, tap_index % 3 : tap_index % 3 + breadth
        ]
        summed = summed + jnp.einsum(
            "oi,birw->borw", weight[tap_index], window, preferred_element_type=jnp.float32
        )
    return (summed, padded)


def conv_backward(upstream, padded, weight, need_input):
    height, breadth = (upstream.shape[2], upstream.shape[3])
    weight_grad = jnp.stack(
        [
            jnp.einsum(
                "borw,birw->oi",
                upstream,
                padded[
                    :,
                    :,
                    tap_index // 3 : tap_index // 3 + height,
                    tap_index % 3 : tap_index % 3 + breadth,
                ],
                preferred_element_type=jnp.float32,
            )
            for tap_index in range(9)
        ]
    )
    if not need_input:
        return (weight_grad, None)
    widened = with_halo(upstream, (("row", 2),), 1)
    widened = jnp.pad(widened, ((0, 0), (0, 0), (0, 0), (1, 1)))
    summed = jnp.zeros((upstream.shape[0], weight.shape[2], height, breadth), jnp.float32)
    for tap_index in range(9):
        start_r = 2 - tap_index // 3
        start_c = 2 - tap_index % 3
        window = widened[:, :, start_r : start_r + height, start_c : start_c + breadth]
        summed = summed + jnp.einsum(
            "oi,borw->birw", weight[tap_index], window, preferred_element_type=jnp.float32
        )
    return (weight_grad, summed)


def norm_sums(values):
    return lax.psum(values, ("img", "row"))


def channel(values):
    return values[None, :, None, None]


def cnn_forward(image, weights, gains, shifts, offset, pixels):
    activation = image.astype(jnp.bfloat16)
    kept = []
    for layer_index in range(4):
        linear, padded = conv_forward(activation, weights[layer_index])
        average = norm_sums(jnp.sum(linear, axis=(0, 2, 3))) / pixels
        centred = linear - channel(average)
        spread = norm_sums(jnp.sum(centred * centred, axis=(0, 2, 3))) / pixels
        inv_std = lax.rsqrt(spread + EPS_NORM)
        normed = centred * channel(inv_std)
        shaped = channel(gains[layer_index]) * normed + channel(shifts[layer_index])
        activation = jax.nn.silu(shaped).astype(jnp.bfloat16)
        kept.append((padded, normed, shaped, inv_std))
    result, padded = conv_forward(activation, weights[4])
    kept.append(padded)
    return (image + result + channel(offset), kept)


def cnn_backward(denoised_grad, kept, weights, gains, pixels, need_input):
    offset_grad = jnp.sum(denoised_grad, axis=(0, 2, 3))
    weight_grads = [None] * 5
    gain_grads = [None] * 4
    shift_grads = [None] * 4
    weight_grads[4], upstream = conv_backward(
        denoised_grad.astype(jnp.bfloat16), kept[4], weights[4], True
    )
    for layer_index in (3, 2, 1, 0):
        padded, normed, shaped, inv_std = kept[layer_index]
        sigmoid_val = jax.nn.sigmoid(shaped)
        shaped_grad = upstream * sigmoid_val * (1.0 + shaped * (1.0 - sigmoid_val))
        shift_local = jnp.sum(shaped_grad, axis=(0, 2, 3))
        gain_local = jnp.sum(shaped_grad * normed, axis=(0, 2, 3))
        shift_total, gain_total = lax.psum((shift_local, gain_local), ("img", "row"))
        gain_vec = gains[layer_index]
        linear_grad = channel(inv_std) * (
            shaped_grad * channel(gain_vec)
            - channel(gain_vec * shift_total / pixels)
            - normed * channel(gain_vec * gain_total / pixels)
        )
        shift_grads[layer_index] = shift_local
        gain_grads[layer_index] = gain_local
        weight_grads[layer_index], upstream = conv_backward(
            linear_grad.astype(jnp.bfloat16),
            padded,
            weights[layer_index],
            layer_index > 0 or need_input,
        )
    image_grad = None
    return (image_grad, weight_grads, jnp.stack(gain_grads), jnp.stack(shift_grads), offset_grad)


def adamw(weight, gradient, moment_one, moment_two, rate):
    first_new = BETA_ONE * moment_one + (1.0 - BETA_ONE) * gradient
    second_new = BETA_TWO * moment_two + (1.0 - BETA_TWO) * gradient * gradient
    corrected = first_new / (1.0 - BETA_ONE**STEP)
    divisor = jnp.sqrt(second_new / (1.0 - BETA_TWO**STEP)) + ADAM_EPS
    updated = weight - rate * (corrected / divisor + DECAY_RATE * weight)
    return (updated, first_new, second_new)


def general_local(arrays):
    (
        kspace, coil_maps, target, row_mask, foreground, anatomy, first_weight, middle_weight, last_weight, norm_gains, norm_shifts, extra_params,
    ) = arrays
    length = kspace.shape[-1]
    forward = dft_table(length, 1.0)
    inverse = dft_table(length, -1.0)
    pixel_total = lax.psum(jnp.sum(foreground).astype(jnp.float32), ("img", "row"))
    inv_count = 1.0 / pixel_total
    middle_low = middle_weight.astype(jnp.bfloat16)
    conv_weights = [
        first_weight.astype(jnp.bfloat16),
        middle_low[0],
        middle_low[1],
        middle_low[2],
        last_weight.astype(jnp.bfloat16),
    ]
    penalty = jnp.exp(extra_params[2])
    offset = extra_params[:2]
    images_here = kspace.shape[1]
    pixels = images_here * kspace.shape[4] * length * lax.axis_size("img") * lax.axis_size("row")
    first_grad = jnp.zeros_like(first_weight)
    middle_grad = jnp.zeros_like(middle_weight)
    last_grad = jnp.zeros_like(last_weight)
    gains_grad = jnp.zeros_like(norm_gains)
    shifts_grad = jnp.zeros_like(norm_shifts)
    offset_grad = jnp.zeros((2,), jnp.float32)
    penalty_grad = jnp.float32(0.0)
    loss_part = jnp.float32(0.0)
    for microbatch in range(kspace.shape[0]):
        limit = jnp.where(anatomy[microbatch] == 0, BRAIN_COILS, COILS)
        coil_on = (jnp.arange(kspace.shape[2])[None, :] < limit[:, None]).astype(jnp.float32)
        maps = coil_maps[microbatch] * coil_on[:, :, None, None, None]
        mask_rows = row_mask[microbatch].astype(jnp.float32)[:, None, None, :, None]
        measured = to_columns(along_width(kspace[microbatch], inverse))
        normal, zero_filled = make_normal(maps, mask_rows, forward, inverse, measured)
        state = zero_filled
        unroll = 0
        denoised, cnn_kept = cnn_forward(
            state, conv_weights, norm_gains, norm_shifts, offset, pixels
        )
        rhs = zero_filled + penalty * denoised
        state, cg_kept = solve(rhs, penalty, normal)
        saved = [(cnn_kept, cg_kept, rhs, denoised)]
        fg_mask = foreground[microbatch].astype(jnp.float32)[:, None]
        difference = state - target[microbatch]
        loss_part = loss_part + jnp.sum(fg_mask * difference * difference)
        state_grad = inv_count * 2.0 * fg_mask * difference
        for unroll in reversed(range(UNROLLS)):
            cnn_kept, cg_kept, rhs, denoised = saved[unroll]
            denoised_grad, penalty_part = solve_backward(
                state_grad, cg_kept, rhs, denoised, penalty, normal
            )
            penalty_grad = penalty_grad + penalty_part
            state_grad, weight_grads, gain_part, shift_part, offset_part = cnn_backward(
                denoised_grad, cnn_kept, conv_weights, norm_gains, pixels, unroll > 0
            )
            first_grad = first_grad + weight_grads[0]
            middle_grad = middle_grad + jnp.stack(weight_grads[1:4])
            last_grad = last_grad + weight_grads[4]
            gains_grad = gains_grad + gain_part
            shifts_grad = shifts_grad + shift_part
            offset_grad = offset_grad + offset_part
    extra_grad = jnp.concatenate([offset_grad, (penalty * penalty_grad)[None]])
    totals = lax.psum(
        (first_grad, middle_grad, last_grad, gains_grad, shifts_grad, extra_grad, loss_part),
        ("img", "row"),
    )
    return totals, pixel_total


BF16 = jnp.bfloat16
F32 = jnp.float32
MESH = pl.DeviceIdType.MESH
TILE = 128
BLOCK = 8
BACK_REACH = 3
FIRST_REACH = 6
GROUP = 4
HOOK_PART = 4
REACH = 8
VMEM_BYTES = 58 * 1024 * 1024


def padded(length):
    return -(-length // TILE) * TILE


def fits(kspace, first_weight, mesh_rows):
    micro, images, coils, _, rows, length = kspace.shape
    channels = first_weight.shape[1]
    return (
        images == 1
        and micro == 2
        and 2 * channels == TILE
        and channels % 16 == 0
        and rows * mesh_rows == length
        and mesh_rows & (mesh_rows - 1) == 0
        and rows % BLOCK == 0
        and (2 * rows) % 16 == 0
        and (coils * rows) % TILE == 0
        and padded(length) > length
    )


def phases(length):
    index = np.arange(length)
    angle = 2.0 * np.pi * (np.outer(index, index) % length) / length
    return np.cos(angle) / np.sqrt(length), np.sin(angle) / np.sqrt(length)


def high_low(table):
    high = table.astype(BF16)
    low = (table - high.astype(F32)).astype(BF16)
    return high, low


def np_high_low(table):
    table = np.asarray(table, np.float32)
    high = table.astype(BF16)
    low = (table - high.astype(np.float32)).astype(BF16)
    return jnp.asarray(high), jnp.asarray(low)


def dot(left, right):
    return jnp.dot(left, right, preferred_element_type=F32)


def dot_nt(left, right):
    return lax.dot_general(left, right, (((1,), (1,)), ((), ())), preferred_element_type=F32)


def knock(peers):
    barrier = pltpu.get_barrier_semaphore()
    for peer in peers:
        pl.semaphore_signal(barrier, inc=1, device_id=peer, device_id_type=MESH)


def admit(peers):
    pl.semaphore_wait(pltpu.get_barrier_semaphore(), len(peers))


def partner(me, step):
    other, bit = 0, 1
    while bit <= step:
        own = lax.rem(lax.div(me, bit), 2)
        other = other + bit * (1 - own if step & bit else own)
        bit *= 2
    return other + lax.div(me, bit) * bit


def row_peers(rows):
    image, row = lax.axis_index("img"), lax.axis_index("row")
    steps = sorted(range(1, rows), key=lambda step: (-step.bit_length(), step))
    return [(image, partner(row, step)) for step in steps]


def image_peers(images):
    image, row = lax.axis_index("img"), lax.axis_index("row")
    return [(lax.rem(image + step, images), row) for step in range(1, images)]


def remote(source, target, send, receive, peer):
    return pltpu.make_async_remote_copy(
        src_ref=source,
        dst_ref=target,
        send_sem=send,
        recv_sem=receive,
        device_id=peer,
        device_id_type=MESH,
    )


def params(vmem=VMEM_BYTES, **kwargs):
    return pltpu.CompilerParams(vmem_limit_bytes=vmem, **kwargs)


def in_vmem():
    return pl.BlockSpec(memory_space=pltpu.VMEM)


def anywhere():
    return pl.BlockSpec(memory_space=pl.ANY)


def three_parts(values):
    high = values.astype(BF16)
    rest = values - high.astype(F32)
    middle = rest.astype(BF16)
    return high, middle, (rest - middle.astype(F32)).astype(BF16)


def join_lanes(pieces, wide):
    short = wide - sum(piece.shape[1] for piece in pieces)
    if short:
        pieces = pieces + [jnp.zeros((pieces[0].shape[0], short), pieces[0].dtype)]
    return jnp.concatenate(pieces, axis=1)


def join_rows(pieces, height):
    short = height - sum(piece.shape[0] for piece in pieces)
    if short:
        pieces = pieces + [jnp.zeros((short, pieces[0].shape[1]), pieces[0].dtype)]
    return jnp.concatenate(pieces, axis=0)


def start_exchange(
    sizes, meet, kspace, maps, target, foreground, row_mask, anatomy, first, middle, last, turn_high, turn_low, pick, cosine, sine,
    fourier_high, fourier_low,
    filled, maps_out, halo, planes, normal, first_table, middle_tables, last_table, middle_back, last_back, counted,
    fields, staged, spread, flat, landed, edges, loaded, send, receive, own, send_flat, receive_flat, send_edge, receive_edge,
):
    micro, coils, rows, length, parts = sizes
    wide = padded(length)
    image, me = lax.axis_index("img"), lax.axis_index("row")
    peers = row_peers(parts)
    slots = [(batch, kind) for batch in range(micro) for kind in (1, 0)]
    loads = {}

    def load_field(index):
        if index < len(slots):
            batch, kind = slots[index]
            for part in range(2):
                source = (kspace, maps)[kind].at[batch, :, part]
                loads[index, part] = pltpu.make_async_copy(source, fields.at[index % 2, part], loaded.at[index, part])
                loads[index, part].start()

    load_field(0)
    load_field(1)
    arrivals = [[] for _ in range(micro)]
    slabs = 2 * rows
    def send_slot(index):
        batch, kind = slots[index]
        total = None
        for part in range(2):
            loads[index, part].wait()
            field = fields[index % 2, part].reshape(coils * rows, length)
            if kind == 0:
                high, low = high_low(field)
                term = (
                    dot_nt(turn_high[part], high)
                    + dot_nt(turn_low[part], high)
                    + dot_nt(turn_high[part], low)
                )
            else:
                term = dot_nt(pick[part], field.astype(BF16))
            total = term if total is None else total + term
        slot = 2 * batch + kind
        staged[slot] = total.astype(BF16).reshape(parts, slabs, coils * rows)
        load_field(index + 2)
        if index == 0:
            meet()
        for step, peer in enumerate(peers):
            copy = remote(
                staged.at[slot, peer[1]], spread.at[slot, me], send.at[slot, step], receive.at[slot, step], peer
            )
            copy.start()
            arrivals[batch].append(copy)
        local = pltpu.make_async_copy(staged.at[slot, me], spread.at[slot, me], own.at[slot])
        local.start()
        arrivals[batch].append(local)

    for index in range(len(slots) - 1):
        send_slot(index)
    flats = exchange_planes(sizes, target, foreground, pick, counted, flat, landed, send_flat, receive_flat, me, peers)
    for batch in range(micro):
        chosen = join_lanes([row_mask[batch].astype(F32)], wide)
        cos_on, sin_on = cosine[...] * chosen, sine[...] * chosen

        def product(left, right):
            return jnp.dot(left, right, precision=PRECISE, preferred_element_type=F32)

        real = product(cos_on, cosine[...]) + product(sin_on, sine[...])
        imag = product(sin_on, cosine[...]) - product(cos_on, sine[...])
        diagonal = [lax.broadcasted_iota(jnp.int32, real.shape, axis) for axis in range(2)]
        real = jnp.where(diagonal[0] == diagonal[1], 0.0, real)
        for block, value in (((0, 0), real), ((0, 1), -imag), ((1, 0), imag), ((1, 1), real)):
            normal[batch, pl.ds(block[0] * wide, wide), pl.ds(block[1] * wide, wide)] = value.astype(BF16)
    put_tables(first, middle, last, first_table, middle_tables, last_table, middle_back, last_back)

    def arrive(batch):
        for copy in arrivals[batch]:
            copy.wait()
        knee = jnp.where(anatomy[0:1, batch : batch + 1] == 0, 0.0, 1.0)
        real, imag = zero_fill(
            (coils, rows, parts, wide),
            knee,
            spread.at[2 * batch],
            spread.at[2 * batch + 1],
            join_lanes([row_mask[batch].astype(F32)], wide),
            fourier_high,
            fourier_low,
            maps_out.at[batch],
        )
        put_pair(filled.at[batch], (real, imag))
        put_edges(edges.at[:, batch], real, imag)
        moved = image_halo(parts, batch, edges, halo, send_edge, receive_edge)
        for copy in moved:
            copy.start()
        if batch == 0:
            send_slot(len(slots) - 1)
            for copy in flats:
                copy.wait()
            for image_batch in range(micro):
                for plane in range(3):
                    at = (3 * image_batch + plane) * rows
                    pieces = [landed[block, :, at : at + rows] for block in range(parts)]
                    planes[image_batch, plane] = join_lanes(pieces, wide)
        for copy in moved:
            copy.wait()

    return arrive


def exchange_planes(
    sizes, target, foreground, pick, counted, flat, landed, send_flat, receive_flat, me, peers
):
    micro, _, rows, length, parts = sizes
    shown = [foreground[batch].astype(F32) for batch in range(micro)]
    count = functools.reduce(jnp.add, [jnp.sum(jnp.sum(s, axis=1, keepdims=True), axis=0, keepdims=True) for s in shown])
    counted[...] = jnp.broadcast_to(count, (1, TILE))
    stack = []
    for batch in range(micro):
        stack += [target[batch, 0], target[batch, 1], shown[batch]]
    stack = jnp.concatenate(stack, axis=0)
    plain = pick[0].reshape(parts, 2 * rows, length)[:, :rows].reshape(length, length)
    turned = functools.reduce(jnp.add, [dot_nt(plain, piece) for piece in three_parts(stack)])
    lanes = flat.shape[2]
    flat[...] = join_lanes([turned], lanes).reshape(parts, rows, lanes)
    landed[me] = flat[me]
    flats = []
    for step, peer in enumerate(peers):
        copy = remote(flat.at[peer[1]], landed.at[me], send_flat.at[step], receive_flat.at[step], peer)
        copy.start()
        flats.append(copy)
    return flats


def put_tables(first, middle, last, first_table, middle_tables, last_table, middle_back, last_back):
    taps = range(3)
    turned = [join_rows([first[tap]], 8).T[:, :2] for tap in range(9)]
    first_table[...] = jnp.concatenate(
        [join_lanes([turned[3 * kr + kw] for kr in taps], 16) for kw in taps], axis=0
    ).astype(BF16)
    last_table[...] = jnp.concatenate(
        [join_rows([jnp.concatenate([last[3 * kr + kw] for kr in taps], axis=1)], 8) for kw in taps], axis=0
    ).astype(BF16)
    turned = [join_rows([last[tap]], 8).T[:, :2] for tap in range(9)]
    last_back[...] = jnp.concatenate(
        [join_lanes([turned[3 * (2 - m) + 2 - n] for m in taps], 16) for n in taps], axis=0
    ).astype(BF16)
    for layer in range(3):
        weights = [middle[layer, tap] for tap in range(9)]
        turned = [weight.T for weight in weights]
        middle_tables[layer] = jnp.concatenate(
            [jnp.concatenate([weights[3 * kr + kw] for kr in taps], axis=1) for kw in taps], axis=0
        ).astype(BF16)
        middle_back[layer] = jnp.concatenate(
            [jnp.concatenate([turned[3 * (2 - m) + 2 - n] for m in taps], axis=1) for n in taps], axis=0
        ).astype(BF16)


def gather_lanes(blocks, coil, rows, wide):
    pieces = [block[:, coil * rows : (coil + 1) * rows] for block in blocks]
    height = pieces[0].shape[0]
    short = wide - rows * len(pieces)
    return jnp.concatenate(pieces + [jnp.zeros((height, short), pieces[0].dtype)], axis=1)


def zero_fill(sizes, knee, fields, senses, chosen, fourier_high, fourier_low, maps_out):
    coils, rows, parts, wide = sizes
    real = jnp.zeros((rows, wide), F32)
    imag = jnp.zeros((rows, wide), F32)
    chosen = chosen.astype(BF16)
    group = 4
    for first in range(0, coils, group):
        stack = []
        for coil in range(first, first + group):
            sense = gather_lanes([senses[s] for s in range(parts)], coil, rows, wide)
            maps_out[coil] = sense if coil < BRAIN_COILS else sense * knee.astype(BF16)
            stack.append(gather_lanes([fields[s] for s in range(parts)], coil, rows, wide) * chosen)
        stack = jnp.concatenate(stack, axis=0)
        turned = dot(stack, fourier_high[...]) + dot(stack, fourier_low[...])
        for place in range(group):
            top = 2 * rows * place
            upper, lower = turned[top : top + rows], turned[top + rows : top + 2 * rows]
            field_re = upper[:, :wide] - lower[:, wide:]
            field_im = upper[:, wide:] + lower[:, :wide]
            sense = maps_out[first + place].astype(F32)
            sense_re, sense_im = sense[:rows], sense[rows:]
            real = real + sense_re * field_re + sense_im * field_im
            imag = imag + sense_re * field_im - sense_im * field_re
    return real, imag


def put_edges(edges, real, imag):
    rows = real.shape[0]
    edges[0] = jnp.concatenate([real[:REACH], imag[:REACH]], axis=0)
    edges[1] = jnp.concatenate([real[rows - REACH :], imag[rows - REACH :]], axis=0)


def lane_row(columns):
    return jnp.sum(columns.T, axis=0, keepdims=True)


def spread_row(row):
    return jnp.broadcast_to(row, (TILE, row.shape[1])).T


def padded_rows(rows):
    return join_rows([join_lanes([row], TILE) for row in rows], 8)


def merge(sums, squares, count):
    total = functools.reduce(jnp.add, sums)
    mean = total / (count * len(sums))
    square = None
    for part, own in zip(sums, squares):
        shift = part / count - mean
        term = own + count * shift * shift
        square = term if square is None else square + term
    return total, square


def repeat_lanes(block, wide):
    return jnp.concatenate([block] * (wide // TILE), axis=1)


def lane_mask(length, wide):
    whole = length // TILE * TILE

    def clear(values):
        tail = values[:, whole:]
        keep = lax.broadcasted_iota(jnp.int32, tail.shape, 1) < length - whole
        return jnp.concatenate([values[:, :whole], jnp.where(keep, tail, 0.0)], axis=1)

    return clear


def fold(values):
    parts = [values[:, at : at + TILE] for at in range(0, values.shape[1], TILE)]
    return functools.reduce(jnp.add, parts)


def put_shifted(stack, values, at):
    channels, wide = values.shape
    stack[0:channels, at : at + wide] = pltpu.roll(values, 1, 1)
    stack[channels : 2 * channels, at : at + wide] = values
    stack[2 * channels : 3 * channels, at : at + wide] = pltpu.roll(values, wide - 1, 1)


def lane_at(column, wide):
    return pl.multiple_of(column * wide, TILE) if not isinstance(column, int) else column * wide


class Sums:
    def __init__(self, parts, images, refs):
        self.message, self.held, self.second, self.held_second, self.send, self.receive = refs
        self.rows, self.cols = row_peers(parts), image_peers(images)

    def copies(self, slot, stage):
        source, target = ((self.message, self.held), (self.second, self.held_second))[stage]
        peers = (self.rows, self.cols)[stage]
        base = stage * len(self.rows)
        return [
            remote(
                source.at[slot],
                target.at[slot + (index,)],
                self.send.at[slot + (base + index,)],
                self.receive.at[slot + (base + index,)],
                peer,
            )
            for index, peer in enumerate(peers)
        ]

    def start(self, slot, stage, values):
        (self.message, self.second)[stage][slot] = values
        for copy in self.copies(slot, stage):
            copy.start()

    def collect(self, slot, stage):
        blocks = [(self.message, self.second)[stage][slot]]
        for index, copy in enumerate(self.copies(slot, stage)):
            copy.wait_recv()
            blocks.append((self.held, self.held_second)[stage][slot + (index,)])
        return blocks

    def settle(self, slot, stages=(0, 1)):
        for stage in stages:
            for copy in self.copies(slot, stage):
                copy.wait_send()

    @staticmethod
    def scratch(slots, parts, images):
        return [
            pltpu.VMEM(slots + (8, TILE), F32),
            pltpu.VMEM(slots + (parts - 1, 8, TILE), F32),
            pltpu.VMEM(slots + (8, TILE), F32),
            pltpu.VMEM(slots + (max(images - 1, 1), 8, TILE), F32),
            pltpu.SemaphoreType.DMA(slots + (parts + images - 2,)),
            pltpu.SemaphoreType.DMA(slots + (parts + images - 2,)),
        ]


class Ends:
    def __init__(self, parts):
        me = lax.axis_index("row")
        self.left, self.right = me > 0, me < parts - 1

    def clear(self, values, column, width):
        if column < 0:
            return jnp.where(self.left, values, 0.0)
        if column >= width:
            return jnp.where(self.right, values, 0.0)
        return values


def ring_pass(table, take, fill, emit, out_rows, width, wide, hook):
    fill(0)
    fill(1)
    product = dot(table, take(0))
    older = product[0:out_rows, :wide] + product[out_rows : 2 * out_rows, wide:]
    newer = product[0:out_rows, wide:]
    last = width // 2
    for couple in range(1, last + 1):
        if hook is not None and couple == last * HOOK_PART // 8:
            hook()
        product = dot(table, take(couple))
        if couple < last:
            fill(couple + 1)
        for place in range(2):
            piece = product[:, place * wide : (place + 1) * wide]
            emit(2 * couple - 2 + place, older + piece[2 * out_rows : 3 * out_rows])
            older = newer + piece[out_rows : 2 * out_rows]
            newer = piece[0:out_rows]


def silu_half(values, scale, offset):
    half = values * scale + offset
    return half, jnp.tanh(half)


def put_image(image, halo, place, stack, ends, reach):
    _, width, wide = image.shape
    blocks = {-REACH: (halo[0, place, :REACH], halo[0, place, REACH:]), width: (halo[1, place, :REACH], halo[1, place, REACH:])}
    for first in range(0, width, 8):
        blocks[first] = (image[0, first : first + 8], image[1, first : first + 8])
    for first, (real, imag) in blocks.items():
        real, imag = ends.clear(real, first, width), ends.clear(imag, first, width)
        rolled = [pltpu.roll(real, 1, 1), pltpu.roll(imag, 1, 1), real, imag, pltpu.roll(real, wide - 1, 1), pltpu.roll(imag, wide - 1, 1)]
        for offset in range(8):
            at = first + offset + reach
            if 0 <= at < width + 2 * reach:
                rows = [block[offset : offset + 1] for block in rolled]
                stack[:, at * wide : (at + 1) * wide] = join_rows(rows, 16).astype(BF16)


def image_halo(parts, batch, edges, halo, send, receive):
    image, me = lax.axis_index("img"), lax.axis_index("row")
    left, right = lax.rem(me + parts - 1, parts), lax.rem(me + 1, parts)
    places = [((image, left), 0), ((image, right), 1)]
    return [
        remote(edges.at[side, batch], halo.at[1 - side, batch], send.at[batch, side], receive.at[batch, side], peer)
        for peer, side in places
    ]


def forward_kernel(
    sizes, kspace, maps, target, foreground, row_mask, anatomy, first, middle_weight, last, turn_high, turn_low, pick,
    cosine, sine, fourier_high, fourier_low, gains, shifts,
    filled, maps_out, planes, normal, middle_back, last_back, layers, coefs, rows_out, images_out, result,
    fields, staged, spread, flat, landed, edges, halo_image, first_table, middle_tables, last_table, counted,
    loaded, send, receive, own, send_flat, receive_flat, send_edge, receive_edge,
    lin, even, odd, pivot, total, square, *refs,
):
    micro, coils, rows, length, parts, images = sizes
    _, _, width, wide = filled.shape
    channels = lin.shape[3]
    count = width * length
    whole = length // TILE * TILE
    stacks = (even, odd)
    sums = Sums(parts, images, refs[:6])
    (saved,) = refs[6:]
    ends = Ends(parts)
    clear = lane_mask(length, wide)
    knock(sums.rows + sums.cols)
    arrive = start_exchange(
        (micro, coils, rows, length, parts), lambda: admit(sums.rows + sums.cols),
        kspace, maps, target, foreground, row_mask, anatomy, first, middle_weight, last, turn_high, turn_low, pick, cosine, sine,
        fourier_high, fourier_low,
        filled, maps_out, halo_image, planes, normal, first_table, middle_tables, last_table, middle_back, last_back, counted,
        fields, staged, spread, flat, landed, edges, loaded, send, receive, own, send_flat, receive_flat, send_edge, receive_edge,
    )

    def band(layer, batch):
        return lin.at[batch, lax.rem(layer, 2)]

    def save(layer, batch):
        kept = band(layer, batch).at[pl.ds(FIRST_REACH - BACK_REACH, width + 2 * BACK_REACH)]
        return pltpu.make_async_copy(kept, layers.at[layer, batch], saved.at[layer, batch])

    def begin(layer, batch, not_first):
        if not_first:
            save(layer - 1, batch).wait()
        moments = jnp.concatenate([total[...], square[...]], axis=0).T
        moments = jnp.sum(moments, axis=0, keepdims=True)
        delta = moments[:, :channels] / count
        spread = moments[:, channels:] - count * delta * delta
        centre = pivot[...].T[0:1]
        sums.start((layer, batch), 0, padded_rows([count * (centre + delta), spread, counted[:, :channels]]))
        save(layer, batch).start()

    def join(blocks, number):
        blocks = [block[:, :channels] for block in blocks]
        added, spread = merge([block[0:1] for block in blocks], [block[1:2] for block in blocks], number)
        return added, spread, functools.reduce(jnp.add, [block[2:3] for block in blocks])

    def middle(layer, batch):
        joined = join(sums.collect((layer, batch), 0), count)
        sums.start((layer, batch), 1, padded_rows(joined))

    def end(layer, batch):
        added, spread, plain = join(sums.collect((layer, batch), 1), count * parts)
        pixels = count * parts * images
        gain, shift = gains[pl.ds(layer, 1), :], shifts[pl.ds(layer, 1), :]
        inverse = lax.rsqrt(spread / pixels + EPS_NORM)
        offset = -(added / pixels) * inverse
        coefs[layer, batch, 0] = spread_row(0.5 * gain * inverse)
        coefs[layer, batch, 1] = spread_row(0.5 * (shift + gain * offset))
        coefs[layer, batch, 2] = spread_row(inverse)
        coefs[layer, batch, 3] = spread_row(offset)
        rows_out[layer, batch] = join_rows([gain, shift, inverse, offset, plain], 8)

    def keeper(out, reach):
        held = []

        def emit(column, value):
            column = column - reach
            out[FIRST_REACH + column] = value
            if not 0 <= column < width:
                return
            if column == 0:
                mean = jnp.sum(clear(value), axis=1, keepdims=True) / length
                pivot[...] = jnp.broadcast_to(mean, pivot.shape)
            if column % BLOCK == 0:
                held[:] = [jnp.zeros((channels, TILE), F32), jnp.zeros((channels, TILE), F32)]
            centre = pivot[...]
            for at in range(0, wide, TILE):
                shift = value[:, at : at + TILE] - centre
                if at >= whole:
                    lane = lax.broadcasted_iota(jnp.int32, shift.shape, 1)
                    shift = jnp.where(lane < length - at, shift, 0.0)
                held[0] = held[0] + shift
                held[1] = held[1] + shift * shift
            if column == BLOCK - 1:
                total[...], square[...] = held
            elif column % BLOCK == BLOCK - 1:
                total[...] += held[0]
                square[...] += held[1]

        return emit

    def first_layer(batch, hook):
        source = images_out.at[batch]
        put_image(filled.at[batch], halo_image, batch, source, ends, FIRST_REACH + 1)
        ring_pass(
            first_table[...],
            lambda couple: source[:, 2 * couple * wide : 2 * (couple + 1) * wide],
            lambda couple: None,
            keeper(band(0, batch), FIRST_REACH),
            channels,
            width + 2 * FIRST_REACH,
            wide,
            hook,
        )

    def inner_layer(layer, batch, table, out_rows, reach, emit, hook):
        source = band(layer, batch)
        scale, offset = repeat_lanes(coefs[layer, batch, 0], wide), repeat_lanes(coefs[layer, batch, 1], wide)

        def fill(couple):
            for place in range(2):
                column = 2 * couple + place - reach - 1
                half, curve = silu_half(source[FIRST_REACH + column], scale, offset)
                active = ends.clear(clear(half * curve + half), column, width)
                put_shifted(stacks[couple % 2], active.astype(BF16), place * wide)

        ring_pass(table, lambda couple: stacks[couple % 2][...], fill, emit, out_rows, width + 2 * reach, wide, hook)

    def place_of(index):
        return lax.div(index, 2), lax.rem(index, 2)

    arrive(0)
    first_layer(0, None)
    begin(0, 0, False)
    arrive(1)
    first_layer(1, lambda: middle(0, 0))
    begin(0, 1, False)
    end(0, 0)

    def layer_step(index, carried):
        layer, batch = place_of(index)
        before = place_of(index - 1)
        reach = FIRST_REACH - 1
        emit = keeper(band(layer, batch), reach)
        inner_layer(layer - 1, batch, middle_tables[layer - 1], channels, reach, emit, lambda: middle(*before))
        begin(layer, batch, True)
        end(*before)
        return carried

    lax.fori_loop(2, 8, layer_step, 0)

    def last_step(batch, carried):
        def emit(column, value):
            result[batch, 0, column : column + 1] = value[0:1]
            result[batch, 1, column : column + 1] = value[1:2]

        inner_layer(3, batch, last_table[...], 8, 0, emit, lambda: pl.when(batch == 0)(lambda: middle(3, 1)))
        pl.when(batch == 0)(lambda: end(3, 1))
        return carried

    lax.fori_loop(0, 2, last_step, 0)
    for batch in range(2):
        save(3, batch).wait()
    for layer in range(4):
        for batch in range(2):
            sums.settle((layer, batch))


def forward(kspace, maps, target, foreground, row_mask, anatomy, first, middle, last, gains, shifts, parts, images):
    micro, coils, _, rows, length = kspace.shape
    wide = padded(length)
    channels = first.shape[2]
    cosine, sine = phases(length)
    fourier = np.zeros((wide, 2, wide))
    fourier[:length, 0, :length] = cosine
    fourier[:length, 1, :length] = sine
    fourier_high, fourier_low = np_high_low(fourier.reshape(wide, 2 * wide))
    inverse = np.stack([np.stack([cosine, sine], 0), np.stack([-sine, cosine], 0)], 0)
    turn = inverse.reshape(2, 2, length, parts, rows).transpose(0, 3, 1, 4, 2).reshape(2, 2 * length, length)
    pick = np.zeros((2, parts, 2, rows, length), np.float32)
    for part in range(2):
        for block in range(parts):
            pick[part, block, part, :, block * rows : (block + 1) * rows] = np.eye(rows)
    pick = jnp.asarray(pick.reshape(2, 2 * length, length).astype(BF16))
    turn_high, turn_low = np_high_low(turn)
    edge = ((0, wide - length), (0, wide - length))
    cosine = jnp.asarray(np.pad(cosine, edge), F32)
    sine = jnp.asarray(np.pad(sine, edge), F32)
    slots = 2 * micro
    lanes = padded(3 * micro * rows)
    shapes = [
        ((micro, 2, rows, wide), F32),
        ((micro, coils, 2 * rows, wide), BF16),
        ((micro, 3, rows, wide), F32),
        ((micro, 2 * wide, 2 * wide), BF16),
        ((3, 3 * channels, 3 * channels), BF16),
        ((3 * channels, 16), BF16),
        ((4, micro, rows + 2 * BACK_REACH, channels, wide), F32),
        ((4, micro, 4, channels, TILE), F32),
        ((4, micro, 8, channels), F32),
        ((micro, 16, (rows + 2 * FIRST_REACH + 2) * wide), BF16),
        ((micro, 2, rows, wide), F32),
    ]
    layers = (4, micro)
    return pl.pallas_call(
        functools.partial(forward_kernel, (micro, coils, rows, length, parts, images)),
        out_shape=[jax.ShapeDtypeStruct(*shape) for shape in shapes],
        in_specs=[anywhere()] * 2 + [in_vmem()] * 16,
        out_specs=[in_vmem()] * 6 + [anywhere()] + [in_vmem()] * 4,
        scratch_shapes=[
            pltpu.VMEM((2, 2, coils, rows, length), F32),
            pltpu.VMEM((slots, parts, 2 * rows, coils * rows), BF16),
            pltpu.VMEM((slots, parts, 2 * rows, coils * rows), BF16),
            pltpu.VMEM((parts, rows, lanes), F32),
            pltpu.VMEM((parts, rows, lanes), F32),
            pltpu.VMEM((2, micro, 2 * REACH, wide), F32),
            pltpu.VMEM((2, micro, 2 * REACH, wide), F32),
            pltpu.VMEM((3 * channels, 16), BF16),
            pltpu.VMEM((3, 3 * channels, 3 * channels), BF16),
            pltpu.VMEM((24, 3 * channels), BF16),
            pltpu.VMEM((1, TILE), F32),
            pltpu.SemaphoreType.DMA((slots, 2)),
            pltpu.SemaphoreType.DMA((slots, parts - 1)),
            pltpu.SemaphoreType.DMA((slots, parts - 1)),
            pltpu.SemaphoreType.DMA((slots,)),
            pltpu.SemaphoreType.DMA((parts - 1,)),
            pltpu.SemaphoreType.DMA((parts - 1,)),
            pltpu.SemaphoreType.DMA((micro, 2)),
            pltpu.SemaphoreType.DMA((micro, 2)),
            pltpu.VMEM((micro, 2, rows + 2 * FIRST_REACH, channels, wide), F32),
            pltpu.VMEM((3 * channels, 2 * wide), BF16),
            pltpu.VMEM((3 * channels, 2 * wide), BF16),
            pltpu.VMEM((channels, TILE), F32),
            pltpu.VMEM((channels, TILE), F32),
            pltpu.VMEM((channels, TILE), F32),
        ]
        + Sums.scratch(layers, parts, images)
        + [pltpu.SemaphoreType.DMA(layers)],
        compiler_params=params(collective_id=1, has_side_effects=True),
        name="forward",
    )(
        kspace, maps, target, foreground, row_mask, anatomy, first, middle, last, turn_high, turn_low, pick, cosine, sine,
        fourier_high, fourier_low, gains, shifts,
    )


def backward_kernel(
    sizes, grad, halo_image, layers, coefs, rows_in, images_in, middle_back, last_back,
    first_sums, middle_sums, last_sums, rows_out,
    upper, lin, stack, thin, inputs, slope, total, along, mix, *refs,
):
    micro, parts, images, length = sizes
    _, _, width, wide = grad.shape
    channels = lin.shape[3]
    pixels = width * length * parts * images
    sums = Sums(parts, images, refs[:6])
    (loaded,) = refs[6:]
    knock(sums.rows + sums.cols)
    ends = Ends(parts)
    clear = lane_mask(length, wide)

    def load(layer, batch):
        return pltpu.make_async_copy(layers.at[layer, batch], lin.at[batch, lax.rem(layer, 2)], loaded.at[layer, batch])

    for layer in (3, 2):
        for batch in range(micro):
            load(layer, batch).start()
    first_sums[...] = jnp.zeros_like(first_sums)
    middle_sums[...] = jnp.zeros_like(middle_sums)
    last_sums[...] = jnp.zeros_like(last_sums)

    def band(layer, batch):
        return upper.at[batch, lax.rem(layer, 2)]

    def begin(layer, batch):
        added = jnp.concatenate([total[...], along[...]], axis=0).T
        added = jnp.sum(added, axis=0, keepdims=True)
        sums.start((layer, batch), 0, padded_rows([added]))

    def middle(layer, batch):
        sums.start((layer, batch), 1, functools.reduce(jnp.add, sums.collect((layer, batch), 0)))

    def end(layer, batch):
        added = functools.reduce(jnp.add, sums.collect((layer, batch), 1))
        shift_sum, gain_sum = added[0:1, :channels], added[0:1, channels:]
        rows = rows_in[layer, batch]
        gain, inverse, offset = rows[0:1], rows[2:3], rows[3:4]
        scale = inverse * gain
        mix[batch, 0] = spread_row(scale)
        mix[batch, 1] = spread_row(-scale * inverse * gain_sum / pixels)
        mix[batch, 2] = spread_row(-scale * (shift_sum + offset * gain_sum) / pixels)
        rows_out[layer, batch] = join_rows([shift_sum, gain_sum], 8)

    def place_of(index):
        return 3 - lax.div(index, 2), lax.rem(index, 2)

    def grad_putter(layer, batch):
        grads, linear = band(layer, batch), lin.at[batch, lax.rem(layer, 2)]
        on_grad, on_layer, base = (repeat_lanes(mix[batch, index], wide) for index in range(3))

        def put(column):
            at = column + BACK_REACH
            upstream = clear(on_grad * grads[at] + on_layer * linear[at] + base)
            put_shifted(stack, ends.clear(upstream, column, width).astype(BF16), at * wide)

        return put

    def add_weights(weight_out, source, reach, around, around_reach, first):
        at = first + around_reach - 1
        columns = [around[:, (at + tap) * wide : (at + tap + GROUP) * wide] for tap in range(3)]
        at = first + reach
        weight_out[...] += dot_nt(source[:, at * wide : (at + GROUP) * wide], jnp.concatenate(columns, axis=0))

    def layer_back(layer, batch, source, reach, table, weight_out, put_grad, hook):
        below = lin.at[batch, lax.rem(layer, 2)]
        out = band(layer, batch)
        scale, offset = repeat_lanes(coefs[layer, batch, 0], wide), repeat_lanes(coefs[layer, batch, 1], wide)
        inverse, centre = repeat_lanes(coefs[layer, batch, 2], wide), repeat_lanes(coefs[layer, batch, 3], wide)

        def fill(couple):
            for place in range(2):
                column = 2 * couple + place - reach - 1
                if put_grad is not None:
                    put_grad(column)
                if not -reach <= column < width + reach:
                    continue
                at = column + BACK_REACH
                half, curve = silu_half(below[at], scale, offset)
                slope[at] = 0.5 * (1.0 + curve) * (1.0 + half * (1.0 - curve))
                if -1 <= column <= width:
                    active = ends.clear(clear(half * curve + half), column, width)
                    inputs[:, (column + 1) * wide : (column + 2) * wide] = active.astype(BF16)

        held = []

        def emit(column, value):
            column = column - reach
            at = column + BACK_REACH
            shaped = clear(value * slope[at])
            out[at] = shaped
            if not 0 <= column < width:
                return
            if column % BLOCK == 0:
                held[:] = [jnp.zeros((channels, TILE), F32), jnp.zeros((channels, TILE), F32)]
            held[0] = held[0] + fold(shaped)
            held[1] = held[1] + fold(shaped * (below[at] * inverse + centre))
            if column == BLOCK - 1:
                total[...], along[...] = held
            elif column % BLOCK == BLOCK - 1:
                total[...] += held[0]
                along[...] += held[1]
            if column % GROUP == GROUP - 1:
                add_weights(weight_out, source, reach + 1, inputs, 1, column + 1 - GROUP)

        ring_pass(
            table,
            lambda couple: source[:, 2 * couple * wide : 2 * (couple + 1) * wide],
            fill,
            emit,
            channels,
            width + 2 * reach,
            wide,
            hook,
        )

    def outer_step(batch, carried):
        put_image(grad.at[batch], halo_image, batch, thin, ends, BACK_REACH + 1)
        pl.when(batch == 0)(lambda: admit(sums.rows + sums.cols))
        load(3, batch).wait()
        hook = lambda: pl.when(batch > 0)(lambda: middle(3, 0))
        layer_back(3, batch, thin, BACK_REACH, last_back[...], last_sums, None, hook)
        begin(3, batch)
        pl.when(batch > 0)(lambda: end(3, 0))
        return carried

    lax.fori_loop(0, 2, outer_step, 0)

    def layer_step(index, carried):
        layer, batch = place_of(index)
        before = place_of(index - 1)
        load(layer, batch).wait()
        layer_back(
            layer,
            batch,
            stack,
            BACK_REACH - 1,
            middle_back[layer],
            middle_sums.at[layer],
            grad_putter(layer + 1, batch),
            lambda: middle(*before),
        )
        pl.when(layer > 0)(lambda: load(layer - 1, batch).start())
        begin(layer, batch)
        end(*before)
        return carried

    lax.fori_loop(2, 8, layer_step, 0)

    def first_step(batch, carried):
        put_grad = grad_putter(0, batch)
        for column in range(width):
            if column == width // 2:
                pl.when(batch == 0)(lambda: middle(0, 1))
            put_grad(column)
            if column % GROUP == GROUP - 1:
                add_weights(first_sums, stack, BACK_REACH, images_in.at[batch], FIRST_REACH + 1, column + 1 - GROUP)
        pl.when(batch == 0)(lambda: end(0, 1))
        return carried

    lax.fori_loop(0, 2, first_step, 0)
    for layer in range(4):
        for batch in range(2):
            sums.settle((layer, batch))


def backward(grad, halo, kept, tables, parts, images, length):
    layers, coefs, rows_in, images_in = kept
    micro, _, width, wide = grad.shape
    channels = layers.shape[3]
    band = (micro, 2, width + 2 * BACK_REACH, channels, wide)
    lanes = (width + 2 * BACK_REACH) * wide
    shapes = [(3 * channels, 48), (3, 3 * channels, 3 * channels), (16, 3 * channels), (4, micro, 8, channels)]
    slots = (4, micro)
    return pl.pallas_call(
        functools.partial(backward_kernel, (micro, parts, images, length)),
        out_shape=[jax.ShapeDtypeStruct(shape, F32) for shape in shapes],
        in_specs=[in_vmem(), in_vmem(), anywhere()] + [in_vmem()] * 5,
        out_specs=[in_vmem()] * 4,
        scratch_shapes=[
            pltpu.VMEM(band, F32),
            pltpu.VMEM(band, F32),
            pltpu.VMEM((3 * channels, lanes), BF16),
            pltpu.VMEM((16, lanes + 2 * wide), BF16),
            pltpu.VMEM((channels, (width + 2) * wide), BF16),
            pltpu.VMEM(band[2:], F32),
            pltpu.VMEM((channels, TILE), F32),
            pltpu.VMEM((channels, TILE), F32),
            pltpu.VMEM((micro, 3, channels, TILE), F32),
        ]
        + Sums.scratch(slots, parts, images)
        + [pltpu.SemaphoreType.DMA(slots)],
        compiler_params=params(collective_id=3, has_side_effects=True),
        name="backward",
    )(grad, halo, layers, coefs, rows_in, images_in, *tables)


def reduce_kernel(parts, images, first_sums, middle_sums, last_sums, scalars, first_grad, middle_grad, last_grad, totals, whole, final, quarter, landed, eighth, landed_rows, send, receive):
    image, me = lax.axis_index("img"), lax.axis_index("row")
    rows, cols = row_peers(parts), image_peers(images)
    knock(rows + cols)
    channels = middle_sums.shape[1] // 3
    taps = [(kr, kw) for kr in range(3) for kw in range(3)]
    pieces = [
        middle_sums[layer, (2 - kr) * channels : (3 - kr) * channels, kw * channels : (kw + 1) * channels]
        for layer in range(3)
        for kr, kw in taps
    ]
    firsts = [first_sums[(2 - kr) * channels : (3 - kr) * channels, 16 * kw + 2 : 16 * kw + 4] for kr, kw in taps]
    pieces.append(join_lanes(firsts, channels))
    for index in range(0, len(pieces), 2):
        at = index // 2 * channels
        whole[at : at + channels] = jnp.concatenate(pieces[index : index + 2], axis=1)
    at = len(pieces) // 2 * channels
    lasts = [last_sums[2 * (2 - kr) : 2 * (3 - kr), kw * channels : (kw + 1) * channels] for kr, kw in taps]
    added = functools.reduce(jnp.add, [scalars[batch] for batch in range(scalars.shape[0])])
    whole[at : at + 24] = jnp.concatenate([join_rows(lasts, 24), join_rows([added[:, :channels]], 24)], axis=1)
    whole[at + 24 :] = jnp.zeros((whole.shape[0] - at - 24, TILE), F32)
    admit(rows + cols)
    big, small = quarter.shape[0], eighth.shape[0]
    images_here, parts_here = len(cols), len(rows)

    def place(index, size):
        return pl.ds(pl.multiple_of(index * size, 8), size)

    sent = []
    for index, peer in enumerate(cols):
        copy = remote(whole.at[place(peer[0], big)], landed.at[index], send.at[index], receive.at[index], peer)
        copy.start()
        sent.append(copy)
    for copy in sent:
        copy.wait_recv()
    total = whole[place(image, big)]
    for index in range(images_here):
        total = total + landed[index]
    quarter[...] = total
    base = images_here
    arrived = []
    for index, peer in enumerate(rows):
        copy = remote(
            quarter.at[place(peer[1], small)], landed_rows.at[index], send.at[base + index], receive.at[base + index], peer
        )
        copy.start()
        arrived.append(copy)
    for copy in arrived:
        copy.wait_recv()
    total = quarter[place(me, small)]
    for index in range(parts_here):
        total = total + landed_rows[index]
    eighth[...] = total
    for copy in sent + arrived:
        copy.wait_send()
    base += parts_here
    returned = []
    mine = pl.ds(pl.multiple_of(image * big + me * small, 8), small)
    for index, peer in enumerate(rows):
        copy = remote(eighth, final.at[mine], send.at[base + index], receive.at[base + index], peer)
        copy.start()
        returned.append(copy)
    final[mine] = total
    for copy in returned:
        copy.wait()
    base += parts_here
    returned = []
    for index, peer in enumerate(cols):
        copy = remote(final.at[place(image, big)], final.at[place(image, big)], send.at[base + index], receive.at[base + index], peer)
        copy.start()
        returned.append(copy)
    for copy in returned:
        copy.wait()
    for index in range(27):
        from_row = index // 2 * channels
        from_lane = index % 2 * channels
        middle_grad[index // 9, index % 9] = final[from_row : from_row + channels, from_lane : from_lane + channels]
    turned = final[13 * channels : 14 * channels, channels:].T
    for tap in range(9):
        first_grad[tap] = turned[2 * tap : 2 * tap + 2]
        last_grad[tap] = final[at + 2 * tap : at + 2 * tap + 2, :channels]
    totals[...] = final[at : at + 8, channels:]


def reduce_all(first_sums, middle_sums, last_sums, scalars, parts, images):
    channels = middle_sums.shape[1] // 3
    unit = 8 * parts * images
    height = -(-(14 * channels + 24) // unit) * unit
    copies = 2 * (parts + images - 2)
    shapes = [(9, 2, channels), (3, 9, channels, channels), (9, 2, channels), (8, channels)]
    return pl.pallas_call(
        functools.partial(reduce_kernel, parts, images),
        out_shape=[jax.ShapeDtypeStruct(shape, F32) for shape in shapes],
        in_specs=[in_vmem()] * 4,
        out_specs=[in_vmem()] * 4,
        scratch_shapes=[
            pltpu.VMEM((height, TILE), F32),
            pltpu.VMEM((height, TILE), F32),
            pltpu.VMEM((height // images, TILE), F32),
            pltpu.VMEM((images - 1, height // images, TILE), F32),
            pltpu.VMEM((height // images // parts, TILE), F32),
            pltpu.VMEM((parts - 1, height // images // parts, TILE), F32),
            pltpu.SemaphoreType.DMA((copies,)),
            pltpu.SemaphoreType.DMA((copies,)),
        ],
        compiler_params=params(collective_id=4, has_side_effects=True),
        name="reduce_all",
    )(first_sums, middle_sums, last_sums, scalars)


def apply_normal(image, maps, normal, diagonal):
    coils, slabs, wide = maps.shape
    rows = slabs // 2
    real, imag = image
    stack, power = [], jnp.zeros((rows, wide), F32)
    for coil in range(coils):
        sense = maps[coil].astype(F32)
        sense_re, sense_im = sense[:rows], sense[rows:]
        power = power + sense_re * sense_re + sense_im * sense_im
        field = [sense_re * real - sense_im * imag, sense_re * imag + sense_im * real]
        stack.append(jnp.concatenate(field, axis=1))
    stack = jnp.concatenate(stack, axis=0).astype(BF16)
    power = diagonal * power
    out_re, out_im = power * real, power * imag
    turned = dot(stack, normal[...])
    for coil in range(coils):
        sense = maps[coil].astype(F32)
        sense_re, sense_im = sense[:rows], sense[rows:]
        field = turned[coil * rows : (coil + 1) * rows]
        field_re, field_im = field[:, :wide], field[:, wide:]
        out_re = out_re + sense_re * field_re + sense_im * field_im
        out_im = out_im + sense_re * field_im - sense_im * field_re
    return out_re, out_im


def pair(ref):
    return ref[0], ref[1]


def put_pair(ref, values):
    ref[0] = values[0]
    ref[1] = values[1]


def blend(*terms):
    return tuple(functools.reduce(jnp.add, [factor * image[part] for factor, image in terms]) for part in range(2))


def inner_of(left, right):
    product = left[0] * right[0] + left[1] * right[1]
    return jnp.sum(jnp.sum(product, axis=1, keepdims=True), axis=0, keepdims=True)


class RowSums:
    def __init__(self, parts, refs):
        self.message, self.held, self.send, self.receive = refs
        self.peers = row_peers(parts)

    def copies(self, slot):
        return [
            remote(
                self.message.at[slot],
                self.held.at[slot + (index,)],
                self.send.at[slot + (index,)],
                self.receive.at[slot + (index,)],
                peer,
            )
            for index, peer in enumerate(self.peers)
        ]

    def start(self, slot, values):
        filler = [jnp.zeros((1, TILE), F32)] * (8 - len(values))
        self.message[slot] = jnp.concatenate([jnp.broadcast_to(value, (1, TILE)) for value in values] + filler, axis=0)
        for copy in self.copies(slot):
            copy.start()

    def finish(self, slot):
        total = self.message[slot]
        for index, copy in enumerate(self.copies(slot)):
            copy.wait_recv()
            total = total + self.held[slot + (index,)]
        return [total[index : index + 1, 0:1] for index in range(8)]

    def settle(self, slot):
        for copy in self.copies(slot):
            copy.wait_send()


def solve_kernel(
    sizes, filled, result, maps, normal, planes, rows_in, row_mask, extra, grad_out, halo, scalars,
    work, edges, send_edge, receive_edge, *refs,
):
    micro, parts, length = sizes
    _, _, rows, wide = filled.shape
    sums = RowSums(parts, refs)
    knock(sums.peers)
    moved = []
    inside = lax.broadcasted_iota(jnp.int32, (rows, wide), 1) < length
    penalty = jnp.exp(jnp.full((1, 1), extra[2], F32))
    inv_count = 1.0 / rows_in[0, 0, 4:5, 0:1]
    diagonals = [jnp.sum(row_mask[batch].astype(F32), axis=1, keepdims=True) / length for batch in range(micro)]
    names = ("denoised", "right", "mapped", "residue", "through", "search", "searched", "slope")

    def at(name, batch):
        return work.at[batch, names.index(name)]

    def get(name, batch):
        return pair(at(name, batch))

    def through_normal(image, batch):
        out = apply_normal(image, maps.at[batch], normal.at[batch], diagonals[batch])
        return blend((1.0, out), (penalty, image))

    for batch in range(micro):
        images = []
        for part in range(2):
            value = filled[batch, part] + result[batch, part] + jnp.full((1, 1), extra[part], F32)
            value = jnp.where(inside, value, 0.0)
            at("denoised", batch)[part] = value
            images.append(filled[batch, part] + penalty * value)
        put_pair(at("right", batch), images)
        mapped = through_normal(images, batch)
        put_pair(at("mapped", batch), mapped)
        if batch == 0:
            admit(sums.peers)
        sums.start((0, batch), [inner_of(images, images), inner_of(images, mapped)])
    ones, twos = [], []
    for batch in range(micro):
        ones.append(sums.finish((0, batch)))
        start, image = get("right", batch), get("mapped", batch)
        left_over = blend((1.0, start), (-ones[batch][0] / ones[batch][1], image))
        put_pair(at("residue", batch), left_over)
        mapped = through_normal(left_over, batch)
        put_pair(at("through", batch), mapped)
        sums.start(
            (1, batch),
            [
                inner_of(left_over, left_over),
                inner_of(left_over, mapped),
                inner_of(left_over, image),
                inner_of(start, mapped),
            ],
        )
    kept = []
    for batch in range(micro):
        twos.append(sums.finish((1, batch)))
        norm_0, curve_0 = ones[batch][:2]
        norm_1 = twos[batch][0]
        factor = norm_1 / norm_0
        curve_1 = twos[batch][1] + factor * (twos[batch][2] + twos[batch][3]) + factor * factor * curve_0
        start, image = get("right", batch), get("mapped", batch)
        direction = blend((1.0, get("residue", batch)), (factor, start))
        image_1 = blend((1.0, get("through", batch)), (factor, image))
        put_pair(at("searched", batch), image_1)
        state = blend((norm_0 / curve_0, start), (norm_1 / curve_1, direction))
        weight = planes[batch, 2]
        difference = [state[part] - planes[batch, part] for part in range(2)]
        grad = [inv_count * 2.0 * weight * difference[part] for part in range(2)]
        put_pair(at("slope", batch), grad)
        masked = [weight * difference[part] for part in range(2)]
        sums.start(
            (2, batch),
            [
                inner_of(grad, direction),
                inner_of(grad, start),
                inner_of(grad, image),
                inner_of(image_1, start),
                inner_of(image_1, image),
            ],
        )
        kept.append((norm_0, curve_0, norm_1, curve_1, factor, inner_of(direction, direction), inner_of(masked, difference)))
    for batch in range(micro):
        grad_search, grad_start, grad_image, cross_start, cross_image = sums.finish((2, batch))[:5]
        norm_0, curve_0, norm_1, curve_1, factor, own_search, own_loss = kept[batch]
        step_0, step_1 = norm_0 / curve_0, norm_1 / curve_1
        start, image, left_over = get("right", batch), get("mapped", batch), get("residue", batch)
        image_1, grad = get("searched", batch), get("slope", batch)
        residue_image = twos[batch][2]
        curve_grad_1 = -grad_search * norm_1 / (curve_1 * curve_1)
        norm_grad_1 = grad_search / curve_1
        search_grad = blend((step_1, grad), (2.0 * curve_grad_1, image_1))
        factor_grad = step_1 * grad_start + 2.0 * curve_grad_1 * cross_start
        joint = step_1 * grad_image + 2.0 * curve_grad_1 * cross_image
        norm_total = norm_grad_1 + factor_grad / norm_0
        residue_full = blend((1.0, search_grad), (2.0 * norm_total, left_over))
        step_grad = grad_start - (joint + 2.0 * norm_total * residue_image)
        curve_grad_0 = -step_grad * norm_0 / (curve_0 * curve_0)
        mapped_grad = blend((-step_0, residue_full), (curve_grad_0, start))
        through = through_normal(mapped_grad, batch)
        norm_grad_0 = -factor_grad * norm_1 / (norm_0 * norm_0) + step_grad / curve_0
        right_grad = blend(
            (1.0, residue_full),
            (factor, search_grad),
            (step_0, grad),
            (curve_grad_0, image),
            (1.0, through),
            (2.0 * norm_grad_0, start),
        )
        penalty_part = (
            curve_grad_1 * own_search + inner_of(mapped_grad, start) + inner_of(right_grad, get("denoised", batch))
        )
        grad_pair = [penalty * right_grad[part] for part in range(2)]
        put_pair(grad_out.at[batch], grad_pair)
        put_edges(edges.at[:, batch], *grad_pair)
        for copy in image_halo(parts, batch, edges, halo, send_edge, receive_edge):
            copy.start()
            moved.append(copy)
        offsets = [jnp.sum(jnp.sum(grad_pair[part], axis=1, keepdims=True), axis=0, keepdims=True) for part in range(2)]
        values = [offsets[0], offsets[1], penalty * penalty_part, own_loss]
        scalars[batch] = join_rows([jnp.broadcast_to(value, (1, TILE)) for value in values], 8)
    for stage in range(3):
        for batch in range(micro):
            sums.settle((stage, batch))
    for copy in moved:
        copy.wait()


def solve_all(filled, result, maps, normal, planes, rows_in, row_mask, extra, parts, length):
    micro, _, rows, wide = filled.shape
    shapes = [(micro, 2, rows, wide), (2, micro, 2 * REACH, wide), (micro, 8, TILE)]
    slots = (3, micro)
    return pl.pallas_call(
        functools.partial(solve_kernel, (micro, parts, length)),
        out_shape=[jax.ShapeDtypeStruct(shape, F32) for shape in shapes],
        in_specs=[in_vmem()] * 7 + [pl.BlockSpec(memory_space=pltpu.SMEM)],
        out_specs=[in_vmem()] * 3,
        scratch_shapes=[
            pltpu.VMEM((micro, 8, 2, rows, wide), F32),
            pltpu.VMEM((2, micro, 2 * REACH, wide), F32),
            pltpu.SemaphoreType.DMA((micro, 2)),
            pltpu.SemaphoreType.DMA((micro, 2)),
            pltpu.VMEM(slots + (8, TILE), F32),
            pltpu.VMEM(slots + (parts - 1, 8, TILE), F32),
            pltpu.SemaphoreType.DMA(slots + (parts - 1,)),
            pltpu.SemaphoreType.DMA(slots + (parts - 1,)),
        ],
        compiler_params=params(collective_id=5, has_side_effects=True),
        name="solve_all",
    )(filled, result, maps, normal, planes, rows_in, row_mask, extra)


def update_kernel(weights, means, squares, grads, rows_back, totals, rows_in, outs):
    first_grad, middle_grad, last_grad = grads
    affine = []
    for row in (1, 0):
        rows = [functools.reduce(jnp.add, [rows_back[layer, batch, row : row + 1] for batch in range(rows_back.shape[1])]) for layer in range(4)]
        affine.append(jnp.concatenate(rows, axis=0))
    extra = join_lanes([totals[index : index + 1, 0:1] for index in range(3)], 3)

    def put(group, at, gradient, refs):
        results = adamw(weights[group][at], gradient, means[group][at], squares[group][at], LEARN_RATES[group])
        for ref, value in zip(refs, results + (results[0].astype(BF16),)):
            ref[at] = value

    everything = (slice(None), slice(None))
    for tap in range(9):
        put(0, tap, first_grad[tap], outs[0:4])
        put(2, tap, last_grad[tap], outs[8:12])
        for layer in range(3):
            put(1, (layer, tap), middle_grad[layer, tap], outs[4:8])
    put(3, everything, affine[0], outs[12:15])
    put(4, everything, affine[1], outs[15:18])
    put(5, everything, extra, outs[18:21])
    outs[21][...] = totals[3:4, 0:1]
    outs[22][...] = rows_in[0, 0, 4:5, 0:1].astype(jnp.int32)


def update(weights, means, squares, grads, rows_back, totals, rows_in):
    shapes = []
    for group, weight in enumerate(weights):
        shapes += [jax.ShapeDtypeStruct(weight.shape, F32)] * 3
        if group < 3:
            shapes.append(jax.ShapeDtypeStruct(weight.shape, BF16))
    shapes += [jax.ShapeDtypeStruct((1, 1), F32), jax.ShapeDtypeStruct((1, 1), jnp.int32)]

    def kernel(*refs):
        update_kernel(refs[0:6], refs[6:12], refs[12:18], refs[18:21], refs[21], refs[22], refs[23], refs[24:])

    return pl.pallas_call(
        kernel,
        out_shape=shapes,
        in_specs=[in_vmem()] * 24,
        out_specs=[in_vmem()] * len(shapes),
        compiler_params=params(),
        name="update",
    )(*weights, *means, *squares, *grads, rows_back, totals, rows_in)


def fast_step(arrays, moments):
    (
        kspace, coil_maps, target, row_mask, foreground, anatomy, first_weight, middle_weight, last_weight, norm_gains, norm_shifts, extra_params,
    ) = arrays
    length = kspace.shape[-1]
    parts, images = lax.axis_size("row"), lax.axis_size("img")
    filled, maps, planes, normal, middle_back, last_back, layers, coefs, rows_out, images_out, result = forward(
        kspace[:, 0], coil_maps[:, 0], target[:, 0], foreground[:, 0], row_mask, anatomy.transpose(1, 0),
        first_weight.transpose(0, 2, 1), middle_weight, last_weight, norm_gains, norm_shifts, parts, images,
    )
    grad, halo, scalars = solve_all(
        filled, result, maps, normal, planes, rows_out, row_mask, extra_params, parts, length
    )
    first_sums, middle_sums, last_sums, rows_back = backward(
        grad, halo, (layers, coefs, rows_out, images_out), (middle_back, last_back), parts, images, length
    )
    *grads, totals = reduce_all(first_sums, middle_sums, last_sums, scalars, parts, images)

    def turn(group):
        first, middle, last, gains, shifts, extra = group
        return [first.transpose(0, 2, 1), middle, last, gains, shifts, extra.reshape(1, 3)]

    weights = (first_weight, middle_weight, last_weight, norm_gains, norm_shifts, extra_params)
    means, squares = zip(*moments)
    outs = list(update(turn(weights), turn(means), turn(squares), grads, rows_back, totals, rows_out))
    outs[0:4] = [value.transpose(0, 2, 1) for value in outs[0:4]]
    outs[18:21] = [value.reshape(3) for value in outs[18:21]]
    return tuple(outs[:21]) + (outs[21].reshape(()), outs[22].reshape(()))


def local(
    kspace,
    coil_maps,
    target,
    row_mask,
    foreground,
    anatomy,
    first_weight,
    middle_weight,
    last_weight,
    norm_gains,
    norm_shifts,
    extra_params,
    first_mean,
    first_square,
    middle_mean,
    middle_square,
    last_mean,
    last_square,
    gains_mean,
    gains_square,
    shifts_mean,
    shifts_square,
    extra_mean,
    extra_square,
):
    arrays = (
        kspace, coil_maps, target, row_mask, foreground, anatomy, first_weight, middle_weight, last_weight, norm_gains, norm_shifts, extra_params,
    )
    moments = (
        (first_mean, first_square),
        (middle_mean, middle_square),
        (last_mean, last_square),
        (gains_mean, gains_square),
        (shifts_mean, shifts_square),
        (extra_mean, extra_square),
    )
    if fits(kspace, first_weight, lax.axis_size("row")):
        return fast_step(arrays, moments)
    totals, pixel_total = general_local(arrays)
    params = (first_weight, middle_weight, last_weight, norm_gains, norm_shifts, extra_params)
    results = []
    for group in range(6):
        updated, first_new, second_new = adamw(
            params[group], totals[group], moments[group][0], moments[group][1], LEARN_RATES[group]
        )
        results.extend([updated, first_new, second_new])
        if group < 3:
            results.append(updated.astype(jnp.bfloat16))
    return tuple(results) + (totals[6], pixel_total.astype(jnp.int32))


def solution(mesh):
    in_specs = (
        P(None, "img", None, None, "row", None),
        P(None, "img", None, None, "row", None),
        P(None, "img", None, "row", None),
        P(None, "img", None),
        P(None, "img", "row", None),
        P(None, "img"),
        P(),
        P(),
        P(),
        P(),
        P(),
        P(),
        P(),
        P(),
        P(),
        P(),
        P(),
        P(),
        P(),
        P(),
        P(),
        P(),
        P(),
        P(),
    )
    out_specs = (
        P(),
        P(),
        P(),
        P(),
        P(),
        P(),
        P(),
        P(),
        P(),
        P(),
        P(),
        P(),
        P(),
        P(),
        P(),
        P(),
        P(),
        P(),
        P(),
        P(),
        P(),
        P(),
        P(),
    )
    return jax.shard_map(local, mesh=mesh, in_specs=in_specs, out_specs=out_specs, check_vma=False)
```

```python
import functools

import jax
import jax.numpy as jnp
import numpy as np
from jax import lax
from jax.experimental import pallas as pl
from jax.experimental.pallas import tpu as pltpu
from jax.sharding import PartitionSpec as P

COILS = 16
BRAIN_COILS = 12
UNROLLS = 1
CG_STEPS = 2
STEP = 10


PRECISE = lax.Precision.HIGHEST
EPS_NORM = 1e-05
BETA_ONE = 0.9
BETA_TWO = 0.999
ADAM_EPS = 1e-08
DECAY_RATE = 0.01
LEARN_RATES = (0.3, 0.05, 0.05, 0.4, 0.4, 0.4)


def with_halo(cells, sides, width):
    for axis, dim in sides:
        count = lax.axis_size(axis)
        ends = count - 1
        head = lax.slice_in_dim(cells, 0, width, axis=dim)
        tail = lax.slice_in_dim(cells, cells.shape[dim] - width, cells.shape[dim], axis=dim)
        cells = jnp.concatenate(
            [
                lax.ppermute(tail, axis, [(i, (i + 1) % count) for i in range(ends)]),
                cells,
                lax.ppermute(head, axis, [((i + 1) % count, i) for i in range(ends)]),
            ],
            axis=dim,
        )
    return cells


def dft_table(length, direction):
    index = jnp.arange(length, dtype=jnp.int32)
    phase = (index[:, None] * index[None, :] % length).astype(jnp.float32) * (2.0 * jnp.pi / length)
    factor = 1.0 / jnp.sqrt(jnp.float32(length))
    cosine = jnp.cos(phase) * factor
    sine = jnp.sin(phase) * factor * direction
    return jnp.stack([jnp.stack([cosine, -sine], 1), jnp.stack([sine, cosine], 1)], 0)


def along_width(field, table):
    return jnp.einsum("bcprw,pwqk->bcqrk", field, table, precision=PRECISE)


def along_height(field, table):
    return jnp.einsum("bcprw,prqk->bcqkw", field, table, precision=PRECISE)


def expand(image, maps):
    real_part, imag_part = (image[:, None, 0], image[:, None, 1])
    maps_re, maps_im = (maps[:, :, 0], maps[:, :, 1])
    return jnp.stack(
        [maps_re * real_part - maps_im * imag_part, maps_re * imag_part + maps_im * real_part], 2
    )


def combine(field, maps):
    field_re, field_im = (field[:, :, 0], field[:, :, 1])
    maps_re, maps_im = (maps[:, :, 0], maps[:, :, 1])
    return jnp.stack(
        [
            jnp.sum(maps_re * field_re + maps_im * field_im, 1),
            jnp.sum(maps_re * field_im - maps_im * field_re, 1),
        ],
        1,
    )


def to_columns(field):
    return lax.all_to_all(
        field.astype(jnp.bfloat16), "row", split_axis=4, concat_axis=3, tiled=True
    ).astype(field.dtype)


def to_rows(field):
    return lax.all_to_all(
        field.astype(jnp.bfloat16), "row", split_axis=3, concat_axis=4, tiled=True
    ).astype(field.dtype)


def make_normal(maps, mask_rows, forward, inverse, measured):
    zero_filled = combine(to_rows(along_height(measured * mask_rows, inverse)), maps)

    def normal(image):
        spectrum = to_columns(along_width(expand(image, maps), forward))
        spectrum = along_height(spectrum, forward) * mask_rows
        spectrum = to_rows(along_height(spectrum, inverse))
        return combine(along_width(spectrum, inverse), maps)

    return (normal, zero_filled)


def inner(left, right):
    return jnp.sum(left * right, axis=(1, 2, 3))


def per_image(values):
    return values[:, None, None, None]


def row_sums(values):
    return lax.psum(values, "row")


def solve(rhs, penalty, normal):
    state = jnp.zeros_like(rhs)
    residue = rhs
    search = rhs
    norm_now = row_sums(inner(residue, residue))
    kept = []
    for iterate in range(CG_STEPS):
        mapped = normal(search) + penalty * search
        curvature = row_sums(inner(search, mapped))
        stepsize = norm_now / curvature
        state = state + per_image(stepsize) * search
        residue = residue - per_image(stepsize) * mapped
        norm_next = row_sums(inner(residue, residue))
        kept.append((search, mapped, residue, norm_now, norm_next, curvature))
        search = residue + per_image(norm_next / norm_now) * search
        norm_now = norm_next
    return (state, kept)


def solve_backward(state_grad, kept, rhs, denoised, penalty, normal):
    search_grad = jnp.zeros_like(rhs)
    residue_grad = jnp.zeros_like(rhs)
    norm_grad = jnp.zeros(rhs.shape[0], jnp.float32)
    penalty_part = jnp.float32(0.0)
    for iterate in reversed(range(CG_STEPS)):
        search, mapped, residue, norm_now, norm_next, curvature = kept[iterate]
        factor_grad, along_search, joint_mapped, residue_mapped = lax.psum(
            (
                inner(search_grad, search),
                inner(state_grad, search),
                inner(residue_grad + search_grad, mapped),
                inner(residue, mapped),
            ),
            "row",
        )
        stepsize = norm_now / curvature
        factor = norm_next / norm_now
        norm_total = norm_grad + factor_grad / norm_now
        residue_full = residue_grad + search_grad + per_image(2.0 * norm_total) * residue
        stepsize_grad = along_search - (joint_mapped + 2.0 * norm_total * residue_mapped)
        curvature_grad = -stepsize_grad * norm_now / (curvature * curvature)
        mapped_grad = -per_image(stepsize) * residue_full + per_image(curvature_grad) * search
        penalty_part = penalty_part + jnp.sum(mapped_grad * search)
        search_grad = (
            per_image(factor) * search_grad
            + per_image(stepsize) * state_grad
            + per_image(curvature_grad) * mapped
            + normal(mapped_grad)
            + penalty * mapped_grad
        )
        residue_grad = residue_full
        norm_grad = -factor_grad * norm_next / (norm_now * norm_now) + stepsize_grad / curvature
    rhs_grad = residue_grad + search_grad + per_image(2.0 * norm_grad) * rhs
    penalty_part = penalty_part + jnp.sum(rhs_grad * denoised)
    return (penalty * rhs_grad, penalty_part)


def conv_forward(activation, weight):
    height, breadth = (activation.shape[2], activation.shape[3])
    padded = with_halo(activation, (("row", 2),), 1)
    padded = jnp.pad(padded, ((0, 0), (0, 0), (0, 0), (1, 1)))
    summed = jnp.zeros((activation.shape[0], weight.shape[1], height, breadth), jnp.float32)
    for tap_index in range(9):
        window = padded[
            :, :, tap_index // 3 : tap_index // 3 + height, tap_index % 3 : tap_index % 3 + breadth
        ]
        summed = summed + jnp.einsum(
            "oi,birw->borw", weight[tap_index], window, preferred_element_type=jnp.float32
        )
    return (summed, padded)


def conv_backward(upstream, padded, weight, need_input):
    height, breadth = (upstream.shape[2], upstream.shape[3])
    weight_grad = jnp.stack(
        [
            jnp.einsum(
                "borw,birw->oi",
                upstream,
                padded[
                    :,
                    :,
                    tap_index // 3 : tap_index // 3 + height,
                    tap_index % 3 : tap_index % 3 + breadth,
                ],
                preferred_element_type=jnp.float32,
            )
            for tap_index in range(9)
        ]
    )
    if not need_input:
        return (weight_grad, None)
    widened = with_halo(upstream, (("row", 2),), 1)
    widened = jnp.pad(widened, ((0, 0), (0, 0), (0, 0), (1, 1)))
    summed = jnp.zeros((upstream.shape[0], weight.shape[2], height, breadth), jnp.float32)
    for tap_index in range(9):
        start_r = 2 - tap_index // 3
        start_c = 2 - tap_index % 3
        window = widened[:, :, start_r : start_r + height, start_c : start_c + breadth]
        summed = summed + jnp.einsum(
            "oi,borw->birw", weight[tap_index], window, preferred_element_type=jnp.float32
        )
    return (weight_grad, summed)


def norm_sums(values):
    return lax.psum(values, ("img", "row"))


def channel(values):
    return values[None, :, None, None]


def cnn_forward(image, weights, gains, shifts, offset, pixels):
    activation = image.astype(jnp.bfloat16)
    kept = []
    for layer_index in range(4):
        linear, padded = conv_forward(activation, weights[layer_index])
        average = norm_sums(jnp.sum(linear, axis=(0, 2, 3))) / pixels
        centred = linear - channel(average)
        spread = norm_sums(jnp.sum(centred * centred, axis=(0, 2, 3))) / pixels
        inv_std = lax.rsqrt(spread + EPS_NORM)
        normed = centred * channel(inv_std)
        shaped = channel(gains[layer_index]) * normed + channel(shifts[layer_index])
        activation = jax.nn.silu(shaped).astype(jnp.bfloat16)
        kept.append((padded, normed, shaped, inv_std))
    result, padded = conv_forward(activation, weights[4])
    kept.append(padded)
    return (image + result + channel(offset), kept)


def cnn_backward(denoised_grad, kept, weights, gains, pixels, need_input):
    offset_grad = jnp.sum(denoised_grad, axis=(0, 2, 3))
    weight_grads = [None] * 5
    gain_grads = [None] * 4
    shift_grads = [None] * 4
    weight_grads[4], upstream = conv_backward(
        denoised_grad.astype(jnp.bfloat16), kept[4], weights[4], True
    )
    for layer_index in (3, 2, 1, 0):
        padded, normed, shaped, inv_std = kept[layer_index]
        sigmoid_val = jax.nn.sigmoid(shaped)
        shaped_grad = upstream * sigmoid_val * (1.0 + shaped * (1.0 - sigmoid_val))
        shift_local = jnp.sum(shaped_grad, axis=(0, 2, 3))
        gain_local = jnp.sum(shaped_grad * normed, axis=(0, 2, 3))
        shift_total, gain_total = lax.psum((shift_local, gain_local), ("img", "row"))
        gain_vec = gains[layer_index]
        linear_grad = channel(inv_std) * (
            shaped_grad * channel(gain_vec)
            - channel(gain_vec * shift_total / pixels)
            - normed * channel(gain_vec * gain_total / pixels)
        )
        shift_grads[layer_index] = shift_local
        gain_grads[layer_index] = gain_local
        weight_grads[layer_index], upstream = conv_backward(
            linear_grad.astype(jnp.bfloat16),
            padded,
            weights[layer_index],
            layer_index > 0 or need_input,
        )
    image_grad = None
    return (image_grad, weight_grads, jnp.stack(gain_grads), jnp.stack(shift_grads), offset_grad)


def adamw(weight, gradient, moment_one, moment_two, rate):
    first_new = BETA_ONE * moment_one + (1.0 - BETA_ONE) * gradient
    second_new = BETA_TWO * moment_two + (1.0 - BETA_TWO) * gradient * gradient
    corrected = first_new / (1.0 - BETA_ONE**STEP)
    divisor = jnp.sqrt(second_new / (1.0 - BETA_TWO**STEP)) + ADAM_EPS
    updated = weight - rate * (corrected / divisor + DECAY_RATE * weight)
    return (updated, first_new, second_new)


def general_local(arrays):
    (
        kspace, coil_maps, target, row_mask, foreground, anatomy, first_weight, middle_weight, last_weight, norm_gains, norm_shifts, extra_params,
    ) = arrays
    length = kspace.shape[-1]
    forward = dft_table(length, 1.0)
    inverse = dft_table(length, -1.0)
    pixel_total = lax.psum(jnp.sum(foreground).astype(jnp.float32), ("img", "row"))
    inv_count = 1.0 / pixel_total
    middle_low = middle_weight.astype(jnp.bfloat16)
    conv_weights = [
        first_weight.astype(jnp.bfloat16),
        middle_low[0],
        middle_low[1],
        middle_low[2],
        last_weight.astype(jnp.bfloat16),
    ]
    penalty = jnp.exp(extra_params[2])
    offset = extra_params[:2]
    images_here = kspace.shape[1]
    pixels = images_here * kspace.shape[4] * length * lax.axis_size("img") * lax.axis_size("row")
    first_grad = jnp.zeros_like(first_weight)
    middle_grad = jnp.zeros_like(middle_weight)
    last_grad = jnp.zeros_like(last_weight)
    gains_grad = jnp.zeros_like(norm_gains)
    shifts_grad = jnp.zeros_like(norm_shifts)
    offset_grad = jnp.zeros((2,), jnp.float32)
    penalty_grad = jnp.float32(0.0)
    loss_part = jnp.float32(0.0)
    for microbatch in range(kspace.shape[0]):
        limit = jnp.where(anatomy[microbatch] == 0, BRAIN_COILS, COILS)
        coil_on = (jnp.arange(kspace.shape[2])[None, :] < limit[:, None]).astype(jnp.float32)
        maps = coil_maps[microbatch] * coil_on[:, :, None, None, None]
        mask_rows = row_mask[microbatch].astype(jnp.float32)[:, None, None, :, None]
        measured = to_columns(along_width(kspace[microbatch], inverse))
        normal, zero_filled = make_normal(maps, mask_rows, forward, inverse, measured)
        state = zero_filled
        unroll = 0
        denoised, cnn_kept = cnn_forward(
            state, conv_weights, norm_gains, norm_shifts, offset, pixels
        )
        rhs = zero_filled + penalty * denoised
        state, cg_kept = solve(rhs, penalty, normal)
        saved = [(cnn_kept, cg_kept, rhs, denoised)]
        fg_mask = foreground[microbatch].astype(jnp.float32)[:, None]
        difference = state - target[microbatch]
        loss_part = loss_part + jnp.sum(fg_mask * difference * difference)
        state_grad = inv_count * 2.0 * fg_mask * difference
        for unroll in reversed(range(UNROLLS)):
            cnn_kept, cg_kept, rhs, denoised = saved[unroll]
            denoised_grad, penalty_part = solve_backward(
                state_grad, cg_kept, rhs, denoised, penalty, normal
            )
            penalty_grad = penalty_grad + penalty_part
            state_grad, weight_grads, gain_part, shift_part, offset_part = cnn_backward(
                denoised_grad, cnn_kept, conv_weights, norm_gains, pixels, unroll > 0
            )
            first_grad = first_grad + weight_grads[0]
            middle_grad = middle_grad + jnp.stack(weight_grads[1:4])
            last_grad = last_grad + weight_grads[4]
            gains_grad = gains_grad + gain_part
            shifts_grad = shifts_grad + shift_part
            offset_grad = offset_grad + offset_part
    extra_grad = jnp.concatenate([offset_grad, (penalty * penalty_grad)[None]])
    totals = lax.psum(
        (first_grad, middle_grad, last_grad, gains_grad, shifts_grad, extra_grad, loss_part),
        ("img", "row"),
    )
    return totals, pixel_total


BF16 = jnp.bfloat16
F32 = jnp.float32
MESH = pl.DeviceIdType.MESH
TILE = 128
BLOCK = 8
BACK_REACH = 3
FIRST_REACH = 6
GROUP = 4
FORWARD_HOOK = 4
BACK_HOOK = 5
REACH = 8
VMEM_BYTES = 58 * 1024 * 1024


def padded(length):
    return -(-length // TILE) * TILE


def fits(kspace, first_weight, mesh_rows):
    micro, images, coils, _, rows, length = kspace.shape
    channels = first_weight.shape[1]
    return (
        images == 1
        and micro == 2
        and 2 * channels == TILE
        and channels % 16 == 0
        and rows * mesh_rows == length
        and mesh_rows & (mesh_rows - 1) == 0
        and rows % BLOCK == 0
        and (2 * rows) % 16 == 0
        and (coils * rows) % TILE == 0
        and padded(length) > length
    )


def phases(length):
    index = np.arange(length)
    angle = 2.0 * np.pi * (np.outer(index, index) % length) / length
    return np.cos(angle) / np.sqrt(length), np.sin(angle) / np.sqrt(length)


def high_low(table):
    high = table.astype(BF16)
    low = (table - high.astype(F32)).astype(BF16)
    return high, low


def np_high_low(table):
    table = np.asarray(table, np.float32)
    high = table.astype(BF16)
    low = (table - high.astype(np.float32)).astype(BF16)
    return jnp.asarray(high), jnp.asarray(low)


def dot(left, right):
    return jnp.dot(left, right, preferred_element_type=F32)


def dot_nt(left, right):
    return lax.dot_general(left, right, (((1,), (1,)), ((), ())), preferred_element_type=F32)


def knock(peers):
    barrier = pltpu.get_barrier_semaphore()
    for peer in peers:
        pl.semaphore_signal(barrier, inc=1, device_id=peer, device_id_type=MESH)


def admit(peers):
    pl.semaphore_wait(pltpu.get_barrier_semaphore(), len(peers))


def partner(me, step):
    other, bit = 0, 1
    while bit <= step:
        own = lax.rem(lax.div(me, bit), 2)
        other = other + bit * (1 - own if step & bit else own)
        bit *= 2
    return other + lax.div(me, bit) * bit


def row_peers(rows):
    image, row = lax.axis_index("img"), lax.axis_index("row")
    steps = sorted(range(1, rows), key=lambda step: (-step.bit_length(), step))
    return [(image, partner(row, step)) for step in steps]


def image_peers(images):
    image, row = lax.axis_index("img"), lax.axis_index("row")
    return [(lax.rem(image + step, images), row) for step in range(1, images)]


def remote(source, target, send, receive, peer):
    return pltpu.make_async_remote_copy(
        src_ref=source,
        dst_ref=target,
        send_sem=send,
        recv_sem=receive,
        device_id=peer,
        device_id_type=MESH,
    )


def params(vmem=VMEM_BYTES, **kwargs):
    return pltpu.CompilerParams(vmem_limit_bytes=vmem, **kwargs)


def in_vmem():
    return pl.BlockSpec(memory_space=pltpu.VMEM)


def anywhere():
    return pl.BlockSpec(memory_space=pl.ANY)


def three_parts(values):
    high = values.astype(BF16)
    rest = values - high.astype(F32)
    middle = rest.astype(BF16)
    return high, middle, (rest - middle.astype(F32)).astype(BF16)


def join_lanes(pieces, wide):
    short = wide - sum(piece.shape[1] for piece in pieces)
    if short:
        pieces = pieces + [jnp.zeros((pieces[0].shape[0], short), pieces[0].dtype)]
    return jnp.concatenate(pieces, axis=1)


def join_rows(pieces, height):
    short = height - sum(piece.shape[0] for piece in pieces)
    if short:
        pieces = pieces + [jnp.zeros((short, pieces[0].shape[1]), pieces[0].dtype)]
    return jnp.concatenate(pieces, axis=0)


def start_exchange(
    sizes, meet, kspace, maps, target, foreground, row_mask, anatomy, first, middle, last, turn_high, turn_low, pick, cosine, sine,
    fourier_high, fourier_low,
    filled, maps_out, halo, planes, normal, first_table, middle_tables, last_table, middle_back, last_back, counted,
    fields, staged, spread, flat, landed, edges, loaded, send, receive, own, send_flat, receive_flat, send_edge, receive_edge,
):
    micro, coils, rows, length, parts = sizes
    wide = padded(length)
    image, me = lax.axis_index("img"), lax.axis_index("row")
    peers = row_peers(parts)
    slots = [(batch, kind) for batch in range(micro) for kind in (1, 0)]
    loads = {}

    def load_field(index):
        if index < len(slots):
            batch, kind = slots[index]
            for part in range(2):
                source = (kspace, maps)[kind].at[batch, :, part]
                loads[index, part] = pltpu.make_async_copy(source, fields.at[index % 2, part], loaded.at[index, part])
                loads[index, part].start()

    load_field(0)
    load_field(1)
    arrivals = [[] for _ in range(micro)]
    slabs = 2 * rows
    def send_slot(index):
        batch, kind = slots[index]
        total = None
        for part in range(2):
            loads[index, part].wait()
            field = fields[index % 2, part].reshape(coils * rows, length)
            if kind == 0:
                high, low = high_low(field)
                term = (
                    dot_nt(turn_high[part], high)
                    + dot_nt(turn_low[part], high)
                    + dot_nt(turn_high[part], low)
                )
            else:
                term = dot_nt(pick[part], field.astype(BF16))
            total = term if total is None else total + term
        slot = 2 * batch + kind
        staged[slot] = total.astype(BF16).reshape(parts, slabs, coils * rows)
        load_field(index + 2)
        if index == 0:
            meet()
        for step, peer in enumerate(peers):
            copy = remote(
                staged.at[slot, peer[1]], spread.at[slot, me], send.at[slot, step], receive.at[slot, step], peer
            )
            copy.start()
            arrivals[batch].append(copy)
        local = pltpu.make_async_copy(staged.at[slot, me], spread.at[slot, me], own.at[slot])
        local.start()
        arrivals[batch].append(local)

    for index in range(len(slots) - 1):
        send_slot(index)
    put_flat = functools.partial(
        exchange_planes, sizes, target, foreground, pick, counted, flat, landed, send_flat, receive_flat, me, peers
    )
    flats = []
    for batch in range(micro):
        chosen = join_lanes([row_mask[batch].astype(F32)], wide)
        cos_on, sin_on = cosine[...] * chosen, sine[...] * chosen

        def product(left, right):
            return jnp.dot(left, right, precision=PRECISE, preferred_element_type=F32)

        real = product(cos_on, cosine[...]) + product(sin_on, sine[...])
        imag = product(sin_on, cosine[...]) - product(cos_on, sine[...])
        diagonal = [lax.broadcasted_iota(jnp.int32, real.shape, axis) for axis in range(2)]
        real = jnp.where(diagonal[0] == diagonal[1], 0.0, real)
        for block, value in (((0, 0), real), ((0, 1), -imag), ((1, 0), imag), ((1, 1), real)):
            normal[batch, pl.ds(block[0] * wide, wide), pl.ds(block[1] * wide, wide)] = value.astype(BF16)
    put_tables(first, middle, last, first_table, middle_tables, last_table, middle_back, last_back)

    def arrive(batch):
        for copy in arrivals[batch]:
            copy.wait()
        knee = jnp.where(anatomy[0:1, batch : batch + 1] == 0, 0.0, 1.0)
        real, imag = zero_fill(
            (coils, rows, parts, wide),
            knee,
            spread.at[2 * batch],
            spread.at[2 * batch + 1],
            join_lanes([row_mask[batch].astype(F32)], wide),
            fourier_high,
            fourier_low,
            maps_out.at[batch],
        )
        put_pair(filled.at[batch], (real, imag))
        put_edges(edges.at[:, batch], real, imag)
        moved = image_halo(parts, batch, edges, halo, send_edge, receive_edge)
        for copy in moved:
            copy.start()
        if batch == 0:
            send_slot(len(slots) - 1)
            flats.extend(put_flat())
        for copy in moved:
            copy.wait()

    def finish():
        for copy in flats:
            copy.wait()
        for batch in range(micro):
            for plane in range(3):
                at = (3 * batch + plane) * rows
                pieces = [landed[block, :, at : at + rows] for block in range(parts)]
                planes[batch, plane] = join_lanes(pieces, wide)

    return arrive, finish


def exchange_planes(
    sizes, target, foreground, pick, counted, flat, landed, send_flat, receive_flat, me, peers
):
    micro, _, rows, length, parts = sizes
    shown = [foreground[batch].astype(F32) for batch in range(micro)]
    count = functools.reduce(jnp.add, [jnp.sum(jnp.sum(s, axis=1, keepdims=True), axis=0, keepdims=True) for s in shown])
    counted[...] = jnp.broadcast_to(count, (1, TILE))
    stack = []
    for batch in range(micro):
        stack += [target[batch, 0], target[batch, 1], shown[batch]]
    stack = jnp.concatenate(stack, axis=0)
    plain = pick[0].reshape(parts, 2 * rows, length)[:, :rows].reshape(length, length)
    turned = functools.reduce(jnp.add, [dot_nt(plain, piece) for piece in three_parts(stack)])
    lanes = flat.shape[2]
    flat[...] = join_lanes([turned], lanes).reshape(parts, rows, lanes)
    landed[me] = flat[me]
    flats = []
    for step, peer in enumerate(peers):
        copy = remote(flat.at[peer[1]], landed.at[me], send_flat.at[step], receive_flat.at[step], peer)
        copy.start()
        flats.append(copy)
    return flats


def put_tables(first, middle, last, first_table, middle_tables, last_table, middle_back, last_back):
    taps = range(3)
    turned = [join_rows([first[tap]], 8).T[:, :2] for tap in range(9)]
    first_table[...] = jnp.concatenate(
        [join_lanes([turned[3 * kr + kw] for kr in taps], 16) for kw in taps], axis=0
    ).astype(BF16)
    last_table[...] = jnp.concatenate(
        [join_rows([jnp.concatenate([last[3 * kr + kw] for kr in taps], axis=1)], 8) for kw in taps], axis=0
    ).astype(BF16)
    turned = [join_rows([last[tap]], 8).T[:, :2] for tap in range(9)]
    last_back[...] = jnp.concatenate(
        [join_lanes([turned[3 * (2 - m) + 2 - n] for m in taps], 16) for n in taps], axis=0
    ).astype(BF16)
    for layer in range(3):
        weights = [middle[layer, tap] for tap in range(9)]
        turned = [weight.T for weight in weights]
        middle_tables[layer] = jnp.concatenate(
            [jnp.concatenate([weights[3 * kr + kw] for kr in taps], axis=1) for kw in taps], axis=0
        ).astype(BF16)
        middle_back[layer] = jnp.concatenate(
            [jnp.concatenate([turned[3 * (2 - m) + 2 - n] for m in taps], axis=1) for n in taps], axis=0
        ).astype(BF16)


def gather_lanes(blocks, coil, rows, wide):
    pieces = [block[:, coil * rows : (coil + 1) * rows] for block in blocks]
    height = pieces[0].shape[0]
    short = wide - rows * len(pieces)
    return jnp.concatenate(pieces + [jnp.zeros((height, short), pieces[0].dtype)], axis=1)


def zero_fill(sizes, knee, fields, senses, chosen, fourier_high, fourier_low, maps_out):
    coils, rows, parts, wide = sizes
    real = jnp.zeros((rows, wide), F32)
    imag = jnp.zeros((rows, wide), F32)
    chosen = chosen.astype(BF16)
    group = 4
    for first in range(0, coils, group):
        stack = []
        for coil in range(first, first + group):
            sense = gather_lanes([senses[s] for s in range(parts)], coil, rows, wide)
            maps_out[coil] = sense if coil < BRAIN_COILS else sense * knee.astype(BF16)
            stack.append(gather_lanes([fields[s] for s in range(parts)], coil, rows, wide) * chosen)
        stack = jnp.concatenate(stack, axis=0)
        turned = dot(stack, fourier_high[...]) + dot(stack, fourier_low[...])
        for place in range(group):
            top = 2 * rows * place
            upper, lower = turned[top : top + rows], turned[top + rows : top + 2 * rows]
            field_re = upper[:, :wide] - lower[:, wide:]
            field_im = upper[:, wide:] + lower[:, :wide]
            sense = maps_out[first + place].astype(F32)
            sense_re, sense_im = sense[:rows], sense[rows:]
            real = real + sense_re * field_re + sense_im * field_im
            imag = imag + sense_re * field_im - sense_im * field_re
    return real, imag


def put_edges(edges, real, imag):
    rows = real.shape[0]
    edges[0] = jnp.concatenate([real[:REACH], imag[:REACH]], axis=0)
    edges[1] = jnp.concatenate([real[rows - REACH :], imag[rows - REACH :]], axis=0)


def lane_row(columns):
    return jnp.sum(columns.T, axis=0, keepdims=True)


def spread_row(row):
    return jnp.broadcast_to(row, (TILE, row.shape[1])).T


def padded_rows(rows):
    return join_rows([join_lanes([row], TILE) for row in rows], 8)


def merge(sums, squares, count):
    total = functools.reduce(jnp.add, sums)
    mean = total / (count * len(sums))
    square = None
    for part, own in zip(sums, squares):
        shift = part / count - mean
        term = own + count * shift * shift
        square = term if square is None else square + term
    return total, square


def repeat_lanes(block, wide):
    return jnp.concatenate([block] * (wide // TILE), axis=1)


def lane_mask(length, wide):
    whole = length // TILE * TILE

    def clear(values):
        tail = values[:, whole:]
        keep = lax.broadcasted_iota(jnp.int32, tail.shape, 1) < length - whole
        return jnp.concatenate([values[:, :whole], jnp.where(keep, tail, 0.0)], axis=1)

    return clear


def fold(values):
    parts = [values[:, at : at + TILE] for at in range(0, values.shape[1], TILE)]
    return functools.reduce(jnp.add, parts)


def put_shifted(stack, values, at):
    channels, wide = values.shape
    stack[0:channels, at : at + wide] = pltpu.roll(values, 1, 1)
    stack[channels : 2 * channels, at : at + wide] = values
    stack[2 * channels : 3 * channels, at : at + wide] = pltpu.roll(values, wide - 1, 1)


def lane_at(column, wide):
    return pl.multiple_of(column * wide, TILE) if not isinstance(column, int) else column * wide


class Sums:
    def __init__(self, parts, images, refs):
        self.message, self.held, self.second, self.held_second, self.send, self.receive = refs
        self.rows, self.cols = row_peers(parts), image_peers(images)

    def copies(self, slot, stage):
        source, target = ((self.message, self.held), (self.second, self.held_second))[stage]
        peers = (self.rows, self.cols)[stage]
        base = stage * len(self.rows)
        return [
            remote(
                source.at[slot],
                target.at[slot + (index,)],
                self.send.at[slot + (base + index,)],
                self.receive.at[slot + (base + index,)],
                peer,
            )
            for index, peer in enumerate(peers)
        ]

    def start(self, slot, stage, values):
        (self.message, self.second)[stage][slot] = values
        for copy in self.copies(slot, stage):
            copy.start()

    def collect(self, slot, stage):
        blocks = [(self.message, self.second)[stage][slot]]
        for index, copy in enumerate(self.copies(slot, stage)):
            copy.wait_recv()
            blocks.append((self.held, self.held_second)[stage][slot + (index,)])
        return blocks

    def settle(self, slot, stages=(0, 1)):
        for stage in stages:
            for copy in self.copies(slot, stage):
                copy.wait_send()

    @staticmethod
    def scratch(slots, parts, images):
        return [
            pltpu.VMEM(slots + (8, TILE), F32),
            pltpu.VMEM(slots + (parts - 1, 8, TILE), F32),
            pltpu.VMEM(slots + (8, TILE), F32),
            pltpu.VMEM(slots + (max(images - 1, 1), 8, TILE), F32),
            pltpu.SemaphoreType.DMA(slots + (parts + images - 2,)),
            pltpu.SemaphoreType.DMA(slots + (parts + images - 2,)),
        ]


class Ends:
    def __init__(self, parts):
        me = lax.axis_index("row")
        self.left, self.right = me > 0, me < parts - 1

    def clear(self, values, column, width):
        if column < 0:
            return jnp.where(self.left, values, 0.0)
        if column >= width:
            return jnp.where(self.right, values, 0.0)
        return values


def ring_pass(table, take, fill, emit, out_rows, width, wide, hook, hook_at):
    fill(0)
    fill(1)
    product = dot(table, take(0))
    older = product[0:out_rows, :wide] + product[out_rows : 2 * out_rows, wide:]
    newer = product[0:out_rows, wide:]
    last = width // 2
    for couple in range(1, last + 1):
        if hook is not None and couple == last * hook_at // 8:
            hook()
        product = dot(table, take(couple))
        if couple < last:
            fill(couple + 1)
        for place in range(2):
            piece = product[:, place * wide : (place + 1) * wide]
            emit(2 * couple - 2 + place, older + piece[2 * out_rows : 3 * out_rows])
            older = newer + piece[out_rows : 2 * out_rows]
            newer = piece[0:out_rows]


def silu_half(values, scale, offset):
    half = values * scale + offset
    return half, jnp.tanh(half)


def put_image(image, halo, place, stack, ends, reach):
    _, width, wide = image.shape
    blocks = {-REACH: (halo[0, place, :REACH], halo[0, place, REACH:]), width: (halo[1, place, :REACH], halo[1, place, REACH:])}
    for first in range(0, width, 8):
        blocks[first] = (image[0, first : first + 8], image[1, first : first + 8])
    for first, (real, imag) in blocks.items():
        real, imag = ends.clear(real, first, width), ends.clear(imag, first, width)
        rolled = [pltpu.roll(real, 1, 1), pltpu.roll(imag, 1, 1), real, imag, pltpu.roll(real, wide - 1, 1), pltpu.roll(imag, wide - 1, 1)]
        for offset in range(8):
            at = first + offset + reach
            if 0 <= at < width + 2 * reach:
                rows = [block[offset : offset + 1] for block in rolled]
                stack[:, at * wide : (at + 1) * wide] = join_rows(rows, 16).astype(BF16)


def image_halo(parts, batch, edges, halo, send, receive):
    image, me = lax.axis_index("img"), lax.axis_index("row")
    left, right = lax.rem(me + parts - 1, parts), lax.rem(me + 1, parts)
    places = [((image, left), 0), ((image, right), 1)]
    return [
        remote(edges.at[side, batch], halo.at[1 - side, batch], send.at[batch, side], receive.at[batch, side], peer)
        for peer, side in places
    ]


def forward_kernel(
    sizes, kspace, maps, target, foreground, row_mask, anatomy, first, middle_weight, last, turn_high, turn_low, pick,
    cosine, sine, fourier_high, fourier_low, gains, shifts,
    filled, maps_out, planes, normal, middle_back, last_back, layers, coefs, rows_out, images_out, result,
    fields, staged, spread, flat, landed, edges, halo_image, first_table, middle_tables, last_table, counted,
    loaded, send, receive, own, send_flat, receive_flat, send_edge, receive_edge,
    lin, even, odd, pivot, total, square, *refs,
):
    micro, coils, rows, length, parts, images = sizes
    _, _, width, wide = filled.shape
    channels = lin.shape[3]
    count = width * length
    whole = length // TILE * TILE
    stacks = (even, odd)
    sums = Sums(parts, images, refs[:6])
    (saved,) = refs[6:]
    ends = Ends(parts)
    clear = lane_mask(length, wide)
    knock(sums.rows + sums.cols)
    arrive, finish = start_exchange(
        (micro, coils, rows, length, parts), lambda: admit(sums.rows + sums.cols),
        kspace, maps, target, foreground, row_mask, anatomy, first, middle_weight, last, turn_high, turn_low, pick, cosine, sine,
        fourier_high, fourier_low,
        filled, maps_out, halo_image, planes, normal, first_table, middle_tables, last_table, middle_back, last_back, counted,
        fields, staged, spread, flat, landed, edges, loaded, send, receive, own, send_flat, receive_flat, send_edge, receive_edge,
    )

    def band(layer, batch):
        return lin.at[batch, lax.rem(layer, 2)]

    def save(layer, batch):
        kept = band(layer, batch).at[pl.ds(FIRST_REACH - BACK_REACH, width + 2 * BACK_REACH)]
        return pltpu.make_async_copy(kept, layers.at[layer, batch], saved.at[layer, batch])

    def begin(layer, batch, not_first):
        if not_first:
            save(layer - 1, batch).wait()
        moments = jnp.concatenate([total[...], square[...]], axis=0).T
        moments = jnp.sum(moments, axis=0, keepdims=True)
        delta = moments[:, :channels] / count
        spread = moments[:, channels:] - count * delta * delta
        centre = pivot[...].T[0:1]
        sums.start((layer, batch), 0, padded_rows([count * (centre + delta), spread, counted[:, :channels]]))
        save(layer, batch).start()

    def join(blocks, number):
        blocks = [block[:, :channels] for block in blocks]
        added, spread = merge([block[0:1] for block in blocks], [block[1:2] for block in blocks], number)
        return added, spread, functools.reduce(jnp.add, [block[2:3] for block in blocks])

    def middle(layer, batch):
        joined = join(sums.collect((layer, batch), 0), count)
        sums.start((layer, batch), 1, padded_rows(joined))

    def end(layer, batch):
        added, spread, plain = join(sums.collect((layer, batch), 1), count * parts)
        pixels = count * parts * images
        gain, shift = gains[pl.ds(layer, 1), :], shifts[pl.ds(layer, 1), :]
        inverse = lax.rsqrt(spread / pixels + EPS_NORM)
        offset = -(added / pixels) * inverse
        coefs[layer, batch, 0] = spread_row(0.5 * gain * inverse)
        coefs[layer, batch, 1] = spread_row(0.5 * (shift + gain * offset))
        coefs[layer, batch, 2] = spread_row(inverse)
        coefs[layer, batch, 3] = spread_row(offset)
        rows_out[layer, batch] = join_rows([gain, shift, inverse, offset, plain], 8)

    def keeper(out, reach):
        held = []

        def emit(column, value):
            column = column - reach
            out[FIRST_REACH + column] = value
            if not 0 <= column < width:
                return
            if column == 0:
                mean = jnp.sum(clear(value), axis=1, keepdims=True) / length
                pivot[...] = jnp.broadcast_to(mean, pivot.shape)
            if column % BLOCK == 0:
                held[:] = [jnp.zeros((channels, TILE), F32), jnp.zeros((channels, TILE), F32)]
            centre = pivot[...]
            for at in range(0, wide, TILE):
                shift = value[:, at : at + TILE] - centre
                if at >= whole:
                    lane = lax.broadcasted_iota(jnp.int32, shift.shape, 1)
                    shift = jnp.where(lane < length - at, shift, 0.0)
                held[0] = held[0] + shift
                held[1] = held[1] + shift * shift
            if column == BLOCK - 1:
                total[...], square[...] = held
            elif column % BLOCK == BLOCK - 1:
                total[...] += held[0]
                square[...] += held[1]

        return emit

    def first_layer(batch, hook):
        source = images_out.at[batch]
        put_image(filled.at[batch], halo_image, batch, source, ends, FIRST_REACH + 1)
        ring_pass(
            first_table[...],
            lambda couple: source[:, 2 * couple * wide : 2 * (couple + 1) * wide],
            lambda couple: None,
            keeper(band(0, batch), FIRST_REACH),
            channels,
            width + 2 * FIRST_REACH,
            wide,
            hook,
            FORWARD_HOOK,
        )

    def inner_layer(layer, batch, table, out_rows, reach, emit, hook):
        source = band(layer, batch)
        scale, offset = repeat_lanes(coefs[layer, batch, 0], wide), repeat_lanes(coefs[layer, batch, 1], wide)

        def fill(couple):
            for place in range(2):
                column = 2 * couple + place - reach - 1
                half, curve = silu_half(source[FIRST_REACH + column], scale, offset)
                active = ends.clear(clear(half * curve + half), column, width)
                put_shifted(stacks[couple % 2], active.astype(BF16), place * wide)

        ring_pass(table, lambda couple: stacks[couple % 2][...], fill, emit, out_rows, width + 2 * reach, wide, hook, FORWARD_HOOK)

    def place_of(index):
        return lax.div(index, 2), lax.rem(index, 2)

    arrive(0)
    first_layer(0, None)
    begin(0, 0, False)
    arrive(1)
    first_layer(1, lambda: middle(0, 0))
    begin(0, 1, False)
    end(0, 0)

    def layer_step(index, carried):
        layer, batch = place_of(index)
        before = place_of(index - 1)
        reach = FIRST_REACH - 1
        emit = keeper(band(layer, batch), reach)
        inner_layer(layer - 1, batch, middle_tables[layer - 1], channels, reach, emit, lambda: middle(*before))
        begin(layer, batch, True)
        end(*before)
        return carried

    lax.fori_loop(2, 8, layer_step, 0)

    def last_step(batch, carried):
        def emit(column, value):
            result[batch, 0, column : column + 1] = value[0:1]
            result[batch, 1, column : column + 1] = value[1:2]

        inner_layer(3, batch, last_table[...], 8, 0, emit, lambda: pl.when(batch == 0)(lambda: middle(3, 1)))
        pl.when(batch == 0)(lambda: end(3, 1))
        return carried

    lax.fori_loop(0, 2, last_step, 0)
    finish()
    for batch in range(2):
        save(3, batch).wait()
    for layer in range(4):
        for batch in range(2):
            sums.settle((layer, batch))


def forward(kspace, maps, target, foreground, row_mask, anatomy, first, middle, last, gains, shifts, parts, images):
    micro, coils, _, rows, length = kspace.shape
    wide = padded(length)
    channels = first.shape[2]
    cosine, sine = phases(length)
    fourier = np.zeros((wide, 2, wide))
    fourier[:length, 0, :length] = cosine
    fourier[:length, 1, :length] = sine
    fourier_high, fourier_low = np_high_low(fourier.reshape(wide, 2 * wide))
    inverse = np.stack([np.stack([cosine, sine], 0), np.stack([-sine, cosine], 0)], 0)
    turn = inverse.reshape(2, 2, length, parts, rows).transpose(0, 3, 1, 4, 2).reshape(2, 2 * length, length)
    pick = np.zeros((2, parts, 2, rows, length), np.float32)
    for part in range(2):
        for block in range(parts):
            pick[part, block, part, :, block * rows : (block + 1) * rows] = np.eye(rows)
    pick = jnp.asarray(pick.reshape(2, 2 * length, length).astype(BF16))
    turn_high, turn_low = np_high_low(turn)
    edge = ((0, wide - length), (0, wide - length))
    cosine = jnp.asarray(np.pad(cosine, edge), F32)
    sine = jnp.asarray(np.pad(sine, edge), F32)
    slots = 2 * micro
    lanes = padded(3 * micro * rows)
    shapes = [
        ((micro, 2, rows, wide), F32),
        ((micro, coils, 2 * rows, wide), BF16),
        ((micro, 3, rows, wide), F32),
        ((micro, 2 * wide, 2 * wide), BF16),
        ((3, 3 * channels, 3 * channels), BF16),
        ((3 * channels, 16), BF16),
        ((4, micro, rows + 2 * BACK_REACH, channels, wide), F32),
        ((4, micro, 4, channels, TILE), F32),
        ((4, micro, 8, channels), F32),
        ((micro, 16, (rows + 2 * FIRST_REACH + 2) * wide), BF16),
        ((micro, 2, rows, wide), F32),
    ]
    layers = (4, micro)
    return pl.pallas_call(
        functools.partial(forward_kernel, (micro, coils, rows, length, parts, images)),
        out_shape=[jax.ShapeDtypeStruct(*shape) for shape in shapes],
        in_specs=[anywhere()] * 2 + [in_vmem()] * 16,
        out_specs=[in_vmem()] * 6 + [anywhere()] + [in_vmem()] * 4,
        scratch_shapes=[
            pltpu.VMEM((2, 2, coils, rows, length), F32),
            pltpu.VMEM((slots, parts, 2 * rows, coils * rows), BF16),
            pltpu.VMEM((slots, parts, 2 * rows, coils * rows), BF16),
            pltpu.VMEM((parts, rows, lanes), F32),
            pltpu.VMEM((parts, rows, lanes), F32),
            pltpu.VMEM((2, micro, 2 * REACH, wide), F32),
            pltpu.VMEM((2, micro, 2 * REACH, wide), F32),
            pltpu.VMEM((3 * channels, 16), BF16),
            pltpu.VMEM((3, 3 * channels, 3 * channels), BF16),
            pltpu.VMEM((24, 3 * channels), BF16),
            pltpu.VMEM((1, TILE), F32),
            pltpu.SemaphoreType.DMA((slots, 2)),
            pltpu.SemaphoreType.DMA((slots, parts - 1)),
            pltpu.SemaphoreType.DMA((slots, parts - 1)),
            pltpu.SemaphoreType.DMA((slots,)),
            pltpu.SemaphoreType.DMA((parts - 1,)),
            pltpu.SemaphoreType.DMA((parts - 1,)),
            pltpu.SemaphoreType.DMA((micro, 2)),
            pltpu.SemaphoreType.DMA((micro, 2)),
            pltpu.VMEM((micro, 2, rows + 2 * FIRST_REACH, channels, wide), F32),
            pltpu.VMEM((3 * channels, 2 * wide), BF16),
            pltpu.VMEM((3 * channels, 2 * wide), BF16),
            pltpu.VMEM((channels, TILE), F32),
            pltpu.VMEM((channels, TILE), F32),
            pltpu.VMEM((channels, TILE), F32),
        ]
        + Sums.scratch(layers, parts, images)
        + [pltpu.SemaphoreType.DMA(layers)],
        compiler_params=params(collective_id=1, has_side_effects=True),
        name="forward",
    )(
        kspace, maps, target, foreground, row_mask, anatomy, first, middle, last, turn_high, turn_low, pick, cosine, sine,
        fourier_high, fourier_low, gains, shifts,
    )


def backward_kernel(
    sizes, grad, halo_image, layers, coefs, rows_in, images_in, middle_back, last_back,
    first_sums, middle_sums, last_sums, rows_out,
    upper, lin, stack, thin, inputs, slope, total, along, mix, *refs,
):
    micro, parts, images, length = sizes
    _, _, width, wide = grad.shape
    channels = lin.shape[3]
    pixels = width * length * parts * images
    sums = Sums(parts, images, refs[:6])
    (loaded,) = refs[6:]
    knock(sums.rows + sums.cols)
    ends = Ends(parts)
    clear = lane_mask(length, wide)

    def load(layer, batch):
        return pltpu.make_async_copy(layers.at[layer, batch], lin.at[batch, lax.rem(layer, 2)], loaded.at[layer, batch])

    for layer in (3, 2):
        for batch in range(micro):
            load(layer, batch).start()
    first_sums[...] = jnp.zeros_like(first_sums)
    middle_sums[...] = jnp.zeros_like(middle_sums)
    last_sums[...] = jnp.zeros_like(last_sums)

    def band(layer, batch):
        return upper.at[batch, lax.rem(layer, 2)]

    def begin(layer, batch):
        added = jnp.concatenate([total[...], along[...]], axis=0).T
        added = jnp.sum(added, axis=0, keepdims=True)
        sums.start((layer, batch), 0, padded_rows([added]))

    def middle(layer, batch):
        sums.start((layer, batch), 1, functools.reduce(jnp.add, sums.collect((layer, batch), 0)))

    def end(layer, batch):
        added = functools.reduce(jnp.add, sums.collect((layer, batch), 1))
        shift_sum, gain_sum = added[0:1, :channels], added[0:1, channels:]
        rows = rows_in[layer, batch]
        gain, inverse, offset = rows[0:1], rows[2:3], rows[3:4]
        scale = inverse * gain
        mix[batch, 0] = spread_row(scale)
        mix[batch, 1] = spread_row(-scale * inverse * gain_sum / pixels)
        mix[batch, 2] = spread_row(-scale * (shift_sum + offset * gain_sum) / pixels)
        rows_out[layer, batch] = join_rows([shift_sum, gain_sum], 8)

    def place_of(index):
        return 3 - lax.div(index, 2), lax.rem(index, 2)

    def grad_putter(layer, batch):
        grads, linear = band(layer, batch), lin.at[batch, lax.rem(layer, 2)]
        on_grad, on_layer, base = (repeat_lanes(mix[batch, index], wide) for index in range(3))

        def put(column):
            at = column + BACK_REACH
            upstream = clear(on_grad * grads[at] + on_layer * linear[at] + base)
            put_shifted(stack, ends.clear(upstream, column, width).astype(BF16), at * wide)

        return put

    def add_weights(weight_out, source, reach, around, around_reach, first):
        at = first + around_reach - 1
        columns = [around[:, (at + tap) * wide : (at + tap + GROUP) * wide] for tap in range(3)]
        at = first + reach
        weight_out[...] += dot_nt(source[:, at * wide : (at + GROUP) * wide], jnp.concatenate(columns, axis=0))

    def layer_back(layer, batch, source, reach, table, weight_out, put_grad, hook):
        below = lin.at[batch, lax.rem(layer, 2)]
        out = band(layer, batch)
        scale, offset = repeat_lanes(coefs[layer, batch, 0], wide), repeat_lanes(coefs[layer, batch, 1], wide)
        inverse, centre = repeat_lanes(coefs[layer, batch, 2], wide), repeat_lanes(coefs[layer, batch, 3], wide)

        def fill(couple):
            for place in range(2):
                column = 2 * couple + place - reach - 1
                if put_grad is not None:
                    put_grad(column)
                if not -reach <= column < width + reach:
                    continue
                at = column + BACK_REACH
                half, curve = silu_half(below[at], scale, offset)
                slope[at] = 0.5 * (1.0 + curve) * (1.0 + half * (1.0 - curve))
                if -1 <= column <= width:
                    active = ends.clear(clear(half * curve + half), column, width)
                    inputs[:, (column + 1) * wide : (column + 2) * wide] = active.astype(BF16)

        held = []

        def emit(column, value):
            column = column - reach
            at = column + BACK_REACH
            shaped = clear(value * slope[at])
            out[at] = shaped
            if not 0 <= column < width:
                return
            if column % BLOCK == 0:
                held[:] = [jnp.zeros((channels, TILE), F32), jnp.zeros((channels, TILE), F32)]
            held[0] = held[0] + fold(shaped)
            held[1] = held[1] + fold(shaped * (below[at] * inverse + centre))
            if column == BLOCK - 1:
                total[...], along[...] = held
            elif column % BLOCK == BLOCK - 1:
                total[...] += held[0]
                along[...] += held[1]
            if column % GROUP == GROUP - 1:
                add_weights(weight_out, source, reach + 1, inputs, 1, column + 1 - GROUP)

        ring_pass(
            table,
            lambda couple: source[:, 2 * couple * wide : 2 * (couple + 1) * wide],
            fill,
            emit,
            channels,
            width + 2 * reach,
            wide,
            hook,
            BACK_HOOK,
        )

    def outer_step(batch, carried):
        put_image(grad.at[batch], halo_image, batch, thin, ends, BACK_REACH + 1)
        pl.when(batch == 0)(lambda: admit(sums.rows + sums.cols))
        load(3, batch).wait()
        hook = lambda: pl.when(batch > 0)(lambda: middle(3, 0))
        layer_back(3, batch, thin, BACK_REACH, last_back[...], last_sums, None, hook)
        begin(3, batch)
        pl.when(batch > 0)(lambda: end(3, 0))
        return carried

    lax.fori_loop(0, 2, outer_step, 0)

    def layer_step(index, carried):
        layer, batch = place_of(index)
        before = place_of(index - 1)
        load(layer, batch).wait()
        layer_back(
            layer,
            batch,
            stack,
            BACK_REACH - 1,
            middle_back[layer],
            middle_sums.at[layer],
            grad_putter(layer + 1, batch),
            lambda: middle(*before),
        )
        pl.when(layer > 0)(lambda: load(layer - 1, batch).start())
        begin(layer, batch)
        end(*before)
        return carried

    lax.fori_loop(2, 8, layer_step, 0)

    def first_step(batch, carried):
        put_grad = grad_putter(0, batch)
        for column in range(width):
            if column == width // 2:
                pl.when(batch == 0)(lambda: middle(0, 1))
            put_grad(column)
            if column % GROUP == GROUP - 1:
                add_weights(first_sums, stack, BACK_REACH, images_in.at[batch], FIRST_REACH + 1, column + 1 - GROUP)
        pl.when(batch == 0)(lambda: end(0, 1))
        return carried

    lax.fori_loop(0, 2, first_step, 0)
    for layer in range(4):
        for batch in range(2):
            sums.settle((layer, batch))


def backward(grad, halo, kept, tables, parts, images, length):
    layers, coefs, rows_in, images_in = kept
    micro, _, width, wide = grad.shape
    channels = layers.shape[3]
    band = (micro, 2, width + 2 * BACK_REACH, channels, wide)
    lanes = (width + 2 * BACK_REACH) * wide
    shapes = [(3 * channels, 48), (3, 3 * channels, 3 * channels), (16, 3 * channels), (4, micro, 8, channels)]
    slots = (4, micro)
    return pl.pallas_call(
        functools.partial(backward_kernel, (micro, parts, images, length)),
        out_shape=[jax.ShapeDtypeStruct(shape, F32) for shape in shapes],
        in_specs=[in_vmem(), in_vmem(), anywhere()] + [in_vmem()] * 5,
        out_specs=[in_vmem()] * 4,
        scratch_shapes=[
            pltpu.VMEM(band, F32),
            pltpu.VMEM(band, F32),
            pltpu.VMEM((3 * channels, lanes), BF16),
            pltpu.VMEM((16, lanes + 2 * wide), BF16),
            pltpu.VMEM((channels, (width + 2) * wide), BF16),
            pltpu.VMEM(band[2:], F32),
            pltpu.VMEM((channels, TILE), F32),
            pltpu.VMEM((channels, TILE), F32),
            pltpu.VMEM((micro, 3, channels, TILE), F32),
        ]
        + Sums.scratch(slots, parts, images)
        + [pltpu.SemaphoreType.DMA(slots)],
        compiler_params=params(collective_id=3, has_side_effects=True),
        name="backward",
    )(grad, halo, layers, coefs, rows_in, images_in, *tables)


def reduce_kernel(parts, images, first_sums, middle_sums, last_sums, scalars, first_grad, middle_grad, last_grad, totals, whole, final, quarter, landed, eighth, landed_rows, send, receive):
    image, me = lax.axis_index("img"), lax.axis_index("row")
    rows, cols = row_peers(parts), image_peers(images)
    knock(rows + cols)
    channels = middle_sums.shape[1] // 3
    taps = [(kr, kw) for kr in range(3) for kw in range(3)]
    pieces = [
        middle_sums[layer, (2 - kr) * channels : (3 - kr) * channels, kw * channels : (kw + 1) * channels]
        for layer in range(3)
        for kr, kw in taps
    ]
    firsts = [first_sums[(2 - kr) * channels : (3 - kr) * channels, 16 * kw + 2 : 16 * kw + 4] for kr, kw in taps]
    pieces.append(join_lanes(firsts, channels))
    for index in range(0, len(pieces), 2):
        at = index // 2 * channels
        whole[at : at + channels] = jnp.concatenate(pieces[index : index + 2], axis=1)
    at = len(pieces) // 2 * channels
    lasts = [last_sums[2 * (2 - kr) : 2 * (3 - kr), kw * channels : (kw + 1) * channels] for kr, kw in taps]
    added = functools.reduce(jnp.add, [scalars[batch] for batch in range(scalars.shape[0])])
    whole[at : at + 24] = jnp.concatenate([join_rows(lasts, 24), join_rows([added[:, :channels]], 24)], axis=1)
    whole[at + 24 :] = jnp.zeros((whole.shape[0] - at - 24, TILE), F32)
    admit(rows + cols)
    big, small = quarter.shape[0], eighth.shape[0]
    images_here, parts_here = len(cols), len(rows)

    def place(index, size):
        return pl.ds(pl.multiple_of(index * size, 8), size)

    sent = []
    for index, peer in enumerate(cols):
        copy = remote(whole.at[place(peer[0], big)], landed.at[index], send.at[index], receive.at[index], peer)
        copy.start()
        sent.append(copy)
    for copy in sent:
        copy.wait_recv()
    total = whole[place(image, big)]
    for index in range(images_here):
        total = total + landed[index]
    quarter[...] = total
    base = images_here
    arrived = []
    for index, peer in enumerate(rows):
        copy = remote(
            quarter.at[place(peer[1], small)], landed_rows.at[index], send.at[base + index], receive.at[base + index], peer
        )
        copy.start()
        arrived.append(copy)
    for copy in arrived:
        copy.wait_recv()
    total = quarter[place(me, small)]
    for index in range(parts_here):
        total = total + landed_rows[index]
    eighth[...] = total
    for copy in sent + arrived:
        copy.wait_send()
    base += parts_here
    returned = []
    mine = pl.ds(pl.multiple_of(image * big + me * small, 8), small)
    for index, peer in enumerate(rows):
        copy = remote(eighth, final.at[mine], send.at[base + index], receive.at[base + index], peer)
        copy.start()
        returned.append(copy)
    final[mine] = total
    for copy in returned:
        copy.wait()
    base += parts_here
    returned = []
    for index, peer in enumerate(cols):
        copy = remote(final.at[place(image, big)], final.at[place(image, big)], send.at[base + index], receive.at[base + index], peer)
        copy.start()
        returned.append(copy)
    for copy in returned:
        copy.wait()
    for index in range(27):
        from_row = index // 2 * channels
        from_lane = index % 2 * channels
        middle_grad[index // 9, index % 9] = final[from_row : from_row + channels, from_lane : from_lane + channels]
    turned = final[13 * channels : 14 * channels, channels:].T
    for tap in range(9):
        first_grad[tap] = turned[2 * tap : 2 * tap + 2]
        last_grad[tap] = final[at + 2 * tap : at + 2 * tap + 2, :channels]
    totals[...] = final[at : at + 8, channels:]


def reduce_all(first_sums, middle_sums, last_sums, scalars, parts, images):
    channels = middle_sums.shape[1] // 3
    unit = 8 * parts * images
    height = -(-(14 * channels + 24) // unit) * unit
    copies = 2 * (parts + images - 2)
    shapes = [(9, 2, channels), (3, 9, channels, channels), (9, 2, channels), (8, channels)]
    return pl.pallas_call(
        functools.partial(reduce_kernel, parts, images),
        out_shape=[jax.ShapeDtypeStruct(shape, F32) for shape in shapes],
        in_specs=[in_vmem()] * 4,
        out_specs=[in_vmem()] * 4,
        scratch_shapes=[
            pltpu.VMEM((height, TILE), F32),
            pltpu.VMEM((height, TILE), F32),
            pltpu.VMEM((height // images, TILE), F32),
            pltpu.VMEM((images - 1, height // images, TILE), F32),
            pltpu.VMEM((height // images // parts, TILE), F32),
            pltpu.VMEM((parts - 1, height // images // parts, TILE), F32),
            pltpu.SemaphoreType.DMA((copies,)),
            pltpu.SemaphoreType.DMA((copies,)),
        ],
        compiler_params=params(collective_id=4, has_side_effects=True),
        name="reduce_all",
    )(first_sums, middle_sums, last_sums, scalars)


def apply_normal(image, maps, normal, diagonal):
    coils, slabs, wide = maps.shape
    rows = slabs // 2
    real, imag = image
    stack, power = [], jnp.zeros((rows, wide), F32)
    for coil in range(coils):
        sense = maps[coil].astype(F32)
        sense_re, sense_im = sense[:rows], sense[rows:]
        power = power + sense_re * sense_re + sense_im * sense_im
        field = [sense_re * real - sense_im * imag, sense_re * imag + sense_im * real]
        stack.append(jnp.concatenate(field, axis=1))
    stack = jnp.concatenate(stack, axis=0).astype(BF16)
    power = diagonal * power
    out_re, out_im = power * real, power * imag
    turned = dot(stack, normal[...])
    for coil in range(coils):
        sense = maps[coil].astype(F32)
        sense_re, sense_im = sense[:rows], sense[rows:]
        field = turned[coil * rows : (coil + 1) * rows]
        field_re, field_im = field[:, :wide], field[:, wide:]
        out_re = out_re + sense_re * field_re + sense_im * field_im
        out_im = out_im + sense_re * field_im - sense_im * field_re
    return out_re, out_im


def pair(ref):
    return ref[0], ref[1]


def put_pair(ref, values):
    ref[0] = values[0]
    ref[1] = values[1]


def blend(*terms):
    return tuple(functools.reduce(jnp.add, [factor * image[part] for factor, image in terms]) for part in range(2))


def inner_of(left, right):
    product = left[0] * right[0] + left[1] * right[1]
    return jnp.sum(jnp.sum(product, axis=1, keepdims=True), axis=0, keepdims=True)


class RowSums:
    def __init__(self, parts, refs):
        self.message, self.held, self.send, self.receive = refs
        self.peers = row_peers(parts)

    def copies(self, slot):
        return [
            remote(
                self.message.at[slot],
                self.held.at[slot + (index,)],
                self.send.at[slot + (index,)],
                self.receive.at[slot + (index,)],
                peer,
            )
            for index, peer in enumerate(self.peers)
        ]

    def start(self, slot, values):
        filler = [jnp.zeros((1, TILE), F32)] * (8 - len(values))
        self.message[slot] = jnp.concatenate([jnp.broadcast_to(value, (1, TILE)) for value in values] + filler, axis=0)
        for copy in self.copies(slot):
            copy.start()

    def finish(self, slot):
        total = self.message[slot]
        for index, copy in enumerate(self.copies(slot)):
            copy.wait_recv()
            total = total + self.held[slot + (index,)]
        return [total[index : index + 1, 0:1] for index in range(8)]

    def settle(self, slot):
        for copy in self.copies(slot):
            copy.wait_send()


def solve_kernel(
    sizes, filled, result, maps, normal, planes, rows_in, row_mask, extra, grad_out, halo, scalars,
    work, edges, send_edge, receive_edge, *refs,
):
    micro, parts, length = sizes
    _, _, rows, wide = filled.shape
    sums = RowSums(parts, refs)
    knock(sums.peers)
    moved = []
    inside = lax.broadcasted_iota(jnp.int32, (rows, wide), 1) < length
    penalty = jnp.exp(jnp.full((1, 1), extra[2], F32))
    inv_count = 1.0 / rows_in[0, 0, 4:5, 0:1]
    diagonals = [jnp.sum(row_mask[batch].astype(F32), axis=1, keepdims=True) / length for batch in range(micro)]
    names = ("denoised", "right", "mapped", "residue", "through", "search", "searched", "slope")

    def at(name, batch):
        return work.at[batch, names.index(name)]

    def get(name, batch):
        return pair(at(name, batch))

    def through_normal(image, batch):
        out = apply_normal(image, maps.at[batch], normal.at[batch], diagonals[batch])
        return blend((1.0, out), (penalty, image))

    for batch in range(micro):
        images = []
        for part in range(2):
            value = filled[batch, part] + result[batch, part] + jnp.full((1, 1), extra[part], F32)
            value = jnp.where(inside, value, 0.0)
            at("denoised", batch)[part] = value
            images.append(filled[batch, part] + penalty * value)
        put_pair(at("right", batch), images)
        mapped = through_normal(images, batch)
        put_pair(at("mapped", batch), mapped)
        if batch == 0:
            admit(sums.peers)
        sums.start((0, batch), [inner_of(images, images), inner_of(images, mapped)])
    ones, twos = [], []
    for batch in range(micro):
        ones.append(sums.finish((0, batch)))
        start, image = get("right", batch), get("mapped", batch)
        left_over = blend((1.0, start), (-ones[batch][0] / ones[batch][1], image))
        put_pair(at("residue", batch), left_over)
        mapped = through_normal(left_over, batch)
        put_pair(at("through", batch), mapped)
        sums.start(
            (1, batch),
            [
                inner_of(left_over, left_over),
                inner_of(left_over, mapped),
                inner_of(left_over, image),
                inner_of(start, mapped),
            ],
        )
    kept = []
    for batch in range(micro):
        twos.append(sums.finish((1, batch)))
        norm_0, curve_0 = ones[batch][:2]
        norm_1 = twos[batch][0]
        factor = norm_1 / norm_0
        curve_1 = twos[batch][1] + factor * (twos[batch][2] + twos[batch][3]) + factor * factor * curve_0
        start, image = get("right", batch), get("mapped", batch)
        direction = blend((1.0, get("residue", batch)), (factor, start))
        image_1 = blend((1.0, get("through", batch)), (factor, image))
        put_pair(at("searched", batch), image_1)
        state = blend((norm_0 / curve_0, start), (norm_1 / curve_1, direction))
        weight = planes[batch, 2]
        difference = [state[part] - planes[batch, part] for part in range(2)]
        grad = [inv_count * 2.0 * weight * difference[part] for part in range(2)]
        put_pair(at("slope", batch), grad)
        masked = [weight * difference[part] for part in range(2)]
        sums.start(
            (2, batch),
            [
                inner_of(grad, direction),
                inner_of(grad, start),
                inner_of(grad, image),
                inner_of(image_1, start),
                inner_of(image_1, image),
            ],
        )
        kept.append((norm_0, curve_0, norm_1, curve_1, factor, inner_of(direction, direction), inner_of(masked, difference)))
    for batch in range(micro):
        grad_search, grad_start, grad_image, cross_start, cross_image = sums.finish((2, batch))[:5]
        norm_0, curve_0, norm_1, curve_1, factor, own_search, own_loss = kept[batch]
        step_0, step_1 = norm_0 / curve_0, norm_1 / curve_1
        start, image, left_over = get("right", batch), get("mapped", batch), get("residue", batch)
        image_1, grad = get("searched", batch), get("slope", batch)
        residue_image = twos[batch][2]
        curve_grad_1 = -grad_search * norm_1 / (curve_1 * curve_1)
        norm_grad_1 = grad_search / curve_1
        search_grad = blend((step_1, grad), (2.0 * curve_grad_1, image_1))
        factor_grad = step_1 * grad_start + 2.0 * curve_grad_1 * cross_start
        joint = step_1 * grad_image + 2.0 * curve_grad_1 * cross_image
        norm_total = norm_grad_1 + factor_grad / norm_0
        residue_full = blend((1.0, search_grad), (2.0 * norm_total, left_over))
        step_grad = grad_start - (joint + 2.0 * norm_total * residue_image)
        curve_grad_0 = -step_grad * norm_0 / (curve_0 * curve_0)
        mapped_grad = blend((-step_0, residue_full), (curve_grad_0, start))
        through = through_normal(mapped_grad, batch)
        norm_grad_0 = -factor_grad * norm_1 / (norm_0 * norm_0) + step_grad / curve_0
        right_grad = blend(
            (1.0, residue_full),
            (factor, search_grad),
            (step_0, grad),
            (curve_grad_0, image),
            (1.0, through),
            (2.0 * norm_grad_0, start),
        )
        penalty_part = (
            curve_grad_1 * own_search + inner_of(mapped_grad, start) + inner_of(right_grad, get("denoised", batch))
        )
        grad_pair = [penalty * right_grad[part] for part in range(2)]
        put_pair(grad_out.at[batch], grad_pair)
        put_edges(edges.at[:, batch], *grad_pair)
        for copy in image_halo(parts, batch, edges, halo, send_edge, receive_edge):
            copy.start()
            moved.append(copy)
        offsets = [jnp.sum(jnp.sum(grad_pair[part], axis=1, keepdims=True), axis=0, keepdims=True) for part in range(2)]
        values = [offsets[0], offsets[1], penalty * penalty_part, own_loss]
        scalars[batch] = join_rows([jnp.broadcast_to(value, (1, TILE)) for value in values], 8)
    for stage in range(3):
        for batch in range(micro):
            sums.settle((stage, batch))
    for copy in moved:
        copy.wait()


def solve_all(filled, result, maps, normal, planes, rows_in, row_mask, extra, parts, length):
    micro, _, rows, wide = filled.shape
    shapes = [(micro, 2, rows, wide), (2, micro, 2 * REACH, wide), (micro, 8, TILE)]
    slots = (3, micro)
    return pl.pallas_call(
        functools.partial(solve_kernel, (micro, parts, length)),
        out_shape=[jax.ShapeDtypeStruct(shape, F32) for shape in shapes],
        in_specs=[in_vmem()] * 7 + [pl.BlockSpec(memory_space=pltpu.SMEM)],
        out_specs=[in_vmem()] * 3,
        scratch_shapes=[
            pltpu.VMEM((micro, 8, 2, rows, wide), F32),
            pltpu.VMEM((2, micro, 2 * REACH, wide), F32),
            pltpu.SemaphoreType.DMA((micro, 2)),
            pltpu.SemaphoreType.DMA((micro, 2)),
            pltpu.VMEM(slots + (8, TILE), F32),
            pltpu.VMEM(slots + (parts - 1, 8, TILE), F32),
            pltpu.SemaphoreType.DMA(slots + (parts - 1,)),
            pltpu.SemaphoreType.DMA(slots + (parts - 1,)),
        ],
        compiler_params=params(collective_id=5, has_side_effects=True),
        name="solve_all",
    )(filled, result, maps, normal, planes, rows_in, row_mask, extra)


def update_kernel(weights, means, squares, grads, rows_back, totals, rows_in, outs):
    first_grad, middle_grad, last_grad = grads
    affine = []
    for row in (1, 0):
        rows = [functools.reduce(jnp.add, [rows_back[layer, batch, row : row + 1] for batch in range(rows_back.shape[1])]) for layer in range(4)]
        affine.append(jnp.concatenate(rows, axis=0))
    extra = join_lanes([totals[index : index + 1, 0:1] for index in range(3)], 3)

    def put(group, at, gradient, refs):
        results = adamw(weights[group][at], gradient, means[group][at], squares[group][at], LEARN_RATES[group])
        for ref, value in zip(refs, results + (results[0].astype(BF16),)):
            ref[at] = value

    everything = (slice(None), slice(None))
    for tap in range(9):
        put(0, tap, first_grad[tap], outs[0:4])
        put(2, tap, last_grad[tap], outs[8:12])
        for layer in range(3):
            put(1, (layer, tap), middle_grad[layer, tap], outs[4:8])
    put(3, everything, affine[0], outs[12:15])
    put(4, everything, affine[1], outs[15:18])
    put(5, everything, extra, outs[18:21])
    outs[21][...] = totals[3:4, 0:1]
    outs[22][...] = rows_in[0, 0, 4:5, 0:1].astype(jnp.int32)


def update(weights, means, squares, grads, rows_back, totals, rows_in):
    shapes = []
    for group, weight in enumerate(weights):
        shapes += [jax.ShapeDtypeStruct(weight.shape, F32)] * 3
        if group < 3:
            shapes.append(jax.ShapeDtypeStruct(weight.shape, BF16))
    shapes += [jax.ShapeDtypeStruct((1, 1), F32), jax.ShapeDtypeStruct((1, 1), jnp.int32)]

    def kernel(*refs):
        update_kernel(refs[0:6], refs[6:12], refs[12:18], refs[18:21], refs[21], refs[22], refs[23], refs[24:])

    return pl.pallas_call(
        kernel,
        out_shape=shapes,
        in_specs=[in_vmem()] * 24,
        out_specs=[in_vmem()] * len(shapes),
        compiler_params=params(),
        name="update",
    )(*weights, *means, *squares, *grads, rows_back, totals, rows_in)


def fast_step(arrays, moments):
    (
        kspace, coil_maps, target, row_mask, foreground, anatomy, first_weight, middle_weight, last_weight, norm_gains, norm_shifts, extra_params,
    ) = arrays
    length = kspace.shape[-1]
    parts, images = lax.axis_size("row"), lax.axis_size("img")
    filled, maps, planes, normal, middle_back, last_back, layers, coefs, rows_out, images_out, result = forward(
        kspace[:, 0], coil_maps[:, 0], target[:, 0], foreground[:, 0], row_mask, anatomy.transpose(1, 0),
        first_weight.transpose(0, 2, 1), middle_weight, last_weight, norm_gains, norm_shifts, parts, images,
    )
    grad, halo, scalars = solve_all(
        filled, result, maps, normal, planes, rows_out, row_mask, extra_params, parts, length
    )
    first_sums, middle_sums, last_sums, rows_back = backward(
        grad, halo, (layers, coefs, rows_out, images_out), (middle_back, last_back), parts, images, length
    )
    *grads, totals = reduce_all(first_sums, middle_sums, last_sums, scalars, parts, images)

    def turn(group):
        first, middle, last, gains, shifts, extra = group
        return [first.transpose(0, 2, 1), middle, last, gains, shifts, extra.reshape(1, 3)]

    weights = (first_weight, middle_weight, last_weight, norm_gains, norm_shifts, extra_params)
    means, squares = zip(*moments)
    outs = list(update(turn(weights), turn(means), turn(squares), grads, rows_back, totals, rows_out))
    outs[0:4] = [value.transpose(0, 2, 1) for value in outs[0:4]]
    outs[18:21] = [value.reshape(3) for value in outs[18:21]]
    return tuple(outs[:21]) + (outs[21].reshape(()), outs[22].reshape(()))


def local(
    kspace,
    coil_maps,
    target,
    row_mask,
    foreground,
    anatomy,
    first_weight,
    middle_weight,
    last_weight,
    norm_gains,
    norm_shifts,
    extra_params,
    first_mean,
    first_square,
    middle_mean,
    middle_square,
    last_mean,
    last_square,
    gains_mean,
    gains_square,
    shifts_mean,
    shifts_square,
    extra_mean,
    extra_square,
):
    arrays = (
        kspace, coil_maps, target, row_mask, foreground, anatomy, first_weight, middle_weight, last_weight, norm_gains, norm_shifts, extra_params,
    )
    moments = (
        (first_mean, first_square),
        (middle_mean, middle_square),
        (last_mean, last_square),
        (gains_mean, gains_square),
        (shifts_mean, shifts_square),
        (extra_mean, extra_square),
    )
    if fits(kspace, first_weight, lax.axis_size("row")):
        return fast_step(arrays, moments)
    totals, pixel_total = general_local(arrays)
    params = (first_weight, middle_weight, last_weight, norm_gains, norm_shifts, extra_params)
    results = []
    for group in range(6):
        updated, first_new, second_new = adamw(
            params[group], totals[group], moments[group][0], moments[group][1], LEARN_RATES[group]
        )
        results.extend([updated, first_new, second_new])
        if group < 3:
            results.append(updated.astype(jnp.bfloat16))
    return tuple(results) + (totals[6], pixel_total.astype(jnp.int32))


def solution(mesh):
    in_specs = (
        P(None, "img", None, None, "row", None),
        P(None, "img", None, None, "row", None),
        P(None, "img", None, "row", None),
        P(None, "img", None),
        P(None, "img", "row", None),
        P(None, "img"),
        P(),
        P(),
        P(),
        P(),
        P(),
        P(),
        P(),
        P(),
        P(),
        P(),
        P(),
        P(),
        P(),
        P(),
        P(),
        P(),
        P(),
        P(),
    )
    out_specs = (
        P(),
        P(),
        P(),
        P(),
        P(),
        P(),
        P(),
        P(),
        P(),
        P(),
        P(),
        P(),
        P(),
        P(),
        P(),
        P(),
        P(),
        P(),
        P(),
        P(),
        P(),
        P(),
        P(),
    )
    return jax.shard_map(local, mesh=mesh, in_specs=in_specs, out_specs=out_specs, check_vma=False)
```

```python
import functools

import jax
import jax.numpy as jnp
import numpy as np
from jax import lax
from jax.experimental import pallas as pl
from jax.experimental.pallas import tpu as pltpu
from jax.sharding import PartitionSpec as P

COILS = 16
BRAIN_COILS = 12
UNROLLS = 1
CG_STEPS = 2
STEP = 10


PRECISE = lax.Precision.HIGHEST
EPS_NORM = 1e-05
BETA_ONE = 0.9
BETA_TWO = 0.999
ADAM_EPS = 1e-08
DECAY_RATE = 0.01
LEARN_RATES = (0.3, 0.05, 0.05, 0.4, 0.4, 0.4)


def with_halo(cells, sides, width):
    for axis, dim in sides:
        count = lax.axis_size(axis)
        ends = count - 1
        head = lax.slice_in_dim(cells, 0, width, axis=dim)
        tail = lax.slice_in_dim(cells, cells.shape[dim] - width, cells.shape[dim], axis=dim)
        cells = jnp.concatenate(
            [
                lax.ppermute(tail, axis, [(i, (i + 1) % count) for i in range(ends)]),
                cells,
                lax.ppermute(head, axis, [((i + 1) % count, i) for i in range(ends)]),
            ],
            axis=dim,
        )
    return cells


def dft_table(length, direction):
    index = jnp.arange(length, dtype=jnp.int32)
    phase = (index[:, None] * index[None, :] % length).astype(jnp.float32) * (2.0 * jnp.pi / length)
    factor = 1.0 / jnp.sqrt(jnp.float32(length))
    cosine = jnp.cos(phase) * factor
    sine = jnp.sin(phase) * factor * direction
    return jnp.stack([jnp.stack([cosine, -sine], 1), jnp.stack([sine, cosine], 1)], 0)


def along_width(field, table):
    return jnp.einsum("bcprw,pwqk->bcqrk", field, table, precision=PRECISE)


def along_height(field, table):
    return jnp.einsum("bcprw,prqk->bcqkw", field, table, precision=PRECISE)


def expand(image, maps):
    real_part, imag_part = (image[:, None, 0], image[:, None, 1])
    maps_re, maps_im = (maps[:, :, 0], maps[:, :, 1])
    return jnp.stack(
        [maps_re * real_part - maps_im * imag_part, maps_re * imag_part + maps_im * real_part], 2
    )


def combine(field, maps):
    field_re, field_im = (field[:, :, 0], field[:, :, 1])
    maps_re, maps_im = (maps[:, :, 0], maps[:, :, 1])
    return jnp.stack(
        [
            jnp.sum(maps_re * field_re + maps_im * field_im, 1),
            jnp.sum(maps_re * field_im - maps_im * field_re, 1),
        ],
        1,
    )


def to_columns(field):
    return lax.all_to_all(
        field.astype(jnp.bfloat16), "row", split_axis=4, concat_axis=3, tiled=True
    ).astype(field.dtype)


def to_rows(field):
    return lax.all_to_all(
        field.astype(jnp.bfloat16), "row", split_axis=3, concat_axis=4, tiled=True
    ).astype(field.dtype)


def make_normal(maps, mask_rows, forward, inverse, measured):
    zero_filled = combine(to_rows(along_height(measured * mask_rows, inverse)), maps)

    def normal(image):
        spectrum = to_columns(along_width(expand(image, maps), forward))
        spectrum = along_height(spectrum, forward) * mask_rows
        spectrum = to_rows(along_height(spectrum, inverse))
        return combine(along_width(spectrum, inverse), maps)

    return (normal, zero_filled)


def inner(left, right):
    return jnp.sum(left * right, axis=(1, 2, 3))


def per_image(values):
    return values[:, None, None, None]


def row_sums(values):
    return lax.psum(values, "row")


def solve(rhs, penalty, normal):
    state = jnp.zeros_like(rhs)
    residue = rhs
    search = rhs
    norm_now = row_sums(inner(residue, residue))
    kept = []
    for iterate in range(CG_STEPS):
        mapped = normal(search) + penalty * search
        curvature = row_sums(inner(search, mapped))
        stepsize = norm_now / curvature
        state = state + per_image(stepsize) * search
        residue = residue - per_image(stepsize) * mapped
        norm_next = row_sums(inner(residue, residue))
        kept.append((search, mapped, residue, norm_now, norm_next, curvature))
        search = residue + per_image(norm_next / norm_now) * search
        norm_now = norm_next
    return (state, kept)


def solve_backward(state_grad, kept, rhs, denoised, penalty, normal):
    search_grad = jnp.zeros_like(rhs)
    residue_grad = jnp.zeros_like(rhs)
    norm_grad = jnp.zeros(rhs.shape[0], jnp.float32)
    penalty_part = jnp.float32(0.0)
    for iterate in reversed(range(CG_STEPS)):
        search, mapped, residue, norm_now, norm_next, curvature = kept[iterate]
        factor_grad, along_search, joint_mapped, residue_mapped = lax.psum(
            (
                inner(search_grad, search),
                inner(state_grad, search),
                inner(residue_grad + search_grad, mapped),
                inner(residue, mapped),
            ),
            "row",
        )
        stepsize = norm_now / curvature
        factor = norm_next / norm_now
        norm_total = norm_grad + factor_grad / norm_now
        residue_full = residue_grad + search_grad + per_image(2.0 * norm_total) * residue
        stepsize_grad = along_search - (joint_mapped + 2.0 * norm_total * residue_mapped)
        curvature_grad = -stepsize_grad * norm_now / (curvature * curvature)
        mapped_grad = -per_image(stepsize) * residue_full + per_image(curvature_grad) * search
        penalty_part = penalty_part + jnp.sum(mapped_grad * search)
        search_grad = (
            per_image(factor) * search_grad
            + per_image(stepsize) * state_grad
            + per_image(curvature_grad) * mapped
            + normal(mapped_grad)
            + penalty * mapped_grad
        )
        residue_grad = residue_full
        norm_grad = -factor_grad * norm_next / (norm_now * norm_now) + stepsize_grad / curvature
    rhs_grad = residue_grad + search_grad + per_image(2.0 * norm_grad) * rhs
    penalty_part = penalty_part + jnp.sum(rhs_grad * denoised)
    return (penalty * rhs_grad, penalty_part)


def conv_forward(activation, weight):
    height, breadth = (activation.shape[2], activation.shape[3])
    padded = with_halo(activation, (("row", 2),), 1)
    padded = jnp.pad(padded, ((0, 0), (0, 0), (0, 0), (1, 1)))
    summed = jnp.zeros((activation.shape[0], weight.shape[1], height, breadth), jnp.float32)
    for tap_index in range(9):
        window = padded[
            :, :, tap_index // 3 : tap_index // 3 + height, tap_index % 3 : tap_index % 3 + breadth
        ]
        summed = summed + jnp.einsum(
            "oi,birw->borw", weight[tap_index], window, preferred_element_type=jnp.float32
        )
    return (summed, padded)


def conv_backward(upstream, padded, weight, need_input):
    height, breadth = (upstream.shape[2], upstream.shape[3])
    weight_grad = jnp.stack(
        [
            jnp.einsum(
                "borw,birw->oi",
                upstream,
                padded[
                    :,
                    :,
                    tap_index // 3 : tap_index // 3 + height,
                    tap_index % 3 : tap_index % 3 + breadth,
                ],
                preferred_element_type=jnp.float32,
            )
            for tap_index in range(9)
        ]
    )
    if not need_input:
        return (weight_grad, None)
    widened = with_halo(upstream, (("row", 2),), 1)
    widened = jnp.pad(widened, ((0, 0), (0, 0), (0, 0), (1, 1)))
    summed = jnp.zeros((upstream.shape[0], weight.shape[2], height, breadth), jnp.float32)
    for tap_index in range(9):
        start_r = 2 - tap_index // 3
        start_c = 2 - tap_index % 3
        window = widened[:, :, start_r : start_r + height, start_c : start_c + breadth]
        summed = summed + jnp.einsum(
            "oi,borw->birw", weight[tap_index], window, preferred_element_type=jnp.float32
        )
    return (weight_grad, summed)


def norm_sums(values):
    return lax.psum(values, ("img", "row"))


def channel(values):
    return values[None, :, None, None]


def cnn_forward(image, weights, gains, shifts, offset, pixels):
    activation = image.astype(jnp.bfloat16)
    kept = []
    for layer_index in range(4):
        linear, padded = conv_forward(activation, weights[layer_index])
        average = norm_sums(jnp.sum(linear, axis=(0, 2, 3))) / pixels
        centred = linear - channel(average)
        spread = norm_sums(jnp.sum(centred * centred, axis=(0, 2, 3))) / pixels
        inv_std = lax.rsqrt(spread + EPS_NORM)
        normed = centred * channel(inv_std)
        shaped = channel(gains[layer_index]) * normed + channel(shifts[layer_index])
        activation = jax.nn.silu(shaped).astype(jnp.bfloat16)
        kept.append((padded, normed, shaped, inv_std))
    result, padded = conv_forward(activation, weights[4])
    kept.append(padded)
    return (image + result + channel(offset), kept)


def cnn_backward(denoised_grad, kept, weights, gains, pixels, need_input):
    offset_grad = jnp.sum(denoised_grad, axis=(0, 2, 3))
    weight_grads = [None] * 5
    gain_grads = [None] * 4
    shift_grads = [None] * 4
    weight_grads[4], upstream = conv_backward(
        denoised_grad.astype(jnp.bfloat16), kept[4], weights[4], True
    )
    for layer_index in (3, 2, 1, 0):
        padded, normed, shaped, inv_std = kept[layer_index]
        sigmoid_val = jax.nn.sigmoid(shaped)
        shaped_grad = upstream * sigmoid_val * (1.0 + shaped * (1.0 - sigmoid_val))
        shift_local = jnp.sum(shaped_grad, axis=(0, 2, 3))
        gain_local = jnp.sum(shaped_grad * normed, axis=(0, 2, 3))
        shift_total, gain_total = lax.psum((shift_local, gain_local), ("img", "row"))
        gain_vec = gains[layer_index]
        linear_grad = channel(inv_std) * (
            shaped_grad * channel(gain_vec)
            - channel(gain_vec * shift_total / pixels)
            - normed * channel(gain_vec * gain_total / pixels)
        )
        shift_grads[layer_index] = shift_local
        gain_grads[layer_index] = gain_local
        weight_grads[layer_index], upstream = conv_backward(
            linear_grad.astype(jnp.bfloat16),
            padded,
            weights[layer_index],
            layer_index > 0 or need_input,
        )
    image_grad = None
    return (image_grad, weight_grads, jnp.stack(gain_grads), jnp.stack(shift_grads), offset_grad)


def adamw(weight, gradient, moment_one, moment_two, rate):
    first_new = BETA_ONE * moment_one + (1.0 - BETA_ONE) * gradient
    second_new = BETA_TWO * moment_two + (1.0 - BETA_TWO) * gradient * gradient
    corrected = first_new / (1.0 - BETA_ONE**STEP)
    divisor = jnp.sqrt(second_new / (1.0 - BETA_TWO**STEP)) + ADAM_EPS
    updated = weight - rate * (corrected / divisor + DECAY_RATE * weight)
    return (updated, first_new, second_new)


def general_local(arrays):
    (
        kspace, coil_maps, target, row_mask, foreground, anatomy, first_weight, middle_weight, last_weight, norm_gains, norm_shifts, extra_params,
    ) = arrays
    length = kspace.shape[-1]
    forward = dft_table(length, 1.0)
    inverse = dft_table(length, -1.0)
    pixel_total = lax.psum(jnp.sum(foreground).astype(jnp.float32), ("img", "row"))
    inv_count = 1.0 / pixel_total
    middle_low = middle_weight.astype(jnp.bfloat16)
    conv_weights = [
        first_weight.astype(jnp.bfloat16),
        middle_low[0],
        middle_low[1],
        middle_low[2],
        last_weight.astype(jnp.bfloat16),
    ]
    penalty = jnp.exp(extra_params[2])
    offset = extra_params[:2]
    images_here = kspace.shape[1]
    pixels = images_here * kspace.shape[4] * length * lax.axis_size("img") * lax.axis_size("row")
    first_grad = jnp.zeros_like(first_weight)
    middle_grad = jnp.zeros_like(middle_weight)
    last_grad = jnp.zeros_like(last_weight)
    gains_grad = jnp.zeros_like(norm_gains)
    shifts_grad = jnp.zeros_like(norm_shifts)
    offset_grad = jnp.zeros((2,), jnp.float32)
    penalty_grad = jnp.float32(0.0)
    loss_part = jnp.float32(0.0)
    for microbatch in range(kspace.shape[0]):
        limit = jnp.where(anatomy[microbatch] == 0, BRAIN_COILS, COILS)
        coil_on = (jnp.arange(kspace.shape[2])[None, :] < limit[:, None]).astype(jnp.float32)
        maps = coil_maps[microbatch] * coil_on[:, :, None, None, None]
        mask_rows = row_mask[microbatch].astype(jnp.float32)[:, None, None, :, None]
        measured = to_columns(along_width(kspace[microbatch], inverse))
        normal, zero_filled = make_normal(maps, mask_rows, forward, inverse, measured)
        state = zero_filled
        unroll = 0
        denoised, cnn_kept = cnn_forward(
            state, conv_weights, norm_gains, norm_shifts, offset, pixels
        )
        rhs = zero_filled + penalty * denoised
        state, cg_kept = solve(rhs, penalty, normal)
        saved = [(cnn_kept, cg_kept, rhs, denoised)]
        fg_mask = foreground[microbatch].astype(jnp.float32)[:, None]
        difference = state - target[microbatch]
        loss_part = loss_part + jnp.sum(fg_mask * difference * difference)
        state_grad = inv_count * 2.0 * fg_mask * difference
        for unroll in reversed(range(UNROLLS)):
            cnn_kept, cg_kept, rhs, denoised = saved[unroll]
            denoised_grad, penalty_part = solve_backward(
                state_grad, cg_kept, rhs, denoised, penalty, normal
            )
            penalty_grad = penalty_grad + penalty_part
            state_grad, weight_grads, gain_part, shift_part, offset_part = cnn_backward(
                denoised_grad, cnn_kept, conv_weights, norm_gains, pixels, unroll > 0
            )
            first_grad = first_grad + weight_grads[0]
            middle_grad = middle_grad + jnp.stack(weight_grads[1:4])
            last_grad = last_grad + weight_grads[4]
            gains_grad = gains_grad + gain_part
            shifts_grad = shifts_grad + shift_part
            offset_grad = offset_grad + offset_part
    extra_grad = jnp.concatenate([offset_grad, (penalty * penalty_grad)[None]])
    totals = lax.psum(
        (first_grad, middle_grad, last_grad, gains_grad, shifts_grad, extra_grad, loss_part),
        ("img", "row"),
    )
    return totals, pixel_total


BF16 = jnp.bfloat16
F32 = jnp.float32
MESH = pl.DeviceIdType.MESH
TILE = 128
BLOCK = 8
BACK_REACH = 3
FIRST_REACH = 6
GROUP = 4
FORWARD_HOOK = 4
BACK_HOOK = 5
REACH = 8
VMEM_BYTES = 58 * 1024 * 1024


def padded(length):
    return -(-length // TILE) * TILE


def fits(kspace, first_weight, mesh_rows):
    micro, images, coils, _, rows, length = kspace.shape
    channels = first_weight.shape[1]
    return (
        images == 1
        and micro == 2
        and 2 * channels == TILE
        and channels % 16 == 0
        and rows * mesh_rows == length
        and mesh_rows & (mesh_rows - 1) == 0
        and rows % BLOCK == 0
        and (2 * rows) % 16 == 0
        and (coils * rows) % TILE == 0
        and padded(length) > length
    )


def phases(length):
    index = np.arange(length)
    angle = 2.0 * np.pi * (np.outer(index, index) % length) / length
    return np.cos(angle) / np.sqrt(length), np.sin(angle) / np.sqrt(length)


def high_low(table):
    high = table.astype(BF16)
    low = (table - high.astype(F32)).astype(BF16)
    return high, low


def np_high_low(table):
    table = np.asarray(table, np.float32)
    high = table.astype(BF16)
    low = (table - high.astype(np.float32)).astype(BF16)
    return jnp.asarray(high), jnp.asarray(low)


def dot(left, right):
    return jnp.dot(left, right, preferred_element_type=F32)


def dot_nt(left, right):
    return lax.dot_general(left, right, (((1,), (1,)), ((), ())), preferred_element_type=F32)


def knock(peers):
    barrier = pltpu.get_barrier_semaphore()
    for peer in peers:
        pl.semaphore_signal(barrier, inc=1, device_id=peer, device_id_type=MESH)


def admit(peers):
    pl.semaphore_wait(pltpu.get_barrier_semaphore(), len(peers))


def partner(me, step):
    other, bit = 0, 1
    while bit <= step:
        own = lax.rem(lax.div(me, bit), 2)
        other = other + bit * (1 - own if step & bit else own)
        bit *= 2
    return other + lax.div(me, bit) * bit


def row_peers(rows):
    image, row = lax.axis_index("img"), lax.axis_index("row")
    steps = sorted(range(1, rows), key=lambda step: (-step.bit_length(), step))
    return [(image, partner(row, step)) for step in steps]


def image_peers(images):
    image, row = lax.axis_index("img"), lax.axis_index("row")
    return [(lax.rem(image + step, images), row) for step in range(1, images)]


def remote(source, target, send, receive, peer):
    return pltpu.make_async_remote_copy(
        src_ref=source,
        dst_ref=target,
        send_sem=send,
        recv_sem=receive,
        device_id=peer,
        device_id_type=MESH,
    )


def params(vmem=VMEM_BYTES, **kwargs):
    return pltpu.CompilerParams(vmem_limit_bytes=vmem, **kwargs)


def in_vmem():
    return pl.BlockSpec(memory_space=pltpu.VMEM)


def anywhere():
    return pl.BlockSpec(memory_space=pl.ANY)


def three_parts(values):
    high = values.astype(BF16)
    rest = values - high.astype(F32)
    middle = rest.astype(BF16)
    return high, middle, (rest - middle.astype(F32)).astype(BF16)


def join_lanes(pieces, wide):
    short = wide - sum(piece.shape[1] for piece in pieces)
    if short:
        pieces = pieces + [jnp.zeros((pieces[0].shape[0], short), pieces[0].dtype)]
    return jnp.concatenate(pieces, axis=1)


def join_rows(pieces, height):
    short = height - sum(piece.shape[0] for piece in pieces)
    if short:
        pieces = pieces + [jnp.zeros((short, pieces[0].shape[1]), pieces[0].dtype)]
    return jnp.concatenate(pieces, axis=0)


def start_exchange(
    sizes, meet, tables, kspace, maps, target, foreground, row_mask, anatomy, first, middle, last, turn_high, turn_low, pick, cosine, sine,
    fourier_high, fourier_low,
    filled, maps_out, halo, planes, normal, first_table, middle_tables, last_table, middle_back, last_back, counted,
    fields, staged, spread, flat, landed, edges, loaded, send, receive, own, send_flat, receive_flat, send_edge, receive_edge,
):
    micro, coils, rows, length, parts = sizes
    wide = padded(length)
    image, me = lax.axis_index("img"), lax.axis_index("row")
    peers = row_peers(parts)
    slots = [(batch, kind) for batch in range(micro) for kind in (1, 0)]
    loads = {}

    def load_field(index):
        if index < len(slots):
            batch, kind = slots[index]
            for part in range(2):
                source = (kspace, maps)[kind].at[batch, :, part]
                loads[index, part] = pltpu.make_async_copy(source, fields.at[index % 2, part], loaded.at[index, part])
                loads[index, part].start()

    load_field(0)
    for copy in tables:
        copy.start()
    load_field(1)
    arrivals = [[] for _ in range(micro)]
    slabs = 2 * rows
    def send_slot(index):
        batch, kind = slots[index]
        total = None
        for part in range(2):
            loads[index, part].wait()
            field = fields[index % 2, part].reshape(coils * rows, length)
            if kind == 0:
                high, low = high_low(field)
                term = (
                    dot_nt(turn_high[part], high)
                    + dot_nt(turn_low[part], high)
                    + dot_nt(turn_high[part], low)
                )
            else:
                term = dot_nt(pick[part], field.astype(BF16))
            total = term if total is None else total + term
        slot = 2 * batch + kind
        staged[slot] = total.astype(BF16).reshape(parts, slabs, coils * rows)
        load_field(index + 2)
        if index == 0:
            meet()
        for step, peer in enumerate(peers):
            copy = remote(
                staged.at[slot, peer[1]], spread.at[slot, me], send.at[slot, step], receive.at[slot, step], peer
            )
            copy.start()
            arrivals[batch].append(copy)
        local = pltpu.make_async_copy(staged.at[slot, me], spread.at[slot, me], own.at[slot])
        local.start()
        arrivals[batch].append(local)

    for index in range(len(slots) - 1):
        send_slot(index)
        if index == 0:
            for copy in tables:
                copy.wait()
    put_flat = functools.partial(
        exchange_planes, sizes, target, foreground, pick, counted, flat, landed, send_flat, receive_flat, me, peers
    )
    flats = []
    for batch in range(micro):
        chosen = join_lanes([row_mask[batch].astype(F32)], wide)
        cos_on, sin_on = cosine[...] * chosen, sine[...] * chosen

        def product(left, right):
            return jnp.dot(left, right, precision=PRECISE, preferred_element_type=F32)

        real = product(cos_on, cosine[...]) + product(sin_on, sine[...])
        imag = product(sin_on, cosine[...]) - product(cos_on, sine[...])
        diagonal = [lax.broadcasted_iota(jnp.int32, real.shape, axis) for axis in range(2)]
        real = jnp.where(diagonal[0] == diagonal[1], 0.0, real)
        for block, value in (((0, 0), real), ((0, 1), -imag), ((1, 0), imag), ((1, 1), real)):
            normal[batch, pl.ds(block[0] * wide, wide), pl.ds(block[1] * wide, wide)] = value.astype(BF16)
    put_tables(first, middle, last, first_table, middle_tables, last_table, middle_back, last_back)

    def arrive(batch):
        for copy in arrivals[batch]:
            copy.wait()
        knee = jnp.where(anatomy[0:1, batch : batch + 1] == 0, 0.0, 1.0)
        real, imag = zero_fill(
            (coils, rows, parts, wide),
            knee,
            spread.at[2 * batch],
            spread.at[2 * batch + 1],
            join_lanes([row_mask[batch].astype(F32)], wide),
            fourier_high,
            fourier_low,
            maps_out.at[batch],
        )
        put_pair(filled.at[batch], (real, imag))
        put_edges(edges.at[:, batch], real, imag)
        moved = image_halo(parts, batch, edges, halo, send_edge, receive_edge)
        for copy in moved:
            copy.start()
        if batch == 0:
            send_slot(len(slots) - 1)
            flats.extend(put_flat())
        for copy in moved:
            copy.wait()

    def finish():
        for copy in flats:
            copy.wait()
        for batch in range(micro):
            for plane in range(3):
                at = (3 * batch + plane) * rows
                pieces = [landed[block, :, at : at + rows] for block in range(parts)]
                planes[batch, plane] = join_lanes(pieces, wide)

    return arrive, finish


def exchange_planes(
    sizes, target, foreground, pick, counted, flat, landed, send_flat, receive_flat, me, peers
):
    micro, _, rows, length, parts = sizes
    shown = [foreground[batch].astype(F32) for batch in range(micro)]
    count = functools.reduce(jnp.add, [jnp.sum(jnp.sum(s, axis=1, keepdims=True), axis=0, keepdims=True) for s in shown])
    counted[...] = jnp.broadcast_to(count, (1, TILE))
    stack = []
    for batch in range(micro):
        stack += [target[batch, 0], target[batch, 1], shown[batch]]
    stack = jnp.concatenate(stack, axis=0)
    plain = pick[0].reshape(parts, 2 * rows, length)[:, :rows].reshape(length, length)
    turned = functools.reduce(jnp.add, [dot_nt(plain, piece) for piece in three_parts(stack)])
    lanes = flat.shape[2]
    flat[...] = join_lanes([turned], lanes).reshape(parts, rows, lanes)
    landed[me] = flat[me]
    flats = []
    for step, peer in enumerate(peers):
        copy = remote(flat.at[peer[1]], landed.at[me], send_flat.at[step], receive_flat.at[step], peer)
        copy.start()
        flats.append(copy)
    return flats


def put_tables(first, middle, last, first_table, middle_tables, last_table, middle_back, last_back):
    taps = range(3)
    turned = [join_rows([first[tap]], 8).T[:, :2] for tap in range(9)]
    first_table[...] = jnp.concatenate(
        [join_lanes([turned[3 * kr + kw] for kr in taps], 16) for kw in taps], axis=0
    ).astype(BF16)
    last_table[...] = jnp.concatenate(
        [join_rows([jnp.concatenate([last[3 * kr + kw] for kr in taps], axis=1)], 8) for kw in taps], axis=0
    ).astype(BF16)
    turned = [join_rows([last[tap]], 8).T[:, :2] for tap in range(9)]
    last_back[...] = jnp.concatenate(
        [join_lanes([turned[3 * (2 - m) + 2 - n] for m in taps], 16) for n in taps], axis=0
    ).astype(BF16)
    for layer in range(3):
        weights = [middle[layer, tap] for tap in range(9)]
        turned = [weight.T for weight in weights]
        middle_tables[layer] = jnp.concatenate(
            [jnp.concatenate([weights[3 * kr + kw] for kr in taps], axis=1) for kw in taps], axis=0
        ).astype(BF16)
        middle_back[layer] = jnp.concatenate(
            [jnp.concatenate([turned[3 * (2 - m) + 2 - n] for m in taps], axis=1) for n in taps], axis=0
        ).astype(BF16)


def gather_lanes(blocks, coil, rows, wide):
    pieces = [block[:, coil * rows : (coil + 1) * rows] for block in blocks]
    height = pieces[0].shape[0]
    short = wide - rows * len(pieces)
    return jnp.concatenate(pieces + [jnp.zeros((height, short), pieces[0].dtype)], axis=1)


def zero_fill(sizes, knee, fields, senses, chosen, fourier_high, fourier_low, maps_out):
    coils, rows, parts, wide = sizes
    real = jnp.zeros((rows, wide), F32)
    imag = jnp.zeros((rows, wide), F32)
    chosen = chosen.astype(BF16)
    group = 4
    for first in range(0, coils, group):
        stack = []
        for coil in range(first, first + group):
            sense = gather_lanes([senses[s] for s in range(parts)], coil, rows, wide)
            maps_out[coil] = sense if coil < BRAIN_COILS else sense * knee.astype(BF16)
            stack.append(gather_lanes([fields[s] for s in range(parts)], coil, rows, wide) * chosen)
        stack = jnp.concatenate(stack, axis=0)
        turned = dot(stack, fourier_high[...]) + dot(stack, fourier_low[...])
        for place in range(group):
            top = 2 * rows * place
            upper, lower = turned[top : top + rows], turned[top + rows : top + 2 * rows]
            field_re = upper[:, :wide] - lower[:, wide:]
            field_im = upper[:, wide:] + lower[:, :wide]
            sense = maps_out[first + place].astype(F32)
            sense_re, sense_im = sense[:rows], sense[rows:]
            real = real + sense_re * field_re + sense_im * field_im
            imag = imag + sense_re * field_im - sense_im * field_re
    return real, imag


def put_edges(edges, real, imag):
    rows = real.shape[0]
    edges[0] = jnp.concatenate([real[:REACH], imag[:REACH]], axis=0)
    edges[1] = jnp.concatenate([real[rows - REACH :], imag[rows - REACH :]], axis=0)


def lane_row(columns):
    return jnp.sum(columns.T, axis=0, keepdims=True)


def spread_row(row):
    return jnp.broadcast_to(row, (TILE, row.shape[1])).T


def padded_rows(rows):
    return join_rows([join_lanes([row], TILE) for row in rows], 8)


def merge(sums, squares, count):
    total = functools.reduce(jnp.add, sums)
    mean = total / (count * len(sums))
    square = None
    for part, own in zip(sums, squares):
        shift = part / count - mean
        term = own + count * shift * shift
        square = term if square is None else square + term
    return total, square


def repeat_lanes(block, wide):
    return jnp.concatenate([block] * (wide // TILE), axis=1)


def lane_mask(length, wide):
    whole = length // TILE * TILE

    def clear(values):
        tail = values[:, whole:]
        keep = lax.broadcasted_iota(jnp.int32, tail.shape, 1) < length - whole
        return jnp.concatenate([values[:, :whole], jnp.where(keep, tail, 0.0)], axis=1)

    return clear


def fold(values):
    parts = [values[:, at : at + TILE] for at in range(0, values.shape[1], TILE)]
    return functools.reduce(jnp.add, parts)


def put_shifted(stack, values, at):
    channels, wide = values.shape
    stack[0:channels, at : at + wide] = pltpu.roll(values, 1, 1)
    stack[channels : 2 * channels, at : at + wide] = values
    stack[2 * channels : 3 * channels, at : at + wide] = pltpu.roll(values, wide - 1, 1)


def lane_at(column, wide):
    return pl.multiple_of(column * wide, TILE) if not isinstance(column, int) else column * wide


class Sums:
    def __init__(self, parts, images, refs):
        self.message, self.held, self.second, self.held_second, self.send, self.receive = refs
        self.rows, self.cols = row_peers(parts), image_peers(images)

    def copies(self, slot, stage):
        source, target = ((self.message, self.held), (self.second, self.held_second))[stage]
        peers = (self.rows, self.cols)[stage]
        base = stage * len(self.rows)
        return [
            remote(
                source.at[slot],
                target.at[slot + (index,)],
                self.send.at[slot + (base + index,)],
                self.receive.at[slot + (base + index,)],
                peer,
            )
            for index, peer in enumerate(peers)
        ]

    def start(self, slot, stage, values):
        (self.message, self.second)[stage][slot] = values
        for copy in self.copies(slot, stage):
            copy.start()

    def collect(self, slot, stage):
        blocks = [(self.message, self.second)[stage][slot]]
        for index, copy in enumerate(self.copies(slot, stage)):
            copy.wait_recv()
            blocks.append((self.held, self.held_second)[stage][slot + (index,)])
        return blocks

    def settle(self, slot, stages=(0, 1)):
        for stage in stages:
            for copy in self.copies(slot, stage):
                copy.wait_send()

    @staticmethod
    def scratch(slots, parts, images):
        return [
            pltpu.VMEM(slots + (8, TILE), F32),
            pltpu.VMEM(slots + (parts - 1, 8, TILE), F32),
            pltpu.VMEM(slots + (8, TILE), F32),
            pltpu.VMEM(slots + (max(images - 1, 1), 8, TILE), F32),
            pltpu.SemaphoreType.DMA(slots + (parts + images - 2,)),
            pltpu.SemaphoreType.DMA(slots + (parts + images - 2,)),
        ]


class Ends:
    def __init__(self, parts):
        me = lax.axis_index("row")
        self.left, self.right = me > 0, me < parts - 1

    def clear(self, values, column, width):
        if column < 0:
            return jnp.where(self.left, values, 0.0)
        if column >= width:
            return jnp.where(self.right, values, 0.0)
        return values


def ring_pass(table, take, fill, emit, out_rows, width, wide, hook, hook_at):
    fill(0)
    fill(1)
    product = dot(table, take(0))
    older = product[0:out_rows, :wide] + product[out_rows : 2 * out_rows, wide:]
    newer = product[0:out_rows, wide:]
    last = width // 2
    for couple in range(1, last + 1):
        if hook is not None and couple == last * hook_at // 8:
            hook()
        product = dot(table, take(couple))
        if couple < last:
            fill(couple + 1)
        for place in range(2):
            piece = product[:, place * wide : (place + 1) * wide]
            emit(2 * couple - 2 + place, older + piece[2 * out_rows : 3 * out_rows])
            older = newer + piece[out_rows : 2 * out_rows]
            newer = piece[0:out_rows]


def silu_half(values, scale, offset):
    half = values * scale + offset
    return half, jnp.tanh(half)


def put_image(image, halo, place, stack, ends, reach):
    _, width, wide = image.shape
    blocks = {-REACH: (halo[0, place, :REACH], halo[0, place, REACH:]), width: (halo[1, place, :REACH], halo[1, place, REACH:])}
    for first in range(0, width, 8):
        blocks[first] = (image[0, first : first + 8], image[1, first : first + 8])
    for first, (real, imag) in blocks.items():
        real, imag = ends.clear(real, first, width), ends.clear(imag, first, width)
        rolled = [pltpu.roll(real, 1, 1), pltpu.roll(imag, 1, 1), real, imag, pltpu.roll(real, wide - 1, 1), pltpu.roll(imag, wide - 1, 1)]
        for offset in range(8):
            at = first + offset + reach
            if 0 <= at < width + 2 * reach:
                rows = [block[offset : offset + 1] for block in rolled]
                stack[:, at * wide : (at + 1) * wide] = join_rows(rows, 16).astype(BF16)


def image_halo(parts, batch, edges, halo, send, receive):
    image, me = lax.axis_index("img"), lax.axis_index("row")
    left, right = lax.rem(me + parts - 1, parts), lax.rem(me + 1, parts)
    places = [((image, left), 0), ((image, right), 1)]
    return [
        remote(edges.at[side, batch], halo.at[1 - side, batch], send.at[batch, side], receive.at[batch, side], peer)
        for peer, side in places
    ]


def forward_kernel(
    sizes, kspace, maps, target, foreground, row_mask, anatomy, first, middle_weight, last, turn_high, turn_low, pick,
    cosine, sine, fourier_high, fourier_low, gains, shifts,
    filled, maps_out, planes, normal, middle_back, last_back, layers, coefs, rows_out, images_out, result,
    fields, staged, spread, flat, landed, edges, halo_image, first_table, middle_tables, last_table, counted,
    loaded, send, receive, own, send_flat, receive_flat, send_edge, receive_edge,
    tables_here, tables_loaded,
    lin, even, odd, pivot, total, square, *refs,
):
    micro, coils, rows, length, parts, images = sizes
    _, _, width, wide = filled.shape
    channels = lin.shape[3]
    count = width * length
    whole = length // TILE * TILE
    stacks = (even, odd)
    sums = Sums(parts, images, refs[:6])
    (saved,) = refs[6:]
    ends = Ends(parts)
    clear = lane_mask(length, wide)
    knock(sums.rows + sums.cols)
    tables = [
        pltpu.make_async_copy(source, target, tables_loaded.at[index])
        for index, (source, target) in enumerate(
            zip((turn_high, turn_low, cosine, sine, fourier_high, fourier_low), tables_here)
        )
    ]
    turn_high, turn_low, cosine, sine, fourier_high, fourier_low = tables_here
    arrive, finish = start_exchange(
        (micro, coils, rows, length, parts), lambda: admit(sums.rows + sums.cols), tables,
        kspace, maps, target, foreground, row_mask, anatomy, first, middle_weight, last, turn_high, turn_low, pick, cosine, sine,
        fourier_high, fourier_low,
        filled, maps_out, halo_image, planes, normal, first_table, middle_tables, last_table, middle_back, last_back, counted,
        fields, staged, spread, flat, landed, edges, loaded, send, receive, own, send_flat, receive_flat, send_edge, receive_edge,
    )

    def band(layer, batch):
        return lin.at[batch, lax.rem(layer, 2)]

    def save(layer, batch):
        kept = band(layer, batch).at[pl.ds(FIRST_REACH - BACK_REACH, width + 2 * BACK_REACH)]
        return pltpu.make_async_copy(kept, layers.at[layer, batch], saved.at[layer, batch])

    def begin(layer, batch, not_first):
        if not_first:
            save(layer - 1, batch).wait()
        moments = jnp.concatenate([total[...], square[...]], axis=0).T
        moments = jnp.sum(moments, axis=0, keepdims=True)
        delta = moments[:, :channels] / count
        spread = moments[:, channels:] - count * delta * delta
        centre = pivot[...].T[0:1]
        sums.start((layer, batch), 0, padded_rows([count * (centre + delta), spread, counted[:, :channels]]))
        save(layer, batch).start()

    def join(blocks, number):
        blocks = [block[:, :channels] for block in blocks]
        added, spread = merge([block[0:1] for block in blocks], [block[1:2] for block in blocks], number)
        return added, spread, functools.reduce(jnp.add, [block[2:3] for block in blocks])

    def middle(layer, batch):
        joined = join(sums.collect((layer, batch), 0), count)
        sums.start((layer, batch), 1, padded_rows(joined))

    def end(layer, batch):
        added, spread, plain = join(sums.collect((layer, batch), 1), count * parts)
        pixels = count * parts * images
        gain, shift = gains[pl.ds(layer, 1), :], shifts[pl.ds(layer, 1), :]
        inverse = lax.rsqrt(spread / pixels + EPS_NORM)
        offset = -(added / pixels) * inverse
        coefs[layer, batch, 0] = spread_row(0.5 * gain * inverse)
        coefs[layer, batch, 1] = spread_row(0.5 * (shift + gain * offset))
        coefs[layer, batch, 2] = spread_row(inverse)
        coefs[layer, batch, 3] = spread_row(offset)
        rows_out[layer, batch] = join_rows([gain, shift, inverse, offset, plain], 8)

    def keeper(out, reach):
        held = []

        def emit(column, value):
            column = column - reach
            out[FIRST_REACH + column] = value
            if not 0 <= column < width:
                return
            if column == 0:
                mean = jnp.sum(clear(value), axis=1, keepdims=True) / length
                pivot[...] = jnp.broadcast_to(mean, pivot.shape)
            if column % BLOCK == 0:
                held[:] = [jnp.zeros((channels, TILE), F32), jnp.zeros((channels, TILE), F32)]
            centre = pivot[...]
            for at in range(0, wide, TILE):
                shift = value[:, at : at + TILE] - centre
                if at >= whole:
                    lane = lax.broadcasted_iota(jnp.int32, shift.shape, 1)
                    shift = jnp.where(lane < length - at, shift, 0.0)
                held[0] = held[0] + shift
                held[1] = held[1] + shift * shift
            if column == BLOCK - 1:
                total[...], square[...] = held
            elif column % BLOCK == BLOCK - 1:
                total[...] += held[0]
                square[...] += held[1]

        return emit

    def first_layer(batch, hook):
        source = images_out.at[batch]
        put_image(filled.at[batch], halo_image, batch, source, ends, FIRST_REACH + 1)
        ring_pass(
            first_table[...],
            lambda couple: source[:, 2 * couple * wide : 2 * (couple + 1) * wide],
            lambda couple: None,
            keeper(band(0, batch), FIRST_REACH),
            channels,
            width + 2 * FIRST_REACH,
            wide,
            hook,
            FORWARD_HOOK,
        )

    def inner_layer(layer, batch, table, out_rows, reach, emit, hook):
        source = band(layer, batch)
        scale, offset = repeat_lanes(coefs[layer, batch, 0], wide), repeat_lanes(coefs[layer, batch, 1], wide)

        def fill(couple):
            for place in range(2):
                column = 2 * couple + place - reach - 1
                half, curve = silu_half(source[FIRST_REACH + column], scale, offset)
                active = ends.clear(clear(half * curve + half), column, width)
                put_shifted(stacks[couple % 2], active.astype(BF16), place * wide)

        ring_pass(table, lambda couple: stacks[couple % 2][...], fill, emit, out_rows, width + 2 * reach, wide, hook, FORWARD_HOOK)

    def place_of(index):
        return lax.div(index, 2), lax.rem(index, 2)

    arrive(0)
    first_layer(0, None)
    begin(0, 0, False)
    arrive(1)
    first_layer(1, lambda: middle(0, 0))
    begin(0, 1, False)
    end(0, 0)

    def layer_step(index, carried):
        layer, batch = place_of(index)
        before = place_of(index - 1)
        reach = FIRST_REACH - 1
        emit = keeper(band(layer, batch), reach)
        inner_layer(layer - 1, batch, middle_tables[layer - 1], channels, reach, emit, lambda: middle(*before))
        begin(layer, batch, True)
        end(*before)
        return carried

    lax.fori_loop(2, 8, layer_step, 0)

    def last_step(batch, carried):
        def emit(column, value):
            result[batch, 0, column : column + 1] = value[0:1]
            result[batch, 1, column : column + 1] = value[1:2]

        inner_layer(3, batch, last_table[...], 8, 0, emit, lambda: pl.when(batch == 0)(lambda: middle(3, 1)))
        pl.when(batch == 0)(lambda: end(3, 1))
        return carried

    lax.fori_loop(0, 2, last_step, 0)
    finish()
    for batch in range(2):
        save(3, batch).wait()
    for layer in range(4):
        for batch in range(2):
            sums.settle((layer, batch))


def forward(kspace, maps, target, foreground, row_mask, anatomy, first, middle, last, gains, shifts, parts, images):
    micro, coils, _, rows, length = kspace.shape
    wide = padded(length)
    channels = first.shape[2]
    cosine, sine = phases(length)
    fourier = np.zeros((wide, 2, wide))
    fourier[:length, 0, :length] = cosine
    fourier[:length, 1, :length] = sine
    fourier_high, fourier_low = np_high_low(fourier.reshape(wide, 2 * wide))
    inverse = np.stack([np.stack([cosine, sine], 0), np.stack([-sine, cosine], 0)], 0)
    turn = inverse.reshape(2, 2, length, parts, rows).transpose(0, 3, 1, 4, 2).reshape(2, 2 * length, length)
    pick = np.zeros((2, parts, 2, rows, length), np.float32)
    for part in range(2):
        for block in range(parts):
            pick[part, block, part, :, block * rows : (block + 1) * rows] = np.eye(rows)
    pick = jnp.asarray(pick.reshape(2, 2 * length, length).astype(BF16))
    turn_high, turn_low = np_high_low(turn)
    edge = ((0, wide - length), (0, wide - length))
    cosine = jnp.asarray(np.pad(cosine, edge), F32)
    sine = jnp.asarray(np.pad(sine, edge), F32)
    slots = 2 * micro
    lanes = padded(3 * micro * rows)
    shapes = [
        ((micro, 2, rows, wide), F32),
        ((micro, coils, 2 * rows, wide), BF16),
        ((micro, 3, rows, wide), F32),
        ((micro, 2 * wide, 2 * wide), BF16),
        ((3, 3 * channels, 3 * channels), BF16),
        ((3 * channels, 16), BF16),
        ((4, micro, rows + 2 * BACK_REACH, channels, wide), F32),
        ((4, micro, 4, channels, TILE), F32),
        ((4, micro, 8, channels), F32),
        ((micro, 16, (rows + 2 * FIRST_REACH + 2) * wide), BF16),
        ((micro, 2, rows, wide), F32),
    ]
    layers = (4, micro)
    return pl.pallas_call(
        functools.partial(forward_kernel, (micro, coils, rows, length, parts, images)),
        out_shape=[jax.ShapeDtypeStruct(*shape) for shape in shapes],
        in_specs=[anywhere()] * 2 + [in_vmem()] * 7 + [anywhere()] * 2 + [in_vmem()] + [anywhere()] * 4 + [in_vmem()] * 2,
        out_specs=[in_vmem()] * 6 + [anywhere()] + [in_vmem()] * 4,
        scratch_shapes=[
            pltpu.VMEM((2, 2, coils, rows, length), F32),
            pltpu.VMEM((slots, parts, 2 * rows, coils * rows), BF16),
            pltpu.VMEM((slots, parts, 2 * rows, coils * rows), BF16),
            pltpu.VMEM((parts, rows, lanes), F32),
            pltpu.VMEM((parts, rows, lanes), F32),
            pltpu.VMEM((2, micro, 2 * REACH, wide), F32),
            pltpu.VMEM((2, micro, 2 * REACH, wide), F32),
            pltpu.VMEM((3 * channels, 16), BF16),
            pltpu.VMEM((3, 3 * channels, 3 * channels), BF16),
            pltpu.VMEM((24, 3 * channels), BF16),
            pltpu.VMEM((1, TILE), F32),
            pltpu.SemaphoreType.DMA((slots, 2)),
            pltpu.SemaphoreType.DMA((slots, parts - 1)),
            pltpu.SemaphoreType.DMA((slots, parts - 1)),
            pltpu.SemaphoreType.DMA((slots,)),
            pltpu.SemaphoreType.DMA((parts - 1,)),
            pltpu.SemaphoreType.DMA((parts - 1,)),
            pltpu.SemaphoreType.DMA((micro, 2)),
            pltpu.SemaphoreType.DMA((micro, 2)),
            [pltpu.VMEM(t.shape, t.dtype) for t in (turn_high, turn_low, cosine, sine, fourier_high, fourier_low)],
            pltpu.SemaphoreType.DMA((6,)),
            pltpu.VMEM((micro, 2, rows + 2 * FIRST_REACH, channels, wide), F32),
            pltpu.VMEM((3 * channels, 2 * wide), BF16),
            pltpu.VMEM((3 * channels, 2 * wide), BF16),
            pltpu.VMEM((channels, TILE), F32),
            pltpu.VMEM((channels, TILE), F32),
            pltpu.VMEM((channels, TILE), F32),
        ]
        + Sums.scratch(layers, parts, images)
        + [pltpu.SemaphoreType.DMA(layers)],
        compiler_params=params(collective_id=1, has_side_effects=True),
        name="forward",
    )(
        kspace, maps, target, foreground, row_mask, anatomy, first, middle, last, turn_high, turn_low, pick, cosine, sine,
        fourier_high, fourier_low, gains, shifts,
    )


def backward_kernel(
    sizes, grad, halo_image, layers, coefs, rows_in, images_in, middle_back, last_back,
    first_sums, middle_sums, last_sums, rows_out,
    upper, lin, stack, thin, inputs, slope, total, along, mix, *refs,
):
    micro, parts, images, length = sizes
    _, _, width, wide = grad.shape
    channels = lin.shape[3]
    pixels = width * length * parts * images
    sums = Sums(parts, images, refs[:6])
    (loaded,) = refs[6:]
    knock(sums.rows + sums.cols)
    ends = Ends(parts)
    clear = lane_mask(length, wide)

    def load(layer, batch):
        return pltpu.make_async_copy(layers.at[layer, batch], lin.at[batch, lax.rem(layer, 2)], loaded.at[layer, batch])

    for layer in (3, 2):
        for batch in range(micro):
            load(layer, batch).start()
    first_sums[...] = jnp.zeros_like(first_sums)
    middle_sums[...] = jnp.zeros_like(middle_sums)
    last_sums[...] = jnp.zeros_like(last_sums)

    def band(layer, batch):
        return upper.at[batch, lax.rem(layer, 2)]

    def begin(layer, batch):
        added = jnp.concatenate([total[...], along[...]], axis=0).T
        added = jnp.sum(added, axis=0, keepdims=True)
        sums.start((layer, batch), 0, padded_rows([added]))

    def middle(layer, batch):
        sums.start((layer, batch), 1, functools.reduce(jnp.add, sums.collect((layer, batch), 0)))

    def end(layer, batch):
        added = functools.reduce(jnp.add, sums.collect((layer, batch), 1))
        shift_sum, gain_sum = added[0:1, :channels], added[0:1, channels:]
        rows = rows_in[layer, batch]
        gain, inverse, offset = rows[0:1], rows[2:3], rows[3:4]
        scale = inverse * gain
        mix[batch, 0] = spread_row(scale)
        mix[batch, 1] = spread_row(-scale * inverse * gain_sum / pixels)
        mix[batch, 2] = spread_row(-scale * (shift_sum + offset * gain_sum) / pixels)
        rows_out[layer, batch] = join_rows([shift_sum, gain_sum], 8)

    def place_of(index):
        return 3 - lax.div(index, 2), lax.rem(index, 2)

    def grad_putter(layer, batch):
        grads, linear = band(layer, batch), lin.at[batch, lax.rem(layer, 2)]
        on_grad, on_layer, base = (repeat_lanes(mix[batch, index], wide) for index in range(3))

        def put(column):
            at = column + BACK_REACH
            upstream = clear(on_grad * grads[at] + on_layer * linear[at] + base)
            put_shifted(stack, ends.clear(upstream, column, width).astype(BF16), at * wide)

        return put

    def add_weights(weight_out, source, reach, around, around_reach, first):
        at = first + around_reach - 1
        columns = [around[:, (at + tap) * wide : (at + tap + GROUP) * wide] for tap in range(3)]
        at = first + reach
        weight_out[...] += dot_nt(source[:, at * wide : (at + GROUP) * wide], jnp.concatenate(columns, axis=0))

    def layer_back(layer, batch, source, reach, table, weight_out, put_grad, hook):
        below = lin.at[batch, lax.rem(layer, 2)]
        out = band(layer, batch)
        scale, offset = repeat_lanes(coefs[layer, batch, 0], wide), repeat_lanes(coefs[layer, batch, 1], wide)
        inverse, centre = repeat_lanes(coefs[layer, batch, 2], wide), repeat_lanes(coefs[layer, batch, 3], wide)

        def fill(couple):
            for place in range(2):
                column = 2 * couple + place - reach - 1
                if put_grad is not None:
                    put_grad(column)
                if not -reach <= column < width + reach:
                    continue
                at = column + BACK_REACH
                half, curve = silu_half(below[at], scale, offset)
                slope[at] = 0.5 * (1.0 + curve) * (1.0 + half * (1.0 - curve))
                if -1 <= column <= width:
                    active = ends.clear(clear(half * curve + half), column, width)
                    inputs[:, (column + 1) * wide : (column + 2) * wide] = active.astype(BF16)

        held = []

        def emit(column, value):
            column = column - reach
            at = column + BACK_REACH
            shaped = clear(value * slope[at])
            out[at] = shaped
            if not 0 <= column < width:
                return
            if column % BLOCK == 0:
                held[:] = [jnp.zeros((channels, TILE), F32), jnp.zeros((channels, TILE), F32)]
            held[0] = held[0] + fold(shaped)
            held[1] = held[1] + fold(shaped * (below[at] * inverse + centre))
            if column == BLOCK - 1:
                total[...], along[...] = held
            elif column % BLOCK == BLOCK - 1:
                total[...] += held[0]
                along[...] += held[1]
            if column % GROUP == GROUP - 1:
                add_weights(weight_out, source, reach + 1, inputs, 1, column + 1 - GROUP)

        ring_pass(
            table,
            lambda couple: source[:, 2 * couple * wide : 2 * (couple + 1) * wide],
            fill,
            emit,
            channels,
            width + 2 * reach,
            wide,
            hook,
            BACK_HOOK,
        )

    def outer_step(batch, carried):
        put_image(grad.at[batch], halo_image, batch, thin, ends, BACK_REACH + 1)
        pl.when(batch == 0)(lambda: admit(sums.rows + sums.cols))
        load(3, batch).wait()
        hook = lambda: pl.when(batch > 0)(lambda: middle(3, 0))
        layer_back(3, batch, thin, BACK_REACH, last_back[...], last_sums, None, hook)
        begin(3, batch)
        pl.when(batch > 0)(lambda: end(3, 0))
        return carried

    lax.fori_loop(0, 2, outer_step, 0)

    def layer_step(index, carried):
        layer, batch = place_of(index)
        before = place_of(index - 1)
        load(layer, batch).wait()
        layer_back(
            layer,
            batch,
            stack,
            BACK_REACH - 1,
            middle_back[layer],
            middle_sums.at[layer],
            grad_putter(layer + 1, batch),
            lambda: middle(*before),
        )
        pl.when(layer > 0)(lambda: load(layer - 1, batch).start())
        begin(layer, batch)
        end(*before)
        return carried

    lax.fori_loop(2, 8, layer_step, 0)

    def first_step(batch, carried):
        put_grad = grad_putter(0, batch)
        for column in range(width):
            if column == width // 2:
                pl.when(batch == 0)(lambda: middle(0, 1))
            put_grad(column)
            if column % GROUP == GROUP - 1:
                add_weights(first_sums, stack, BACK_REACH, images_in.at[batch], FIRST_REACH + 1, column + 1 - GROUP)
        pl.when(batch == 0)(lambda: end(0, 1))
        return carried

    lax.fori_loop(0, 2, first_step, 0)
    for layer in range(4):
        for batch in range(2):
            sums.settle((layer, batch))


def backward(grad, halo, kept, tables, parts, images, length):
    layers, coefs, rows_in, images_in = kept
    micro, _, width, wide = grad.shape
    channels = layers.shape[3]
    band = (micro, 2, width + 2 * BACK_REACH, channels, wide)
    lanes = (width + 2 * BACK_REACH) * wide
    shapes = [(3 * channels, 48), (3, 3 * channels, 3 * channels), (16, 3 * channels), (4, micro, 8, channels)]
    slots = (4, micro)
    return pl.pallas_call(
        functools.partial(backward_kernel, (micro, parts, images, length)),
        out_shape=[jax.ShapeDtypeStruct(shape, F32) for shape in shapes],
        in_specs=[in_vmem(), in_vmem(), anywhere()] + [in_vmem()] * 5,
        out_specs=[in_vmem()] * 4,
        scratch_shapes=[
            pltpu.VMEM(band, F32),
            pltpu.VMEM(band, F32),
            pltpu.VMEM((3 * channels, lanes), BF16),
            pltpu.VMEM((16, lanes + 2 * wide), BF16),
            pltpu.VMEM((channels, (width + 2) * wide), BF16),
            pltpu.VMEM(band[2:], F32),
            pltpu.VMEM((channels, TILE), F32),
            pltpu.VMEM((channels, TILE), F32),
            pltpu.VMEM((micro, 3, channels, TILE), F32),
        ]
        + Sums.scratch(slots, parts, images)
        + [pltpu.SemaphoreType.DMA(slots)],
        compiler_params=params(collective_id=3, has_side_effects=True),
        name="backward",
    )(grad, halo, layers, coefs, rows_in, images_in, *tables)


def reduce_kernel(parts, images, first_sums, middle_sums, last_sums, scalars, first_grad, middle_grad, last_grad, totals, whole, final, quarter, landed, eighth, landed_rows, send, receive):
    image, me = lax.axis_index("img"), lax.axis_index("row")
    rows, cols = row_peers(parts), image_peers(images)
    knock(rows + cols)
    channels = middle_sums.shape[1] // 3
    taps = [(kr, kw) for kr in range(3) for kw in range(3)]
    pieces = [
        middle_sums[layer, (2 - kr) * channels : (3 - kr) * channels, kw * channels : (kw + 1) * channels]
        for layer in range(3)
        for kr, kw in taps
    ]
    firsts = [first_sums[(2 - kr) * channels : (3 - kr) * channels, 16 * kw + 2 : 16 * kw + 4] for kr, kw in taps]
    pieces.append(join_lanes(firsts, channels))
    for index in range(0, len(pieces), 2):
        at = index // 2 * channels
        whole[at : at + channels] = jnp.concatenate(pieces[index : index + 2], axis=1)
    at = len(pieces) // 2 * channels
    lasts = [last_sums[2 * (2 - kr) : 2 * (3 - kr), kw * channels : (kw + 1) * channels] for kr, kw in taps]
    added = functools.reduce(jnp.add, [scalars[batch] for batch in range(scalars.shape[0])])
    whole[at : at + 24] = jnp.concatenate([join_rows(lasts, 24), join_rows([added[:, :channels]], 24)], axis=1)
    whole[at + 24 :] = jnp.zeros((whole.shape[0] - at - 24, TILE), F32)
    admit(rows + cols)
    big, small = quarter.shape[0], eighth.shape[0]
    images_here, parts_here = len(cols), len(rows)

    def place(index, size):
        return pl.ds(pl.multiple_of(index * size, 8), size)

    sent = []
    for index, peer in enumerate(cols):
        copy = remote(whole.at[place(peer[0], big)], landed.at[index], send.at[index], receive.at[index], peer)
        copy.start()
        sent.append(copy)
    for copy in sent:
        copy.wait_recv()
    total = whole[place(image, big)]
    for index in range(images_here):
        total = total + landed[index]
    quarter[...] = total
    base = images_here
    arrived = []
    for index, peer in enumerate(rows):
        copy = remote(
            quarter.at[place(peer[1], small)], landed_rows.at[index], send.at[base + index], receive.at[base + index], peer
        )
        copy.start()
        arrived.append(copy)
    for copy in arrived:
        copy.wait_recv()
    total = quarter[place(me, small)]
    for index in range(parts_here):
        total = total + landed_rows[index]
    eighth[...] = total
    for copy in sent + arrived:
        copy.wait_send()
    base += parts_here
    returned = []
    mine = pl.ds(pl.multiple_of(image * big + me * small, 8), small)
    for index, peer in enumerate(rows):
        copy = remote(eighth, final.at[mine], send.at[base + index], receive.at[base + index], peer)
        copy.start()
        returned.append(copy)
    final[mine] = total
    for copy in returned:
        copy.wait()
    base += parts_here
    returned = []
    for index, peer in enumerate(cols):
        copy = remote(final.at[place(image, big)], final.at[place(image, big)], send.at[base + index], receive.at[base + index], peer)
        copy.start()
        returned.append(copy)
    for copy in returned:
        copy.wait()
    for index in range(27):
        from_row = index // 2 * channels
        from_lane = index % 2 * channels
        middle_grad[index // 9, index % 9] = final[from_row : from_row + channels, from_lane : from_lane + channels]
    turned = final[13 * channels : 14 * channels, channels:].T
    for tap in range(9):
        first_grad[tap] = turned[2 * tap : 2 * tap + 2]
        last_grad[tap] = final[at + 2 * tap : at + 2 * tap + 2, :channels]
    totals[...] = final[at : at + 8, channels:]


def reduce_all(first_sums, middle_sums, last_sums, scalars, parts, images):
    channels = middle_sums.shape[1] // 3
    unit = 8 * parts * images
    height = -(-(14 * channels + 24) // unit) * unit
    copies = 2 * (parts + images - 2)
    shapes = [(9, 2, channels), (3, 9, channels, channels), (9, 2, channels), (8, channels)]
    return pl.pallas_call(
        functools.partial(reduce_kernel, parts, images),
        out_shape=[jax.ShapeDtypeStruct(shape, F32) for shape in shapes],
        in_specs=[in_vmem()] * 4,
        out_specs=[in_vmem()] * 4,
        scratch_shapes=[
            pltpu.VMEM((height, TILE), F32),
            pltpu.VMEM((height, TILE), F32),
            pltpu.VMEM((height // images, TILE), F32),
            pltpu.VMEM((images - 1, height // images, TILE), F32),
            pltpu.VMEM((height // images // parts, TILE), F32),
            pltpu.VMEM((parts - 1, height // images // parts, TILE), F32),
            pltpu.SemaphoreType.DMA((copies,)),
            pltpu.SemaphoreType.DMA((copies,)),
        ],
        compiler_params=params(collective_id=4, has_side_effects=True),
        name="reduce_all",
    )(first_sums, middle_sums, last_sums, scalars)


def apply_normal(image, maps, normal, diagonal):
    coils, slabs, wide = maps.shape
    rows = slabs // 2
    real, imag = image
    stack, power = [], jnp.zeros((rows, wide), F32)
    for coil in range(coils):
        sense = maps[coil].astype(F32)
        sense_re, sense_im = sense[:rows], sense[rows:]
        power = power + sense_re * sense_re + sense_im * sense_im
        field = [sense_re * real - sense_im * imag, sense_re * imag + sense_im * real]
        stack.append(jnp.concatenate(field, axis=1))
    stack = jnp.concatenate(stack, axis=0).astype(BF16)
    power = diagonal * power
    out_re, out_im = power * real, power * imag
    turned = dot(stack, normal[...])
    for coil in range(coils):
        sense = maps[coil].astype(F32)
        sense_re, sense_im = sense[:rows], sense[rows:]
        field = turned[coil * rows : (coil + 1) * rows]
        field_re, field_im = field[:, :wide], field[:, wide:]
        out_re = out_re + sense_re * field_re + sense_im * field_im
        out_im = out_im + sense_re * field_im - sense_im * field_re
    return out_re, out_im


def pair(ref):
    return ref[0], ref[1]


def put_pair(ref, values):
    ref[0] = values[0]
    ref[1] = values[1]


def blend(*terms):
    return tuple(functools.reduce(jnp.add, [factor * image[part] for factor, image in terms]) for part in range(2))


def inner_of(left, right):
    product = left[0] * right[0] + left[1] * right[1]
    return jnp.sum(jnp.sum(product, axis=1, keepdims=True), axis=0, keepdims=True)


class RowSums:
    def __init__(self, parts, refs):
        self.message, self.held, self.send, self.receive = refs
        self.peers = row_peers(parts)

    def copies(self, slot):
        return [
            remote(
                self.message.at[slot],
                self.held.at[slot + (index,)],
                self.send.at[slot + (index,)],
                self.receive.at[slot + (index,)],
                peer,
            )
            for index, peer in enumerate(self.peers)
        ]

    def start(self, slot, values):
        filler = [jnp.zeros((1, TILE), F32)] * (8 - len(values))
        self.message[slot] = jnp.concatenate([jnp.broadcast_to(value, (1, TILE)) for value in values] + filler, axis=0)
        for copy in self.copies(slot):
            copy.start()

    def finish(self, slot):
        total = self.message[slot]
        for index, copy in enumerate(self.copies(slot)):
            copy.wait_recv()
            total = total + self.held[slot + (index,)]
        return [total[index : index + 1, 0:1] for index in range(8)]

    def settle(self, slot):
        for copy in self.copies(slot):
            copy.wait_send()


def solve_kernel(
    sizes, filled, result, maps, normal, planes, rows_in, row_mask, extra, grad_out, halo, scalars,
    work, edges, send_edge, receive_edge, *refs,
):
    micro, parts, length = sizes
    _, _, rows, wide = filled.shape
    sums = RowSums(parts, refs)
    knock(sums.peers)
    moved = []
    inside = lax.broadcasted_iota(jnp.int32, (rows, wide), 1) < length
    penalty = jnp.exp(jnp.full((1, 1), extra[2], F32))
    inv_count = 1.0 / rows_in[0, 0, 4:5, 0:1]
    diagonals = [jnp.sum(row_mask[batch].astype(F32), axis=1, keepdims=True) / length for batch in range(micro)]
    names = ("denoised", "right", "mapped", "residue", "through", "search", "searched", "slope")

    def at(name, batch):
        return work.at[batch, names.index(name)]

    def get(name, batch):
        return pair(at(name, batch))

    def through_normal(image, batch):
        out = apply_normal(image, maps.at[batch], normal.at[batch], diagonals[batch])
        return blend((1.0, out), (penalty, image))

    for batch in range(micro):
        images = []
        for part in range(2):
            value = filled[batch, part] + result[batch, part] + jnp.full((1, 1), extra[part], F32)
            value = jnp.where(inside, value, 0.0)
            at("denoised", batch)[part] = value
            images.append(filled[batch, part] + penalty * value)
        put_pair(at("right", batch), images)
        mapped = through_normal(images, batch)
        put_pair(at("mapped", batch), mapped)
        if batch == 0:
            admit(sums.peers)
        sums.start((0, batch), [inner_of(images, images), inner_of(images, mapped)])
    ones, twos = [], []
    for batch in range(micro):
        ones.append(sums.finish((0, batch)))
        start, image = get("right", batch), get("mapped", batch)
        left_over = blend((1.0, start), (-ones[batch][0] / ones[batch][1], image))
        put_pair(at("residue", batch), left_over)
        mapped = through_normal(left_over, batch)
        put_pair(at("through", batch), mapped)
        sums.start(
            (1, batch),
            [
                inner_of(left_over, left_over),
                inner_of(left_over, mapped),
                inner_of(left_over, image),
                inner_of(start, mapped),
            ],
        )
    kept = []
    for batch in range(micro):
        twos.append(sums.finish((1, batch)))
        norm_0, curve_0 = ones[batch][:2]
        norm_1 = twos[batch][0]
        factor = norm_1 / norm_0
        curve_1 = twos[batch][1] + factor * (twos[batch][2] + twos[batch][3]) + factor * factor * curve_0
        start, image = get("right", batch), get("mapped", batch)
        direction = blend((1.0, get("residue", batch)), (factor, start))
        image_1 = blend((1.0, get("through", batch)), (factor, image))
        put_pair(at("searched", batch), image_1)
        state = blend((norm_0 / curve_0, start), (norm_1 / curve_1, direction))
        weight = planes[batch, 2]
        difference = [state[part] - planes[batch, part] for part in range(2)]
        grad = [inv_count * 2.0 * weight * difference[part] for part in range(2)]
        put_pair(at("slope", batch), grad)
        masked = [weight * difference[part] for part in range(2)]
        sums.start(
            (2, batch),
            [
                inner_of(grad, direction),
                inner_of(grad, start),
                inner_of(grad, image),
                inner_of(image_1, start),
                inner_of(image_1, image),
            ],
        )
        kept.append((norm_0, curve_0, norm_1, curve_1, factor, inner_of(direction, direction), inner_of(masked, difference)))
    for batch in range(micro):
        grad_search, grad_start, grad_image, cross_start, cross_image = sums.finish((2, batch))[:5]
        norm_0, curve_0, norm_1, curve_1, factor, own_search, own_loss = kept[batch]
        step_0, step_1 = norm_0 / curve_0, norm_1 / curve_1
        start, image, left_over = get("right", batch), get("mapped", batch), get("residue", batch)
        image_1, grad = get("searched", batch), get("slope", batch)
        residue_image = twos[batch][2]
        curve_grad_1 = -grad_search * norm_1 / (curve_1 * curve_1)
        norm_grad_1 = grad_search / curve_1
        search_grad = blend((step_1, grad), (2.0 * curve_grad_1, image_1))
        factor_grad = step_1 * grad_start + 2.0 * curve_grad_1 * cross_start
        joint = step_1 * grad_image + 2.0 * curve_grad_1 * cross_image
        norm_total = norm_grad_1 + factor_grad / norm_0
        residue_full = blend((1.0, search_grad), (2.0 * norm_total, left_over))
        step_grad = grad_start - (joint + 2.0 * norm_total * residue_image)
        curve_grad_0 = -step_grad * norm_0 / (curve_0 * curve_0)
        mapped_grad = blend((-step_0, residue_full), (curve_grad_0, start))
        through = through_normal(mapped_grad, batch)
        norm_grad_0 = -factor_grad * norm_1 / (norm_0 * norm_0) + step_grad / curve_0
        right_grad = blend(
            (1.0, residue_full),
            (factor, search_grad),
            (step_0, grad),
            (curve_grad_0, image),
            (1.0, through),
            (2.0 * norm_grad_0, start),
        )
        penalty_part = (
            curve_grad_1 * own_search + inner_of(mapped_grad, start) + inner_of(right_grad, get("denoised", batch))
        )
        grad_pair = [penalty * right_grad[part] for part in range(2)]
        put_pair(grad_out.at[batch], grad_pair)
        put_edges(edges.at[:, batch], *grad_pair)
        for copy in image_halo(parts, batch, edges, halo, send_edge, receive_edge):
            copy.start()
            moved.append(copy)
        offsets = [jnp.sum(jnp.sum(grad_pair[part], axis=1, keepdims=True), axis=0, keepdims=True) for part in range(2)]
        values = [offsets[0], offsets[1], penalty * penalty_part, own_loss]
        scalars[batch] = join_rows([jnp.broadcast_to(value, (1, TILE)) for value in values], 8)
    for stage in range(3):
        for batch in range(micro):
            sums.settle((stage, batch))
    for copy in moved:
        copy.wait()


def solve_all(filled, result, maps, normal, planes, rows_in, row_mask, extra, parts, length):
    micro, _, rows, wide = filled.shape
    shapes = [(micro, 2, rows, wide), (2, micro, 2 * REACH, wide), (micro, 8, TILE)]
    slots = (3, micro)
    return pl.pallas_call(
        functools.partial(solve_kernel, (micro, parts, length)),
        out_shape=[jax.ShapeDtypeStruct(shape, F32) for shape in shapes],
        in_specs=[in_vmem()] * 7 + [pl.BlockSpec(memory_space=pltpu.SMEM)],
        out_specs=[in_vmem()] * 3,
        scratch_shapes=[
            pltpu.VMEM((micro, 8, 2, rows, wide), F32),
            pltpu.VMEM((2, micro, 2 * REACH, wide), F32),
            pltpu.SemaphoreType.DMA((micro, 2)),
            pltpu.SemaphoreType.DMA((micro, 2)),
            pltpu.VMEM(slots + (8, TILE), F32),
            pltpu.VMEM(slots + (parts - 1, 8, TILE), F32),
            pltpu.SemaphoreType.DMA(slots + (parts - 1,)),
            pltpu.SemaphoreType.DMA(slots + (parts - 1,)),
        ],
        compiler_params=params(collective_id=5, has_side_effects=True),
        name="solve_all",
    )(filled, result, maps, normal, planes, rows_in, row_mask, extra)


def update_kernel(weights, means, squares, grads, rows_back, totals, rows_in, outs):
    first_grad, middle_grad, last_grad = grads
    affine = []
    for row in (1, 0):
        rows = [functools.reduce(jnp.add, [rows_back[layer, batch, row : row + 1] for batch in range(rows_back.shape[1])]) for layer in range(4)]
        affine.append(jnp.concatenate(rows, axis=0))
    extra = join_lanes([totals[index : index + 1, 0:1] for index in range(3)], 3)

    def put(group, at, gradient, refs):
        results = adamw(weights[group][at], gradient, means[group][at], squares[group][at], LEARN_RATES[group])
        for ref, value in zip(refs, results + (results[0].astype(BF16),)):
            ref[at] = value

    everything = (slice(None), slice(None))
    for tap in range(9):
        put(0, tap, first_grad[tap], outs[0:4])
        put(2, tap, last_grad[tap], outs[8:12])
        for layer in range(3):
            put(1, (layer, tap), middle_grad[layer, tap], outs[4:8])
    put(3, everything, affine[0], outs[12:15])
    put(4, everything, affine[1], outs[15:18])
    put(5, everything, extra, outs[18:21])
    outs[21][...] = totals[3:4, 0:1]
    outs[22][...] = rows_in[0, 0, 4:5, 0:1].astype(jnp.int32)


def update(weights, means, squares, grads, rows_back, totals, rows_in):
    shapes = []
    for group, weight in enumerate(weights):
        shapes += [jax.ShapeDtypeStruct(weight.shape, F32)] * 3
        if group < 3:
            shapes.append(jax.ShapeDtypeStruct(weight.shape, BF16))
    shapes += [jax.ShapeDtypeStruct((1, 1), F32), jax.ShapeDtypeStruct((1, 1), jnp.int32)]

    def kernel(*refs):
        update_kernel(refs[0:6], refs[6:12], refs[12:18], refs[18:21], refs[21], refs[22], refs[23], refs[24:])

    return pl.pallas_call(
        kernel,
        out_shape=shapes,
        in_specs=[in_vmem()] * 24,
        out_specs=[in_vmem()] * len(shapes),
        compiler_params=params(),
        name="update",
    )(*weights, *means, *squares, *grads, rows_back, totals, rows_in)


def fast_step(arrays, moments):
    (
        kspace, coil_maps, target, row_mask, foreground, anatomy, first_weight, middle_weight, last_weight, norm_gains, norm_shifts, extra_params,
    ) = arrays
    length = kspace.shape[-1]
    parts, images = lax.axis_size("row"), lax.axis_size("img")
    filled, maps, planes, normal, middle_back, last_back, layers, coefs, rows_out, images_out, result = forward(
        kspace[:, 0], coil_maps[:, 0], target[:, 0], foreground[:, 0], row_mask, anatomy.transpose(1, 0),
        first_weight.transpose(0, 2, 1), middle_weight, last_weight, norm_gains, norm_shifts, parts, images,
    )
    grad, halo, scalars = solve_all(
        filled, result, maps, normal, planes, rows_out, row_mask, extra_params, parts, length
    )
    first_sums, middle_sums, last_sums, rows_back = backward(
        grad, halo, (layers, coefs, rows_out, images_out), (middle_back, last_back), parts, images, length
    )
    *grads, totals = reduce_all(first_sums, middle_sums, last_sums, scalars, parts, images)

    def turn(group):
        first, middle, last, gains, shifts, extra = group
        return [first.transpose(0, 2, 1), middle, last, gains, shifts, extra.reshape(1, 3)]

    weights = (first_weight, middle_weight, last_weight, norm_gains, norm_shifts, extra_params)
    means, squares = zip(*moments)
    outs = list(update(turn(weights), turn(means), turn(squares), grads, rows_back, totals, rows_out))
    outs[0:4] = [value.transpose(0, 2, 1) for value in outs[0:4]]
    outs[18:21] = [value.reshape(3) for value in outs[18:21]]
    return tuple(outs[:21]) + (outs[21].reshape(()), outs[22].reshape(()))


def local(
    kspace,
    coil_maps,
    target,
    row_mask,
    foreground,
    anatomy,
    first_weight,
    middle_weight,
    last_weight,
    norm_gains,
    norm_shifts,
    extra_params,
    first_mean,
    first_square,
    middle_mean,
    middle_square,
    last_mean,
    last_square,
    gains_mean,
    gains_square,
    shifts_mean,
    shifts_square,
    extra_mean,
    extra_square,
):
    arrays = (
        kspace, coil_maps, target, row_mask, foreground, anatomy, first_weight, middle_weight, last_weight, norm_gains, norm_shifts, extra_params,
    )
    moments = (
        (first_mean, first_square),
        (middle_mean, middle_square),
        (last_mean, last_square),
        (gains_mean, gains_square),
        (shifts_mean, shifts_square),
        (extra_mean, extra_square),
    )
    if fits(kspace, first_weight, lax.axis_size("row")):
        return fast_step(arrays, moments)
    totals, pixel_total = general_local(arrays)
    params = (first_weight, middle_weight, last_weight, norm_gains, norm_shifts, extra_params)
    results = []
    for group in range(6):
        updated, first_new, second_new = adamw(
            params[group], totals[group], moments[group][0], moments[group][1], LEARN_RATES[group]
        )
        results.extend([updated, first_new, second_new])
        if group < 3:
            results.append(updated.astype(jnp.bfloat16))
    return tuple(results) + (totals[6], pixel_total.astype(jnp.int32))


def solution(mesh):
    in_specs = (
        P(None, "img", None, None, "row", None),
        P(None, "img", None, None, "row", None),
        P(None, "img", None, "row", None),
        P(None, "img", None),
        P(None, "img", "row", None),
        P(None, "img"),
        P(),
        P(),
        P(),
        P(),
        P(),
        P(),
        P(),
        P(),
        P(),
        P(),
        P(),
        P(),
        P(),
        P(),
        P(),
        P(),
        P(),
        P(),
    )
    out_specs = (
        P(),
        P(),
        P(),
        P(),
        P(),
        P(),
        P(),
        P(),
        P(),
        P(),
        P(),
        P(),
        P(),
        P(),
        P(),
        P(),
        P(),
        P(),
        P(),
        P(),
        P(),
        P(),
        P(),
    )
    return jax.shard_map(local, mesh=mesh, in_specs=in_specs, out_specs=out_specs, check_vma=False)
```
